32 devices in a mesh: dp: 8 (over y, x, core), tensor: 4 (over z).
Axes of the slice: x: 2, y: 2, z: 4, core: 2. Of those that a mesh axis runs over, the one named last changes fastest.
Arguments:
- tokens: bfloat16 [8192, 1024], P(('dp', 'tensor')), may hold values from -6 to 6
- encoder_states: bfloat16 [16384, 1024], P('dp'), may hold values from -6 to 6
- tok_lengths: int32 [8, 4], P('dp'), may hold values from 1 to 512, 1024 in all within a row
- enc_lengths: int32 [8, 4], P('dp'), may hold values from 1 to 1024, 2048 in all within a row
- pad_mask: int32 [8192], P('dp'), may hold values 0 or 1
- first_gain: float32 [1024], replicated, may hold values from 0.5 to 1.5
- first_shift: float32 [1024], replicated, may hold values from -1.5 to 1.5
- causal_query: bfloat16 [1024, 1024], P(None, 'tensor'), may hold values from -0.1875 to 0.1875
- causal_key: bfloat16 [1024, 1024], P(None, 'tensor'), may hold values from -0.1875 to 0.1875
- causal_value: bfloat16 [1024, 1024], P(None, 'tensor'), may hold values from -0.1875 to 0.1875
- causal_out: bfloat16 [1024, 1024], P('tensor'), may hold values from -1.5 to 1.5
- second_gain: float32 [1024], replicated, may hold values from 0.5 to 1.5
- second_shift: float32 [1024], replicated, may hold values from -1.5 to 1.5
- cross_query: bfloat16 [1024, 1024], P(None, 'tensor'), may hold values from -0.1875 to 0.1875
- cross_key: bfloat16 [1024, 1024], P(None, 'tensor'), may hold values from -0.1875 to 0.1875
- cross_value: bfloat16 [1024, 1024], P(None, 'tensor'), may hold values from -0.1875 to 0.1875
- cross_out: bfloat16 [1024, 1024], P('tensor'), may hold values from -1.5 to 1.5
- third_gain: float32 [1024], replicated, may hold values from 0.5 to 1.5
- third_shift: float32 [1024], replicated, may hold values from -1.5 to 1.5
- expand_weight: bfloat16 [1024, 4096], P(None, 'tensor'), may hold values from -0.1875 to 0.1875
- reduce_weight: bfloat16 [4096, 1024], P('tensor'), may hold values from -0.125 to 0.125
- cotangent: bfloat16 [8192, 1024], P(('dp', 'tensor')), may hold values from -6 to 6
Outputs:
- output: bfloat16 [8192, 1024], P(('dp', 'tensor'))
- tokens_grad: bfloat16 [8192, 1024], P(('dp', 'tensor'))
- encoder_grad: bfloat16 [16384, 1024], P(('dp', 'tensor'))
- first_gain_grad: float32 [1024], replicated
- first_shift_grad: float32 [1024], replicated
- causal_query_grad: float32 [1024, 1024], P(None, 'tensor')
- causal_key_grad: float32 [1024, 1024], P(None, 'tensor')
- causal_value_grad: float32 [1024, 1024], P(None, 'tensor')
- causal_out_grad: float32 [1024, 1024], P('tensor')
- second_gain_grad: float32 [1024], replicated
- second_shift_grad: float32 [1024], replicated
- cross_query_grad: float32 [1024, 1024], P(None, 'tensor')
- cross_key_grad: float32 [1024, 1024], P(None, 'tensor')
- cross_value_grad: float32 [1024, 1024], P(None, 'tensor')
- cross_out_grad: float32 [1024, 1024], P('tensor')
- third_gain_grad: float32 [1024], replicated
- third_shift_grad: float32 [1024], replicated
- expand_weight_grad: float32 [1024, 4096], P(None, 'tensor')
- reduce_weight_grad: float32 [4096, 1024], P('tensor')
The draws below stay inside these ranges and needn't reach their ends.
Inputs may be any that keep to these rules, and one draw needn't show every extreme that they name: `tok_lengths`: each row sums to 1024; its largest entry is exactly 512. `enc_lengths`: each row sums to 2048; its largest entry is exactly 1024.
All inputs are finite; a program needn't handle non-finite values. No bound on the sum of `pad_mask` on one device may be relied on, other than what follows from the above.
Results may differ from the reference program's by a relative error of at most 0.03.
Values may be sent and summed in bfloat16 or wider, within the bound.
A program may use at most 192 MiB of HBM per device.

```python
import math
import jax
import jax.numpy as jnp
import numpy as np
from jax import lax

D = 1024
HEADS = 16
HEAD_DIM = 64
FF = 4096
TOK_DEV = 1024
ENC_DEV = 2048
UTT_DEV = 4
SLOTS = 8
TOKENS = 8192
ENC_TOKENS = 16384


def set_ends(values, stream_key, least, top_value):
    spot = [jax.random.randint(jax.random.fold_in(stream_key, axis), (), 0, length) for axis, length in enumerate(values.shape)]
    longest = values.shape.index(max(values.shape))
    beside = spot[:longest] + [(spot[longest] + 1) % values.shape[longest]] + spot[longest + 1:]
    return values.at[tuple(spot)].set(least).at[tuple(beside)].set(top_value)


def shard_levels(stream_key, shape, pieces, smallest, high):
    def one(axis_at, parts):
        draws = jax.random.uniform(jax.random.fold_in(jax.random.fold_in(stream_key, 6), axis_at), (parts,), jnp.float32, smallest / len(pieces), high / len(pieces))
        return jnp.repeat(jnp.exp(draws), shape[axis_at] // parts).reshape((-1,) + (1,) * (len(shape) - axis_at - 1))

    level = one(*pieces[0])
    for cut in pieces[1:]:
        level = level * one(*cut)
    return level


def split_up(count, total, most, skew):
    weights = [(1 << 20) // math.isqrt(grade ** skew) + 1 for grade in range(2, count + 1)]
    spare, holding = total - most - (count - 1), [1] * (count - 1)
    while spare > 0:
        movable = [i for i in range(count - 1) if holding[i] < most]
        mass, remaining = sum([weights[i] for i in movable]), spare
        for i in movable:
            extra = min(most - holding[i], max(1, remaining * weights[i] // mass), spare)
            holding[i] = holding[i] + extra
            spare = spare - extra
    return np.array([most] + holding)


def uneven_parts(key, number_of, total, most, lean):
    if number_of == 2:
        one = jax.random.randint(key, (), max(1, total - most), min(most, total - 1) + 1)
        return jnp.stack([one, total - one])
    tallies = jnp.asarray(split_up(number_of, total, most, lean), jnp.int32)
    couples = (number_of - 1) // 2
    giver, sink = tallies[1:1 + 2 * couples:2], tallies[2:2 + 2 * couples:2]
    slack = jnp.minimum(giver - 1, most - sink)
    moved = jax.random.randint(jax.random.fold_in(key, 1), (couples,), 0, 1 << 20) % (slack + 1)
    tallies = tallies.at[1:1 + 2 * couples:2].set(giver - moved).at[2:2 + 2 * couples:2].set(sink + moved)
    return tallies[jax.random.permutation(jax.random.fold_in(key, 2), number_of)]


def noise(stream_key, dims, scale, bound, split=(), held_as=jnp.bfloat16):
    values = jax.random.normal(stream_key, dims, jnp.float32) * scale
    if len(split) > 0:
        values = shard_levels(stream_key, dims, split, -0.22, 0.18) * values
    return jnp.clip(values, min=-bound, max=bound).astype(held_as)


def setup_inputs(seed: int = 0) -> dict:
    streams_of = jax.random.split(jax.random.key(seed), 23)
    return {
        "tokens": noise(streams_of[0], (TOKENS, D), 1.0, 6.0, ((0, 32),)),
        "encoder_states": noise(streams_of[1], (ENC_TOKENS, D), 1.0, 6.0, ((0, 8),)),
        "tok_lengths": jax.vmap(lambda own: uneven_parts(own, UTT_DEV, TOK_DEV, TOK_DEV // 2, 2))(jax.random.split(streams_of[2], SLOTS)).reshape((SLOTS, UTT_DEV)).astype(jnp.int32),
        "enc_lengths": jax.vmap(lambda own: uneven_parts(own, UTT_DEV, ENC_DEV, ENC_DEV // 2, 2))(jax.random.split(streams_of[3], SLOTS)).reshape((SLOTS, UTT_DEV)).astype(jnp.int32),
        "pad_mask": set_ends((jax.random.randint(streams_of[4], (TOKENS,), 0, 8) < 7).astype(jnp.int32), jax.random.fold_in(streams_of[4], 1), 0, 1),
        "first_gain": jnp.clip(1.0 + 0.1 * jax.random.normal(streams_of[5], (D,), jnp.float32), 0.5, 1.5),
        "first_shift": noise(streams_of[6], (D,), 0.3, 1.5, (), jnp.float32),
        "causal_query": noise(streams_of[7], (D, D), D ** -0.5, 0.1875, ((1, 4),)),
        "causal_key": noise(streams_of[8], (D, D), D ** -0.5, 0.1875, ((1, 4),)),
        "causal_value": noise(streams_of[9], (D, D), D ** -0.5, 0.1875, ((1, 4),)),
        "causal_out": noise(streams_of[10], (D, D), (max(D // 64, 1)) ** -0.5, 1.5, ((0, 4),)),
        "second_gain": jnp.clip(1.0 + 0.1 * jax.random.normal(streams_of[11], (D,), jnp.float32), 0.5, 1.5),
        "second_shift": noise(streams_of[12], (D,), 0.3, 1.5, (), jnp.float32),
        "cross_query": noise(streams_of[13], (D, D), D ** -0.5, 0.1875, ((1, 4),)),
        "cross_key": noise(streams_of[14], (D, D), D ** -0.5, 0.1875, ((1, 4),)),
        "cross_value": noise(streams_of[15], (D, D), D ** -0.5, 0.1875, ((1, 4),)),
        "cross_out": noise(streams_of[16], (D, D), (max(D // 64, 1)) ** -0.5, 1.5, ((0, 4),)),
        "third_gain": jnp.clip(1.0 + 0.1 * jax.random.normal(streams_of[17], (D,), jnp.float32), 0.5, 1.5),
        "third_shift": noise(streams_of[18], (D,), 0.3, 1.5, (), jnp.float32),
        "expand_weight": noise(streams_of[19], (D, FF), D ** -0.5, 0.1875, ((1, 4),)),
        "reduce_weight": noise(streams_of[20], (FF, D), (FF // 2) ** -0.5, 0.125, ((0, 4),)),
        "cotangent": noise(streams_of[21], (TOKENS, D), 1.0, 6.0, ((0, 32),)),
    }


@jax.custom_vjp
def low(v):
    return lax.optimization_barrier(v.astype(jnp.bfloat16)).astype(jnp.float32)

@jax.custom_vjp
def low_back(v):
    return v

def low_keep(v):
    return (low(v), None)

def low_pass(kept, grad):
    return (grad,)

def back_keep(v):
    return (v, None)

def back_low(kept, grad):
    return (low(grad),)
low.defvjp(low_keep, low_pass)
low_back.defvjp(back_keep, back_low)

def rounded_both(value):
    return low(low_back(value))

def highest(left, right):
    return jnp.dot(left, right, precision=lax.Precision.HIGHEST)

def smooth_gate(values):
    inner = jnp.tanh(0.7978845608 * (values + 0.044715 * values * values * values))
    return 0.5 * values * (1.0 + inner)

def normalize(rows, gain, shift):
    centred = rows - lax.optimization_barrier(jnp.mean(rows, axis=-1, keepdims=True))
    inverse = lax.rsqrt(lax.optimization_barrier(jnp.mean(centred * centred, axis=-1, keepdims=True)) + 1e-05)
    return centred * inverse * gain + shift

def segment_ids(lengths, count):
    ends = jnp.cumsum(lengths, dtype=jnp.int32)
    places = jnp.arange(count, dtype=jnp.int32)
    return lax.optimization_barrier(jnp.sum((places[:, None] >= ends[None, :]).astype(jnp.int32), axis=1))

def attend(queries, keys, values, allowed):
    raw = low_back(jnp.einsum('qhd,khd->hqk', queries, keys, precision=lax.Precision.HIGHEST))
    scores = jnp.where(allowed[None], raw * HEAD_DIM ** (-0.5), -1e+30)
    top = lax.optimization_barrier(jnp.max(scores, axis=-1, keepdims=True))
    expo = jnp.exp(scores - top)
    probs = low(expo / lax.optimization_barrier(jnp.sum(expo, axis=-1, keepdims=True)))
    return jnp.einsum('hqk,khd->qhd', probs, values, precision=lax.Precision.HIGHEST)

def blocked(queries, keys, values, allowed):
    count = queries.shape[0]
    block = min(512, count)
    query_blocks = queries.reshape(count // block, block, HEADS, HEAD_DIM)
    mask_blocks = allowed.reshape(count // block, block, allowed.shape[1])
    key_heads = keys.reshape(keys.shape[0], HEADS, HEAD_DIM)
    value_heads = values.reshape(values.shape[0], HEADS, HEAD_DIM)
    step = jax.checkpoint(lambda pair: attend(pair[0], key_heads, value_heads, pair[1]))
    mixed = lax.map(step, (query_blocks, mask_blocks))
    return mixed.reshape(count, HEADS * HEAD_DIM)

def layer(rows, encoder, first_gain, first_shift, causal_query, causal_key, causal_value, causal_out, second_gain, second_shift, cross_query, cross_key, cross_value, cross_out, third_gain, third_shift, expand_weight, reduce_weight, self_allowed, cross_allowed):
    first = low(normalize(rows, first_gain, first_shift))
    query = rounded_both(highest(first, causal_query))
    key = rounded_both(highest(first, causal_key))
    value = rounded_both(highest(first, causal_value))
    mixed = rounded_both(blocked(query, key, value, self_allowed))
    after_self = rows + low_back(highest(mixed, causal_out))
    second = low(normalize(after_self, second_gain, second_shift))
    cquery = rounded_both(highest(second, cross_query))
    ckey = rounded_both(highest(encoder, cross_key))
    cvalue = rounded_both(highest(encoder, cross_value))
    cmixed = rounded_both(blocked(cquery, ckey, cvalue, cross_allowed))
    after_cross = after_self + low_back(highest(cmixed, cross_out))
    third = low(normalize(after_cross, third_gain, third_shift))
    hidden = low(low_back(smooth_gate(highest(third, expand_weight))))
    return after_cross + low_back(highest(hidden, reduce_weight))

def reference(tokens, encoder_states, tok_lengths, enc_lengths, pad_mask, first_gain, first_shift, causal_query, causal_key, causal_value, causal_out, second_gain, second_shift, cross_query, cross_key, cross_value, cross_out, third_gain, third_shift, expand_weight, reduce_weight, cotangent):
    slots = tok_lengths.shape[0]
    params = tuple((p.astype(jnp.float32) for p in (first_gain, first_shift, causal_query, causal_key, causal_value, causal_out, second_gain, second_shift, cross_query, cross_key, cross_value, cross_out, third_gain, third_shift, expand_weight, reduce_weight)))
    tok_view = tokens.astype(jnp.float32).reshape(slots, TOK_DEV, D)
    enc_view = encoder_states.astype(jnp.float32).reshape(slots, ENC_DEV, D)
    cot_view = cotangent.astype(jnp.float32).reshape(slots, TOK_DEV, D)
    mask_view = pad_mask.reshape(slots, TOK_DEV)

    def one_slot(totals, item):
        rows, encoder, lengths, elengths, keep, cot = item
        seg = segment_ids(lengths, TOK_DEV)
        eseg = segment_ids(elengths, ENC_DEV)
        places = jnp.arange(TOK_DEV, dtype=jnp.int32)
        self_allowed = (seg[:, None] == seg[None, :]) & (places[None, :] <= places[:, None]) & ((keep[None, :] == 1) | (places[None, :] == places[:, None]))
        cross_allowed = seg[:, None] == eseg[None, :]

        def forward(rows_in, encoder_in, *weights):
            return layer(rows_in, encoder_in, *weights, self_allowed, cross_allowed)
        out, pull = jax.vjp(forward, rows, encoder, *params)
        grads = pull(cot)
        totals = tuple((a + b for a, b in zip(totals, grads[2:])))
        return (totals, (out.astype(jnp.bfloat16), grads[0].astype(jnp.bfloat16), grads[1].astype(jnp.bfloat16)))
    start = tuple((jnp.zeros_like(p) for p in params))
    totals, (outs, rows_grad, enc_grad) = lax.scan(one_slot, start, (tok_view, enc_view, tok_lengths, enc_lengths, mask_view, cot_view))
    return (outs.reshape(slots * TOK_DEV, D), rows_grad.reshape(slots * TOK_DEV, D), enc_grad.reshape(slots * ENC_DEV, D)) + totals
```

```python
import functools

import jax
import jax.numpy as jnp
from jax import lax
from jax.experimental import pallas as pl
from jax.experimental.pallas import tpu as pltpu
from jax.sharding import PartitionSpec as P

HEAD_DIM = 64


eps = 1e-05
tanh_coeff = 0.7978845608
cubic_coeff = 0.044715


def smooth_gate(values):
    inner = jnp.tanh(tanh_coeff * (values + cubic_coeff * values * values * values))
    return 0.5 * values * (1.0 + inner)


def smooth_slope(values):
    inner = jnp.tanh(tanh_coeff * (values + cubic_coeff * values * values * values))
    return 0.5 * (1.0 + inner) + 0.5 * values * (1.0 - inner * inner) * tanh_coeff * (
        1.0 + 3.0 * cubic_coeff * values * values
    )


def segment_ids(lengths, count):
    ends = jnp.cumsum(lengths, dtype=jnp.int32)
    places = jnp.arange(count, dtype=jnp.int32)
    return jnp.sum((places[:, None] >= ends[None, :]).astype(jnp.int32), axis=1)


def normalize(rows, gain, shift):
    centred = rows - jnp.mean(rows, axis=1, keepdims=True)
    inverse = lax.rsqrt(jnp.mean(centred * centred, axis=1, keepdims=True) + eps)
    unit = centred * inverse
    return (unit * gain + shift, unit, inverse)


def normalize_back(grad_out, unit, inverse, gain):
    scaled = grad_out * gain
    inner = (
        scaled
        - jnp.mean(scaled, axis=1, keepdims=True)
        - unit * jnp.mean(scaled * unit, axis=1, keepdims=True)
    )
    return (inner * inverse, jnp.sum(grad_out * unit, axis=0), jnp.sum(grad_out, axis=0))


def along_rows(left, right):
    return lax.dot_general(
        left, right, (((0,), (0,)), ((), ())), preferred_element_type=jnp.float32
    )


def against(left, weight):
    return lax.dot_general(
        left, weight, (((1,), (1,)), ((), ())), preferred_element_type=jnp.float32
    )


def spread_normed(rows):
    return lax.all_gather(rows, "tensor", axis=0, tiled=True)


def spread_grads(rows):
    return lax.all_gather(rows, "tensor", axis=0, tiled=True)


def sum_branch(left, weight, rows):

    def term(start, count):
        return jnp.dot(left, weight, preferred_element_type=jnp.float32)

    return lax.psum_scatter(
        term(jnp.int32(0), lax.axis_size("tensor") * rows).astype(jnp.bfloat16),
        "tensor",
        scatter_dimension=0,
        tiled=True,
    ).astype(jnp.float32)


def sum_inputs(pairs, rows):

    def term(start, count):
        total = jnp.zeros((count, pairs[0][1].shape[0]), jnp.float32)
        for left, weight in pairs:
            total = total + against(left, weight)
        return total

    return lax.psum_scatter(
        term(jnp.int32(0), lax.axis_size("tensor") * rows).astype(jnp.bfloat16),
        "tensor",
        scatter_dimension=0,
        tiled=True,
    ).astype(jnp.float32)


BF=jnp.bfloat16
F32=jnp.float32

def head_mask(rows, width, h):
    lane = lax.broadcasted_iota(jnp.int32, (rows, width), 1)
    return (lane // HEAD_DIM) == h

def dot(a,b,ca,cb):
    return lax.dot_general(a,b,(((ca,),(cb,)),((),())),preferred_element_type=F32)

def fwd_kernel(causal, heads, bq, bk, lo_ref, hi_ref, q_ref, k_ref, v_ref, rs_ref, ks_ref, o_ref, lse_ref, acc):
    count, width = q_ref.shape
    def one(qb, _):
        q0 = pl.multiple_of(qb*bq, bq)
        qv = q_ref[pl.ds(q0,bq),:] * BF(HEAD_DIM**-0.5)
        rseg = rs_ref[pl.ds(q0,bq),0:1]
        qm = [jnp.where(head_mask(bq,width,h), qv, BF(0)) for h in range(heads)]
        acc[...] = jnp.zeros_like(acc)
        lane = lax.broadcasted_iota(jnp.int32,(bq,128),1)
        def inner(kb, carry):
            k0 = pl.multiple_of(kb*bk, bk)
            kv = k_ref[pl.ds(k0,bk),:]
            vv = v_ref[pl.ds(k0,bk),:]
            kseg = ks_ref[0:1,pl.ds(k0,bk)]
            if causal:
                kpad = ks_ref[1:2,pl.ds(k0,bk)]
                ri = lax.broadcasted_iota(jnp.int32,(bq,bk),0)+q0
                ci = lax.broadcasted_iota(jnp.int32,(bq,bk),1)+k0
                ok = ((rseg==kpad)&(ci<=ri))|(ci==ri)
            else:
                ok = rseg==kseg
            ms, ls = carry
            new_m, new_l = [], []
            parts=None
            alphas=[]
            for h in range(heads):
                s = dot(qm[h],kv,1,1)
                s = jnp.where(ok,s,-1e30)
                m = jnp.maximum(ms[h], jnp.max(s,axis=1,keepdims=True))
                p = jnp.exp(s-m)
                al = jnp.exp(ms[h]-m)
                new_m.append(m); new_l.append(ls[h]*al+jnp.sum(p,axis=1,keepdims=True))
                vm = jnp.where(head_mask(bk,width,h),vv,BF(0))
                t = dot(p.astype(BF),vm,1,0)
                parts = t if parts is None else parts+t
                alphas.append(al)
            lane2 = lax.broadcasted_iota(jnp.int32,(bq,width),1)//HEAD_DIM
            sc = alphas[heads-1]
            for h in range(heads-1):
                sc = jnp.where(lane2==h, alphas[h], sc)
            acc[...] = acc[...]*sc + parts
            return (tuple(new_m),tuple(new_l))
        init = (tuple(jnp.full((bq,1),-1e30,F32) for _ in range(heads)), tuple(jnp.zeros((bq,1),F32) for _ in range(heads)))
        ms, ls = lax.fori_loop(lo_ref[qb], hi_ref[qb], inner, init)
        lane2 = lax.broadcasted_iota(jnp.int32,(bq,width),1)//HEAD_DIM
        inv = [1.0/l for l in ls]
        sc = inv[heads-1]
        for h in range(heads-1):
            sc = jnp.where(lane2==h, inv[h], sc)
        o_ref[pl.ds(q0,bq),:] = (acc[...]*sc).astype(BF)
        st = jnp.zeros((bq,128),F32)
        for h in range(heads):
            st = jnp.where(lane==h, ms[h]+jnp.log(ls[h]), st)
        stt = jnp.transpose(st)
        lse_ref[:,pl.ds(q0,bq)] = stt[0:8,:]
        return 0
    lax.fori_loop(0,count//bq,one,0)

def attend_fwd(q,k,v,rseg,kseg,lo,hi,causal,bq=256,bk=256):
    count,width=q.shape
    heads=width//HEAD_DIM
    vm=pl.BlockSpec(memory_space=pltpu.VMEM); sm=pl.BlockSpec(memory_space=pltpu.SMEM)
    return pl.pallas_call(functools.partial(fwd_kernel,causal,heads,bq,bk),
        out_shape=(jax.ShapeDtypeStruct((count,width),BF),jax.ShapeDtypeStruct((8,count),F32)),
        in_specs=[sm,sm,vm,vm,vm,vm,vm],out_specs=(vm,vm),
        scratch_shapes=[pltpu.VMEM((bq,width),F32)],
        compiler_params=pltpu.CompilerParams(vmem_limit_bytes=40<<20),
        name="attend_fwd",
    )(lo,hi,q,k,v,rseg,kseg)

def bwd_kernel(causal, heads, bq, bk, lo_ref, hi_ref, q_ref, k_ref, v_ref, o_ref, do_ref, lse_ref, rs_ref, ks_ref,
               dq_ref, dk_ref, dv_ref, dka, dva, qm, dom, dqa):
    count,width=q_ref.shape
    dka[...]=jnp.zeros_like(dka); dva[...]=jnp.zeros_like(dva)
    def one(qb,_):
        q0=pl.multiple_of(qb*bq,bq)
        qv=q_ref[pl.ds(q0,bq),:]*BF(HEAD_DIM**-0.5)
        dov=do_ref[pl.ds(q0,bq),:]
        prod=dov.astype(F32)*o_ref[pl.ds(q0,bq),:].astype(F32)
        row=lax.broadcasted_iota(jnp.int32,(8,width),0); col=lax.broadcasted_iota(jnp.int32,(8,width),1)//HEAD_DIM
        sel=(row==col).astype(F32)
        delta=lax.dot_general(sel,prod,(((1,),(1,)),((),())),precision=lax.Precision.HIGHEST,preferred_element_type=F32)
        for h in range(heads):
            hm=head_mask(bq,width,h)
            qm[pl.ds(h*bq,bq),:]=jnp.where(hm,qv,BF(0))
            dom[pl.ds(h*bq,bq),:]=jnp.where(hm,dov,BF(0))
        dqa[...]=jnp.zeros_like(dqa)
        rseg=rs_ref[0:1,pl.ds(q0,bq)]
        lse=lse_ref[:,pl.ds(q0,bq)]
        def inner(kb,_):
            k0=pl.multiple_of(kb*bk,bk)
            kv=k_ref[pl.ds(k0,bk),:]; vv=v_ref[pl.ds(k0,bk),:]
            if causal:
                kpad=ks_ref[pl.ds(k0,bk),1:2]
                ri=lax.broadcasted_iota(jnp.int32,(bk,bq),1)+q0
                ci=lax.broadcasted_iota(jnp.int32,(bk,bq),0)+k0
                ok=((rseg==kpad)&(ci<=ri))|(ci==ri)
            else:
                ok=rseg==ks_ref[pl.ds(k0,bk),0:1]
            ps=[];dss=[]
            dq=None
            for h in range(heads):
                st=dot(kv,qm[pl.ds(h*bq,bq),:],1,1)
                p=jnp.where(ok,jnp.exp(st-lse[h:h+1,:]),0.0)
                dp=dot(vv,dom[pl.ds(h*bq,bq),:],1,1)
                ds=(p*(dp-delta[h:h+1,:])).astype(BF)
                ps.append(p.astype(BF)); dss.append(ds)
                km=jnp.where(head_mask(bk,width,h),kv,BF(0))
                t=dot(ds,km,0,0)
                dq=t if dq is None else dq+t
            dqa[...]+=dq
            pcat=jnp.concatenate(ps,axis=1); dcat=jnp.concatenate(dss,axis=1)
            dva[pl.ds(k0,bk),:]+=dot(pcat,dom[...],1,0)
            dka[pl.ds(k0,bk),:]+=dot(dcat,qm[...],1,0)
            return 0
        lax.fori_loop(lo_ref[qb],hi_ref[qb],inner,0)
        dq_ref[pl.ds(q0,bq),:]=(dqa[...]*(HEAD_DIM**-0.5)).astype(BF)
        return 0
    lax.fori_loop(0,count//bq,one,0)
    dk_ref[...]=dka[...].astype(BF)
    dv_ref[...]=dva[...].astype(BF)

def attend_bwd(q,k,v,o,do,lse,rseg,kseg,lo,hi,causal,bq=256,bk=256):
    count,width=q.shape; keys=k.shape[0]
    heads=width//HEAD_DIM
    vm=pl.BlockSpec(memory_space=pltpu.VMEM); sm=pl.BlockSpec(memory_space=pltpu.SMEM)
    return pl.pallas_call(functools.partial(bwd_kernel,causal,heads,bq,bk),
        out_shape=(jax.ShapeDtypeStruct((count,width),BF),jax.ShapeDtypeStruct((keys,width),BF),jax.ShapeDtypeStruct((keys,width),BF)),
        in_specs=[sm,sm]+[vm]*8,out_specs=(vm,vm,vm),
        scratch_shapes=[pltpu.VMEM((keys,width),F32),pltpu.VMEM((keys,width),F32),pltpu.VMEM((heads*bq,width),BF),pltpu.VMEM((heads*bq,width),BF),pltpu.VMEM((bq,width),F32)],
        compiler_params=pltpu.CompilerParams(vmem_limit_bytes=40<<20),
        name="attend_bwd",
    )(lo,hi,q,k,v,o,do,lse,rseg,kseg)

def ranges(tok_lengths, enc_lengths, pad, count, frames, bq, bk):
    tend=jnp.cumsum(tok_lengths,dtype=jnp.int32); eend=jnp.cumsum(enc_lengths,dtype=jnp.int32)
    places=jnp.arange(count,dtype=jnp.int32)
    tseg=jnp.sum((places[:,None]>=tend[None,:]).astype(jnp.int32),axis=1)
    eseg=jnp.sum((jnp.arange(frames,dtype=jnp.int32)[:,None]>=eend[None,:]).astype(jnp.int32),axis=1)
    starts=jnp.arange(count//bq,dtype=jnp.int32)*bq
    first=tseg[::bq]; last=tseg[bq-1::bq]
    onehot=lambda s:(s[:,None]==jnp.arange(tend.shape[0])[None,:]).astype(jnp.int32)
    pick=lambda arr,s: jnp.sum(onehot(s)*arr[None,:],axis=1)
    tstart=tend-tok_lengths; estart=eend-enc_lengths
    slo=pick(tstart,first)//bk; shi=(starts+bq+bk-1)//bk
    clo=pick(estart,first)//bk; chi=(pick(eend,last)+bk-1)//bk
    kpad=jnp.where(pad==1,tseg,-1)
    return tseg,eseg,kpad,slo,shi,clo,chi


def on_device(
    tokens,
    encoder_states,
    tok_lengths,
    enc_lengths,
    pad_mask,
    first_gain,
    first_shift,
    causal_query,
    causal_key,
    causal_value,
    causal_out,
    second_gain,
    second_shift,
    cross_query,
    cross_key,
    cross_value,
    cross_out,
    third_gain,
    third_shift,
    expand_weight,
    reduce_weight,
    cotangent,
):
    share = tokens.shape[0]
    length = pad_mask.shape[0]
    frames = encoder_states.shape[0]
    heads = causal_query.shape[1] // HEAD_DIM
    scale = HEAD_DIM ** (-0.5)
    token_seg, frame_seg, key_seg, self_lo, self_hi, cross_lo, cross_hi = ranges(
        tok_lengths[0], enc_lengths[0], pad_mask, length, frames, 256, 512
    )
    self_keys = jnp.stack([token_seg, key_seg] + [token_seg] * 6)
    cross_keys = jnp.stack([frame_seg] * 8)
    seg_col, seg_row = token_seg[:, None], token_seg[None, :]
    residual = tokens.astype(jnp.float32)
    first_out, first_unit, first_inv = normalize(residual, first_gain, first_shift)
    first_all = spread_normed(first_out.astype(jnp.bfloat16))
    query = jnp.dot(first_all, causal_query, preferred_element_type=jnp.float32).astype(
        jnp.bfloat16
    )
    keyed = jnp.dot(first_all, causal_key, preferred_element_type=jnp.float32).astype(jnp.bfloat16)
    valued = jnp.dot(first_all, causal_value, preferred_element_type=jnp.float32).astype(
        jnp.bfloat16
    )
    mixed, self_logsum = attend_fwd(
        query, keyed, valued, seg_col, self_keys, self_lo, self_hi, True, 256, 512
    )
    after_self = residual + sum_branch(mixed, causal_out, share)
    second_out, second_unit, second_inv = normalize(after_self, second_gain, second_shift)
    second_all = spread_normed(second_out.astype(jnp.bfloat16))
    cquery = jnp.dot(second_all, cross_query, preferred_element_type=jnp.float32).astype(
        jnp.bfloat16
    )
    ckeyed = jnp.dot(encoder_states, cross_key, preferred_element_type=jnp.float32).astype(
        jnp.bfloat16
    )
    cvalued = jnp.dot(encoder_states, cross_value, preferred_element_type=jnp.float32).astype(
        jnp.bfloat16
    )
    cmixed, cross_logsum = attend_fwd(
        cquery, ckeyed, cvalued, seg_col, cross_keys, cross_lo, cross_hi, False, 256, 512
    )
    after_cross = after_self + sum_branch(cmixed, cross_out, share)
    third_out, third_unit, third_inv = normalize(after_cross, third_gain, third_shift)
    third_all = spread_normed(third_out.astype(jnp.bfloat16))
    pre_act = jnp.dot(third_all, expand_weight, preferred_element_type=jnp.float32)
    hidden = smooth_gate(pre_act).astype(jnp.bfloat16)
    output = (after_cross + sum_branch(hidden, reduce_weight, share)).astype(jnp.bfloat16)
    grad_res = cotangent.astype(jnp.float32)
    grad_top = spread_grads(grad_res.astype(jnp.bfloat16))
    reduce_grad = along_rows(hidden, grad_top)
    grad_hidden = against(grad_top, reduce_weight)
    grad_expand_in = (grad_hidden * smooth_slope(pre_act)).astype(jnp.bfloat16)
    expand_grad = along_rows(third_all, grad_expand_in)
    third_in = sum_inputs(((grad_expand_in, expand_weight),), share)
    back_rows, third_gain_grad, third_shift_grad = normalize_back(
        third_in, third_unit, third_inv, third_gain
    )
    grad_res = grad_res + back_rows
    grad_top = spread_grads(grad_res.astype(jnp.bfloat16))
    cross_out_grad = along_rows(cmixed, grad_top)
    grad_cmixed = against(grad_top, cross_out).astype(jnp.bfloat16)
    grad_cquery, grad_ckey, grad_cvalue = attend_bwd(
        cquery, ckeyed, cvalued, cmixed, grad_cmixed, cross_logsum, seg_row, cross_keys.T,
        cross_lo, cross_hi, False, 256, 512,
    )
    cross_query_grad = along_rows(second_all, grad_cquery)
    cross_key_grad = along_rows(encoder_states, grad_ckey)
    cross_value_grad = along_rows(encoder_states, grad_cvalue)
    encoder_grad = lax.psum_scatter(
        (against(grad_ckey, cross_key) + against(grad_cvalue, cross_value)).astype(jnp.bfloat16),
        "tensor",
        scatter_dimension=0,
        tiled=True,
    )
    second_in = sum_inputs(((grad_cquery, cross_query),), share)
    back_rows, second_gain_grad, second_shift_grad = normalize_back(
        second_in, second_unit, second_inv, second_gain
    )
    grad_res = grad_res + back_rows
    grad_top = spread_grads(grad_res.astype(jnp.bfloat16))
    causal_out_grad = along_rows(mixed, grad_top)
    grad_mixed = against(grad_top, causal_out).astype(jnp.bfloat16)
    grad_query, grad_key, grad_value = attend_bwd(
        query, keyed, valued, mixed, grad_mixed, self_logsum, seg_row, self_keys.T,
        self_lo, self_hi, True, 256, 512,
    )
    causal_query_grad = along_rows(first_all, grad_query)
    causal_key_grad = along_rows(first_all, grad_key)
    causal_value_grad = along_rows(first_all, grad_value)
    first_in = sum_inputs(
        ((grad_query, causal_query), (grad_key, causal_key), (grad_value, causal_value)), share
    )
    back_rows, first_gain_grad, first_shift_grad = normalize_back(
        first_in, first_unit, first_inv, first_gain
    )
    tokens_grad = (grad_res + back_rows).astype(jnp.bfloat16)
    (
        causal_query_grad,
        causal_key_grad,
        causal_value_grad,
        causal_out_grad,
        cross_query_grad,
        cross_key_grad,
        cross_value_grad,
        cross_out_grad,
        expand_grad,
        reduce_grad,
    ) = lax.psum(
        (
            causal_query_grad,
            causal_key_grad,
            causal_value_grad,
            causal_out_grad,
            cross_query_grad,
            cross_key_grad,
            cross_value_grad,
            cross_out_grad,
            expand_grad,
            reduce_grad,
        ),
        "dp",
    )
    (
        first_gain_grad,
        first_shift_grad,
        second_gain_grad,
        second_shift_grad,
        third_gain_grad,
        third_shift_grad,
    ) = lax.psum(
        (
            first_gain_grad,
            first_shift_grad,
            second_gain_grad,
            second_shift_grad,
            third_gain_grad,
            third_shift_grad,
        ),
        ("dp", "tensor"),
    )
    return (
        output,
        tokens_grad,
        encoder_grad,
        first_gain_grad,
        first_shift_grad,
        causal_query_grad,
        causal_key_grad,
        causal_value_grad,
        causal_out_grad,
        second_gain_grad,
        second_shift_grad,
        cross_query_grad,
        cross_key_grad,
        cross_value_grad,
        cross_out_grad,
        third_gain_grad,
        third_shift_grad,
        expand_grad,
        reduce_grad,
    )


def solution(mesh):
    in_specs = (
        P(("dp", "tensor"), None),
        P("dp", None),
        P("dp", None),
        P("dp", None),
        P("dp"),
        P(),
        P(),
        P(None, "tensor"),
        P(None, "tensor"),
        P(None, "tensor"),
        P("tensor", None),
        P(),
        P(),
        P(None, "tensor"),
        P(None, "tensor"),
        P(None, "tensor"),
        P("tensor", None),
        P(),
        P(),
        P(None, "tensor"),
        P("tensor", None),
        P(("dp", "tensor"), None),
    )
    out_specs = (
        P(("dp", "tensor"), None),
        P(("dp", "tensor"), None),
        P(("dp", "tensor"), None),
        P(),
        P(),
        P(None, "tensor"),
        P(None, "tensor"),
        P(None, "tensor"),
        P("tensor", None),
        P(),
        P(),
        P(None, "tensor"),
        P(None, "tensor"),
        P(None, "tensor"),
        P("tensor", None),
        P(),
        P(),
        P(None, "tensor"),
        P("tensor", None),
    )
    return jax.shard_map(
        on_device, mesh=mesh, in_specs=in_specs, out_specs=out_specs, check_vma=False
    )
```

```python
import functools

import jax
import jax.numpy as jnp
from jax import lax
from jax.experimental import pallas as pl
from jax.experimental.pallas import tpu as pltpu
from jax.sharding import PartitionSpec as P

HEAD_DIM = 64


eps = 1e-05
tanh_coeff = 0.7978845608
cubic_coeff = 0.044715


def smooth_gate(values):
    inner = jnp.tanh(tanh_coeff * (values + cubic_coeff * values * values * values))
    return 0.5 * values * (1.0 + inner)


def smooth_slope(values):
    inner = jnp.tanh(tanh_coeff * (values + cubic_coeff * values * values * values))
    return 0.5 * (1.0 + inner) + 0.5 * values * (1.0 - inner * inner) * tanh_coeff * (
        1.0 + 3.0 * cubic_coeff * values * values
    )


BF=jnp.bfloat16
F32=jnp.float32

def head_mask(rows, width, h):
    lane = lax.broadcasted_iota(jnp.int32, (rows, width), 1)
    return (lane // HEAD_DIM) == h

def dot(a,b,ca,cb):
    return lax.dot_general(a,b,(((ca,),(cb,)),((),())),preferred_element_type=F32)

def fwd_kernel(causal, heads, bq, bk, lo_ref, hi_ref, q_ref, k_ref, v_ref, rs_ref, ks_ref, o_ref, lse_ref, acc):
    count, width = q_ref.shape
    def one(qb, _):
        q0 = pl.multiple_of(qb*bq, bq)
        qv = q_ref[pl.ds(q0,bq),:] * BF(HEAD_DIM**-0.5)
        rseg = rs_ref[pl.ds(q0,bq),0:1]
        qm = [jnp.where(head_mask(bq,width,h), qv, BF(0)) for h in range(heads)]
        acc[...] = jnp.zeros_like(acc)
        lane = lax.broadcasted_iota(jnp.int32,(bq,128),1)
        def inner(kb, carry):
            k0 = pl.multiple_of(kb*bk, bk)
            kv = k_ref[pl.ds(k0,bk),:]
            vv = v_ref[pl.ds(k0,bk),:]
            kseg = ks_ref[0:1,pl.ds(k0,bk)]
            if causal:
                kpad = ks_ref[1:2,pl.ds(k0,bk)]
                ri = lax.broadcasted_iota(jnp.int32,(bq,bk),0)+q0
                ci = lax.broadcasted_iota(jnp.int32,(bq,bk),1)+k0
                ok = ((rseg==kpad)&(ci<=ri))|(ci==ri)
            else:
                ok = rseg==kseg
            ms, ls = carry
            new_m, new_l = [], []
            parts=None
            alphas=[]
            for h in range(heads):
                s = dot(qm[h],kv,1,1)
                s = jnp.where(ok,s,-1e30)
                m = jnp.maximum(ms[h], jnp.max(s,axis=1,keepdims=True))
                p = jnp.exp(s-m)
                al = jnp.exp(ms[h]-m)
                new_m.append(m); new_l.append(ls[h]*al+jnp.sum(p,axis=1,keepdims=True))
                vm = jnp.where(head_mask(bk,width,h),vv,BF(0))
                t = dot(p.astype(BF),vm,1,0)
                parts = t if parts is None else parts+t
                alphas.append(al)
            lane2 = lax.broadcasted_iota(jnp.int32,(bq,width),1)//HEAD_DIM
            sc = alphas[heads-1]
            for h in range(heads-1):
                sc = jnp.where(lane2==h, alphas[h], sc)
            acc[...] = acc[...]*sc + parts
            return (tuple(new_m),tuple(new_l))
        init = (tuple(jnp.full((bq,1),-1e30,F32) for _ in range(heads)), tuple(jnp.zeros((bq,1),F32) for _ in range(heads)))
        ms, ls = lax.fori_loop(lo_ref[qb], hi_ref[qb], inner, init)
        lane2 = lax.broadcasted_iota(jnp.int32,(bq,width),1)//HEAD_DIM
        inv = [1.0/l for l in ls]
        sc = inv[heads-1]
        for h in range(heads-1):
            sc = jnp.where(lane2==h, inv[h], sc)
        o_ref[pl.ds(q0,bq),:] = (acc[...]*sc).astype(BF)
        st = jnp.zeros((bq,128),F32)
        for h in range(heads):
            st = jnp.where(lane==h, ms[h]+jnp.log(ls[h]), st)
        stt = jnp.transpose(st)
        lse_ref[:,pl.ds(q0,bq)] = stt[0:8,:]
        return 0
    lax.fori_loop(0,count//bq,one,0)

def attend_fwd(q,k,v,rseg,kseg,lo,hi,causal,bq=256,bk=256):
    count,width=q.shape
    heads=width//HEAD_DIM
    vm=pl.BlockSpec(memory_space=pltpu.VMEM); sm=pl.BlockSpec(memory_space=pltpu.SMEM)
    return pl.pallas_call(functools.partial(fwd_kernel,causal,heads,bq,bk),
        out_shape=(jax.ShapeDtypeStruct((count,width),BF),jax.ShapeDtypeStruct((8,count),F32)),
        in_specs=[sm,sm,vm,vm,vm,vm,vm],out_specs=(vm,vm),
        scratch_shapes=[pltpu.VMEM((bq,width),F32)],
        compiler_params=pltpu.CompilerParams(vmem_limit_bytes=40<<20),
        name="attend_fwd",
    )(lo,hi,q,k,v,rseg,kseg)

def bwd_kernel(causal, heads, bq, bk, lo_ref, hi_ref, q_ref, k_ref, v_ref, o_ref, do_ref, lse_ref, rs_ref, ks_ref,
               dq_ref, dk_ref, dv_ref, dka, dva, qm, dom, dqa):
    count,width=q_ref.shape
    dka[...]=jnp.zeros_like(dka); dva[...]=jnp.zeros_like(dva)
    def one(qb,_):
        q0=pl.multiple_of(qb*bq,bq)
        qv=q_ref[pl.ds(q0,bq),:]*BF(HEAD_DIM**-0.5)
        dov=do_ref[pl.ds(q0,bq),:]
        prod=dov.astype(F32)*o_ref[pl.ds(q0,bq),:].astype(F32)
        row=lax.broadcasted_iota(jnp.int32,(8,width),0); col=lax.broadcasted_iota(jnp.int32,(8,width),1)//HEAD_DIM
        sel=(row==col).astype(F32)
        delta=lax.dot_general(sel,prod,(((1,),(1,)),((),())),precision=lax.Precision.HIGHEST,preferred_element_type=F32)
        for h in range(heads):
            hm=head_mask(bq,width,h)
            qm[pl.ds(h*bq,bq),:]=jnp.where(hm,qv,BF(0))
            dom[pl.ds(h*bq,bq),:]=jnp.where(hm,dov,BF(0))
        dqa[...]=jnp.zeros_like(dqa)
        rseg=rs_ref[0:1,pl.ds(q0,bq)]
        lse=lse_ref[:,pl.ds(q0,bq)]
        def inner(kb,_):
            k0=pl.multiple_of(kb*bk,bk)
            kv=k_ref[pl.ds(k0,bk),:]; vv=v_ref[pl.ds(k0,bk),:]
            if causal:
                kpad=ks_ref[pl.ds(k0,bk),1:2]
                ri=lax.broadcasted_iota(jnp.int32,(bk,bq),1)+q0
                ci=lax.broadcasted_iota(jnp.int32,(bk,bq),0)+k0
                ok=((rseg==kpad)&(ci<=ri))|(ci==ri)
            else:
                ok=rseg==ks_ref[pl.ds(k0,bk),0:1]
            ps=[];dss=[]
            dq=None
            for h in range(heads):
                st=dot(kv,qm[pl.ds(h*bq,bq),:],1,1)
                p=jnp.where(ok,jnp.exp(st-lse[h:h+1,:]),0.0)
                dp=dot(vv,dom[pl.ds(h*bq,bq),:],1,1)
                ds=(p*(dp-delta[h:h+1,:])).astype(BF)
                ps.append(p.astype(BF)); dss.append(ds)
                km=jnp.where(head_mask(bk,width,h),kv,BF(0))
                t=dot(ds,km,0,0)
                dq=t if dq is None else dq+t
            dqa[...]+=dq
            pcat=jnp.concatenate(ps,axis=1); dcat=jnp.concatenate(dss,axis=1)
            dva[pl.ds(k0,bk),:]+=dot(pcat,dom[...],1,0)
            dka[pl.ds(k0,bk),:]+=dot(dcat,qm[...],1,0)
            return 0
        lax.fori_loop(lo_ref[qb],hi_ref[qb],inner,0)
        dq_ref[pl.ds(q0,bq),:]=(dqa[...]*(HEAD_DIM**-0.5)).astype(BF)
        return 0
    lax.fori_loop(0,count//bq,one,0)
    dk_ref[...]=dka[...].astype(BF)
    dv_ref[...]=dva[...].astype(BF)

def attend_bwd(q,k,v,o,do,lse,rseg,kseg,lo,hi,causal,bq=256,bk=256):
    count,width=q.shape; keys=k.shape[0]
    heads=width//HEAD_DIM
    vm=pl.BlockSpec(memory_space=pltpu.VMEM); sm=pl.BlockSpec(memory_space=pltpu.SMEM)
    return pl.pallas_call(functools.partial(bwd_kernel,causal,heads,bq,bk),
        out_shape=(jax.ShapeDtypeStruct((count,width),BF),jax.ShapeDtypeStruct((keys,width),BF),jax.ShapeDtypeStruct((keys,width),BF)),
        in_specs=[sm,sm]+[vm]*8,out_specs=(vm,vm,vm),
        scratch_shapes=[pltpu.VMEM((keys,width),F32),pltpu.VMEM((keys,width),F32),pltpu.VMEM((heads*bq,width),BF),pltpu.VMEM((heads*bq,width),BF),pltpu.VMEM((bq,width),F32)],
        compiler_params=pltpu.CompilerParams(vmem_limit_bytes=40<<20),
        name="attend_bwd",
    )(lo,hi,q,k,v,o,do,lse,rseg,kseg)

def ranges(tok_lengths, enc_lengths, pad, count, frames, bq, bk):
    tend=jnp.cumsum(tok_lengths,dtype=jnp.int32); eend=jnp.cumsum(enc_lengths,dtype=jnp.int32)
    places=jnp.arange(count,dtype=jnp.int32)
    tseg=jnp.sum((places[:,None]>=tend[None,:]).astype(jnp.int32),axis=1)
    eseg=jnp.sum((jnp.arange(frames,dtype=jnp.int32)[:,None]>=eend[None,:]).astype(jnp.int32),axis=1)
    starts=jnp.arange(count//bq,dtype=jnp.int32)*bq
    first=tseg[::bq]; last=tseg[bq-1::bq]
    onehot=lambda s:(s[:,None]==jnp.arange(tend.shape[0])[None,:]).astype(jnp.int32)
    pick=lambda arr,s: jnp.sum(onehot(s)*arr[None,:],axis=1)
    tstart=tend-tok_lengths; estart=eend-enc_lengths
    slo=pick(tstart,first)//bk; shi=(starts+bq+bk-1)//bk
    clo=pick(estart,first)//bk; chi=(pick(eend,last)+bk-1)//bk
    kpad=jnp.where(pad==1,tseg,-1)
    return tseg,eseg,kpad,slo,shi,clo,chi


def along_rows(left, right):
    return lax.dot_general(
        left, right, (((0,), (0,)), ((), ())), preferred_element_type=jnp.float32
    )


def against(left, weight):
    return lax.dot_general(
        left, weight, (((1,), (1,)), ((), ())), preferred_element_type=jnp.float32
    )


def times(left, weight):
    return jnp.dot(left, weight, preferred_element_type=jnp.float32)


def moments(rows):
    centred = rows - jnp.mean(rows, axis=1, keepdims=True)
    inverse = lax.rsqrt(jnp.mean(centred * centred, axis=1, keepdims=True) + eps)
    return centred * inverse, inverse


def normalize_back(grad_out, unit, inverse, gain):
    scaled = grad_out * gain
    inner = (
        scaled
        - jnp.mean(scaled, axis=1, keepdims=True)
        - unit * jnp.mean(scaled * unit, axis=1, keepdims=True)
    )
    return (inner * inverse, jnp.sum(grad_out * unit, axis=0), jnp.sum(grad_out, axis=0))


class Place:
    def __init__(self):
        self.dp = lax.axis_size("dp")
        self.tensor = lax.axis_size("tensor")
        self.d = lax.axis_index("dp")
        self.t = lax.axis_index("tensor")
        self.core = self.d % 2
        self.half = self.t // 2
        self.side = self.t % 2
        self.keeper = self.core == self.half
        self.shard = jnp.where(self.keeper, self.t, self.t ^ 2)

    def swap(self, value, d_flip, t_flip, only=None):
        pairs = []
        for d in range(self.dp):
            for t in range(self.tensor):
                keeper = d % 2 == t // 2
                if only is None or only == keeper:
                    pairs.append((d * self.tensor + t, (d ^ d_flip) * self.tensor + (t ^ t_flip)))
        return lax.ppermute(value, ("dp", "tensor"), pairs)

    def home(self, value):
        return jnp.where(self.keeper, value, self.swap(value, 1, 2, False))

    def ordered(self, mine, other, which):
        return jnp.where(
            which == 0, jnp.concatenate([mine, other]), jnp.concatenate([other, mine])
        )

    def part(self, value, which, parts):
        size = value.shape[0] // parts
        return lax.dynamic_slice_in_dim(value, which * size, size, 0)

    def both_cores(self, half_rows):
        return self.ordered(half_rows, self.swap(half_rows, 1, 0), self.core)

    def spread_columns(self, value):
        near, far = self.part(value, self.core, 2), self.part(value, 1 - self.core, 2)
        return jnp.concatenate(
            [near, self.swap(far, 1, 0), self.swap(near, 0, 1), self.swap(far, 1, 1)], axis=1
        )

    def order(self):
        return [self.shard, self.shard ^ 2, self.shard ^ 1, self.shard ^ 3]

    def sum_half(self, value):
        near, far = self.part(value, self.core, 2), self.part(value, 1 - self.core, 2)
        return near.astype(jnp.float32) + self.swap(far.astype(jnp.bfloat16), 1, 0).astype(jnp.float32)

    def sum_group_half(self, value):
        mine = self.sum_half(value).astype(jnp.bfloat16)
        return mine.astype(jnp.float32) + self.swap(mine, 0, 1).astype(jnp.float32)

    def sum_group_quarter(self, value):
        mine = self.sum_half(value)
        near, far = self.part(mine, self.side, 2), self.part(mine, 1 - self.side, 2)
        return near + self.swap(far.astype(jnp.bfloat16), 0, 1).astype(jnp.float32)

    def moved_weight(self, weight):
        piece = self.swap(self.part(weight, self.d, self.dp), 0, 2)
        return jnp.where(self.keeper, weight, lax.all_gather(piece, "dp", axis=0, tiled=True))

    def whole_weight(self, weight):
        piece = self.part(weight, self.d, self.dp)
        every = lax.all_gather(piece, ("dp", "tensor"), axis=0, tiled=False)
        every = every.reshape((self.dp, self.tensor) + piece.shape)
        return jnp.swapaxes(every, 0, 1).reshape((self.tensor,) + weight.shape)

    def sum_weight(self, grad):
        groups = [[d for d in range(self.dp) if d % 2 == c] for c in range(2)]
        piece = lax.psum_scatter(
            grad.astype(jnp.bfloat16), "dp", scatter_dimension=0, axis_index_groups=groups, tiled=True
        )
        total = piece.astype(jnp.float32) + self.swap(piece, 0, 2, False).astype(jnp.float32)
        total = total.astype(jnp.bfloat16)
        near, far = self.part(total, self.core, 2), self.part(total, 1 - self.core, 2)
        piece = jnp.where(self.keeper, near, self.swap(far, 1, 0, True))
        return lax.all_gather(piece, "dp", axis=0, tiled=True).astype(jnp.float32)


def on_device(
    tokens,
    encoder_states,
    tok_lengths,
    enc_lengths,
    pad_mask,
    first_gain,
    first_shift,
    causal_query,
    causal_key,
    causal_value,
    causal_out,
    second_gain,
    second_shift,
    cross_query,
    cross_key,
    cross_value,
    cross_out,
    third_gain,
    third_shift,
    expand_weight,
    reduce_weight,
    cotangent,
):
    place = Place()
    width = causal_query.shape[1]
    length = pad_mask.shape[0]
    frames = encoder_states.shape[0]

    def of_group(value):
        return jnp.where(place.keeper, value, place.swap(value, 1, 0))

    def half_rows(quarter):
        return place.ordered(quarter, place.swap(quarter, 0, 1), place.side)

    def quarter_of(half):
        return place.part(half, place.side, 2)

    tok_lengths, enc_lengths, pad_mask = of_group(tok_lengths), of_group(enc_lengths), of_group(pad_mask)
    block_q, block_k = 256, 512
    token_seg, frame_seg, key_seg, self_lo, self_hi, cross_lo, cross_hi = ranges(
        tok_lengths[0], enc_lengths[0], pad_mask, length, frames, block_q, block_k
    )
    self_keys = jnp.stack([token_seg, key_seg] + [token_seg] * 6)
    cross_keys = jnp.stack([frame_seg] * 8)
    seg_col, seg_row = token_seg[:, None], token_seg[None, :]

    first_weight = place.moved_weight(
        jnp.concatenate([causal_query, causal_key, causal_value], axis=1)
    )
    tokens_here = place.home(tokens)
    tokens_half = half_rows(tokens_here)
    residual = tokens_half.astype(jnp.float32)
    unit, inverse = moments(residual)
    first_all = place.both_cores((unit * first_gain + first_shift).astype(jnp.bfloat16))
    mixed_in = times(first_all, first_weight).astype(jnp.bfloat16)
    query, keyed, valued = (mixed_in[:, i * width : (i + 1) * width] for i in range(3))

    encoder = of_group(encoder_states)
    cross_weight = place.moved_weight(jnp.concatenate([cross_key, cross_value], axis=1))
    cross_in = times(encoder, cross_weight).astype(jnp.bfloat16)
    ckeyed, cvalued = cross_in[:, :width], cross_in[:, width:]
    causal_out_all = place.whole_weight(causal_out)
    cross_out_all = place.whole_weight(cross_out)
    cross_query_all = place.whole_weight(cross_query)
    order = place.order()
    pick = lambda every, which: lax.dynamic_index_in_dim(every, which, 0, keepdims=False)
    causal_out_perm = jnp.concatenate([pick(causal_out_all, s) for s in order])
    cross_out_perm = jnp.concatenate([pick(cross_out_all, s) for s in order])
    cross_query_perm = jnp.concatenate([pick(cross_query_all, s) for s in order], axis=1)
    causal_out_here, cross_out_here = causal_out_perm[:width], cross_out_perm[:width]
    cross_query_here = cross_query_perm[:, :width]

    mixed, self_logsum = attend_fwd(
        query, keyed, valued, seg_col, self_keys, self_lo, self_hi, True, block_q, block_k
    )
    after_self = residual + times(place.spread_columns(mixed), causal_out_perm)
    second_unit, second_inv = moments(after_self)
    second_all = place.both_cores((second_unit * second_gain + second_shift).astype(jnp.bfloat16))
    cquery = times(second_all, cross_query_here).astype(jnp.bfloat16)
    cmixed, cross_logsum = attend_fwd(
        cquery, ckeyed, cvalued, seg_col, cross_keys, cross_lo, cross_hi, False, block_q, block_k
    )
    after_cross = after_self + times(place.spread_columns(cmixed), cross_out_perm)
    third_unit, third_inv = moments(after_cross)
    third_all = place.both_cores((third_unit * third_gain + third_shift).astype(jnp.bfloat16))

    ff_weight = place.moved_weight(jnp.concatenate([expand_weight, reduce_weight], axis=1))
    hidden_width = expand_weight.shape[1]
    expand_here, reduce_here = ff_weight[:, :hidden_width], ff_weight[:, hidden_width:]
    cot_half = half_rows(place.home(cotangent))
    grad_top = place.both_cores(cot_half)
    grad_hidden = against(grad_top, reduce_here).astype(jnp.bfloat16)

    pre_act = times(third_all, expand_here)
    hidden = smooth_gate(pre_act).astype(jnp.bfloat16)
    grad_expand_in = (grad_hidden.astype(jnp.float32) * smooth_slope(pre_act)).astype(jnp.bfloat16)
    third_in = place.sum_group_half(against(grad_expand_in, expand_here))
    back_rows, third_gain_grad, third_shift_grad = normalize_back(
        third_in, third_unit, third_inv, third_gain
    )
    grad_res = cot_half.astype(jnp.float32) + back_rows
    out_here = quarter_of(after_cross) + place.sum_group_quarter(times(hidden, reduce_here))
    output = place.home(out_here.astype(jnp.bfloat16))
    reduce_grad = along_rows(hidden, grad_top)
    expand_grad = along_rows(third_all, grad_expand_in)

    grad_top = place.both_cores(grad_res.astype(jnp.bfloat16))
    cross_out_grad = along_rows(cmixed, grad_top)
    grad_cmixed = against(grad_top, cross_out_here).astype(jnp.bfloat16)
    grad_cquery, grad_ckey, grad_cvalue = attend_bwd(
        cquery, ckeyed, cvalued, cmixed, grad_cmixed, cross_logsum, seg_row, cross_keys.T,
        cross_lo, cross_hi, False, block_q, block_k,
    )
    grad_cross_in = jnp.concatenate([grad_ckey, grad_cvalue], axis=1)
    cross_grad = along_rows(encoder, grad_cross_in)
    cross_query_grad = along_rows(second_all, grad_cquery)
    encoder_grad = place.home(
        place.sum_group_quarter(against(grad_cross_in, cross_weight)).astype(jnp.bfloat16)
    )
    second_in = against(place.spread_columns(grad_cquery), cross_query_perm)
    back_rows, second_gain_grad, second_shift_grad = normalize_back(
        second_in, second_unit, second_inv, second_gain
    )
    grad_res = grad_res + back_rows
    grad_top = place.both_cores(grad_res.astype(jnp.bfloat16))
    causal_out_grad = along_rows(mixed, grad_top)
    grad_mixed = against(grad_top, causal_out_here).astype(jnp.bfloat16)
    grad_query, grad_key, grad_value = attend_bwd(
        query, keyed, valued, mixed, grad_mixed, self_logsum, seg_row, self_keys.T,
        self_lo, self_hi, True, block_q, block_k,
    )
    grad_in = jnp.concatenate([grad_query, grad_key, grad_value], axis=1)
    causal_grad = along_rows(first_all, grad_in)
    first_in = place.sum_group_quarter(against(grad_in, first_weight))
    first_unit, first_inv = moments(tokens_here.astype(jnp.float32))
    back_rows, first_gain_grad, first_shift_grad = normalize_back(
        first_in, first_unit, first_inv, first_gain
    )
    tokens_grad = place.home((quarter_of(grad_res) + back_rows).astype(jnp.bfloat16))

    ff_grad = place.sum_weight(jnp.concatenate([expand_grad, reduce_grad.T], axis=1))
    expand_grad, reduce_grad = ff_grad[:, :hidden_width], ff_grad[:, hidden_width:].T
    cross_grads = place.sum_weight(jnp.concatenate([cross_grad, cross_query_grad], axis=1))
    cross_key_grad, cross_value_grad, cross_query_grad = (
        cross_grads[:, i * width : (i + 1) * width] for i in range(3)
    )
    causal_grads = place.sum_weight(causal_grad)
    causal_query_grad, causal_key_grad, causal_value_grad = (
        causal_grads[:, i * width : (i + 1) * width] for i in range(3)
    )
    cross_out_grad = place.sum_weight(cross_out_grad)
    causal_out_grad = place.sum_weight(causal_out_grad)
    once = (place.side == 0).astype(jnp.float32)
    (
        first_gain_grad,
        first_shift_grad,
        second_gain_grad,
        second_shift_grad,
        third_gain_grad,
        third_shift_grad,
    ) = lax.psum(
        (
            first_gain_grad,
            first_shift_grad,
            second_gain_grad * once,
            second_shift_grad * once,
            third_gain_grad * once,
            third_shift_grad * once,
        ),
        ("dp", "tensor"),
    )
    return (
        output,
        tokens_grad,
        encoder_grad,
        first_gain_grad,
        first_shift_grad,
        causal_query_grad,
        causal_key_grad,
        causal_value_grad,
        causal_out_grad,
        second_gain_grad,
        second_shift_grad,
        cross_query_grad,
        cross_key_grad,
        cross_value_grad,
        cross_out_grad,
        third_gain_grad,
        third_shift_grad,
        expand_grad,
        reduce_grad,
    )


def solution(mesh):
    in_specs = (
        P(("dp", "tensor"), None),
        P("dp", None),
        P("dp", None),
        P("dp", None),
        P("dp"),
        P(),
        P(),
        P(None, "tensor"),
        P(None, "tensor"),
        P(None, "tensor"),
        P("tensor", None),
        P(),
        P(),
        P(None, "tensor"),
        P(None, "tensor"),
        P(None, "tensor"),
        P("tensor", None),
        P(),
        P(),
        P(None, "tensor"),
        P("tensor", None),
        P(("dp", "tensor"), None),
    )
    out_specs = (
        P(("dp", "tensor"), None),
        P(("dp", "tensor"), None),
        P(("dp", "tensor"), None),
        P(),
        P(),
        P(None, "tensor"),
        P(None, "tensor"),
        P(None, "tensor"),
        P("tensor", None),
        P(),
        P(),
        P(None, "tensor"),
        P(None, "tensor"),
        P(None, "tensor"),
        P("tensor", None),
        P(),
        P(),
        P(None, "tensor"),
        P("tensor", None),
    )
    return jax.shard_map(
        on_device, mesh=mesh, in_specs=in_specs, out_specs=out_specs, check_vma=False
    )
```

```python
import functools

import jax
import jax.numpy as jnp
from jax import lax
from jax.experimental import pallas as pl
from jax.experimental.pallas import tpu as pltpu
from jax.sharding import PartitionSpec as P

HEAD_DIM = 64


eps = 1e-05
tanh_coeff = 0.7978845608
cubic_coeff = 0.044715


def smooth_gate(values):
    inner = jnp.tanh(tanh_coeff * (values + cubic_coeff * values * values * values))
    return 0.5 * values * (1.0 + inner)


def smooth_slope(values):
    inner = jnp.tanh(tanh_coeff * (values + cubic_coeff * values * values * values))
    return 0.5 * (1.0 + inner) + 0.5 * values * (1.0 - inner * inner) * tanh_coeff * (
        1.0 + 3.0 * cubic_coeff * values * values
    )


BF=jnp.bfloat16
F32=jnp.float32

def head_mask(rows, width, h):
    lane = lax.broadcasted_iota(jnp.int32, (rows, width), 1)
    return (lane // HEAD_DIM) == h

def dot(a,b,ca,cb):
    return lax.dot_general(a,b,(((ca,),(cb,)),((),())),preferred_element_type=F32)

def fwd_kernel(causal, heads, bq, bk, lo_ref, hi_ref, q_ref, k_ref, v_ref, rs_ref, ks_ref, o_ref, lse_ref, acc):
    count, width = q_ref.shape
    def one(qb, _):
        q0 = pl.multiple_of(qb*bq, bq)
        qv = q_ref[pl.ds(q0,bq),:] * BF(HEAD_DIM**-0.5)
        rseg = rs_ref[pl.ds(q0,bq),0:1]
        qm = [jnp.where(head_mask(bq,width,h), qv, BF(0)) for h in range(heads)]
        acc[...] = jnp.zeros_like(acc)
        lane = lax.broadcasted_iota(jnp.int32,(bq,128),1)
        def inner(kb, carry):
            k0 = pl.multiple_of(kb*bk, bk)
            kv = k_ref[pl.ds(k0,bk),:]
            vv = v_ref[pl.ds(k0,bk),:]
            kseg = ks_ref[0:1,pl.ds(k0,bk)]
            if causal:
                kpad = ks_ref[1:2,pl.ds(k0,bk)]
                ri = lax.broadcasted_iota(jnp.int32,(bq,bk),0)+q0
                ci = lax.broadcasted_iota(jnp.int32,(bq,bk),1)+k0
                ok = ((rseg==kpad)&(ci<=ri))|(ci==ri)
            else:
                ok = rseg==kseg
            ms, ls = carry
            new_m, new_l = [], []
            parts=None
            alphas=[]
            for h in range(heads):
                s = dot(qm[h],kv,1,1)
                s = jnp.where(ok,s,-1e30)
                m = jnp.maximum(ms[h], jnp.max(s,axis=1,keepdims=True))
                p = jnp.exp(s-m)
                al = jnp.exp(ms[h]-m)
                new_m.append(m); new_l.append(ls[h]*al+jnp.sum(p,axis=1,keepdims=True))
                vm = jnp.where(head_mask(bk,width,h),vv,BF(0))
                t = dot(p.astype(BF),vm,1,0)
                parts = t if parts is None else parts+t
                alphas.append(al)
            lane2 = lax.broadcasted_iota(jnp.int32,(bq,width),1)//HEAD_DIM
            sc = alphas[heads-1]
            for h in range(heads-1):
                sc = jnp.where(lane2==h, alphas[h], sc)
            acc[...] = acc[...]*sc + parts
            return (tuple(new_m),tuple(new_l))
        init = (tuple(jnp.full((bq,1),-1e30,F32) for _ in range(heads)), tuple(jnp.zeros((bq,1),F32) for _ in range(heads)))
        ms, ls = lax.fori_loop(lo_ref[qb], hi_ref[qb], inner, init)
        lane2 = lax.broadcasted_iota(jnp.int32,(bq,width),1)//HEAD_DIM
        inv = [1.0/l for l in ls]
        sc = inv[heads-1]
        for h in range(heads-1):
            sc = jnp.where(lane2==h, inv[h], sc)
        o_ref[pl.ds(q0,bq),:] = (acc[...]*sc).astype(BF)
        st = jnp.zeros((bq,128),F32)
        for h in range(heads):
            st = jnp.where(lane==h, ms[h]+jnp.log(ls[h]), st)
        stt = jnp.transpose(st)
        lse_ref[:,pl.ds(q0,bq)] = stt[0:8,:]
        return 0
    lax.fori_loop(0,count//bq,one,0)

def attend_fwd(q,k,v,rseg,kseg,lo,hi,causal,bq=256,bk=256):
    count,width=q.shape
    heads=width//HEAD_DIM
    vm=pl.BlockSpec(memory_space=pltpu.VMEM); sm=pl.BlockSpec(memory_space=pltpu.SMEM)
    return pl.pallas_call(functools.partial(fwd_kernel,causal,heads,bq,bk),
        out_shape=(jax.ShapeDtypeStruct((count,width),BF),jax.ShapeDtypeStruct((8,count),F32)),
        in_specs=[sm,sm,vm,vm,vm,vm,vm],out_specs=(vm,vm),
        scratch_shapes=[pltpu.VMEM((bq,width),F32)],
        compiler_params=pltpu.CompilerParams(vmem_limit_bytes=40<<20),
        cost_estimate=pl.CostEstimate(flops=22_000_000_000, bytes_accessed=8_000_000, transcendentals=0),
        name="attend_fwd",
    )(lo,hi,q,k,v,rseg,kseg)

def bwd_kernel(causal, heads, bq, bk, lo_ref, hi_ref, q_ref, k_ref, v_ref, o_ref, do_ref, lse_ref, rs_ref, ks_ref,
               dq_ref, dk_ref, dv_ref, dka, dva, qm, dom, dqa):
    count,width=q_ref.shape
    dka[...]=jnp.zeros_like(dka); dva[...]=jnp.zeros_like(dva)
    def one(qb,_):
        q0=pl.multiple_of(qb*bq,bq)
        qv=q_ref[pl.ds(q0,bq),:]*BF(HEAD_DIM**-0.5)
        dov=do_ref[pl.ds(q0,bq),:]
        prod=dov.astype(F32)*o_ref[pl.ds(q0,bq),:].astype(F32)
        row=lax.broadcasted_iota(jnp.int32,(8,width),0); col=lax.broadcasted_iota(jnp.int32,(8,width),1)//HEAD_DIM
        sel=(row==col).astype(F32)
        delta=lax.dot_general(sel,prod,(((1,),(1,)),((),())),precision=lax.Precision.HIGHEST,preferred_element_type=F32)
        for h in range(heads):
            hm=head_mask(bq,width,h)
            qm[pl.ds(h*bq,bq),:]=jnp.where(hm,qv,BF(0))
            dom[pl.ds(h*bq,bq),:]=jnp.where(hm,dov,BF(0))
        dqa[...]=jnp.zeros_like(dqa)
        rseg=rs_ref[0:1,pl.ds(q0,bq)]
        lse=lse_ref[:,pl.ds(q0,bq)]
        def inner(kb,_):
            k0=pl.multiple_of(kb*bk,bk)
            kv=k_ref[pl.ds(k0,bk),:]; vv=v_ref[pl.ds(k0,bk),:]
            if causal:
                kpad=ks_ref[pl.ds(k0,bk),1:2]
                ri=lax.broadcasted_iota(jnp.int32,(bk,bq),1)+q0
                ci=lax.broadcasted_iota(jnp.int32,(bk,bq),0)+k0
                ok=((rseg==kpad)&(ci<=ri))|(ci==ri)
            else:
                ok=rseg==ks_ref[pl.ds(k0,bk),0:1]
            ps=[];dss=[]
            dq=None
            for h in range(heads):
                st=dot(kv,qm[pl.ds(h*bq,bq),:],1,1)
                p=jnp.where(ok,jnp.exp(st-lse[h:h+1,:]),0.0)
                dp=dot(vv,dom[pl.ds(h*bq,bq),:],1,1)
                ds=(p*(dp-delta[h:h+1,:])).astype(BF)
                ps.append(p.astype(BF)); dss.append(ds)
                km=jnp.where(head_mask(bk,width,h),kv,BF(0))
                t=dot(ds,km,0,0)
                dq=t if dq is None else dq+t
            dqa[...]+=dq
            pcat=jnp.concatenate(ps,axis=1); dcat=jnp.concatenate(dss,axis=1)
            dva[pl.ds(k0,bk),:]+=dot(pcat,dom[...],1,0)
            dka[pl.ds(k0,bk),:]+=dot(dcat,qm[...],1,0)
            return 0
        lax.fori_loop(lo_ref[qb],hi_ref[qb],inner,0)
        dq_ref[pl.ds(q0,bq),:]=(dqa[...]*(HEAD_DIM**-0.5)).astype(BF)
        return 0
    lax.fori_loop(0,count//bq,one,0)
    dk_ref[...]=dka[...].astype(BF)
    dv_ref[...]=dva[...].astype(BF)

def attend_bwd(q,k,v,o,do,lse,rseg,kseg,lo,hi,causal,bq=256,bk=256):
    count,width=q.shape; keys=k.shape[0]
    heads=width//HEAD_DIM
    vm=pl.BlockSpec(memory_space=pltpu.VMEM); sm=pl.BlockSpec(memory_space=pltpu.SMEM)
    return pl.pallas_call(functools.partial(bwd_kernel,causal,heads,bq,bk),
        out_shape=(jax.ShapeDtypeStruct((count,width),BF),jax.ShapeDtypeStruct((keys,width),BF),jax.ShapeDtypeStruct((keys,width),BF)),
        in_specs=[sm,sm]+[vm]*8,out_specs=(vm,vm,vm),
        scratch_shapes=[pltpu.VMEM((keys,width),F32),pltpu.VMEM((keys,width),F32),pltpu.VMEM((heads*bq,width),BF),pltpu.VMEM((heads*bq,width),BF),pltpu.VMEM((bq,width),F32)],
        compiler_params=pltpu.CompilerParams(vmem_limit_bytes=40<<20),
        cost_estimate=pl.CostEstimate(flops=30_000_000_000, bytes_accessed=8_000_000, transcendentals=0),
        name="attend_bwd",
    )(lo,hi,q,k,v,o,do,lse,rseg,kseg)

def ranges(tok_lengths, enc_lengths, pad, count, frames, bq, bk):
    tend=jnp.cumsum(tok_lengths,dtype=jnp.int32); eend=jnp.cumsum(enc_lengths,dtype=jnp.int32)
    places=jnp.arange(count,dtype=jnp.int32)
    tseg=jnp.sum((places[:,None]>=tend[None,:]).astype(jnp.int32),axis=1)
    eseg=jnp.sum((jnp.arange(frames,dtype=jnp.int32)[:,None]>=eend[None,:]).astype(jnp.int32),axis=1)
    starts=jnp.arange(count//bq,dtype=jnp.int32)*bq
    first=tseg[::bq]; last=tseg[bq-1::bq]
    onehot=lambda s:(s[:,None]==jnp.arange(tend.shape[0])[None,:]).astype(jnp.int32)
    pick=lambda arr,s: jnp.sum(onehot(s)*arr[None,:],axis=1)
    tstart=tend-tok_lengths; estart=eend-enc_lengths
    slo=pick(tstart,first)//bk; shi=(starts+bq+bk-1)//bk
    clo=pick(estart,first)//bk; chi=(pick(eend,last)+bk-1)//bk
    kpad=jnp.where(pad==1,tseg,-1)
    return tseg,eseg,kpad,slo,shi,clo,chi


def along_rows(left, right):
    return lax.dot_general(
        left, right, (((0,), (0,)), ((), ())), preferred_element_type=jnp.float32
    )


def against(left, weight):
    return lax.dot_general(
        left, weight, (((1,), (1,)), ((), ())), preferred_element_type=jnp.float32
    )


def times(left, weight):
    return jnp.dot(left, weight, preferred_element_type=jnp.float32)


def moments(rows):
    centred = rows - jnp.mean(rows, axis=1, keepdims=True)
    inverse = lax.rsqrt(jnp.mean(centred * centred, axis=1, keepdims=True) + eps)
    return centred * inverse, inverse


def normalize_back(grad_out, unit, inverse, gain):
    scaled = grad_out * gain
    inner = (
        scaled
        - jnp.mean(scaled, axis=1, keepdims=True)
        - unit * jnp.mean(scaled * unit, axis=1, keepdims=True)
    )
    return (inner * inverse, jnp.sum(grad_out * unit, axis=0), jnp.sum(grad_out, axis=0))


class Place:
    def __init__(self):
        self.dp = lax.axis_size("dp")
        self.tensor = lax.axis_size("tensor")
        self.d = lax.axis_index("dp")
        self.t = lax.axis_index("tensor")
        self.core = self.d % 2
        self.half = self.t // 2
        self.side = self.t % 2
        self.keeper = self.core == self.half
        self.shard = jnp.where(self.keeper, self.t, self.t ^ 2)

    def swap(self, value, d_flip, t_flip, only=None):
        pairs = []
        for d in range(self.dp):
            for t in range(self.tensor):
                keeper = d % 2 == t // 2
                if only is None or only == keeper:
                    pairs.append((d * self.tensor + t, (d ^ d_flip) * self.tensor + (t ^ t_flip)))
        return lax.ppermute(value, ("dp", "tensor"), pairs)

    def home(self, value):
        return jnp.where(self.keeper, value, self.swap(value, 1, 2, False))

    def ordered(self, mine, other, which):
        return jnp.where(
            which == 0, jnp.concatenate([mine, other]), jnp.concatenate([other, mine])
        )

    def part(self, value, which, parts):
        size = value.shape[0] // parts
        return lax.dynamic_slice_in_dim(value, which * size, size, 0)

    def both_cores(self, half_rows):
        return self.ordered(half_rows, self.swap(half_rows, 1, 0), self.core)

    def spread_columns(self, value):
        near, far = self.part(value, self.core, 2), self.part(value, 1 - self.core, 2)
        return jnp.concatenate(
            [near, self.swap(far, 1, 0), self.swap(near, 0, 1), self.swap(far, 1, 1)], axis=1
        )

    def order(self):
        return [self.shard, self.shard ^ 2, self.shard ^ 1, self.shard ^ 3]

    def sum_half(self, value):
        near, far = self.part(value, self.core, 2), self.part(value, 1 - self.core, 2)
        return near.astype(jnp.float32) + self.swap(far.astype(jnp.bfloat16), 1, 0).astype(jnp.float32)

    def sum_group_half(self, value):
        mine = self.sum_half(value).astype(jnp.bfloat16)
        return mine.astype(jnp.float32) + self.swap(mine, 0, 1).astype(jnp.float32)

    def sum_group_quarter(self, value):
        mine = self.sum_half(value)
        near, far = self.part(mine, self.side, 2), self.part(mine, 1 - self.side, 2)
        return near + self.swap(far.astype(jnp.bfloat16), 0, 1).astype(jnp.float32)

    def moved_weight(self, weight):
        piece = self.swap(self.part(weight, self.d, self.dp), 0, 2)
        return jnp.where(self.keeper, weight, lax.all_gather(piece, "dp", axis=0, tiled=True))

    def whole_weight(self, weight):
        piece = self.part(weight, self.d, self.dp)
        every = lax.all_gather(piece, ("dp", "tensor"), axis=0, tiled=False)
        every = every.reshape((self.dp, self.tensor) + piece.shape)
        return jnp.swapaxes(every, 0, 1).reshape((self.tensor,) + weight.shape)


def sum_kernel(dp, shapes, units, *refs):
    count = len(shapes)
    ins, outs = refs[:count], refs[count : 2 * count]
    rest = refs[2 * count :]
    bits = [b for b in (2, 4, 8, 16, 32, 64) if b < dp]
    steps = len(bits)
    per = steps + 1
    land = [rest[u * 2 * per : u * 2 * per + per] for u in range(len(units))]
    hold = [rest[u * 2 * per + per : (u + 1) * 2 * per] for u in range(len(units))]
    send_sem, recv_sem = rest[len(units) * 2 * per :]
    d, t = lax.axis_index("dp"), lax.axis_index("tensor")
    keeper = (d % 2) == (t // 2)
    MESH = pl.DeviceIdType.MESH

    barrier = pltpu.get_barrier_semaphore()
    around = [(d ^ b, t) for b in bits] + [(d, t ^ 2), (d ^ 1, t)]
    for device in around:
        pl.semaphore_signal(barrier, inc=1, device_id=device, device_id_type=MESH)
    pl.semaphore_wait(barrier, len(around))

    def my(bit):
        return (d // bit) % 2

    def order(u):
        return bits if units[u][3] == 0 else bits[::-1]

    def source(u, step):
        array, first, rows, _ = units[u]
        return (ins[array], first) if step == 0 else (hold[u][step - 1], 0)

    def copy(u, stage, src, dst, device):
        return pltpu.make_async_remote_copy(
            src_ref=src, dst_ref=dst, send_sem=send_sem.at[u, stage], recv_sem=recv_sem.at[u, stage],
            device_id=device, device_id_type=MESH,
        )

    def quarter(u):
        array, first, rows, _ = units[u]
        place = first
        for step, bit in enumerate(order(u)):
            place = place + my(bit) * (rows >> (step + 1))
        return place

    def scatter_copy(u, step):
        ref, first = source(u, step)
        size = units[u][2] >> (step + 1)
        bit = order(u)[step]
        start = pl.multiple_of(first + (1 - my(bit)) * size, 16)
        return copy(u, step, ref.at[pl.ds(start, size)], land[u][step], (d ^ bit, t))

    def plane_copy(u):
        ref, first = source(u, steps)
        return copy(u, steps, ref, land[u][steps], (d, t ^ 2))

    def gather_copy(u, step):
        array, first, rows, _ = units[u]
        bit = order(u)[steps - 1 - step]
        size = rows >> (steps - step)
        start = quarter(u)
        for back in range(step):
            done = order(u)[steps - 1 - back]
            start = start - my(done) * (rows >> (steps - back))
        block = outs[array].at[pl.ds(pl.multiple_of(start, 16), size)]
        return copy(u, steps + 1 + step, block, block, (d ^ bit, t))

    def core_copy(u):
        array, first, rows, _ = units[u]
        block = outs[array].at[pl.ds(first, rows)]
        return copy(u, 2 * steps + 1, block, block, (d ^ 1, t))

    def add(dst, dst_first, left, left_first, right, rows):
        chunk = min(rows, 32)

        def body(i, _):
            at = i * chunk
            a = left[pl.ds(pl.multiple_of(left_first + at, 16), chunk), :].astype(jnp.float32)
            b = right[pl.ds(pl.multiple_of(at, 16), chunk), :].astype(jnp.float32)
            dst[pl.ds(pl.multiple_of(dst_first + at, 16), chunk), :] = (a + b).astype(jnp.bfloat16)
            return 0

        lax.fori_loop(0, rows // chunk, body, 0)

    def begin(u, stage):
        if stage < steps:
            scatter_copy(u, stage).start()
        elif stage == steps:

            @pl.when(jnp.logical_not(keeper))
            def _():
                plane_copy(u).start()
        else:

            @pl.when(keeper)
            def _():
                (gather_copy(u, stage - steps - 1) if stage <= 2 * steps else core_copy(u)).start()

    def end(u, stage):
        array, first, rows, _ = units[u]
        if stage < steps:
            one = scatter_copy(u, stage)
            one.wait_recv()
            ref, row = source(u, stage)
            size = rows >> (stage + 1)
            add(hold[u][stage], 0, ref, row + my(order(u)[stage]) * size, land[u][stage], size)
            one.wait_send()
        elif stage == steps:

            @pl.when(jnp.logical_not(keeper))
            def _():
                plane_copy(u).wait_send()

            @pl.when(keeper)
            def _():
                plane_copy(u).wait_recv()
                ref, row = source(u, steps)
                add(outs[array], quarter(u), ref, row, land[u][steps], rows >> steps)
        elif stage <= 2 * steps:

            @pl.when(keeper)
            def _():
                gather_copy(u, stage - steps - 1).wait()
        else:

            @pl.when(keeper)
            def _():
                core_copy(u).wait_send()

            @pl.when(jnp.logical_not(keeper))
            def _():
                core_copy(u).wait_recv()

    last = 2 * steps + 2
    wave = sorted({u // 2 for u in range(len(units))})
    for tick in range(len(wave) + last):
        for stage in reversed(range(last + 1)):
            pair = tick - stage
            if 0 <= pair < len(wave):
                for u in (2 * pair, 2 * pair + 1):
                    if stage > 0:
                        end(u, stage - 1)
                    if stage < last:
                        begin(u, stage)


def sum_weights(grads, split, collective_id):
    dp = lax.axis_size("dp")
    shapes = [grad.shape for grad in grads]
    units = []
    for pair in range(len(grads) // 2):
        rows = shapes[2 * pair][0] // split[pair]
        for part in range(split[pair]):
            for side in range(2):
                units.append((2 * pair + side, part * rows, rows, side))
    steps = 0
    while 2 << steps < dp:
        steps += 1
    scratch = []
    for array, first, rows, side in units:
        width = shapes[array][1]
        sizes = [rows >> (k + 1) for k in range(steps)] + [rows >> steps]
        scratch += [pltpu.VMEM((size, width), jnp.bfloat16) for size in sizes]
        scratch += [pltpu.VMEM((size, width), jnp.bfloat16) for size in sizes]
    stages = 2 * steps + 2
    vmem = pl.BlockSpec(memory_space=pltpu.VMEM)
    return pl.pallas_call(
        functools.partial(sum_kernel, dp, shapes, units),
        out_shape=[jax.ShapeDtypeStruct(shape, jnp.bfloat16) for shape in shapes],
        in_specs=[vmem] * len(grads),
        out_specs=[vmem] * len(grads),
        scratch_shapes=scratch
        + [pltpu.SemaphoreType.DMA((len(units), stages)), pltpu.SemaphoreType.DMA((len(units), stages))],
        compiler_params=pltpu.CompilerParams(
            collective_id=collective_id, has_side_effects=True, vmem_limit_bytes=56 << 20
        ),
        cost_estimate=pl.CostEstimate(flops=100_000_000_000, bytes_accessed=16_000_000, transcendentals=0),
        name="sum_weights",
    )(*grads)


def on_device(
    tokens,
    encoder_states,
    tok_lengths,
    enc_lengths,
    pad_mask,
    first_gain,
    first_shift,
    causal_query,
    causal_key,
    causal_value,
    causal_out,
    second_gain,
    second_shift,
    cross_query,
    cross_key,
    cross_value,
    cross_out,
    third_gain,
    third_shift,
    expand_weight,
    reduce_weight,
    cotangent,
):
    place = Place()
    width = causal_query.shape[1]
    length = pad_mask.shape[0]
    frames = encoder_states.shape[0]

    def of_group(value):
        return jnp.where(place.keeper, value, place.swap(value, 1, 0))

    def half_rows(quarter):
        return place.ordered(quarter, place.swap(quarter, 0, 1), place.side)

    def quarter_of(half):
        return place.part(half, place.side, 2)

    tok_lengths, enc_lengths, pad_mask = of_group(tok_lengths), of_group(enc_lengths), of_group(pad_mask)
    block_q, block_k = 256, 512
    token_seg, frame_seg, key_seg, self_lo, self_hi, cross_lo, cross_hi = ranges(
        tok_lengths[0], enc_lengths[0], pad_mask, length, frames, block_q, block_k
    )
    self_keys = jnp.stack([token_seg, key_seg] + [token_seg] * 6)
    cross_keys = jnp.stack([frame_seg] * 8)
    seg_col, seg_row = token_seg[:, None], token_seg[None, :]

    first_weight = place.moved_weight(
        jnp.concatenate([causal_query, causal_key, causal_value], axis=1)
    )
    tokens_here = place.home(tokens)
    tokens_half = half_rows(tokens_here)
    residual = tokens_half.astype(jnp.float32)
    unit, inverse = moments(residual)
    first_all = place.both_cores((unit * first_gain + first_shift).astype(jnp.bfloat16))
    mixed_in = times(first_all, first_weight).astype(jnp.bfloat16)
    query, keyed, valued = (mixed_in[:, i * width : (i + 1) * width] for i in range(3))

    encoder = of_group(encoder_states)
    cross_weight = place.moved_weight(jnp.concatenate([cross_key, cross_value], axis=1))
    cross_in = times(encoder, cross_weight).astype(jnp.bfloat16)
    ckeyed, cvalued = cross_in[:, :width], cross_in[:, width:]
    causal_out_all = place.whole_weight(causal_out)
    cross_out_all = place.whole_weight(cross_out)
    cross_query_all = place.whole_weight(cross_query)
    order = place.order()
    pick = lambda every, which: lax.dynamic_index_in_dim(every, which, 0, keepdims=False)
    causal_out_perm = jnp.concatenate([pick(causal_out_all, s) for s in order])
    cross_out_perm = jnp.concatenate([pick(cross_out_all, s) for s in order])
    cross_query_perm = jnp.concatenate([pick(cross_query_all, s) for s in order], axis=1)
    causal_out_here, cross_out_here = causal_out_perm[:width], cross_out_perm[:width]
    cross_query_here = cross_query_perm[:, :width]

    mixed, self_logsum = attend_fwd(
        query, keyed, valued, seg_col, self_keys, self_lo, self_hi, True, block_q, block_k
    )
    after_self = residual + times(place.spread_columns(mixed), causal_out_perm)
    second_unit, second_inv = moments(after_self)
    second_all = place.both_cores((second_unit * second_gain + second_shift).astype(jnp.bfloat16))
    cquery = times(second_all, cross_query_here).astype(jnp.bfloat16)
    cmixed, cross_logsum = attend_fwd(
        cquery, ckeyed, cvalued, seg_col, cross_keys, cross_lo, cross_hi, False, block_q, block_k
    )
    after_cross = after_self + times(place.spread_columns(cmixed), cross_out_perm)
    third_unit, third_inv = moments(after_cross)
    third_all = place.both_cores((third_unit * third_gain + third_shift).astype(jnp.bfloat16))

    ff_weight = place.moved_weight(jnp.concatenate([expand_weight, reduce_weight], axis=1))
    hidden_width = expand_weight.shape[1]
    expand_here, reduce_here = ff_weight[:, :hidden_width], ff_weight[:, hidden_width:]
    cot_half = half_rows(place.home(cotangent))
    grad_top = place.both_cores(cot_half)
    grad_hidden = against(grad_top, reduce_here).astype(jnp.bfloat16)

    pre_act = times(third_all, expand_here)
    hidden = smooth_gate(pre_act).astype(jnp.bfloat16)
    grad_expand_in = (grad_hidden.astype(jnp.float32) * smooth_slope(pre_act)).astype(jnp.bfloat16)
    third_in = place.sum_group_half(against(grad_expand_in, expand_here))
    back_rows, third_gain_grad, third_shift_grad = normalize_back(
        third_in, third_unit, third_inv, third_gain
    )
    grad_res = cot_half.astype(jnp.float32) + back_rows
    out_here = quarter_of(after_cross) + place.sum_group_quarter(times(hidden, reduce_here))
    output = place.home(out_here.astype(jnp.bfloat16))
    reduce_grad = along_rows(hidden, grad_top)
    expand_grad = along_rows(third_all, grad_expand_in)

    grad_top = place.both_cores(grad_res.astype(jnp.bfloat16))
    cross_out_grad = along_rows(cmixed, grad_top)
    grad_cmixed = against(grad_top, cross_out_here).astype(jnp.bfloat16)
    grad_cquery, grad_ckey, grad_cvalue = attend_bwd(
        cquery, ckeyed, cvalued, cmixed, grad_cmixed, cross_logsum, seg_row, cross_keys.T,
        cross_lo, cross_hi, False, block_q, block_k,
    )
    grad_cross_in = jnp.concatenate([grad_ckey, grad_cvalue], axis=1)
    cross_grad = along_rows(encoder, grad_cross_in)
    cross_query_grad = along_rows(second_all, grad_cquery)
    encoder_grad = place.home(
        place.sum_group_quarter(against(grad_cross_in, cross_weight)).astype(jnp.bfloat16)
    )
    second_in = against(place.spread_columns(grad_cquery), cross_query_perm)
    back_rows, second_gain_grad, second_shift_grad = normalize_back(
        second_in, second_unit, second_inv, second_gain
    )
    grad_res = grad_res + back_rows
    grad_top = place.both_cores(grad_res.astype(jnp.bfloat16))
    causal_out_grad = along_rows(mixed, grad_top)
    grad_mixed = against(grad_top, causal_out_here).astype(jnp.bfloat16)
    grad_query, grad_key, grad_value = attend_bwd(
        query, keyed, valued, mixed, grad_mixed, self_logsum, seg_row, self_keys.T,
        self_lo, self_hi, True, block_q, block_k,
    )
    grad_in = jnp.concatenate([grad_query, grad_key, grad_value], axis=1)
    causal_grad = along_rows(first_all, grad_in)
    first_in = place.sum_group_quarter(against(grad_in, first_weight))
    first_unit, first_inv = moments(tokens_here.astype(jnp.float32))
    back_rows, first_gain_grad, first_shift_grad = normalize_back(
        first_in, first_unit, first_inv, first_gain
    )
    tokens_grad = place.home((quarter_of(grad_res) + back_rows).astype(jnp.bfloat16))

    bf16 = jnp.bfloat16
    sums = sum_weights(
        [
            expand_grad.astype(bf16),
            reduce_grad.astype(bf16),
            jnp.concatenate([cross_grad, cross_query_grad], axis=1).astype(bf16),
            causal_grad.astype(bf16),
            cross_out_grad.astype(bf16),
            causal_out_grad.astype(bf16),
        ],
        (2, 1, 1),
        0,
    )
    expand_grad, reduce_grad, cross_grads, causal_grads, cross_out_grad, causal_out_grad = (
        value.astype(jnp.float32) for value in sums
    )
    cross_key_grad, cross_value_grad, cross_query_grad = (
        cross_grads[:, i * width : (i + 1) * width] for i in range(3)
    )
    causal_query_grad, causal_key_grad, causal_value_grad = (
        causal_grads[:, i * width : (i + 1) * width] for i in range(3)
    )
    once = (place.side == 0).astype(jnp.float32)
    (
        first_gain_grad,
        first_shift_grad,
        second_gain_grad,
        second_shift_grad,
        third_gain_grad,
        third_shift_grad,
    ) = lax.psum(
        (
            first_gain_grad,
            first_shift_grad,
            second_gain_grad * once,
            second_shift_grad * once,
            third_gain_grad * once,
            third_shift_grad * once,
        ),
        ("dp", "tensor"),
    )
    return (
        output,
        tokens_grad,
        encoder_grad,
        first_gain_grad,
        first_shift_grad,
        causal_query_grad,
        causal_key_grad,
        causal_value_grad,
        causal_out_grad,
        second_gain_grad,
        second_shift_grad,
        cross_query_grad,
        cross_key_grad,
        cross_value_grad,
        cross_out_grad,
        third_gain_grad,
        third_shift_grad,
        expand_grad,
        reduce_grad,
    )


def solution(mesh):
    in_specs = (
        P(("dp", "tensor"), None),
        P("dp", None),
        P("dp", None),
        P("dp", None),
        P("dp"),
        P(),
        P(),
        P(None, "tensor"),
        P(None, "tensor"),
        P(None, "tensor"),
        P("tensor", None),
        P(),
        P(),
        P(None, "tensor"),
        P(None, "tensor"),
        P(None, "tensor"),
        P("tensor", None),
        P(),
        P(),
        P(None, "tensor"),
        P("tensor", None),
        P(("dp", "tensor"), None),
    )
    out_specs = (
        P(("dp", "tensor"), None),
        P(("dp", "tensor"), None),
        P(("dp", "tensor"), None),
        P(),
        P(),
        P(None, "tensor"),
        P(None, "tensor"),
        P(None, "tensor"),
        P("tensor", None),
        P(),
        P(),
        P(None, "tensor"),
        P(None, "tensor"),
        P(None, "tensor"),
        P("tensor", None),
        P(),
        P(),
        P(None, "tensor"),
        P("tensor", None),
    )
    return jax.shard_map(
        on_device, mesh=mesh, in_specs=in_specs, out_specs=out_specs, check_vma=False
    )
```

```python
import functools

import jax
import jax.numpy as jnp
from jax import lax
from jax.experimental import pallas as pl
from jax.experimental.pallas import tpu as pltpu
from jax.sharding import PartitionSpec as P

HEAD_DIM = 64


eps = 1e-05
tanh_coeff = 0.7978845608
cubic_coeff = 0.044715


def smooth_gate(values):
    inner = jnp.tanh(tanh_coeff * (values + cubic_coeff * values * values * values))
    return 0.5 * values * (1.0 + inner)


def smooth_slope(values):
    inner = jnp.tanh(tanh_coeff * (values + cubic_coeff * values * values * values))
    return 0.5 * (1.0 + inner) + 0.5 * values * (1.0 - inner * inner) * tanh_coeff * (
        1.0 + 3.0 * cubic_coeff * values * values
    )


BF=jnp.bfloat16
F32=jnp.float32

def head_mask(rows, width, h):
    lane = lax.broadcasted_iota(jnp.int32, (rows, width), 1)
    return (lane // HEAD_DIM) == h

def dot(a,b,ca,cb):
    return lax.dot_general(a,b,(((ca,),(cb,)),((),())),preferred_element_type=F32)

def fwd_kernel(causal, heads, bq, bk, lo_ref, hi_ref, q_ref, k_ref, v_ref, rs_ref, ks_ref, o_ref, lse_ref, acc):
    count, width = q_ref.shape
    def one(qb, _):
        q0 = pl.multiple_of(qb*bq, bq)
        qv = q_ref[pl.ds(q0,bq),:] * BF(HEAD_DIM**-0.5)
        rseg = rs_ref[pl.ds(q0,bq),0:1]
        qm = [jnp.where(head_mask(bq,width,h), qv, BF(0)) for h in range(heads)]
        acc[...] = jnp.zeros_like(acc)
        lane = lax.broadcasted_iota(jnp.int32,(bq,128),1)
        def inner(kb, carry):
            k0 = pl.multiple_of(kb*bk, bk)
            kv = k_ref[pl.ds(k0,bk),:]
            vv = v_ref[pl.ds(k0,bk),:]
            kseg = ks_ref[0:1,pl.ds(k0,bk)]
            if causal:
                kpad = ks_ref[1:2,pl.ds(k0,bk)]
                ri = lax.broadcasted_iota(jnp.int32,(bq,bk),0)+q0
                ci = lax.broadcasted_iota(jnp.int32,(bq,bk),1)+k0
                ok = ((rseg==kpad)&(ci<=ri))|(ci==ri)
            else:
                ok = rseg==kseg
            ms, ls = carry
            new_m, new_l = [], []
            parts=None
            alphas=[]
            for h in range(heads):
                s = dot(qm[h],kv,1,1)
                s = jnp.where(ok,s,-1e30)
                m = jnp.maximum(ms[h], jnp.max(s,axis=1,keepdims=True))
                p = jnp.exp(s-m)
                al = jnp.exp(ms[h]-m)
                new_m.append(m); new_l.append(ls[h]*al+jnp.sum(p,axis=1,keepdims=True))
                vm = jnp.where(head_mask(bk,width,h),vv,BF(0))
                t = dot(p.astype(BF),vm,1,0)
                parts = t if parts is None else parts+t
                alphas.append(al)
            lane2 = lax.broadcasted_iota(jnp.int32,(bq,width),1)//HEAD_DIM
            sc = alphas[heads-1]
            for h in range(heads-1):
                sc = jnp.where(lane2==h, alphas[h], sc)
            acc[...] = acc[...]*sc + parts
            return (tuple(new_m),tuple(new_l))
        init = (tuple(jnp.full((bq,1),-1e30,F32) for _ in range(heads)), tuple(jnp.zeros((bq,1),F32) for _ in range(heads)))
        ms, ls = lax.fori_loop(lo_ref[qb], hi_ref[qb], inner, init)
        lane2 = lax.broadcasted_iota(jnp.int32,(bq,width),1)//HEAD_DIM
        inv = [1.0/l for l in ls]
        sc = inv[heads-1]
        for h in range(heads-1):
            sc = jnp.where(lane2==h, inv[h], sc)
        o_ref[pl.ds(q0,bq),:] = (acc[...]*sc).astype(BF)
        st = jnp.zeros((bq,128),F32)
        for h in range(heads):
            st = jnp.where(lane==h, ms[h]+jnp.log(ls[h]), st)
        stt = jnp.transpose(st)
        lse_ref[:,pl.ds(q0,bq)] = stt[0:8,:]
        return 0
    lax.fori_loop(0,count//bq,one,0)

def attend_fwd(q,k,v,rseg,kseg,lo,hi,causal,bq=256,bk=256):
    count,width=q.shape
    heads=width//HEAD_DIM
    vm=pl.BlockSpec(memory_space=pltpu.VMEM); sm=pl.BlockSpec(memory_space=pltpu.SMEM)
    return pl.pallas_call(functools.partial(fwd_kernel,causal,heads,bq,bk),
        out_shape=(jax.ShapeDtypeStruct((count,width),BF),jax.ShapeDtypeStruct((8,count),F32)),
        in_specs=[sm,sm,vm,vm,vm,vm,vm],out_specs=(vm,vm),
        scratch_shapes=[pltpu.VMEM((bq,width),F32)],
        compiler_params=pltpu.CompilerParams(vmem_limit_bytes=40<<20),
        cost_estimate=pl.CostEstimate(flops=22_000_000_000, bytes_accessed=8_000_000, transcendentals=0),
        name="attend_fwd",
    )(lo,hi,q,k,v,rseg,kseg)

def bwd_kernel(causal, heads, bq, bk, lo_ref, hi_ref, q_ref, k_ref, v_ref, o_ref, do_ref, lse_ref, rs_ref, ks_ref,
               dq_ref, dk_ref, dv_ref, dka, dva, qm, dom, dqa):
    count,width=q_ref.shape
    dka[...]=jnp.zeros_like(dka); dva[...]=jnp.zeros_like(dva)
    def one(qb,_):
        q0=pl.multiple_of(qb*bq,bq)
        qv=q_ref[pl.ds(q0,bq),:]*BF(HEAD_DIM**-0.5)
        dov=do_ref[pl.ds(q0,bq),:]
        prod=dov.astype(F32)*o_ref[pl.ds(q0,bq),:].astype(F32)
        row=lax.broadcasted_iota(jnp.int32,(8,width),0); col=lax.broadcasted_iota(jnp.int32,(8,width),1)//HEAD_DIM
        sel=(row==col).astype(F32)
        delta=lax.dot_general(sel,prod,(((1,),(1,)),((),())),precision=lax.Precision.HIGHEST,preferred_element_type=F32)
        for h in range(heads):
            hm=head_mask(bq,width,h)
            qm[pl.ds(h*bq,bq),:]=jnp.where(hm,qv,BF(0))
            dom[pl.ds(h*bq,bq),:]=jnp.where(hm,dov,BF(0))
        dqa[...]=jnp.zeros_like(dqa)
        rseg=rs_ref[0:1,pl.ds(q0,bq)]
        lse=lse_ref[:,pl.ds(q0,bq)]
        def inner(kb,_):
            k0=pl.multiple_of(kb*bk,bk)
            kv=k_ref[pl.ds(k0,bk),:]; vv=v_ref[pl.ds(k0,bk),:]
            if causal:
                kpad=ks_ref[pl.ds(k0,bk),1:2]
                ri=lax.broadcasted_iota(jnp.int32,(bk,bq),1)+q0
                ci=lax.broadcasted_iota(jnp.int32,(bk,bq),0)+k0
                ok=((rseg==kpad)&(ci<=ri))|(ci==ri)
            else:
                ok=rseg==ks_ref[pl.ds(k0,bk),0:1]
            ps=[];dss=[]
            dq=None
            for h in range(heads):
                st=dot(kv,qm[pl.ds(h*bq,bq),:],1,1)
                p=jnp.where(ok,jnp.exp(st-lse[h:h+1,:]),0.0)
                dp=dot(vv,dom[pl.ds(h*bq,bq),:],1,1)
                ds=(p*(dp-delta[h:h+1,:])).astype(BF)
                ps.append(p.astype(BF)); dss.append(ds)
                km=jnp.where(head_mask(bk,width,h),kv,BF(0))
                t=dot(ds,km,0,0)
                dq=t if dq is None else dq+t
            dqa[...]+=dq
            pcat=jnp.concatenate(ps,axis=1); dcat=jnp.concatenate(dss,axis=1)
            dva[pl.ds(k0,bk),:]+=dot(pcat,dom[...],1,0)
            dka[pl.ds(k0,bk),:]+=dot(dcat,qm[...],1,0)
            return 0
        lax.fori_loop(lo_ref[qb],hi_ref[qb],inner,0)
        dq_ref[pl.ds(q0,bq),:]=(dqa[...]*(HEAD_DIM**-0.5)).astype(BF)
        return 0
    lax.fori_loop(0,count//bq,one,0)
    dk_ref[...]=dka[...].astype(BF)
    dv_ref[...]=dva[...].astype(BF)

def attend_bwd(q,k,v,o,do,lse,rseg,kseg,lo,hi,causal,bq=256,bk=256):
    count,width=q.shape; keys=k.shape[0]
    heads=width//HEAD_DIM
    vm=pl.BlockSpec(memory_space=pltpu.VMEM); sm=pl.BlockSpec(memory_space=pltpu.SMEM)
    return pl.pallas_call(functools.partial(bwd_kernel,causal,heads,bq,bk),
        out_shape=(jax.ShapeDtypeStruct((count,width),BF),jax.ShapeDtypeStruct((keys,width),BF),jax.ShapeDtypeStruct((keys,width),BF)),
        in_specs=[sm,sm]+[vm]*8,out_specs=(vm,vm,vm),
        scratch_shapes=[pltpu.VMEM((keys,width),F32),pltpu.VMEM((keys,width),F32),pltpu.VMEM((heads*bq,width),BF),pltpu.VMEM((heads*bq,width),BF),pltpu.VMEM((bq,width),F32)],
        compiler_params=pltpu.CompilerParams(vmem_limit_bytes=40<<20),
        cost_estimate=pl.CostEstimate(flops=30_000_000_000, bytes_accessed=8_000_000, transcendentals=0),
        name="attend_bwd",
    )(lo,hi,q,k,v,o,do,lse,rseg,kseg)

def ranges(tok_lengths, enc_lengths, pad, count, frames, bq, bk):
    tend=jnp.cumsum(tok_lengths,dtype=jnp.int32); eend=jnp.cumsum(enc_lengths,dtype=jnp.int32)
    places=jnp.arange(count,dtype=jnp.int32)
    tseg=jnp.sum((places[:,None]>=tend[None,:]).astype(jnp.int32),axis=1)
    eseg=jnp.sum((jnp.arange(frames,dtype=jnp.int32)[:,None]>=eend[None,:]).astype(jnp.int32),axis=1)
    starts=jnp.arange(count//bq,dtype=jnp.int32)*bq
    first=tseg[::bq]; last=tseg[bq-1::bq]
    onehot=lambda s:(s[:,None]==jnp.arange(tend.shape[0])[None,:]).astype(jnp.int32)
    pick=lambda arr,s: jnp.sum(onehot(s)*arr[None,:],axis=1)
    tstart=tend-tok_lengths; estart=eend-enc_lengths
    slo=pick(tstart,first)//bk; shi=(starts+bq+bk-1)//bk
    clo=pick(estart,first)//bk; chi=(pick(eend,last)+bk-1)//bk
    kpad=jnp.where(pad==1,tseg,-1)
    return tseg,eseg,kpad,slo,shi,clo,chi


def along_rows(left, right):
    return lax.dot_general(
        left, right, (((0,), (0,)), ((), ())), preferred_element_type=jnp.float32
    )


def against(left, weight):
    return lax.dot_general(
        left, weight, (((1,), (1,)), ((), ())), preferred_element_type=jnp.float32
    )


def times(left, weight):
    return jnp.dot(left, weight, preferred_element_type=jnp.float32)


def moments(rows):
    centred = rows - jnp.mean(rows, axis=1, keepdims=True)
    inverse = lax.rsqrt(jnp.mean(centred * centred, axis=1, keepdims=True) + eps)
    return centred * inverse, inverse


def normalize_back(grad_out, unit, inverse, gain):
    scaled = grad_out * gain
    inner = (
        scaled
        - jnp.mean(scaled, axis=1, keepdims=True)
        - unit * jnp.mean(scaled * unit, axis=1, keepdims=True)
    )
    return (inner * inverse, jnp.sum(grad_out * unit, axis=0), jnp.sum(grad_out, axis=0))


class Place:
    def __init__(self):
        self.dp = lax.axis_size("dp")
        self.tensor = lax.axis_size("tensor")
        self.d = lax.axis_index("dp")
        self.t = lax.axis_index("tensor")
        self.core = self.d % 2
        self.half = self.t // 2
        self.side = self.t % 2
        self.keeper = self.core == self.half
        self.shard = jnp.where(self.keeper, self.t, self.t ^ 2)

    def swap(self, value, d_flip, t_flip, only=None):
        pairs = []
        for d in range(self.dp):
            for t in range(self.tensor):
                keeper = d % 2 == t // 2
                if only is None or only == keeper:
                    pairs.append((d * self.tensor + t, (d ^ d_flip) * self.tensor + (t ^ t_flip)))
        return lax.ppermute(value, ("dp", "tensor"), pairs)

    def home(self, value):
        return jnp.where(self.keeper, value, self.swap(value, 1, 2, False))

    def ordered(self, mine, other, which):
        return jnp.where(
            which == 0, jnp.concatenate([mine, other]), jnp.concatenate([other, mine])
        )

    def part(self, value, which, parts):
        size = value.shape[0] // parts
        return lax.dynamic_slice_in_dim(value, which * size, size, 0)

    def both_cores(self, half_rows):
        return self.ordered(half_rows, self.swap(half_rows, 1, 0), self.core)

    def spread_columns(self, value):
        near, far = self.part(value, self.core, 2), self.part(value, 1 - self.core, 2)
        return jnp.concatenate(
            [near, self.swap(far, 1, 0), self.swap(near, 0, 1), self.swap(far, 1, 1)], axis=1
        )

    def order(self):
        return [self.shard, self.shard ^ 2, self.shard ^ 1, self.shard ^ 3]

    def sum_half(self, value):
        near, far = self.part(value, self.core, 2), self.part(value, 1 - self.core, 2)
        return near.astype(jnp.float32) + self.swap(far.astype(jnp.bfloat16), 1, 0).astype(jnp.float32)

    def sum_group_half(self, value):
        mine = self.sum_half(value).astype(jnp.bfloat16)
        return mine.astype(jnp.float32) + self.swap(mine, 0, 1).astype(jnp.float32)

    def sum_group_quarter(self, value):
        mine = self.sum_half(value)
        near, far = self.part(mine, self.side, 2), self.part(mine, 1 - self.side, 2)
        return near + self.swap(far.astype(jnp.bfloat16), 0, 1).astype(jnp.float32)

    def moved_weight(self, weight):
        piece = self.swap(self.part(weight, self.d, self.dp), 0, 2)
        return jnp.where(self.keeper, weight, lax.all_gather(piece, "dp", axis=0, tiled=True))

    def whole_weight(self, weight):
        piece = self.part(weight, self.d, self.dp)
        every = lax.all_gather(piece, ("dp", "tensor"), axis=0, tiled=False)
        every = every.reshape((self.dp, self.tensor) + piece.shape)
        return jnp.swapaxes(every, 0, 1).reshape((self.tensor,) + weight.shape)


class Copies:
    def __init__(self, send_sem, recv_sem):
        self.send_sem, self.recv_sem, self.known = send_sem, recv_sem, {}

    def __call__(self, name, src, dst, device):
        at = self.known.setdefault(name, len(self.known))
        return pltpu.make_async_remote_copy(
            src_ref=src,
            dst_ref=dst,
            send_sem=self.send_sem.at[at],
            recv_sem=self.recv_sem.at[at],
            device_id=device,
            device_id_type=pl.DeviceIdType.MESH,
        )


def greet(devices):
    barrier = pltpu.get_barrier_semaphore()
    for device in devices:
        pl.semaphore_signal(
            barrier, inc=1, device_id=device, device_id_type=pl.DeviceIdType.MESH
        )
    pl.semaphore_wait(barrier, len(devices))


def rows_of(ref, start, size, step=16):
    return ref.at[pl.ds(pl.multiple_of(start, step), size)]


def norm_rows(src, src_first, dst, dst_first, rows, gain, shift):
    chunk = 64

    def body(i, _):
        at = i * chunk
        x = src[pl.ds(pl.multiple_of(src_first + at, 16), chunk), :].astype(jnp.float32)
        unit, inverse = moments(x)
        dst[pl.ds(pl.multiple_of(dst_first + at, 16), chunk), :] = (
            unit * gain[...] + shift[...]
        ).astype(jnp.bfloat16)
        return 0

    lax.fori_loop(0, rows // chunk, body, 0)


def sum_kernel(dp, counts, units, spans, *refs):
    arrays, row_arrays = counts
    it = iter(refs)
    take = lambda count: [next(it) for _ in range(count)]
    ins, parts = take(arrays), take(row_arrays)
    small_in, after, tokens, grad_in, gain = take(5)
    outs, row_outs = take(arrays), take(row_arrays)
    (small_out,) = take(1)
    bits = [b for b in (2, 4, 8, 16, 32, 64) if b < dp]
    steps = len(bits)
    land, hold = [], []
    for unit in units:
        own = 0 if unit[4] else steps
        hold.append(take(own))
        land.append(([None] * (steps - own)) + take(own + 1))
    row_land = [take(2) for _ in range(row_arrays)]
    row_hold = [take(2) for _ in range(row_arrays)]
    small_hold, small_land, small_send, small_recv, row_send, row_recv, send_sem, recv_sem = take(8)
    d, t = lax.axis_index("dp"), lax.axis_index("tensor")
    core, side = d % 2, t % 2
    keeper = core == t // 2
    other = jnp.logical_not(keeper)
    MESH = pl.DeviceIdType.MESH

    around = [(d ^ b, t) for b in bits] + [(d ^ 1, t), (d, t ^ 2), (d, t ^ 1)]
    greet(around + [(d ^ 1, t ^ 2)])

    def my(bit):
        return (d // bit) % 2

    def order(u):
        return bits if units[u][3] == 0 else bits[::-1]

    def source(u, step):
        array, first, rows, _, summed = units[u]
        if summed:
            return ins[array], first >> steps
        return (ins[array], first) if step == 0 else (hold[u][step - 1], 0)

    def copy(u, stage, src, dst, device):
        return pltpu.make_async_remote_copy(
            src_ref=src, dst_ref=dst, send_sem=send_sem.at[u, stage], recv_sem=recv_sem.at[u, stage],
            device_id=device, device_id_type=MESH,
        )

    def quarter(u):
        place = units[u][1]
        for step, bit in enumerate(order(u)):
            place = place + my(bit) * (units[u][2] >> (step + 1))
        return place

    def scatter_copy(u, step):
        ref, first = source(u, step)
        size = units[u][2] >> (step + 1)
        bit = order(u)[step]
        return copy(u, step, rows_of(ref, first + (1 - my(bit)) * size, size), land[u][step], (d ^ bit, t))

    def plane_copy(u):
        ref, first = source(u, steps)
        return copy(u, steps, rows_of(ref, first, units[u][2] >> steps), land[u][steps], (d, t ^ 2))

    def gather_copy(u, step):
        array, first, rows = units[u][:3]
        bit = order(u)[steps - 1 - step]
        size = rows >> (steps - step)
        start = quarter(u)
        for back in range(step):
            start = start - my(order(u)[steps - 1 - back]) * (rows >> (steps - back))
        block = rows_of(outs[array], start, size)
        return copy(u, steps + 1 + step, block, block, (d ^ bit, t))

    def core_copy(u):
        array, first, rows = units[u][:3]
        block = outs[array].at[pl.ds(first, rows)]
        return copy(u, 2 * steps + 1, block, block, (d ^ 1, t))

    def add(dst, dst_first, left, left_first, right, rows):
        chunk = min(rows, 32)

        def body(i, _):
            at = i * chunk
            a = left[pl.ds(pl.multiple_of(left_first + at, 16), chunk), :].astype(jnp.float32)
            b = right[pl.ds(pl.multiple_of(at, 16), chunk), :].astype(jnp.float32)
            dst[pl.ds(pl.multiple_of(dst_first + at, 16), chunk), :] = (a + b).astype(jnp.bfloat16)
            return 0

        lax.fori_loop(0, rows // chunk, body, 0)

    def begin(u, stage):
        if stage < steps:
            if not units[u][4]:
                scatter_copy(u, stage).start()
        elif stage == steps:

            @pl.when(other)
            def _():
                plane_copy(u).start()
        else:

            @pl.when(keeper)
            def _():
                (gather_copy(u, stage - steps - 1) if stage <= 2 * steps else core_copy(u)).start()

    def end(u, stage):
        array, first, rows = units[u][:3]
        if stage < steps:
            if not units[u][4]:
                one = scatter_copy(u, stage)
                one.wait_recv()
                ref, row = source(u, stage)
                size = rows >> (stage + 1)
                add(hold[u][stage], 0, ref, row + my(order(u)[stage]) * size, land[u][stage], size)
                one.wait_send()
        elif stage == steps:

            @pl.when(other)
            def _():
                plane_copy(u).wait_send()

            @pl.when(keeper)
            def _():
                plane_copy(u).wait_recv()
                ref, row = source(u, steps)
                add(outs[array], quarter(u), ref, row, land[u][steps], rows >> steps)
        elif stage <= 2 * steps:

            @pl.when(keeper)
            def _():
                gather_copy(u, stage - steps - 1).wait()
        else:

            @pl.when(keeper)
            def _():
                core_copy(u).wait_send()

            @pl.when(other)
            def _():
                core_copy(u).wait_recv()

    def row_copy(a, stage):
        size = spans[a]
        if stage == 0:
            src, dst, device = rows_of(parts[a], (1 - core) * 2 * size, 2 * size), row_land[a][0], (d ^ 1, t)
        elif stage == 1:
            src, dst, device = rows_of(row_hold[a][0], (1 - side) * size, size), row_land[a][1], (d, t ^ 1)
        else:
            src, dst, device = row_hold[a][1], row_outs[a], (d ^ 1, t ^ 2)
        return pltpu.make_async_remote_copy(
            src_ref=src, dst_ref=dst, send_sem=row_send.at[a, stage], recv_sem=row_recv.at[a, stage],
            device_id=device, device_id_type=MESH,
        )

    def row_quarter(a):
        size = spans[a]

        def body(i, _):
            at = pl.ds(pl.multiple_of(i * 32, 32), 32)
            total = row_hold[a][0][pl.ds(pl.multiple_of(side * size + i * 32, 32), 32), :].astype(jnp.float32)
            total = total + row_land[a][1][at, :].astype(jnp.float32)
            if a == 1:
                total = total + after[at, :]
            elif a == 2:
                unit, inverse = moments(tokens[at, :].astype(jnp.float32))
                total = grad_in[at, :] + normalize_back(total, unit, inverse, gain[...])[0]
            row_hold[a][1][at, :] = total.astype(jnp.bfloat16)
            return 0

        lax.fori_loop(0, size // 32, body, 0)

    def row_end(a, stage):
        if stage == 0:
            row_copy(a, 0).wait()
            add(row_hold[a][0], 0, parts[a], core * 2 * spans[a], row_land[a][0], 2 * spans[a])
            row_copy(a, 1).start()
        elif stage == 1:
            row_copy(a, 1).wait()
            row_quarter(a)

            @pl.when(keeper)
            def _():
                row_outs[a][...] = row_hold[a][1][...]

            @pl.when(other)
            def _():
                row_copy(a, 2).start()
        else:

            @pl.when(other)
            def _():
                row_copy(a, 2).wait()

    def small_copy(step):
        return pltpu.make_async_remote_copy(
            src_ref=small_hold.at[step], dst_ref=small_land.at[step], send_sem=small_send.at[step],
            recv_sem=small_recv.at[step], device_id=around[step], device_id_type=MESH,
        )

    def small_step(step):
        small_copy(step).wait()
        total = small_hold[step] + small_land[step]
        if step + 1 < len(around):
            small_hold[step + 1] = total
            small_copy(step + 1).start()
        else:
            small_out[...] = total

    for a in range(row_arrays):
        row_copy(a, 0).start()
    small_hold[0] = small_in[...]
    small_copy(0).start()
    last = 2 * steps + 2
    waves = len(units) // 2
    for tick in range(waves + last):
        for stage in reversed(range(last + 1)):
            pair = tick - stage
            if 0 <= pair < waves:
                for u in (2 * pair, 2 * pair + 1):
                    if stage > 0:
                        end(u, stage - 1)
                    if stage < last:
                        begin(u, stage)
        if tick < len(around):
            small_step(tick)
        for a in range(row_arrays):
            if tick == a:
                row_end(a, 0)
            if tick == a + 2:
                row_end(a, 1)
    for a in range(row_arrays):
        row_end(a, 2)


def sum_all(grads, split, summed, parts, norm_grads, after, tokens, grad_in, gain, collective_id):
    dp = lax.axis_size("dp")
    steps = 0
    while 2 << steps < dp:
        steps += 1
    shapes, units, scratch = [], [], []
    bf16, f32 = jnp.bfloat16, jnp.float32
    for index, grad in enumerate(grads):
        scale = 1 << steps if summed[index // 2] else 1
        shapes.append((grad.shape[0] * scale, grad.shape[1]))
    for pair in range(len(grads) // 2):
        rows = shapes[2 * pair][0] // split[pair]
        for part in range(split[pair]):
            for side in range(2):
                units.append((2 * pair + side, part * rows, rows, side, summed[pair]))
    for array, first, rows, side, done in units:
        width = shapes[array][1]
        if not done:
            scratch += [pltpu.VMEM((rows >> (k + 1), width), bf16) for k in range(steps)] * 2
        scratch.append(pltpu.VMEM((rows >> steps, width), bf16))
    stages = 2 * steps + 2
    vmem = pl.BlockSpec(memory_space=pltpu.VMEM)
    spans = [part.shape[0] // 4 for part in parts]
    wide = norm_grads.shape[1]
    row_land = [pltpu.VMEM((many * span, wide), bf16) for span in spans for many in (2, 1)]
    semaphores = pltpu.SemaphoreType.DMA
    return pl.pallas_call(
        functools.partial(sum_kernel, dp, (len(grads), len(parts)), units, spans),
        out_shape=[jax.ShapeDtypeStruct(shape, bf16) for shape in shapes]
        + [jax.ShapeDtypeStruct((span, wide), bf16) for span in spans]
        + [jax.ShapeDtypeStruct(norm_grads.shape, f32)],
        in_specs=[vmem] * (len(grads) + len(parts) + 5),
        out_specs=[vmem] * (len(grads) + len(parts) + 1),
        scratch_shapes=scratch
        + row_land * 2
        + [pltpu.VMEM((steps + 3,) + norm_grads.shape, f32)] * 2
        + [semaphores((steps + 3,))] * 2
        + [semaphores((len(parts), 3))] * 2
        + [semaphores((len(units), stages))] * 2,
        compiler_params=pltpu.CompilerParams(
            collective_id=collective_id, has_side_effects=True, vmem_limit_bytes=60 << 20
        ),
        cost_estimate=pl.CostEstimate(flops=100_000_000_000, bytes_accessed=16_000_000, transcendentals=0),
        name="sum_all",
    )(*grads, *parts, norm_grads, after, tokens, grad_in, gain[None])


def start_kernel(*refs):
    (tokens, gain, shift, *weights, out_weight, encoder) = refs[:8]
    (rows_half, normed, query, keyed, valued, moved, whole, encoder_out) = refs[8:16]
    send_sem, recv_sem = refs[16:]
    d, t = lax.axis_index("dp"), lax.axis_index("tensor")
    core, side, column = d % 2, t % 2, (d // 2) % 4
    keeper = core == t // 2
    other = jnp.logical_not(keeper)
    away = jnp.where(keeper, 0, 1)
    count = tokens.shape[0]
    copy = Copies(send_sem, recv_sem)
    pieces = 4
    piece = count // pieces

    greet(
        [(d ^ 2, t), (d ^ 4, t), (d ^ 6, t), (d ^ 1, t), (d, t ^ 1), (d, t ^ 2), (d, t ^ 3), (d ^ 1, t ^ 2)]
    )

    def place(s, p):
        return rows_of(rows_half, s * count + p * piece, piece)

    def swap_tokens(p):
        return copy(("swap", p), tokens.at[pl.ds(p * piece, piece)], place(side, p), (d ^ 1, t ^ 2))

    def pass_tokens(p, src):
        return copy(("pass", p), src, place(side, p), (d, t ^ 1))

    part = weights[0].shape[0] // 4

    def move(a):
        return copy(
            ("move", a), rows_of(weights[a], column * part, part), rows_of(moved.at[a], column * part, part), (d, t ^ 2)
        )

    def share(a, m):
        block = rows_of(moved.at[a], column * part, part)
        return copy(("share", a, m), block, block, (d ^ (2 * m), t))

    shard_rows = out_weight.shape[0]
    slim = shard_rows // 8
    slice_at = core * (4 * slim) + column * slim

    def spread(x):
        block = (2 if x % 2 else 0) + away
        return copy(
            ("spread", x), rows_of(out_weight, slice_at, slim),
            rows_of(whole, block * shard_rows + slice_at, slim), (d, t ^ x),
        )

    def level(j, m):
        block = rows_of(whole, j * shard_rows + slice_at, slim)
        return copy(("level", j, m), block, block, (d ^ (2 * m), t))

    def hand(j):
        at = core * (4 * slim)
        return copy(
            ("hand", j), rows_of(whole, j * shard_rows + at, 4 * slim),
            rows_of(whole, (j ^ 1) * shard_rows + at, 4 * slim), (d ^ 1, t),
        )

    def give(s):
        block = rows_of(normed, core * (2 * count) + s * count, count)
        return copy(("give", 0), block, block, (d ^ 1, t))

    def give_late(s):
        block = rows_of(normed, core * (2 * count) + s * count, count)
        return copy(("give", 1), block, block, (d ^ 1, t))

    encoder_copy = copy("encoder", encoder, encoder_out, (d ^ 1, t))

    @pl.when(other)
    def _():
        for p in range(pieces):
            swap_tokens(p).start()

    @pl.when(keeper)
    def _():
        for p in range(pieces):
            pass_tokens(p, tokens.at[pl.ds(p * piece, piece)]).start()
        for a in range(3):
            move(a).start()

    for x in (1, 2, 3):
        spread(x).start()

    @pl.when(keeper)
    def _():
        encoder_copy.start()
        rows_half[pl.ds(pl.multiple_of(side * count, 16), count), :] = tokens[...]

    whole[pl.ds(pl.multiple_of(away * shard_rows + slice_at, 16), slim), :] = out_weight[
        pl.ds(pl.multiple_of(slice_at, 16), slim), :
    ]

    @pl.when(other)
    def _():
        for p in range(pieces):
            swap_tokens(p).wait_recv()
            pass_tokens(p, place(side, p)).start()
        for a in range(3):
            move(a).wait_recv()
            for m in (1, 2, 3):
                share(a, m).start()

    mine = core * (2 * count)
    norm_rows(rows_half, side * count, normed, mine + side * count, count, gain, shift)
    give(side).start()

    for p in range(pieces):
        copy(("pass", p), place(1 - side, p), place(1 - side, p), (d, t ^ 1)).wait_recv()
    norm_rows(rows_half, (1 - side) * count, normed, mine + (1 - side) * count, count, gain, shift)
    give_late(1 - side).start()

    for x in (1, 2, 3):
        spread(x).wait_recv()
    for j in range(4):
        for m in (1, 2, 3):
            level(j, m).start()

    @pl.when(keeper)
    def _():
        for a in range(3):
            moved[a] = weights[a][...]
        encoder_out[...] = encoder[...]

    @pl.when(other)
    def _():
        for a in range(3):
            for m in (1, 2, 3):
                share(a, m).wait_recv()

    def project(first):
        def body(i, _):
            at = pl.ds(pl.multiple_of(first + i * 256, 256), 256)
            for a, out in enumerate((query, keyed, valued)):
                out[at, :] = jnp.dot(
                    normed[at, :], moved[a], preferred_element_type=jnp.float32
                ).astype(jnp.bfloat16)
            return 0

        lax.fori_loop(0, (2 * count) // 256, body, 0)

    project(mine)

    give(side).wait()
    give_late(1 - side).wait()
    project((1 - core) * (2 * count))

    for j in range(4):
        for m in (1, 2, 3):
            level(j, m).wait_recv()
    for j in range(4):
        hand(j).start()
    for j in range(4):
        for m in (1, 2, 3):
            level(j, m).wait_send()
    for x in (1, 2, 3):
        spread(x).wait_send()
    for j in range(4):
        hand(j).wait()

    @pl.when(keeper)
    def _():
        for p in range(pieces):
            pass_tokens(p, tokens.at[pl.ds(p * piece, piece)]).wait_send()
        for a in range(3):
            move(a).wait_send()
        encoder_copy.wait_send()

    @pl.when(other)
    def _():
        for p in range(pieces):
            swap_tokens(p).wait_send()
            pass_tokens(p, place(side, p)).wait_send()
        for a in range(3):
            for m in (1, 2, 3):
                share(a, m).wait_send()
        encoder_copy.wait_recv()


def start_layer(tokens, gain, shift, weights, out_weight, encoder, collective_id):
    rows, wide = tokens.shape
    width = weights[0].shape[1]
    bf16 = jnp.bfloat16
    shape = jax.ShapeDtypeStruct
    vmem = pl.BlockSpec(memory_space=pltpu.VMEM)
    return pl.pallas_call(
        start_kernel,
        out_shape=(
            shape((2 * rows, wide), bf16),
            shape((4 * rows, wide), bf16),
            shape((4 * rows, width), bf16),
            shape((4 * rows, width), bf16),
            shape((4 * rows, width), bf16),
            shape((3,) + weights[0].shape, bf16),
            shape((4 * out_weight.shape[0], out_weight.shape[1]), bf16),
            shape(encoder.shape, bf16),
        ),
        in_specs=[vmem] * 8,
        out_specs=(vmem,) * 8,
        scratch_shapes=[
            pltpu.SemaphoreType.DMA((64,)),
            pltpu.SemaphoreType.DMA((64,)),
        ],
        compiler_params=pltpu.CompilerParams(
            collective_id=collective_id, has_side_effects=True, vmem_limit_bytes=56 << 20
        ),
        cost_estimate=pl.CostEstimate(flops=35_000_000_000, bytes_accessed=16_000_000, transcendentals=0),
        name="start_layer",
    )(tokens, gain[None], shift[None], *weights, out_weight, encoder)


def add_dot(left, right, over_rows=False):
    return lax.dot_general(
        left, right, (((1,), (1 if over_rows else 0,)), ((), ())), preferred_element_type=jnp.float32
    )


class Exchange:
    def __init__(self, copy, mine, land, core, d, t, chunk):
        self.copy, self.mine, self.land, self.core, self.chunk = copy, mine, land, core, chunk
        self.half = mine.shape[0] // 2
        self.to = [(d ^ 1, t), (d, t ^ 1), (d ^ 1, t ^ 1)]

    def one(self, j, ch):
        core = self.core if j == 1 else 1 - self.core
        return self.copy(
            ("exchange", j, ch),
            rows_of(self.mine, core * self.half + ch * self.chunk, self.chunk),
            self.land.at[j, pl.ds(ch * self.chunk, self.chunk)],
            self.to[j],
        )

    def start(self, ch):
        for j in (1, 2, 0):
            self.one(j, ch).start()

    def arrive(self, ch):
        for j in range(3):
            self.one(j, ch).wait_recv()

    def pieces(self, ch):
        first = self.core * self.half + ch * self.chunk
        own = self.mine[pl.ds(pl.multiple_of(first, 16), self.chunk), :]
        return [own] + [self.land[j, pl.ds(ch * self.chunk, self.chunk), :] for j in range(3)]

    def sent(self, ch):
        for j in range(3):
            self.one(j, ch).wait_send()


def by_rows(rows, step, body):
    def turn(i, _):
        body(pl.multiple_of(i * step, step))
        return 0

    lax.fori_loop(0, rows // step, turn, 0)


def forward_kernel(*refs):
    (mixed, out_all, start, gain, shift, weight) = refs[:6]
    (after, normed, result) = refs[6:9]
    (land, product, send_sem, recv_sem) = refs[9:]
    d, t = lax.axis_index("dp"), lax.axis_index("tensor")
    core = d % 2
    chunk = product.shape[0]
    half = after.shape[0]
    width = mixed.shape[1]
    copy = Copies(send_sem, recv_sem)
    greet([(d ^ 1, t), (d, t ^ 1), (d ^ 1, t ^ 1)])
    exchange = Exchange(copy, mixed, land, core, d, t, chunk)

    def give(ch):
        block = rows_of(normed, core * half + ch * chunk, chunk)
        return copy(("give", ch), block, block, (d ^ 1, t))

    chunks = half // chunk
    for ch in range(chunks):
        exchange.start(ch)
    for ch in range(chunks):
        exchange.arrive(ch)
        product[...] = sum(
            add_dot(piece, out_all[j * width : (j + 1) * width, :])
            for j, piece in enumerate(exchange.pieces(ch))
        )

        def rows(at, ch=ch):
            x = start[pl.ds(pl.multiple_of(ch * chunk + at, 16), 32), :].astype(jnp.float32)
            x = x + product[pl.ds(at, 32), :]
            after[pl.ds(pl.multiple_of(ch * chunk + at, 16), 32), :] = x
            unit, inverse = moments(x)
            normed[pl.ds(pl.multiple_of(core * half + ch * chunk + at, 16), 32), :] = (
                unit * gain[...] + shift[...]
            ).astype(jnp.bfloat16)

        by_rows(chunk, 32, rows)
        give(ch).start()

    def project(first, rows):
        at = pl.ds(pl.multiple_of(first, 16), rows)
        result[at, :] = add_dot(normed[at, :], weight[...]).astype(jnp.bfloat16)

    project(core * half, half)
    for ch in range(chunks):
        give(ch).wait()
    project((1 - core) * half, half)
    for ch in range(chunks):
        exchange.sent(ch)


def forward_step(mixed, out_all, start, gain, shift, weight, collective_id):
    rows, width = mixed.shape
    half, wide = start.shape
    chunk = half // 4
    shape = jax.ShapeDtypeStruct
    vmem = pl.BlockSpec(memory_space=pltpu.VMEM)
    return pl.pallas_call(
        forward_kernel,
        out_shape=(
            shape((half, wide), jnp.float32),
            shape((rows, wide), jnp.bfloat16),
            shape((rows, weight.shape[1]), jnp.bfloat16),
        ),
        in_specs=[vmem] * 6,
        out_specs=(vmem,) * 3,
        scratch_shapes=[
            pltpu.VMEM((3, half, width), jnp.bfloat16),
            pltpu.VMEM((chunk, wide), jnp.float32),
            pltpu.SemaphoreType.DMA((20,)),
            pltpu.SemaphoreType.DMA((20,)),
        ],
        compiler_params=pltpu.CompilerParams(
            collective_id=collective_id, has_side_effects=True, vmem_limit_bytes=56 << 20
        ),
        cost_estimate=pl.CostEstimate(flops=20_000_000_000, bytes_accessed=8_000_000, transcendentals=0),
        name="forward_step",
    )(mixed, out_all, start, gain[None], shift[None], weight)


def backward_kernel(*refs):
    (grad_query, query_all, after, gain, grad_in, weight) = refs[:6]
    (grad_res, grad_top, result, norm_grads) = refs[6:10]
    (land, product, send_sem, recv_sem) = refs[10:]
    d, t = lax.axis_index("dp"), lax.axis_index("tensor")
    core = d % 2
    chunk = product.shape[0]
    half = after.shape[0]
    copy = Copies(send_sem, recv_sem)
    greet([(d ^ 1, t), (d, t ^ 1), (d ^ 1, t ^ 1)])
    exchange = Exchange(copy, grad_query, land, core, d, t, chunk)

    def give(ch):
        block = rows_of(grad_top, core * half + ch * chunk, chunk)
        return copy(("give", ch), block, block, (d ^ 1, t))

    chunks = half // chunk
    for ch in range(chunks):
        exchange.start(ch)
    norm_grads[...] = jnp.zeros_like(norm_grads)
    for ch in range(chunks):
        exchange.arrive(ch)
        product[...] = sum(add_dot(piece, query_all[j], True) for j, piece in enumerate(exchange.pieces(ch)))

        def rows(at, ch=ch):
            here = pl.ds(pl.multiple_of(ch * chunk + at, 16), 32)
            unit, inverse = moments(after[here, :])
            back, gain_grad, shift_grad = normalize_back(product[pl.ds(at, 32), :], unit, inverse, gain[...])
            total = grad_in[here, :] + back
            grad_res[here, :] = total
            grad_top[pl.ds(pl.multiple_of(core * half + ch * chunk + at, 16), 32), :] = total.astype(jnp.bfloat16)
            norm_grads[0:1, :] += gain_grad[None]
            norm_grads[1:2, :] += shift_grad[None]

        by_rows(chunk, 32, rows)
        give(ch).start()

    def project(first, rows):
        at = pl.ds(pl.multiple_of(first, 16), rows)
        result[at, :] = add_dot(grad_top[at, :], weight[...], True).astype(jnp.bfloat16)

    project(core * half, half)
    for ch in range(chunks):
        give(ch).wait()
    project((1 - core) * half, half)
    for ch in range(chunks):
        exchange.sent(ch)


def backward_step(grad_query, query_all, after, gain, grad_in, weight, collective_id):
    rows, width = grad_query.shape
    half, wide = after.shape
    chunk = half // 4
    shape = jax.ShapeDtypeStruct
    vmem = pl.BlockSpec(memory_space=pltpu.VMEM)
    return pl.pallas_call(
        backward_kernel,
        out_shape=(
            shape((half, wide), jnp.float32),
            shape((rows, wide), jnp.bfloat16),
            shape((rows, weight.shape[0]), jnp.bfloat16),
            shape((8, wide), jnp.float32),
        ),
        in_specs=[vmem] * 6,
        out_specs=(vmem,) * 4,
        scratch_shapes=[
            pltpu.VMEM((3, half, width), jnp.bfloat16),
            pltpu.VMEM((chunk, wide), jnp.float32),
            pltpu.SemaphoreType.DMA((20,)),
            pltpu.SemaphoreType.DMA((20,)),
        ],
        compiler_params=pltpu.CompilerParams(
            collective_id=collective_id, has_side_effects=True, vmem_limit_bytes=56 << 20
        ),
        cost_estimate=pl.CostEstimate(flops=20_000_000_000, bytes_accessed=8_000_000, transcendentals=0),
        name="backward_step",
    )(grad_query, query_all, after, gain[None], grad_in, weight)


def hidden_kernel(*refs):
    (mixed, out_all, start, gain, shift, expand, reduce, grad_out, cot) = refs[:9]
    (after, normed, hidden, grad_pre, grad_res, grad_top, result, norm_grads) = refs[9:17]
    (land, product, own, far_send, far_land, sum_send, sum_land, send_sem, recv_sem) = refs[17:]
    d, t = lax.axis_index("dp"), lax.axis_index("tensor")
    core = d % 2
    chunk = product.shape[0]
    half = after.shape[0]
    width = mixed.shape[1]
    chunks = half // chunk
    copy = Copies(send_sem, recv_sem)
    greet([(d ^ 1, t), (d, t ^ 1), (d ^ 1, t ^ 1)])
    exchange = Exchange(copy, mixed, land, core, d, t, chunk)

    def give(name, ref, ch):
        block = rows_of(ref, core * half + ch * chunk, chunk)
        return copy((name, ch), block, block, (d ^ 1, t))

    def slab(ref, ch):
        return ref.at[pl.ds(ch * chunk, chunk)]

    def far(ch):
        return copy(("far", ch), slab(far_send, ch), slab(far_land, ch), (d ^ 1, t))

    def whole(ch):
        return copy(("whole", ch), slab(sum_send, ch), slab(sum_land, ch), (d, t ^ 1))

    def residual(ch):
        exchange.arrive(ch)
        product[...] = sum(
            add_dot(piece, out_all[j * width : (j + 1) * width, :])
            for j, piece in enumerate(exchange.pieces(ch))
        )

        def rows(at):
            here = pl.ds(pl.multiple_of(ch * chunk + at, 16), 32)
            x = start[here, :] + product[pl.ds(at, 32), :]
            after[here, :] = x
            unit, inverse = moments(x)
            normed[pl.ds(pl.multiple_of(core * half + ch * chunk + at, 16), 32), :] = (
                unit * gain[...] + shift[...]
            ).astype(jnp.bfloat16)

        by_rows(chunk, 32, rows)
        give("normed", normed, ch).start()

    def feed(first):
        every = pl.ds(pl.multiple_of(first, 16), chunk)
        product[...] = add_dot(normed[every, :], expand[...])
        own[...] = add_dot(grad_out[every, :], reduce[...], True)

        def rows(at):
            here = pl.ds(pl.multiple_of(first + at, 16), 32)
            z = product[pl.ds(at, 32), :]
            inner = jnp.tanh(tanh_coeff * (z + cubic_coeff * z * z * z))
            hidden[here, :] = (0.5 * z * (1.0 + inner)).astype(jnp.bfloat16)
            slope = 0.5 * (1.0 + inner) + 0.5 * z * (1.0 - inner * inner) * tanh_coeff * (
                1.0 + 3.0 * cubic_coeff * z * z
            )
            upper = own[pl.ds(at, 32), :].astype(jnp.bfloat16).astype(jnp.float32)
            grad_pre[here, :] = (upper * slope).astype(jnp.bfloat16)

        by_rows(chunk, 32, rows)
        return add_dot(grad_pre[pl.ds(pl.multiple_of(first, 16), chunk), :], expand[...], True)

    def both(ch):
        copy(
            ("normed", ch), *([rows_of(normed, (1 - core) * half + ch * chunk, chunk)] * 2), (d ^ 1, t)
        ).wait_recv()
        far_send[pl.ds(ch * chunk, chunk), :] = feed((1 - core) * half + ch * chunk).astype(jnp.bfloat16)
        far(ch).start()
        own[...] = feed(core * half + ch * chunk)
        far(ch).wait_recv()

        def rows(at):
            here = pl.ds(pl.multiple_of(ch * chunk + at, 16), 32)
            sum_send[here, :] = (own[pl.ds(at, 32), :] + far_land[here, :].astype(jnp.float32)).astype(jnp.bfloat16)

        by_rows(chunk, 32, rows)
        whole(ch).start()

    def back(ch):
        whole(ch).wait_recv()

        def rows(at):
            here = pl.ds(pl.multiple_of(ch * chunk + at, 16), 32)
            grad = sum_send[here, :].astype(jnp.float32) + sum_land[here, :].astype(jnp.float32)
            unit, inverse = moments(after[here, :])
            down, gain_grad, shift_grad = normalize_back(grad, unit, inverse, gain[...])
            total = cot[here, :].astype(jnp.float32) + down
            grad_res[here, :] = total
            grad_top[pl.ds(pl.multiple_of(core * half + ch * chunk + at, 16), 32), :] = total.astype(jnp.bfloat16)
            norm_grads[0:1, :] += gain_grad[None]
            norm_grads[1:2, :] += shift_grad[None]

        by_rows(chunk, 32, rows)
        give("top", grad_top, ch).start()

    def project(first, rows):
        at = pl.ds(pl.multiple_of(first, 16), rows)
        result[at, :] = add_dot(grad_top[at, :], out_all[:width, :], True).astype(jnp.bfloat16)

    for ch in range(chunks):
        exchange.start(ch)
    norm_grads[...] = jnp.zeros_like(norm_grads)
    residual(0)
    residual(1)
    both(0)
    residual(2)
    both(1)
    residual(3)
    both(2)
    back(0)
    both(3)
    back(1)
    back(2)
    back(3)
    project(core * half, half)
    for ch in range(chunks):
        copy(
            ("top", ch), *([rows_of(grad_top, (1 - core) * half + ch * chunk, chunk)] * 2), (d ^ 1, t)
        ).wait_recv()
    project((1 - core) * half, half)
    for ch in range(chunks):
        exchange.sent(ch)
        give("normed", normed, ch).wait_send()
        give("top", grad_top, ch).wait_send()
        far(ch).wait_send()
        whole(ch).wait_send()


def hidden_step(mixed, out_all, start, gain, shift, expand, reduce, grad_out, cot, collective_id):
    rows, width = mixed.shape
    half, wide = start.shape
    inner = expand.shape[1]
    chunk = half // 4
    bf16, f32 = jnp.bfloat16, jnp.float32
    shape = jax.ShapeDtypeStruct
    vmem = pl.BlockSpec(memory_space=pltpu.VMEM)
    return pl.pallas_call(
        hidden_kernel,
        out_shape=(
            shape((half, wide), f32),
            shape((rows, wide), bf16),
            shape((rows, inner), bf16),
            shape((rows, inner), bf16),
            shape((half, wide), f32),
            shape((rows, wide), bf16),
            shape((rows, width), bf16),
            shape((8, wide), f32),
        ),
        in_specs=[vmem] * 9,
        out_specs=(vmem,) * 8,
        scratch_shapes=[
            pltpu.VMEM((3, half, width), bf16),
            pltpu.VMEM((chunk, max(wide, inner)), f32),
            pltpu.VMEM((chunk, max(wide, inner)), f32),
            pltpu.VMEM((half, wide), bf16),
            pltpu.VMEM((half, wide), bf16),
            pltpu.VMEM((half, wide), bf16),
            pltpu.VMEM((half, wide), bf16),
            pltpu.SemaphoreType.DMA((32,)),
            pltpu.SemaphoreType.DMA((32,)),
        ],
        compiler_params=pltpu.CompilerParams(
            collective_id=collective_id, has_side_effects=True, vmem_limit_bytes=60 << 20
        ),
        cost_estimate=pl.CostEstimate(flops=50_000_000_000, bytes_accessed=16_000_000, transcendentals=0),
        name="hidden_step",
    )(mixed, out_all, start, gain[None], shift[None], expand, reduce, grad_out, cot)


def on_device(
    tokens,
    encoder_states,
    tok_lengths,
    enc_lengths,
    pad_mask,
    first_gain,
    first_shift,
    causal_query,
    causal_key,
    causal_value,
    causal_out,
    second_gain,
    second_shift,
    cross_query,
    cross_key,
    cross_value,
    cross_out,
    third_gain,
    third_shift,
    expand_weight,
    reduce_weight,
    cotangent,
):
    place = Place()
    width = causal_query.shape[1]
    length = pad_mask.shape[0]
    frames = encoder_states.shape[0]

    def of_group(value):
        return jnp.where(place.keeper, value, place.swap(value, 1, 0))

    def half_rows(quarter):
        return place.ordered(quarter, place.swap(quarter, 0, 1), place.side)

    def quarter_of(half):
        return place.part(half, place.side, 2)

    tok_lengths, enc_lengths, pad_mask = of_group(tok_lengths), of_group(enc_lengths), of_group(pad_mask)
    block_q, block_k = 256, 512
    token_seg, frame_seg, key_seg, self_lo, self_hi, cross_lo, cross_hi = ranges(
        tok_lengths[0], enc_lengths[0], pad_mask, length, frames, block_q, block_k
    )
    self_keys = jnp.stack([token_seg, key_seg] + [token_seg] * 6)
    cross_keys = jnp.stack([frame_seg] * 8)
    seg_col, seg_row = token_seg[:, None], token_seg[None, :]

    cross_weight = place.moved_weight(jnp.concatenate([cross_key, cross_value, cross_query], axis=1))
    cross_query_here = cross_weight[:, 2 * width :]
    cross_weight = cross_weight[:, : 2 * width]
    tokens_half, first_all, query, keyed, valued, moved, causal_out_perm, encoder = start_layer(
        tokens,
        first_gain,
        first_shift,
        (causal_query, causal_key, causal_value),
        causal_out,
        encoder_states,
        1,
    )
    tokens_here = quarter_of(tokens_half)
    cross_in = times(encoder, cross_weight).astype(jnp.bfloat16)
    ckeyed, cvalued = cross_in[:, :width], cross_in[:, width:]
    cross_out_all = place.whole_weight(cross_out)
    cross_query_all = place.whole_weight(cross_query)
    order = place.order()
    pick = lambda every, which: lax.dynamic_index_in_dim(every, which, 0, keepdims=False)
    cross_out_perm = jnp.concatenate([pick(cross_out_all, s) for s in order])
    cross_query_every = jnp.stack([pick(cross_query_all, s) for s in order])
    causal_out_here, cross_out_here = causal_out_perm[:width], cross_out_perm[:width]

    mixed, self_logsum = attend_fwd(
        query, keyed, valued, seg_col, self_keys, self_lo, self_hi, True, block_q, block_k
    )
    after_self, second_all, cquery = forward_step(
        mixed, causal_out_perm, tokens_half, second_gain, second_shift, cross_query_here, 2
    )
    cmixed, cross_logsum = attend_fwd(
        cquery, ckeyed, cvalued, seg_col, cross_keys, cross_lo, cross_hi, False, block_q, block_k
    )
    ff_weight = place.moved_weight(jnp.concatenate([expand_weight, reduce_weight], axis=1))
    hidden_width = expand_weight.shape[1]
    expand_here, reduce_here = ff_weight[:, :hidden_width], ff_weight[:, hidden_width:]
    cot_half = half_rows(place.home(cotangent))
    grad_top = place.both_cores(cot_half)

    after_cross, third_all, hidden, grad_expand_in, grad_res, grad_top2, grad_cmixed, third_grads = hidden_step(
        cmixed, cross_out_perm, after_self, third_gain, third_shift, expand_here, reduce_here, grad_top, cot_half, 3
    )
    third_gain_grad, third_shift_grad = third_grads[0], third_grads[1]
    out_term = times(hidden, reduce_here).astype(jnp.bfloat16)
    reduce_grad = along_rows(hidden, grad_top)
    expand_grad = along_rows(third_all, grad_expand_in)

    cross_out_grad = along_rows(cmixed, grad_top2)
    grad_cquery, grad_ckey, grad_cvalue = attend_bwd(
        cquery, ckeyed, cvalued, cmixed, grad_cmixed, cross_logsum, seg_row, cross_keys.T,
        cross_lo, cross_hi, False, block_q, block_k,
    )
    grad_cross_in = jnp.concatenate([grad_ckey, grad_cvalue], axis=1)
    cross_grad = along_rows(encoder, grad_cross_in)
    cross_query_grad = along_rows(second_all, grad_cquery)
    encoder_term = against(grad_cross_in, cross_weight).astype(jnp.bfloat16)
    grad_res, grad_top, grad_mixed, second_grads = backward_step(
        grad_cquery, cross_query_every, after_self, second_gain, grad_res, causal_out_here, 4
    )
    second_gain_grad, second_shift_grad = second_grads[0], second_grads[1]
    causal_out_grad = along_rows(mixed, grad_top)
    grad_query, grad_key, grad_value = attend_bwd(
        query, keyed, valued, mixed, grad_mixed, self_logsum, seg_row, self_keys.T,
        self_lo, self_hi, True, block_q, block_k,
    )
    grad_in = jnp.concatenate([grad_query, grad_key, grad_value], axis=1)
    causal_grad = along_rows(first_all, grad_in)
    first_term = (
        against(grad_query, moved[0]) + against(grad_key, moved[1]) + against(grad_value, moved[2])
    )
    first_rows = (first_all.astype(jnp.float32) - first_shift) / first_gain
    first_gain_grad = jnp.sum(first_term * first_rows, axis=0)
    first_shift_grad = jnp.sum(first_term, axis=0)
    bf16 = jnp.bfloat16
    once = (place.side == 0).astype(jnp.float32)
    none = jnp.zeros_like(first_gain_grad)
    norm_grads = jnp.stack(
        [
            first_gain_grad,
            first_shift_grad,
            second_gain_grad * once,
            second_shift_grad * once,
            third_gain_grad * once,
            third_shift_grad * once,
            none,
            none,
        ]
    )
    *sums, encoder_grad, output, tokens_grad, norm_grads = sum_all(
        [
            expand_grad.astype(bf16),
            reduce_grad.astype(bf16),
            jnp.concatenate([cross_grad, cross_query_grad], axis=1).astype(bf16),
            causal_grad.astype(bf16),
            cross_out_grad.astype(bf16),
            causal_out_grad.astype(bf16),
        ],
        (2, 1, 1),
        (False, False, False),
        [encoder_term, out_term, first_term.astype(bf16)],
        norm_grads,
        quarter_of(after_cross),
        tokens_here,
        quarter_of(grad_res),
        first_gain,
        0,
    )
    (
        first_gain_grad,
        first_shift_grad,
        second_gain_grad,
        second_shift_grad,
        third_gain_grad,
        third_shift_grad,
    ) = (norm_grads[i] for i in range(6))
    expand_grad, reduce_grad, cross_grads, causal_grads, cross_out_grad, causal_out_grad = (
        value.astype(jnp.float32) for value in sums
    )
    cross_key_grad, cross_value_grad, cross_query_grad = (
        cross_grads[:, i * width : (i + 1) * width] for i in range(3)
    )
    causal_query_grad, causal_key_grad, causal_value_grad = (
        causal_grads[:, i * width : (i + 1) * width] for i in range(3)
    )
    return (
        output,
        tokens_grad,
        encoder_grad,
        first_gain_grad,
        first_shift_grad,
        causal_query_grad,
        causal_key_grad,
        causal_value_grad,
        causal_out_grad,
        second_gain_grad,
        second_shift_grad,
        cross_query_grad,
        cross_key_grad,
        cross_value_grad,
        cross_out_grad,
        third_gain_grad,
        third_shift_grad,
        expand_grad,
        reduce_grad,
    )


def solution(mesh):
    in_specs = (
        P(("dp", "tensor"), None),
        P("dp", None),
        P("dp", None),
        P("dp", None),
        P("dp"),
        P(),
        P(),
        P(None, "tensor"),
        P(None, "tensor"),
        P(None, "tensor"),
        P("tensor", None),
        P(),
        P(),
        P(None, "tensor"),
        P(None, "tensor"),
        P(None, "tensor"),
        P("tensor", None),
        P(),
        P(),
        P(None, "tensor"),
        P("tensor", None),
        P(("dp", "tensor"), None),
    )
    out_specs = (
        P(("dp", "tensor"), None),
        P(("dp", "tensor"), None),
        P(("dp", "tensor"), None),
        P(),
        P(),
        P(None, "tensor"),
        P(None, "tensor"),
        P(None, "tensor"),
        P("tensor", None),
        P(),
        P(),
        P(None, "tensor"),
        P(None, "tensor"),
        P(None, "tensor"),
        P("tensor", None),
        P(),
        P(),
        P(None, "tensor"),
        P("tensor", None),
    )
    return jax.shard_map(
        on_device, mesh=mesh, in_specs=in_specs, out_specs=out_specs, check_vma=False
    )
```

```python
import functools

import jax
import jax.numpy as jnp
from jax import lax
from jax.experimental import pallas as pl
from jax.experimental.pallas import tpu as pltpu
from jax.sharding import PartitionSpec as P

HEAD_DIM = 64


eps = 1e-05
tanh_coeff = 0.7978845608
cubic_coeff = 0.044715


def smooth_gate(values):
    inner = jnp.tanh(tanh_coeff * (values + cubic_coeff * values * values * values))
    return 0.5 * values * (1.0 + inner)


def smooth_slope(values):
    inner = jnp.tanh(tanh_coeff * (values + cubic_coeff * values * values * values))
    return 0.5 * (1.0 + inner) + 0.5 * values * (1.0 - inner * inner) * tanh_coeff * (
        1.0 + 3.0 * cubic_coeff * values * values
    )


BF=jnp.bfloat16
F32=jnp.float32

def head_mask(rows, width, h):
    lane = lax.broadcasted_iota(jnp.int32, (rows, width), 1)
    return (lane // HEAD_DIM) == h

def dot(a,b,ca,cb):
    return lax.dot_general(a,b,(((ca,),(cb,)),((),())),preferred_element_type=F32)

def fwd_kernel(causal, heads, bq, bk, lo_ref, hi_ref, q_ref, k_ref, v_ref, rs_ref, ks_ref, o_ref, lse_ref, acc):
    count, width = q_ref.shape
    def one(qb, _):
        q0 = pl.multiple_of(qb*bq, bq)
        qv = q_ref[pl.ds(q0,bq),:] * BF(HEAD_DIM**-0.5)
        rseg = rs_ref[pl.ds(q0,bq),0:1]
        qm = [jnp.where(head_mask(bq,width,h), qv, BF(0)) for h in range(heads)]
        acc[...] = jnp.zeros_like(acc)
        lane = lax.broadcasted_iota(jnp.int32,(bq,128),1)
        def inner(kb, carry):
            k0 = pl.multiple_of(kb*bk, bk)
            kv = k_ref[pl.ds(k0,bk),:]
            vv = v_ref[pl.ds(k0,bk),:]
            kseg = ks_ref[0:1,pl.ds(k0,bk)]
            if causal:
                kpad = ks_ref[1:2,pl.ds(k0,bk)]
                ri = lax.broadcasted_iota(jnp.int32,(bq,bk),0)+q0
                ci = lax.broadcasted_iota(jnp.int32,(bq,bk),1)+k0
                ok = ((rseg==kpad)&(ci<=ri))|(ci==ri)
            else:
                ok = rseg==kseg
            ms, ls = carry
            new_m, new_l = [], []
            parts=None
            alphas=[]
            for h in range(heads):
                s = dot(qm[h],kv,1,1)
                s = jnp.where(ok,s,-1e30)
                m = jnp.maximum(ms[h], jnp.max(s,axis=1,keepdims=True))
                p = jnp.exp(s-m)
                al = jnp.exp(ms[h]-m)
                new_m.append(m); new_l.append(ls[h]*al+jnp.sum(p,axis=1,keepdims=True))
                vm = jnp.where(head_mask(bk,width,h),vv,BF(0))
                t = dot(p.astype(BF),vm,1,0)
                parts = t if parts is None else parts+t
                alphas.append(al)
            lane2 = lax.broadcasted_iota(jnp.int32,(bq,width),1)//HEAD_DIM
            sc = alphas[heads-1]
            for h in range(heads-1):
                sc = jnp.where(lane2==h, alphas[h], sc)
            acc[...] = acc[...]*sc + parts
            return (tuple(new_m),tuple(new_l))
        init = (tuple(jnp.full((bq,1),-1e30,F32) for _ in range(heads)), tuple(jnp.zeros((bq,1),F32) for _ in range(heads)))
        ms, ls = lax.fori_loop(lo_ref[qb], hi_ref[qb], inner, init)
        lane2 = lax.broadcasted_iota(jnp.int32,(bq,width),1)//HEAD_DIM
        inv = [1.0/l for l in ls]
        sc = inv[heads-1]
        for h in range(heads-1):
            sc = jnp.where(lane2==h, inv[h], sc)
        o_ref[pl.ds(q0,bq),:] = (acc[...]*sc).astype(BF)
        st = jnp.zeros((bq,128),F32)
        for h in range(heads):
            st = jnp.where(lane==h, ms[h]+jnp.log(ls[h]), st)
        stt = jnp.transpose(st)
        lse_ref[:,pl.ds(q0,bq)] = stt[0:8,:]
        return 0
    lax.fori_loop(0,count//bq,one,0)

def attend_fwd(q,k,v,rseg,kseg,lo,hi,causal,bq=256,bk=256):
    count,width=q.shape
    heads=width//HEAD_DIM
    vm=pl.BlockSpec(memory_space=pltpu.VMEM); sm=pl.BlockSpec(memory_space=pltpu.SMEM)
    return pl.pallas_call(functools.partial(fwd_kernel,causal,heads,bq,bk),
        out_shape=(jax.ShapeDtypeStruct((count,width),BF),jax.ShapeDtypeStruct((8,count),F32)),
        in_specs=[sm,sm,vm,vm,vm,vm,vm],out_specs=(vm,vm),
        scratch_shapes=[pltpu.VMEM((bq,width),F32)],
        compiler_params=pltpu.CompilerParams(vmem_limit_bytes=40<<20),
        cost_estimate=pl.CostEstimate(flops=22_000_000_000, bytes_accessed=8_000_000, transcendentals=0),
        name="attend_fwd",
    )(lo,hi,q,k,v,rseg,kseg)

def bwd_kernel(causal, heads, bq, bk, lo_ref, hi_ref, q_ref, k_ref, v_ref, o_ref, do_ref, lse_ref, rs_ref, ks_ref,
               dq_ref, dk_ref, dv_ref, dka, dva, qm, dom, dqa):
    count,width=q_ref.shape
    dka[...]=jnp.zeros_like(dka); dva[...]=jnp.zeros_like(dva)
    def one(qb,_):
        q0=pl.multiple_of(qb*bq,bq)
        qv=q_ref[pl.ds(q0,bq),:]*BF(HEAD_DIM**-0.5)
        dov=do_ref[pl.ds(q0,bq),:]
        prod=dov.astype(F32)*o_ref[pl.ds(q0,bq),:].astype(F32)
        row=lax.broadcasted_iota(jnp.int32,(8,width),0); col=lax.broadcasted_iota(jnp.int32,(8,width),1)//HEAD_DIM
        sel=(row==col).astype(F32)
        delta=lax.dot_general(sel,prod,(((1,),(1,)),((),())),precision=lax.Precision.HIGHEST,preferred_element_type=F32)
        for h in range(heads):
            hm=head_mask(bq,width,h)
            qm[pl.ds(h*bq,bq),:]=jnp.where(hm,qv,BF(0))
            dom[pl.ds(h*bq,bq),:]=jnp.where(hm,dov,BF(0))
        dqa[...]=jnp.zeros_like(dqa)
        rseg=rs_ref[0:1,pl.ds(q0,bq)]
        lse=lse_ref[:,pl.ds(q0,bq)]
        def inner(kb,_):
            k0=pl.multiple_of(kb*bk,bk)
            kv=k_ref[pl.ds(k0,bk),:]; vv=v_ref[pl.ds(k0,bk),:]
            if causal:
                kpad=ks_ref[pl.ds(k0,bk),1:2]
                ri=lax.broadcasted_iota(jnp.int32,(bk,bq),1)+q0
                ci=lax.broadcasted_iota(jnp.int32,(bk,bq),0)+k0
                ok=((rseg==kpad)&(ci<=ri))|(ci==ri)
            else:
                ok=rseg==ks_ref[pl.ds(k0,bk),0:1]
            ps=[];dss=[]
            dq=None
            for h in range(heads):
                st=dot(kv,qm[pl.ds(h*bq,bq),:],1,1)
                p=jnp.where(ok,jnp.exp(st-lse[h:h+1,:]),0.0)
                dp=dot(vv,dom[pl.ds(h*bq,bq),:],1,1)
                ds=(p*(dp-delta[h:h+1,:])).astype(BF)
                ps.append(p.astype(BF)); dss.append(ds)
                km=jnp.where(head_mask(bk,width,h),kv,BF(0))
                t=dot(ds,km,0,0)
                dq=t if dq is None else dq+t
            dqa[...]+=dq
            pcat=jnp.concatenate(ps,axis=1); dcat=jnp.concatenate(dss,axis=1)
            dva[pl.ds(k0,bk),:]+=dot(pcat,dom[...],1,0)
            dka[pl.ds(k0,bk),:]+=dot(dcat,qm[...],1,0)
            return 0
        lax.fori_loop(lo_ref[qb],hi_ref[qb],inner,0)
        dq_ref[pl.ds(q0,bq),:]=(dqa[...]*(HEAD_DIM**-0.5)).astype(BF)
        return 0
    lax.fori_loop(0,count//bq,one,0)
    dk_ref[...]=dka[...].astype(BF)
    dv_ref[...]=dva[...].astype(BF)

def attend_bwd(q,k,v,o,do,lse,rseg,kseg,lo,hi,causal,bq=256,bk=256):
    count,width=q.shape; keys=k.shape[0]
    heads=width//HEAD_DIM
    vm=pl.BlockSpec(memory_space=pltpu.VMEM); sm=pl.BlockSpec(memory_space=pltpu.SMEM)
    return pl.pallas_call(functools.partial(bwd_kernel,causal,heads,bq,bk),
        out_shape=(jax.ShapeDtypeStruct((count,width),BF),jax.ShapeDtypeStruct((keys,width),BF),jax.ShapeDtypeStruct((keys,width),BF)),
        in_specs=[sm,sm]+[vm]*8,out_specs=(vm,vm,vm),
        scratch_shapes=[pltpu.VMEM((keys,width),F32),pltpu.VMEM((keys,width),F32),pltpu.VMEM((heads*bq,width),BF),pltpu.VMEM((heads*bq,width),BF),pltpu.VMEM((bq,width),F32)],
        compiler_params=pltpu.CompilerParams(vmem_limit_bytes=40<<20),
        cost_estimate=pl.CostEstimate(flops=30_000_000_000, bytes_accessed=8_000_000, transcendentals=0),
        name="attend_bwd",
    )(lo,hi,q,k,v,o,do,lse,rseg,kseg)

def ranges(tok_lengths, enc_lengths, pad, count, frames, bq, bk):
    tend=jnp.cumsum(tok_lengths,dtype=jnp.int32); eend=jnp.cumsum(enc_lengths,dtype=jnp.int32)
    places=jnp.arange(count,dtype=jnp.int32)
    tseg=jnp.sum((places[:,None]>=tend[None,:]).astype(jnp.int32),axis=1)
    eseg=jnp.sum((jnp.arange(frames,dtype=jnp.int32)[:,None]>=eend[None,:]).astype(jnp.int32),axis=1)
    starts=jnp.arange(count//bq,dtype=jnp.int32)*bq
    first=tseg[::bq]; last=tseg[bq-1::bq]
    onehot=lambda s:(s[:,None]==jnp.arange(tend.shape[0])[None,:]).astype(jnp.int32)
    pick=lambda arr,s: jnp.sum(onehot(s)*arr[None,:],axis=1)
    tstart=tend-tok_lengths; estart=eend-enc_lengths
    slo=pick(tstart,first)//bk; shi=(starts+bq+bk-1)//bk
    clo=pick(estart,first)//bk; chi=(pick(eend,last)+bk-1)//bk
    kpad=jnp.where(pad==1,tseg,-1)
    return tseg,eseg,kpad,slo,shi,clo,chi


def along_rows(left, right):
    return lax.dot_general(
        left, right, (((0,), (0,)), ((), ())), preferred_element_type=jnp.float32
    )


def against(left, weight):
    return lax.dot_general(
        left, weight, (((1,), (1,)), ((), ())), preferred_element_type=jnp.float32
    )


def times(left, weight):
    return jnp.dot(left, weight, preferred_element_type=jnp.float32)


def moments(rows):
    centred = rows - jnp.mean(rows, axis=1, keepdims=True)
    inverse = lax.rsqrt(jnp.mean(centred * centred, axis=1, keepdims=True) + eps)
    return centred * inverse, inverse


def normalize_back(grad_out, unit, inverse, gain):
    scaled = grad_out * gain
    inner = (
        scaled
        - jnp.mean(scaled, axis=1, keepdims=True)
        - unit * jnp.mean(scaled * unit, axis=1, keepdims=True)
    )
    return (inner * inverse, jnp.sum(grad_out * unit, axis=0), jnp.sum(grad_out, axis=0))


class Place:
    def __init__(self):
        self.dp = lax.axis_size("dp")
        self.tensor = lax.axis_size("tensor")
        self.d = lax.axis_index("dp")
        self.t = lax.axis_index("tensor")
        self.core = self.d % 2
        self.half = self.t // 2
        self.side = self.t % 2
        self.keeper = self.core == self.half
        self.shard = jnp.where(self.keeper, self.t, self.t ^ 2)

    def swap(self, value, d_flip, t_flip, only=None):
        pairs = []
        for d in range(self.dp):
            for t in range(self.tensor):
                keeper = d % 2 == t // 2
                if only is None or only == keeper:
                    pairs.append((d * self.tensor + t, (d ^ d_flip) * self.tensor + (t ^ t_flip)))
        return lax.ppermute(value, ("dp", "tensor"), pairs)

    def home(self, value):
        return jnp.where(self.keeper, value, self.swap(value, 1, 2, False))

    def ordered(self, mine, other, which):
        return jnp.where(
            which == 0, jnp.concatenate([mine, other]), jnp.concatenate([other, mine])
        )

    def part(self, value, which, parts):
        size = value.shape[0] // parts
        return lax.dynamic_slice_in_dim(value, which * size, size, 0)

    def both_cores(self, half_rows):
        return self.ordered(half_rows, self.swap(half_rows, 1, 0), self.core)

    def spread_columns(self, value):
        near, far = self.part(value, self.core, 2), self.part(value, 1 - self.core, 2)
        return jnp.concatenate(
            [near, self.swap(far, 1, 0), self.swap(near, 0, 1), self.swap(far, 1, 1)], axis=1
        )

    def order(self):
        return [self.shard, self.shard ^ 2, self.shard ^ 1, self.shard ^ 3]

    def sum_half(self, value):
        near, far = self.part(value, self.core, 2), self.part(value, 1 - self.core, 2)
        return near.astype(jnp.float32) + self.swap(far.astype(jnp.bfloat16), 1, 0).astype(jnp.float32)

    def sum_group_half(self, value):
        mine = self.sum_half(value).astype(jnp.bfloat16)
        return mine.astype(jnp.float32) + self.swap(mine, 0, 1).astype(jnp.float32)

    def sum_group_quarter(self, value):
        mine = self.sum_half(value)
        near, far = self.part(mine, self.side, 2), self.part(mine, 1 - self.side, 2)
        return near + self.swap(far.astype(jnp.bfloat16), 0, 1).astype(jnp.float32)

    def sum_columns(self, grad, order):
        columns = self.dp // 2
        bits = columns.bit_length() - 1
        turned = [sum(((c >> b) & 1) << (bits - 1 - b) for b in range(bits)) for c in range(columns)]
        groups = [[2 * (turned[c] if order == 0 else c) + core for c in range(columns)] for core in range(2)]
        return lax.psum_scatter(
            grad.astype(jnp.bfloat16), "dp", scatter_dimension=0, axis_index_groups=groups, tiled=True
        )

    def cross_planes(self, grads):
        return [
            (grad.astype(jnp.float32) + self.swap(grad, 0, 2, False).astype(jnp.float32)).astype(jnp.bfloat16)
            for grad in grads
        ]

    def moved_weight(self, weight):
        piece = self.swap(self.part(weight, self.d, self.dp), 0, 2)
        return jnp.where(self.keeper, weight, lax.all_gather(piece, "dp", axis=0, tiled=True))

    def whole_weight(self, weight):
        piece = self.part(weight, self.d, self.dp)
        every = lax.all_gather(piece, ("dp", "tensor"), axis=0, tiled=False)
        every = every.reshape((self.dp, self.tensor) + piece.shape)
        return jnp.swapaxes(every, 0, 1).reshape((self.tensor,) + weight.shape)


class Copies:
    def __init__(self, send_sem, recv_sem):
        self.send_sem, self.recv_sem, self.known = send_sem, recv_sem, {}

    def __call__(self, name, src, dst, device):
        at = self.known.setdefault(name, len(self.known))
        return pltpu.make_async_remote_copy(
            src_ref=src,
            dst_ref=dst,
            send_sem=self.send_sem.at[at],
            recv_sem=self.recv_sem.at[at],
            device_id=device,
            device_id_type=pl.DeviceIdType.MESH,
        )


def greet(devices):
    barrier = pltpu.get_barrier_semaphore()
    for device in devices:
        pl.semaphore_signal(
            barrier, inc=1, device_id=device, device_id_type=pl.DeviceIdType.MESH
        )
    pl.semaphore_wait(barrier, len(devices))


def rows_of(ref, start, size, step=16):
    return ref.at[pl.ds(pl.multiple_of(start, step), size)]


def norm_rows(src, src_first, dst, dst_first, rows, gain, shift):
    chunk = 64

    def body(i, _):
        at = i * chunk
        x = src[pl.ds(pl.multiple_of(src_first + at, 16), chunk), :].astype(jnp.float32)
        unit, inverse = moments(x)
        dst[pl.ds(pl.multiple_of(dst_first + at, 16), chunk), :] = (
            unit * gain[...] + shift[...]
        ).astype(jnp.bfloat16)
        return 0

    lax.fori_loop(0, rows // chunk, body, 0)


def sum_kernel(dp, counts, units, spans, *refs):
    arrays, row_arrays = counts
    it = iter(refs)
    take = lambda count: [next(it) for _ in range(count)]
    ins, parts = take(arrays), take(row_arrays)
    small_in, after, tokens, grad_in, gain = take(5)
    outs, row_outs = take(arrays), take(row_arrays)
    (small_out,) = take(1)
    bits = [b for b in (2, 4, 8, 16, 32, 64) if b < dp]
    steps = len(bits)
    land, hold = [], []
    for unit in units:
        hold.append(take(0 if unit[4] else steps))
        land.append(take(0 if unit[4] else steps + 1))
    row_land = [take(2) for _ in range(row_arrays)]
    row_hold = [take(2) for _ in range(row_arrays)]
    small_hold, small_land, small_send, small_recv, row_send, row_recv, send_sem, recv_sem = take(8)
    d, t = lax.axis_index("dp"), lax.axis_index("tensor")
    core, side = d % 2, t % 2
    keeper = core == t // 2
    other = jnp.logical_not(keeper)
    MESH = pl.DeviceIdType.MESH

    around = [(d ^ b, t) for b in bits] + [(d ^ 1, t), (d, t ^ 2), (d, t ^ 1)]
    greet(around + [(d ^ 1, t ^ 2)])

    def my(bit):
        return (d // bit) % 2

    def order(u):
        return bits if units[u][3] == 0 else bits[::-1]

    def source(u, step):
        array, first, rows, _, summed = units[u]
        if summed:
            return ins[array], first >> steps
        return (ins[array], first) if step == 0 else (hold[u][step - 1], 0)

    def copy(u, stage, src, dst, device):
        return pltpu.make_async_remote_copy(
            src_ref=src, dst_ref=dst, send_sem=send_sem.at[u, stage], recv_sem=recv_sem.at[u, stage],
            device_id=device, device_id_type=MESH,
        )

    def quarter(u):
        place = units[u][1]
        for step, bit in enumerate(order(u)):
            place = place + my(bit) * (units[u][2] >> (step + 1))
        return place

    def scatter_copy(u, step):
        ref, first = source(u, step)
        size = units[u][2] >> (step + 1)
        bit = order(u)[step]
        return copy(u, step, rows_of(ref, first + (1 - my(bit)) * size, size), land[u][step], (d ^ bit, t))

    def plane_copy(u):
        ref, first = source(u, steps)
        return copy(u, steps, rows_of(ref, first, units[u][2] >> steps), land[u][steps], (d, t ^ 2))

    def gather_copy(u, step):
        array, first, rows = units[u][:3]
        bit = order(u)[steps - 1 - step]
        size = rows >> (steps - step)
        start = quarter(u)
        for back in range(step):
            start = start - my(order(u)[steps - 1 - back]) * (rows >> (steps - back))
        block = rows_of(outs[array], start, size)
        return copy(u, steps + 1 + step, block, block, (d ^ bit, t))

    def core_copy(u):
        array, first, rows = units[u][:3]
        block = outs[array].at[pl.ds(first, rows)]
        return copy(u, 2 * steps + 1, block, block, (d ^ 1, t))

    def add(dst, dst_first, left, left_first, right, rows):
        chunk = min(rows, 32)

        def body(i, _):
            at = i * chunk
            a = left[pl.ds(pl.multiple_of(left_first + at, 16), chunk), :].astype(jnp.float32)
            b = right[pl.ds(pl.multiple_of(at, 16), chunk), :].astype(jnp.float32)
            dst[pl.ds(pl.multiple_of(dst_first + at, 16), chunk), :] = (a + b).astype(jnp.bfloat16)
            return 0

        lax.fori_loop(0, rows // chunk, body, 0)

    def begin(u, stage):
        if stage < steps:
            if not units[u][4]:
                scatter_copy(u, stage).start()
        elif stage == steps:
            if units[u][4]:
                return

            @pl.when(other)
            def _():
                plane_copy(u).start()
        else:

            @pl.when(keeper)
            def _():
                (gather_copy(u, stage - steps - 1) if stage <= 2 * steps else core_copy(u)).start()

    def end(u, stage):
        array, first, rows = units[u][:3]
        if stage < steps:
            if not units[u][4]:
                one = scatter_copy(u, stage)
                one.wait_recv()
                ref, row = source(u, stage)
                size = rows >> (stage + 1)
                add(hold[u][stage], 0, ref, row + my(order(u)[stage]) * size, land[u][stage], size)
                one.wait_send()
        elif stage == steps and units[u][4]:

            @pl.when(keeper)
            def _():
                size = rows >> steps
                ref, row = source(u, steps)
                outs[array][pl.ds(pl.multiple_of(quarter(u), 16), size), :] = ref[pl.ds(row, size), :]
        elif stage == steps:

            @pl.when(other)
            def _():
                plane_copy(u).wait_send()

            @pl.when(keeper)
            def _():
                plane_copy(u).wait_recv()
                ref, row = source(u, steps)
                add(outs[array], quarter(u), ref, row, land[u][steps], rows >> steps)
        elif stage <= 2 * steps:

            @pl.when(keeper)
            def _():
                gather_copy(u, stage - steps - 1).wait()
        else:

            @pl.when(keeper)
            def _():
                core_copy(u).wait_send()

            @pl.when(other)
            def _():
                core_copy(u).wait_recv()

    def row_copy(a, stage):
        size = spans[a]
        if stage == 0:
            src, dst, device = rows_of(parts[a], (1 - core) * 2 * size, 2 * size), row_land[a][0], (d ^ 1, t)
        elif stage == 1:
            src, dst, device = rows_of(row_hold[a][0], (1 - side) * size, size), row_land[a][1], (d, t ^ 1)
        else:
            src, dst, device = row_hold[a][1], row_outs[a], (d ^ 1, t ^ 2)
        return pltpu.make_async_remote_copy(
            src_ref=src, dst_ref=dst, send_sem=row_send.at[a, stage], recv_sem=row_recv.at[a, stage],
            device_id=device, device_id_type=MESH,
        )

    def row_quarter(a):
        size = spans[a]

        def body(i, _):
            at = pl.ds(pl.multiple_of(i * 32, 32), 32)
            total = row_hold[a][0][pl.ds(pl.multiple_of(side * size + i * 32, 32), 32), :].astype(jnp.float32)
            total = total + row_land[a][1][at, :].astype(jnp.float32)
            if a == 1:
                total = total + after[at, :]
            elif a == 2:
                unit, inverse = moments(tokens[at, :].astype(jnp.float32))
                total = grad_in[at, :] + normalize_back(total, unit, inverse, gain[...])[0]
            row_hold[a][1][at, :] = total.astype(jnp.bfloat16)
            return 0

        lax.fori_loop(0, size // 32, body, 0)

    def row_half(a):
        row_copy(a, 0).wait()
        add(row_hold[a][0], 0, parts[a], core * 2 * spans[a], row_land[a][0], 2 * spans[a])

    def row_sum(a):
        row_copy(a, 1).wait()
        row_quarter(a)

    def row_home(a):
        @pl.when(keeper)
        def _():
            row_outs[a][...] = row_hold[a][1][...]

        @pl.when(other)
        def _():
            row_copy(a, 2).start()

    def row_done(a):
        @pl.when(other)
        def _():
            row_copy(a, 2).wait()

    def small_copy(step):
        return pltpu.make_async_remote_copy(
            src_ref=small_hold.at[step], dst_ref=small_land.at[step], send_sem=small_send.at[step],
            recv_sem=small_recv.at[step], device_id=around[step], device_id_type=MESH,
        )

    def small_step(step):
        small_copy(step).wait()
        total = small_hold[step] + small_land[step]
        if step + 1 < len(around):
            small_hold[step + 1] = total
            small_copy(step + 1).start()
        else:
            small_out[...] = total

    last = 2 * steps + 2
    pairs = range(len(units) // 2)
    fresh = [p for p in pairs if not units[2 * p][4]]
    ready = [p for p in pairs if units[2 * p][4]]

    def advance(p, stage):
        for u in (2 * p, 2 * p + 1):
            if 0 < stage <= last:
                end(u, stage - 1)
            if 0 <= stage < last:
                begin(u, stage)

    def tick(now):
        for p in ready:
            stage = now + 1
            if now == steps:
                for u in (2 * p, 2 * p + 1):
                    end(u, steps)
                    begin(u, stage)
            elif now > steps:
                advance(p, stage)
        for p in fresh:
            advance(p, now)

    small_hold[0] = small_in[...]
    small_copy(0).start()
    encoder_rows, output_rows, token_rows = range(row_arrays)
    for a in (output_rows, encoder_rows, token_rows):
        row_copy(a, 0).start()
    tick(0)
    row_half(output_rows)
    row_copy(output_rows, 1).start()
    row_half(encoder_rows)
    row_half(token_rows)
    small_step(0)
    row_sum(output_rows)
    row_home(output_rows)
    row_copy(encoder_rows, 1).start()
    small_step(1)
    for now in range(1, steps + 1):
        tick(now)
        small_step(now + 1)
    row_sum(encoder_rows)
    row_copy(token_rows, 1).start()
    small_step(steps + 2)
    tick(steps + 1)
    row_home(encoder_rows)
    row_sum(token_rows)
    row_home(token_rows)
    for now in range(steps + 2, last + 1):
        tick(now)
    for a in (output_rows, encoder_rows, token_rows):
        row_done(a)


def sum_all(grads, split, summed, parts, norm_grads, after, tokens, grad_in, gain, collective_id):
    dp = lax.axis_size("dp")
    steps = 0
    while 2 << steps < dp:
        steps += 1
    shapes, units, scratch = [], [], []
    bf16, f32 = jnp.bfloat16, jnp.float32
    for index, grad in enumerate(grads):
        scale = 1 << steps if summed[index // 2] else 1
        shapes.append((grad.shape[0] * scale, grad.shape[1]))
    for pair in range(len(grads) // 2):
        rows = shapes[2 * pair][0] // split[pair]
        for part in range(split[pair]):
            for side in range(2):
                units.append((2 * pair + side, part * rows, rows, side, summed[pair]))
    for array, first, rows, side, done in units:
        width = shapes[array][1]
        if not done:
            scratch += [pltpu.VMEM((rows >> (k + 1), width), bf16) for k in range(steps)] * 2
            scratch.append(pltpu.VMEM((rows >> steps, width), bf16))
    stages = 2 * steps + 2
    vmem = pl.BlockSpec(memory_space=pltpu.VMEM)
    spans = [part.shape[0] // 4 for part in parts]
    wide = norm_grads.shape[1]
    row_land = [pltpu.VMEM((many * span, wide), bf16) for span in spans for many in (2, 1)]
    semaphores = pltpu.SemaphoreType.DMA
    return pl.pallas_call(
        functools.partial(sum_kernel, dp, (len(grads), len(parts)), units, spans),
        out_shape=[jax.ShapeDtypeStruct(shape, bf16) for shape in shapes]
        + [jax.ShapeDtypeStruct((span, wide), bf16) for span in spans]
        + [jax.ShapeDtypeStruct(norm_grads.shape, f32)],
        in_specs=[vmem] * (len(grads) + len(parts) + 5),
        out_specs=[vmem] * (len(grads) + len(parts) + 1),
        scratch_shapes=scratch
        + row_land * 2
        + [pltpu.VMEM((steps + 3,) + norm_grads.shape, f32)] * 2
        + [semaphores((steps + 3,))] * 2
        + [semaphores((len(parts), 3))] * 2
        + [semaphores((len(units), stages))] * 2,
        compiler_params=pltpu.CompilerParams(
            collective_id=collective_id, has_side_effects=True, vmem_limit_bytes=60 << 20
        ),
        cost_estimate=pl.CostEstimate(flops=100_000_000_000, bytes_accessed=16_000_000, transcendentals=0),
        name="sum_all",
    )(*grads, *parts, norm_grads, after, tokens, grad_in, gain[None])


class Move:
    def __init__(self, name, copy, sources, moved, d, t):
        self.name, self.copy, self.sources, self.moved = name, copy, sources, moved
        self.d, self.t, self.column = d, t, (d // 2) % 4
        self.keeper = d % 2 == t // 2
        self.other = jnp.logical_not(self.keeper)

    def block(self, ref):
        part = ref.shape[0] // 4
        return rows_of(ref, self.column * part, part)

    def fetch(self, a):
        return self.copy(
            (self.name, a), self.block(self.sources[a]), self.block(self.moved[a]), (self.d, self.t ^ 2)
        )

    def share(self, a, m):
        block = self.block(self.moved[a])
        return self.copy((self.name, a, m), block, block, (self.d ^ (2 * m), self.t))

    def start(self):
        @pl.when(self.keeper)
        def _():
            for a in range(len(self.moved)):
                self.fetch(a).start()

    def relay(self, which):
        @pl.when(self.other)
        def _():
            for a in which:
                self.fetch(a).wait_recv()
                for m in (1, 2, 3):
                    self.share(a, m).start()

    def ready(self, which):
        @pl.when(self.keeper)
        def _():
            for a in which:
                self.moved[a][...] = self.sources[a][...]

        @pl.when(self.other)
        def _():
            for a in which:
                for m in (1, 2, 3):
                    self.share(a, m).wait_recv()

    def finish(self):
        @pl.when(self.keeper)
        def _():
            for a in range(len(self.moved)):
                self.fetch(a).wait_send()

        @pl.when(self.other)
        def _():
            for a in range(len(self.moved)):
                for m in (1, 2, 3):
                    self.share(a, m).wait_send()


class HalfRows:
    def __init__(self, name, copy, rows, half, first, far_first, d, t):
        self.name, self.copy, self.rows, self.half, self.first = name, copy, rows, half, first
        self.far_first = far_first
        self.d, self.t, self.side = d, t, t % 2
        self.keeper = d % 2 == t // 2
        self.other = jnp.logical_not(self.keeper)
        self.count = rows.shape[0]
        self.piece = self.count // 4

    def place(self, s, p):
        return rows_of(self.half, self.first + s * self.count + p * self.piece, self.piece)

    def own(self, p):
        return self.rows.at[pl.ds(p * self.piece, self.piece)]

    def swap(self, p):
        at = rows_of(self.half, self.far_first + self.side * self.count + p * self.piece, self.piece)
        return self.copy((self.name, "swap", p), self.own(p), at, (self.d ^ 1, self.t ^ 2))

    def through(self, p, source):
        return self.copy((self.name, "pass", p), source, self.place(self.side, p), (self.d, self.t ^ 1))

    def start(self):
        @pl.when(self.other)
        def _():
            for p in range(4):
                self.swap(p).start()

        @pl.when(self.keeper)
        def _():
            for p in range(4):
                self.through(p, self.own(p)).start()
            at = pl.multiple_of(self.first + self.side * self.count, 16)
            self.half[pl.ds(at, self.count), :] = self.rows[...]

    def relay(self):
        @pl.when(self.other)
        def _():
            for p in range(4):
                self.swap(p).wait_recv()
                self.through(p, self.place(self.side, p)).start()

    def arrive(self):
        for p in range(4):
            block = self.place(1 - self.side, p)
            self.copy((self.name, "pass", p), block, block, (self.d, self.t ^ 1)).wait_recv()

    def finish(self):
        @pl.when(self.keeper)
        def _():
            for p in range(4):
                self.through(p, self.own(p)).wait_send()

        @pl.when(self.other)
        def _():
            for p in range(4):
                self.swap(p).wait_send()
                self.through(p, self.place(self.side, p)).wait_send()


class Whole:
    def __init__(self, name, copy, source, whole, d, t):
        self.name, self.copy, self.source, self.whole = name, copy, source, whole
        self.d, self.t = d, t
        self.away = jnp.where(d % 2 == t // 2, 0, 1)
        self.rows = source.shape[0]
        self.slim = self.rows // 8
        self.half_at = (d % 2) * (4 * self.slim)
        self.at = self.half_at + ((d // 2) % 4) * self.slim

    def block(self, j):
        return rows_of(self.whole, j * self.rows + self.at, self.slim)

    def far(self):
        return self.copy(
            (self.name, "far"), rows_of(self.source, self.at, self.slim), self.block(self.away), (self.d, self.t ^ 2)
        )

    def near(self, late):
        j = 1 - self.away if late else self.away
        return self.copy((self.name, "near", late), self.block(j), self.block(j + 2), (self.d, self.t ^ 1))

    def level(self, j, m):
        block = rows_of(self.whole, j * self.rows + self.at, self.slim)
        return self.copy((self.name, "level", j, m), block, block, (self.d ^ (2 * m), self.t))

    def hand(self, j):
        return self.copy(
            (self.name, "hand", j),
            rows_of(self.whole, j * self.rows + self.half_at, 4 * self.slim),
            rows_of(self.whole, (j ^ 1) * self.rows + self.half_at, 4 * self.slim),
            (self.d ^ 1, self.t),
        )

    def start(self):
        self.far().start()
        self.whole[pl.ds(pl.multiple_of(self.away * self.rows + self.at, 16), self.slim), :] = self.source[
            pl.ds(pl.multiple_of(self.at, 16), self.slim), :
        ]
        self.near(False).start()

    def pass_on(self):
        self.far().wait_recv()
        self.near(True).start()
        for m in (1, 2, 3):
            for j in (0, 1):
                self.level(j, m).start()

    def across(self):
        self.near(False).wait_recv()
        self.near(True).wait_recv()
        for m in (1, 2, 3):
            for j in (2, 3):
                self.level(j, m).start()

    def hand_over(self):
        for m in (1, 2, 3):
            for j in range(4):
                self.level(j, m).wait_recv()
        for j in range(4):
            self.hand(j).start()

    def finish(self):
        self.far().wait_send()
        self.near(False).wait_send()
        self.near(True).wait_send()
        for m in (1, 2, 3):
            for j in range(4):
                self.level(j, m).wait_send()
        for j in range(4):
            self.hand(j).wait()


def start_kernel(*refs):
    (tokens, gain, shift, *weights, out_weight, next_out, encoder, expand) = refs[:10]
    (rows_half, normed, query, keyed, valued, moved, whole, next_whole, encoder_out, expand_slice) = refs[10:20]
    send_sem, recv_sem = refs[20:]
    d, t = lax.axis_index("dp"), lax.axis_index("tensor")
    core, side = d % 2, t % 2
    keeper = core == t // 2
    other = jnp.logical_not(keeper)
    count = tokens.shape[0]
    copy = Copies(send_sem, recv_sem)
    move = Move("move", copy, weights, [moved.at[a] for a in range(3)], d, t)
    every = Whole("whole", copy, out_weight, whole, d, t)
    after = Whole("next", copy, next_out, next_whole, d, t)
    rows = HalfRows("tokens", copy, tokens, rows_half, 0, 0, d, t)

    greet(
        [(d ^ 2, t), (d ^ 4, t), (d ^ 6, t), (d ^ 1, t), (d, t ^ 1), (d, t ^ 2), (d ^ 1, t ^ 2)]
    )

    def give(name, s):
        block = rows_of(normed, core * (2 * count) + s * count, count)
        return copy(("give", name), block, block, (d ^ 1, t))

    encoder_copy = copy("encoder", encoder, encoder_out, (d ^ 1, t))
    slim = expand_slice.shape[0]
    hop = copy("hop", rows_of(expand, d * slim, slim), expand_slice, (d, t ^ 2))

    every.start()
    after.start()
    rows.start()
    move.start()
    every.pass_on()
    after.pass_on()

    @pl.when(keeper)
    def _():
        encoder_copy.start()

    every.across()
    after.across()
    rows.relay()
    mine = core * (2 * count)
    norm_rows(rows_half, side * count, normed, mine + side * count, count, gain, shift)
    give(0, side).start()
    move.relay(range(3))
    hop.start()
    rows.arrive()
    norm_rows(rows_half, (1 - side) * count, normed, mine + (1 - side) * count, count, gain, shift)
    give(1, 1 - side).start()
    every.hand_over()
    after.hand_over()

    @pl.when(keeper)
    def _():
        encoder_out[...] = encoder[...]

    def project(first):
        def body(i, _):
            at = pl.ds(pl.multiple_of(first + i * 256, 256), 256)
            for a, out in enumerate((query, keyed, valued)):
                out[at, :] = jnp.dot(
                    normed[at, :], moved[a], preferred_element_type=jnp.float32
                ).astype(jnp.bfloat16)
            return 0

        lax.fori_loop(0, (2 * count) // 256, body, 0)

    move.ready(range(3))
    project(mine)
    give(0, side).wait()
    give(1, 1 - side).wait()
    project((1 - core) * (2 * count))
    every.finish()
    after.finish()
    move.finish()
    rows.finish()
    hop.wait()

    @pl.when(keeper)
    def _():
        encoder_copy.wait_send()

    @pl.when(other)
    def _():
        encoder_copy.wait_recv()


def start_layer(tokens, gain, shift, weights, out_weight, next_out, encoder, expand, collective_id):
    rows, wide = tokens.shape
    dp = lax.axis_size("dp")
    width = weights[0].shape[1]
    bf16 = jnp.bfloat16
    shape = jax.ShapeDtypeStruct
    vmem = pl.BlockSpec(memory_space=pltpu.VMEM)
    return pl.pallas_call(
        start_kernel,
        out_shape=(
            shape((2 * rows, wide), bf16),
            shape((4 * rows, wide), bf16),
            shape((4 * rows, width), bf16),
            shape((4 * rows, width), bf16),
            shape((4 * rows, width), bf16),
            shape((3,) + weights[0].shape, bf16),
            shape((4 * out_weight.shape[0], out_weight.shape[1]), bf16),
            shape((4 * next_out.shape[0], next_out.shape[1]), bf16),
            shape(encoder.shape, bf16),
            shape((expand.shape[0] // dp, expand.shape[1]), bf16),
        ),
        in_specs=[vmem] * 9 + [pl.BlockSpec(memory_space=pl.ANY)],
        out_specs=(vmem,) * 9 + (pl.BlockSpec(memory_space=pl.ANY),),
        scratch_shapes=[
            pltpu.SemaphoreType.DMA((72,)),
            pltpu.SemaphoreType.DMA((72,)),
        ],
        compiler_params=pltpu.CompilerParams(
            collective_id=collective_id, has_side_effects=True, vmem_limit_bytes=56 << 20
        ),
        cost_estimate=pl.CostEstimate(flops=35_000_000_000, bytes_accessed=16_000_000, transcendentals=0),
        name="start_layer",
    )(tokens, gain[None], shift[None], *weights, out_weight, next_out, encoder, expand)


def add_dot(left, right, over_rows=False):
    return lax.dot_general(
        left, right, (((1,), (1 if over_rows else 0,)), ((), ())), preferred_element_type=jnp.float32
    )


class Exchange:
    def __init__(self, copy, mine, land, core, d, t, chunk):
        self.copy, self.mine, self.land, self.core, self.chunk = copy, mine, land, core, chunk
        self.half = mine.shape[0] // 2
        self.to = [(d ^ 1, t), (d, t ^ 1), (d ^ 1, t ^ 1)]

    def one(self, j, ch):
        core = self.core if j == 1 else 1 - self.core
        return self.copy(
            ("exchange", j, ch),
            rows_of(self.mine, core * self.half + ch * self.chunk, self.chunk),
            self.land.at[j, pl.ds(ch * self.chunk, self.chunk)],
            self.to[j],
        )

    def start(self, ch):
        for j in (1, 2, 0):
            self.one(j, ch).start()

    def arrive(self, ch):
        for j in range(3):
            self.one(j, ch).wait_recv()

    def pieces(self, ch):
        first = self.core * self.half + ch * self.chunk
        own = self.mine[pl.ds(pl.multiple_of(first, 16), self.chunk), :]
        return [own] + [self.land[j, pl.ds(ch * self.chunk, self.chunk), :] for j in range(3)]

    def sent(self, ch):
        for j in range(3):
            self.one(j, ch).wait_send()


def by_rows(rows, step, body):
    def turn(i, _):
        body(pl.multiple_of(i * step, step))
        return 0

    lax.fori_loop(0, rows // step, turn, 0)


def forward_kernel(*refs):
    (mixed, out_all, start, gain, shift, *weights) = refs[:8]
    (after, normed, result, moved) = refs[8:12]
    (land, product, send_sem, recv_sem) = refs[12:]
    d, t = lax.axis_index("dp"), lax.axis_index("tensor")
    core = d % 2
    chunk = product.shape[0]
    half = after.shape[0]
    width = mixed.shape[1]
    copy = Copies(send_sem, recv_sem)
    greet(
        [(d ^ 1, t), (d, t ^ 1), (d ^ 1, t ^ 1), (d ^ 2, t), (d ^ 4, t), (d ^ 6, t), (d, t ^ 2)]
    )
    exchange = Exchange(copy, mixed, land, core, d, t, chunk)
    move = Move("move", copy, weights, [moved.at[a] for a in range(3)], d, t)

    def give(ch):
        block = rows_of(normed, core * half + ch * chunk, chunk)
        return copy(("give", ch), block, block, (d ^ 1, t))

    chunks = half // chunk
    for ch in range(chunks):
        exchange.start(ch)
    move.start()
    for ch in range(chunks):
        exchange.arrive(ch)
        product[...] = sum(
            add_dot(piece, out_all[j * width : (j + 1) * width, :])
            for j, piece in enumerate(exchange.pieces(ch))
        )

        def rows(at, ch=ch):
            x = start[pl.ds(pl.multiple_of(ch * chunk + at, 16), 32), :].astype(jnp.float32)
            x = x + product[pl.ds(at, 32), :]
            after[pl.ds(pl.multiple_of(ch * chunk + at, 16), 32), :] = x
            unit, inverse = moments(x)
            normed[pl.ds(pl.multiple_of(core * half + ch * chunk + at, 16), 32), :] = (
                unit * gain[...] + shift[...]
            ).astype(jnp.bfloat16)

        by_rows(chunk, 32, rows)
        give(ch).start()
        if ch < 3:
            move.relay([ch])

    def project(first, rows):
        at = pl.ds(pl.multiple_of(first, 16), rows)
        result[at, :] = add_dot(normed[at, :], moved[0]).astype(jnp.bfloat16)

    move.ready([0])
    project(core * half, half)
    for ch in range(chunks):
        give(ch).wait()
    project((1 - core) * half, half)
    move.ready([1, 2])
    for ch in range(chunks):
        exchange.sent(ch)
    move.finish()


def forward_step(mixed, out_all, start, gain, shift, weights, collective_id):
    rows, width = mixed.shape
    half, wide = start.shape
    chunk = half // 4
    shape = jax.ShapeDtypeStruct
    vmem = pl.BlockSpec(memory_space=pltpu.VMEM)
    return pl.pallas_call(
        forward_kernel,
        out_shape=(
            shape((half, wide), jnp.float32),
            shape((rows, wide), jnp.bfloat16),
            shape((rows, width), jnp.bfloat16),
            shape((3,) + weights[0].shape, jnp.bfloat16),
        ),
        in_specs=[vmem] * 8,
        out_specs=(vmem,) * 4,
        scratch_shapes=[
            pltpu.VMEM((3, half, width), jnp.bfloat16),
            pltpu.VMEM((chunk, wide), jnp.float32),
            pltpu.SemaphoreType.DMA((56,)),
            pltpu.SemaphoreType.DMA((56,)),
        ],
        compiler_params=pltpu.CompilerParams(
            collective_id=collective_id, has_side_effects=True, vmem_limit_bytes=56 << 20
        ),
        cost_estimate=pl.CostEstimate(flops=20_000_000_000, bytes_accessed=8_000_000, transcendentals=0),
        name="forward_step",
    )(mixed, out_all, start, gain[None], shift[None], *weights)


def backward_kernel(*refs):
    wide = refs[2].shape[1]
    (grad_query, query_all, after, gain, grad_in, weight) = refs[:6]
    (grad_res, grad_top, result, norm_grads) = refs[6:10]
    (land, product, send_sem, recv_sem) = refs[10:]
    d, t = lax.axis_index("dp"), lax.axis_index("tensor")
    core = d % 2
    chunk = product.shape[0]
    half = after.shape[0]
    copy = Copies(send_sem, recv_sem)
    greet([(d ^ 1, t), (d, t ^ 1), (d ^ 1, t ^ 1)])
    exchange = Exchange(copy, grad_query, land, core, d, t, chunk)

    def give(ch):
        block = rows_of(grad_top, core * half + ch * chunk, chunk)
        return copy(("give", ch), block, block, (d ^ 1, t))

    chunks = half // chunk
    for ch in range(chunks):
        exchange.start(ch)
    norm_grads[...] = jnp.zeros_like(norm_grads)
    for ch in range(chunks):
        exchange.arrive(ch)
        product[...] = sum(add_dot(piece, query_all[j * wide : (j + 1) * wide, :], True) for j, piece in enumerate(exchange.pieces(ch)))

        def rows(at, ch=ch):
            here = pl.ds(pl.multiple_of(ch * chunk + at, 16), 32)
            unit, inverse = moments(after[here, :])
            back, gain_grad, shift_grad = normalize_back(product[pl.ds(at, 32), :], unit, inverse, gain[...])
            total = grad_in[here, :] + back
            grad_res[here, :] = total
            grad_top[pl.ds(pl.multiple_of(core * half + ch * chunk + at, 16), 32), :] = total.astype(jnp.bfloat16)
            norm_grads[0:1, :] += gain_grad[None]
            norm_grads[1:2, :] += shift_grad[None]

        by_rows(chunk, 32, rows)
        give(ch).start()

    def project(first, rows):
        at = pl.ds(pl.multiple_of(first, 16), rows)
        result[at, :] = add_dot(grad_top[at, :], weight[...], True).astype(jnp.bfloat16)

    project(core * half, half)
    for ch in range(chunks):
        give(ch).wait()
    project((1 - core) * half, half)
    for ch in range(chunks):
        exchange.sent(ch)


def backward_step(grad_query, query_all, after, gain, grad_in, weight, collective_id):
    rows, width = grad_query.shape
    half, wide = after.shape
    chunk = half // 4
    shape = jax.ShapeDtypeStruct
    vmem = pl.BlockSpec(memory_space=pltpu.VMEM)
    return pl.pallas_call(
        backward_kernel,
        out_shape=(
            shape((half, wide), jnp.float32),
            shape((rows, wide), jnp.bfloat16),
            shape((rows, weight.shape[0]), jnp.bfloat16),
            shape((8, wide), jnp.float32),
        ),
        in_specs=[vmem] * 6,
        out_specs=(vmem,) * 4,
        scratch_shapes=[
            pltpu.VMEM((3, half, width), jnp.bfloat16),
            pltpu.VMEM((chunk, wide), jnp.float32),
            pltpu.SemaphoreType.DMA((20,)),
            pltpu.SemaphoreType.DMA((20,)),
        ],
        compiler_params=pltpu.CompilerParams(
            collective_id=collective_id, has_side_effects=True, vmem_limit_bytes=56 << 20
        ),
        cost_estimate=pl.CostEstimate(flops=20_000_000_000, bytes_accessed=8_000_000, transcendentals=0),
        name="backward_step",
    )(grad_query, query_all, after, gain[None], grad_in, weight)


def hidden_kernel(*refs):
    (mixed, out_all, start, gain, shift, cot, cot_pair, next_query, *ff_weights) = refs[:12]
    (after, normed, hidden, grad_pre, grad_res, grad_top, result, norm_grads, query_all, grad_out) = refs[12:22]
    (land, product, own, far_send, far_land, sum_send, sum_land, expand, reduce) = refs[22:31]
    (send_sem, recv_sem, local_sem) = refs[31:]
    d, t = lax.axis_index("dp"), lax.axis_index("tensor")
    core = d % 2
    chunk = product.shape[0]
    half = after.shape[0]
    width = mixed.shape[1]
    chunks = half // chunk
    copy = Copies(send_sem, recv_sem)
    greet(
        [(d ^ 1, t), (d, t ^ 1), (d ^ 1, t ^ 1), (d ^ 2, t), (d ^ 4, t), (d ^ 6, t), (d, t ^ 2)]
    )
    exchange = Exchange(copy, mixed, land, core, d, t, chunk)
    every = Whole("query", copy, next_query, query_all, d, t)

    def give(name, ref, ch):
        block = rows_of(ref, core * half + ch * chunk, chunk)
        return copy((name, ch), block, block, (d ^ 1, t))

    def slab(ref, ch):
        return ref.at[pl.ds(ch * chunk, chunk)]

    def far(ch):
        return copy(("far", ch), slab(far_send, ch), slab(far_land, ch), (d ^ 1, t))

    def whole(ch):
        return copy(("whole", ch), slab(sum_send, ch), slab(sum_land, ch), (d, t ^ 1))

    def residual(ch):
        exchange.arrive(ch)
        product[...] = sum(
            add_dot(piece, out_all[j * width : (j + 1) * width, :])
            for j, piece in enumerate(exchange.pieces(ch))
        )

        def rows(at):
            here = pl.ds(pl.multiple_of(ch * chunk + at, 16), 32)
            x = start[here, :] + product[pl.ds(at, 32), :]
            after[here, :] = x
            unit, inverse = moments(x)
            normed[pl.ds(pl.multiple_of(core * half + ch * chunk + at, 16), 32), :] = (
                unit * gain[...] + shift[...]
            ).astype(jnp.bfloat16)

        by_rows(chunk, 32, rows)
        give("normed", normed, ch).start()

    def feed(first):
        every = pl.ds(pl.multiple_of(first, 16), chunk)
        product[...] = add_dot(normed[every, :], expand[...])
        own[...] = add_dot(grad_out[every, :], reduce[...], True)

        def rows(at):
            here = pl.ds(pl.multiple_of(first + at, 16), 32)
            z = product[pl.ds(at, 32), :]
            inner = jnp.tanh(tanh_coeff * (z + cubic_coeff * z * z * z))
            hidden[here, :] = (0.5 * z * (1.0 + inner)).astype(jnp.bfloat16)
            slope = 0.5 * (1.0 + inner) + 0.5 * z * (1.0 - inner * inner) * tanh_coeff * (
                1.0 + 3.0 * cubic_coeff * z * z
            )
            upper = own[pl.ds(at, 32), :].astype(jnp.bfloat16).astype(jnp.float32)
            grad_pre[here, :] = (upper * slope).astype(jnp.bfloat16)

        by_rows(chunk, 32, rows)
        return add_dot(grad_pre[pl.ds(pl.multiple_of(first, 16), chunk), :], expand[...], True)

    def both(ch):
        copy(
            ("normed", ch), *([rows_of(normed, (1 - core) * half + ch * chunk, chunk)] * 2), (d ^ 1, t)
        ).wait_recv()
        far_send[pl.ds(ch * chunk, chunk), :] = feed((1 - core) * half + ch * chunk).astype(jnp.bfloat16)
        far(ch).start()
        own[...] = feed(core * half + ch * chunk)
        far(ch).wait_recv()

        def rows(at):
            here = pl.ds(pl.multiple_of(ch * chunk + at, 16), 32)
            sum_send[here, :] = (own[pl.ds(at, 32), :] + far_land[here, :].astype(jnp.float32)).astype(jnp.bfloat16)

        by_rows(chunk, 32, rows)
        whole(ch).start()

    def back(ch):
        whole(ch).wait_recv()

        def rows(at):
            here = pl.ds(pl.multiple_of(ch * chunk + at, 16), 32)
            grad = sum_send[here, :].astype(jnp.float32) + sum_land[here, :].astype(jnp.float32)
            unit, inverse = moments(after[here, :])
            down, gain_grad, shift_grad = normalize_back(grad, unit, inverse, gain[...])
            top = grad_out[pl.ds(pl.multiple_of(core * half + ch * chunk + at, 16), 32), :]
            total = top.astype(jnp.float32) + down
            grad_res[here, :] = total
            grad_top[pl.ds(pl.multiple_of(core * half + ch * chunk + at, 16), 32), :] = total.astype(jnp.bfloat16)
            norm_grads[0:1, :] += gain_grad[None]
            norm_grads[1:2, :] += shift_grad[None]

        by_rows(chunk, 32, rows)
        give("top", grad_top, ch).start()

    def project(first, rows):
        at = pl.ds(pl.multiple_of(first, 16), rows)
        result[at, :] = add_dot(grad_top[at, :], out_all[:width, :], True).astype(jnp.bfloat16)

    for ch in range(chunks):
        exchange.start(ch)
    keeper = core == t // 2

    def fetch(which, act):
        for a, weight in enumerate((expand, reduce)):
            act(pltpu.make_async_copy(ff_weights[2 * which + a], weight, local_sem.at[a]))

    def both_ways(act):
        @pl.when(keeper)
        def _():
            fetch(0, act)

        @pl.when(jnp.logical_not(keeper))
        def _():
            fetch(1, act)

    both_ways(lambda one: one.start())
    count = cot.shape[0]
    side = t % 2
    grad_out[pl.ds(pl.multiple_of(core * half + side * count, 16), count), :] = cot[...]
    grad_out[pl.ds(pl.multiple_of(core * half + (1 - side) * count, 16), count), :] = cot_pair[...]
    block = rows_of(grad_out, core * half, half)
    spread = copy("cot", block, block, (d ^ 1, t))
    spread.start()
    every.start()
    norm_grads[...] = jnp.zeros_like(norm_grads)
    residual(0)
    residual(1)
    both_ways(lambda one: one.wait())
    every.pass_on()
    spread.wait()
    both(0)
    residual(2)
    both(1)
    residual(3)
    both(2)
    every.across()
    back(0)
    both(3)
    back(1)
    back(2)
    every.hand_over()
    back(3)
    project(core * half, half)
    for ch in range(chunks):
        copy(
            ("top", ch), *([rows_of(grad_top, (1 - core) * half + ch * chunk, chunk)] * 2), (d ^ 1, t)
        ).wait_recv()
    project((1 - core) * half, half)
    for ch in range(chunks):
        exchange.sent(ch)
        give("normed", normed, ch).wait_send()
        give("top", grad_top, ch).wait_send()
        far(ch).wait_send()
        whole(ch).wait_send()
    every.finish()


def hidden_step(mixed, out_all, start, gain, shift, cot, cot_pair, next_query, ff_weights, collective_id):
    rows, width = mixed.shape
    half, wide = start.shape
    inner = ff_weights[0].shape[1]
    chunk = half // 4
    bf16, f32 = jnp.bfloat16, jnp.float32
    shape = jax.ShapeDtypeStruct
    vmem = pl.BlockSpec(memory_space=pltpu.VMEM)
    return pl.pallas_call(
        hidden_kernel,
        out_shape=(
            shape((half, wide), f32),
            shape((rows, wide), bf16),
            shape((rows, inner), bf16),
            shape((rows, inner), bf16),
            shape((half, wide), f32),
            shape((rows, wide), bf16),
            shape((rows, width), bf16),
            shape((8, wide), f32),
            shape((4 * next_query.shape[0], next_query.shape[1]), bf16),
            shape((rows, wide), bf16),
        ),
        in_specs=[vmem] * 8 + [pl.BlockSpec(memory_space=pl.ANY)] * 4,
        out_specs=(vmem,) * 10,
        scratch_shapes=[
            pltpu.VMEM((3, half, width), bf16),
            pltpu.VMEM((chunk, max(wide, inner)), f32),
            pltpu.VMEM((chunk, max(wide, inner)), f32),
            pltpu.VMEM((half, wide), bf16),
            pltpu.VMEM((half, wide), bf16),
            pltpu.VMEM((half, wide), bf16),
            pltpu.VMEM((half, wide), bf16),
            pltpu.VMEM(ff_weights[0].shape, bf16),
            pltpu.VMEM(ff_weights[1].shape, bf16),
            pltpu.SemaphoreType.DMA((56,)),
            pltpu.SemaphoreType.DMA((56,)),
            pltpu.SemaphoreType.DMA((2,)),
        ],
        compiler_params=pltpu.CompilerParams(
            collective_id=collective_id, has_side_effects=True, vmem_limit_bytes=60 << 20
        ),
        cost_estimate=pl.CostEstimate(flops=50_000_000_000, bytes_accessed=16_000_000, transcendentals=0),
        name="hidden_step",
    )(mixed, out_all, start, gain[None], shift[None], cot, cot_pair, next_query, *ff_weights)


def on_device(
    tokens,
    encoder_states,
    tok_lengths,
    enc_lengths,
    pad_mask,
    first_gain,
    first_shift,
    causal_query,
    causal_key,
    causal_value,
    causal_out,
    second_gain,
    second_shift,
    cross_query,
    cross_key,
    cross_value,
    cross_out,
    third_gain,
    third_shift,
    expand_weight,
    reduce_weight,
    cotangent,
):
    place = Place()
    width = causal_query.shape[1]
    length = pad_mask.shape[0]
    frames = encoder_states.shape[0]

    def of_group(value):
        return jnp.where(place.keeper, value, place.swap(value, 1, 0))

    def half_rows(quarter):
        return place.ordered(quarter, place.swap(quarter, 0, 1), place.side)

    def quarter_of(half):
        return place.part(half, place.side, 2)

    tok_lengths, enc_lengths, pad_mask = of_group(tok_lengths), of_group(enc_lengths), of_group(pad_mask)
    block_q, block_k = 256, 512
    token_seg, frame_seg, key_seg, self_lo, self_hi, cross_lo, cross_hi = ranges(
        tok_lengths[0], enc_lengths[0], pad_mask, length, frames, block_q, block_k
    )
    self_keys = jnp.stack([token_seg, key_seg] + [token_seg] * 6)
    cross_keys = jnp.stack([frame_seg] * 8)
    seg_col, seg_row = token_seg[:, None], token_seg[None, :]

    tokens_half, first_all, query, keyed, valued, moved, causal_out_perm, cross_out_perm, encoder, expand_piece = start_layer(
        tokens,
        first_gain,
        first_shift,
        (causal_query, causal_key, causal_value),
        causal_out,
        cross_out,
        encoder_states,
        expand_weight,
        1,
    )
    tokens_here = quarter_of(tokens_half)
    causal_out_here = causal_out_perm[:width]
    hidden_width = expand_weight.shape[1]
    expand_moved = lax.all_gather(expand_piece, "dp", axis=0, tiled=True)
    reduce_piece = place.part(reduce_weight, place.d, place.dp)
    reduce_piece, query = lax.optimization_barrier((reduce_piece, query))
    reduce_piece = place.swap(reduce_piece, 0, 2)

    mixed, self_logsum = attend_fwd(
        query, keyed, valued, seg_col, self_keys, self_lo, self_hi, True, block_q, block_k
    )
    mixed, reduce_piece, cot_here = lax.optimization_barrier((mixed, reduce_piece, cotangent))
    reduce_moved = lax.all_gather(reduce_piece, "dp", axis=0, tiled=True)
    cot_here = place.home(cot_here)
    after_self, second_all, cquery, cross_moved = forward_step(
        mixed,
        causal_out_perm,
        tokens_half,
        second_gain,
        second_shift,
        (cross_query, cross_key, cross_value),
        2,
    )
    cquery, cot_here = lax.optimization_barrier((cquery, cot_here))
    cot_pair = place.swap(cot_here, 0, 1)
    ckeyed = times(encoder, cross_moved[1]).astype(jnp.bfloat16)
    cvalued = times(encoder, cross_moved[2]).astype(jnp.bfloat16)
    cmixed, cross_logsum = attend_fwd(
        cquery, ckeyed, cvalued, seg_col, cross_keys, cross_lo, cross_hi, False, block_q, block_k
    )
    after_cross, third_all, hidden, grad_expand_in, grad_res, grad_top2, grad_cmixed, third_grads, cross_query_every, grad_top = hidden_step(
        cmixed, cross_out_perm, after_self, third_gain, third_shift, cot_here, cot_pair, cross_query,
        (expand_weight, reduce_weight, expand_moved, reduce_moved), 3
    )
    third_gain_grad, third_shift_grad = third_grads[0], third_grads[1]
    out_term = times(hidden, jnp.where(place.keeper, reduce_weight, reduce_moved)).astype(jnp.bfloat16)
    reduce_grad = along_rows(hidden, grad_top)
    expand_grad = along_rows(third_all, grad_expand_in)

    cross_out_grad = along_rows(cmixed, grad_top2)
    expand_grad, reduce_grad = place.sum_columns(expand_grad, 0), place.sum_columns(reduce_grad, 1)
    grad_cquery, grad_ckey, grad_cvalue = attend_bwd(
        cquery, ckeyed, cvalued, cmixed, grad_cmixed, cross_logsum, seg_row, cross_keys.T,
        cross_lo, cross_hi, False, block_q, block_k,
    )
    grad_cross_in = jnp.concatenate([grad_ckey, grad_cvalue], axis=1)
    cross_grad = along_rows(encoder, grad_cross_in)
    cross_query_grad = along_rows(second_all, grad_cquery)
    encoder_term = (against(grad_ckey, cross_moved[1]) + against(grad_cvalue, cross_moved[2])).astype(jnp.bfloat16)
    grad_res, grad_top, grad_mixed, second_grads = backward_step(
        grad_cquery, cross_query_every, after_self, second_gain, grad_res, causal_out_here, 4
    )
    second_gain_grad, second_shift_grad = second_grads[0], second_grads[1]
    causal_out_grad = along_rows(mixed, grad_top)
    grad_mixed, expand_grad, reduce_grad = lax.optimization_barrier((grad_mixed, expand_grad, reduce_grad))
    expand_grad, reduce_grad = place.cross_planes([expand_grad, reduce_grad])
    grad_query, grad_key, grad_value = attend_bwd(
        query, keyed, valued, mixed, grad_mixed, self_logsum, seg_row, self_keys.T,
        self_lo, self_hi, True, block_q, block_k,
    )
    grad_in = jnp.concatenate([grad_query, grad_key, grad_value], axis=1)
    causal_grad = along_rows(first_all, grad_in)
    first_term = (
        against(grad_query, moved[0]) + against(grad_key, moved[1]) + against(grad_value, moved[2])
    )
    first_rows = (first_all.astype(jnp.float32) - first_shift) / first_gain
    first_gain_grad = jnp.sum(first_term * first_rows, axis=0)
    first_shift_grad = jnp.sum(first_term, axis=0)
    bf16 = jnp.bfloat16
    once = (place.side == 0).astype(jnp.float32)
    none = jnp.zeros_like(first_gain_grad)
    norm_grads = jnp.stack(
        [
            first_gain_grad,
            first_shift_grad,
            second_gain_grad * once,
            second_shift_grad * once,
            third_gain_grad * once,
            third_shift_grad * once,
            none,
            none,
        ]
    )
    *sums, encoder_grad, output, tokens_grad, norm_grads = sum_all(
        [
            expand_grad,
            reduce_grad,
            jnp.concatenate([cross_grad, cross_query_grad], axis=1).astype(bf16),
            causal_grad.astype(bf16),
            cross_out_grad.astype(bf16),
            causal_out_grad.astype(bf16),
        ],
        (1, 1, 1),
        (True, False, False),
        [encoder_term, out_term, first_term.astype(bf16)],
        norm_grads,
        quarter_of(after_cross),
        tokens_here,
        quarter_of(grad_res),
        first_gain,
        0,
    )
    (
        first_gain_grad,
        first_shift_grad,
        second_gain_grad,
        second_shift_grad,
        third_gain_grad,
        third_shift_grad,
    ) = (norm_grads[i] for i in range(6))
    expand_grad, reduce_grad, cross_grads, causal_grads, cross_out_grad, causal_out_grad = (
        value.astype(jnp.float32) for value in sums
    )
    cross_key_grad, cross_value_grad, cross_query_grad = (
        cross_grads[:, i * width : (i + 1) * width] for i in range(3)
    )
    causal_query_grad, causal_key_grad, causal_value_grad = (
        causal_grads[:, i * width : (i + 1) * width] for i in range(3)
    )
    return (
        output,
        tokens_grad,
        encoder_grad,
        first_gain_grad,
        first_shift_grad,
        causal_query_grad,
        causal_key_grad,
        causal_value_grad,
        causal_out_grad,
        second_gain_grad,
        second_shift_grad,
        cross_query_grad,
        cross_key_grad,
        cross_value_grad,
        cross_out_grad,
        third_gain_grad,
        third_shift_grad,
        expand_grad,
        reduce_grad,
    )


def solution(mesh):
    in_specs = (
        P(("dp", "tensor"), None),
        P("dp", None),
        P("dp", None),
        P("dp", None),
        P("dp"),
        P(),
        P(),
        P(None, "tensor"),
        P(None, "tensor"),
        P(None, "tensor"),
        P("tensor", None),
        P(),
        P(),
        P(None, "tensor"),
        P(None, "tensor"),
        P(None, "tensor"),
        P("tensor", None),
        P(),
        P(),
        P(None, "tensor"),
        P("tensor", None),
        P(("dp", "tensor"), None),
    )
    out_specs = (
        P(("dp", "tensor"), None),
        P(("dp", "tensor"), None),
        P(("dp", "tensor"), None),
        P(),
        P(),
        P(None, "tensor"),
        P(None, "tensor"),
        P(None, "tensor"),
        P("tensor", None),
        P(),
        P(),
        P(None, "tensor"),
        P(None, "tensor"),
        P(None, "tensor"),
        P("tensor", None),
        P(),
        P(),
        P(None, "tensor"),
        P("tensor", None),
    )
    return jax.shard_map(
        on_device, mesh=mesh, in_specs=in_specs, out_specs=out_specs, check_vma=False
    )
```

```python
import functools

import jax
import jax.numpy as jnp
from jax import lax
from jax.experimental import pallas as pl
from jax.experimental.pallas import tpu as pltpu
from jax.sharding import PartitionSpec as P

HEAD_DIM = 64


eps = 1e-05
tanh_coeff = 0.7978845608
cubic_coeff = 0.044715


def smooth_gate(values):
    inner = jnp.tanh(tanh_coeff * (values + cubic_coeff * values * values * values))
    return 0.5 * values * (1.0 + inner)


def smooth_slope(values):
    inner = jnp.tanh(tanh_coeff * (values + cubic_coeff * values * values * values))
    return 0.5 * (1.0 + inner) + 0.5 * values * (1.0 - inner * inner) * tanh_coeff * (
        1.0 + 3.0 * cubic_coeff * values * values
    )


BF=jnp.bfloat16
F32=jnp.float32

def head_mask(rows, width, h):
    lane = lax.broadcasted_iota(jnp.int32, (rows, width), 1)
    return (lane // HEAD_DIM) == h

def dot(a,b,ca,cb):
    return lax.dot_general(a,b,(((ca,),(cb,)),((),())),preferred_element_type=F32)

def fwd_kernel(causal, heads, bq, bk, lo_ref, hi_ref, q_ref, k_ref, v_ref, rs_ref, ks_ref, o_ref, lse_ref, acc):
    count, width = q_ref.shape
    def one(qb, _):
        q0 = pl.multiple_of(qb*bq, bq)
        qv = q_ref[pl.ds(q0,bq),:] * BF(HEAD_DIM**-0.5)
        rseg = rs_ref[pl.ds(q0,bq),0:1]
        qm = [jnp.where(head_mask(bq,width,h), qv, BF(0)) for h in range(heads)]
        acc[...] = jnp.zeros_like(acc)
        lane = lax.broadcasted_iota(jnp.int32,(bq,128),1)
        def inner(kb, carry):
            k0 = pl.multiple_of(kb*bk, bk)
            kv = k_ref[pl.ds(k0,bk),:]
            vv = v_ref[pl.ds(k0,bk),:]
            kseg = ks_ref[0:1,pl.ds(k0,bk)]
            if causal:
                kpad = ks_ref[1:2,pl.ds(k0,bk)]
                ri = lax.broadcasted_iota(jnp.int32,(bq,bk),0)+q0
                ci = lax.broadcasted_iota(jnp.int32,(bq,bk),1)+k0
                ok = ((rseg==kpad)&(ci<=ri))|(ci==ri)
            else:
                ok = rseg==kseg
            ms, ls = carry
            new_m, new_l = [], []
            parts=None
            alphas=[]
            for h in range(heads):
                s = dot(qm[h],kv,1,1)
                s = jnp.where(ok,s,-1e30)
                m = jnp.maximum(ms[h], jnp.max(s,axis=1,keepdims=True))
                p = jnp.exp(s-m)
                al = jnp.exp(ms[h]-m)
                new_m.append(m); new_l.append(ls[h]*al+jnp.sum(p,axis=1,keepdims=True))
                vm = jnp.where(head_mask(bk,width,h),vv,BF(0))
                t = dot(p.astype(BF),vm,1,0)
                parts = t if parts is None else parts+t
                alphas.append(al)
            lane2 = lax.broadcasted_iota(jnp.int32,(bq,width),1)//HEAD_DIM
            sc = alphas[heads-1]
            for h in range(heads-1):
                sc = jnp.where(lane2==h, alphas[h], sc)
            acc[...] = acc[...]*sc + parts
            return (tuple(new_m),tuple(new_l))
        init = (tuple(jnp.full((bq,1),-1e30,F32) for _ in range(heads)), tuple(jnp.zeros((bq,1),F32) for _ in range(heads)))
        ms, ls = lax.fori_loop(lo_ref[qb], hi_ref[qb], inner, init)
        lane2 = lax.broadcasted_iota(jnp.int32,(bq,width),1)//HEAD_DIM
        inv = [1.0/l for l in ls]
        sc = inv[heads-1]
        for h in range(heads-1):
            sc = jnp.where(lane2==h, inv[h], sc)
        o_ref[pl.ds(q0,bq),:] = (acc[...]*sc).astype(BF)
        st = jnp.zeros((bq,128),F32)
        for h in range(heads):
            st = jnp.where(lane==h, ms[h]+jnp.log(ls[h]), st)
        stt = jnp.transpose(st)
        lse_ref[:,pl.ds(q0,bq)] = stt[0:8,:]
        return 0
    lax.fori_loop(0,count//bq,one,0)

def attend_fwd(q,k,v,rseg,kseg,lo,hi,causal,bq=256,bk=256):
    count,width=q.shape
    heads=width//HEAD_DIM
    vm=pl.BlockSpec(memory_space=pltpu.VMEM); sm=pl.BlockSpec(memory_space=pltpu.SMEM)
    return pl.pallas_call(functools.partial(fwd_kernel,causal,heads,bq,bk),
        out_shape=(jax.ShapeDtypeStruct((count,width),BF),jax.ShapeDtypeStruct((8,count),F32)),
        in_specs=[sm,sm,vm,vm,vm,vm,vm],out_specs=(vm,vm),
        scratch_shapes=[pltpu.VMEM((bq,width),F32)],
        compiler_params=pltpu.CompilerParams(vmem_limit_bytes=40<<20),
        cost_estimate=pl.CostEstimate(flops=22_000_000_000, bytes_accessed=8_000_000, transcendentals=0),
        name="attend_fwd",
    )(lo,hi,q,k,v,rseg,kseg)

def bwd_kernel(causal, heads, bq, bk, lo_ref, hi_ref, q_ref, k_ref, v_ref, o_ref, do_ref, lse_ref, rs_ref, ks_ref,
               dq_ref, dkv_ref, dka, dva, qm, dom, dqa):
    count,width=q_ref.shape
    dka[...]=jnp.zeros_like(dka); dva[...]=jnp.zeros_like(dva)
    def one(qb,_):
        q0=pl.multiple_of(qb*bq,bq)
        qv=q_ref[pl.ds(q0,bq),:]*BF(HEAD_DIM**-0.5)
        dov=do_ref[pl.ds(q0,bq),:]
        prod=dov.astype(F32)*o_ref[pl.ds(q0,bq),:].astype(F32)
        row=lax.broadcasted_iota(jnp.int32,(8,width),0); col=lax.broadcasted_iota(jnp.int32,(8,width),1)//HEAD_DIM
        sel=(row==col).astype(F32)
        delta=lax.dot_general(sel,prod,(((1,),(1,)),((),())),precision=lax.Precision.HIGHEST,preferred_element_type=F32)
        for h in range(heads):
            hm=head_mask(bq,width,h)
            qm[pl.ds(h*bq,bq),:]=jnp.where(hm,qv,BF(0))
            dom[pl.ds(h*bq,bq),:]=jnp.where(hm,dov,BF(0))
        dqa[...]=jnp.zeros_like(dqa)
        rseg=rs_ref[0:1,pl.ds(q0,bq)]
        lse=lse_ref[:,pl.ds(q0,bq)]
        def inner(kb,_):
            k0=pl.multiple_of(kb*bk,bk)
            kv=k_ref[pl.ds(k0,bk),:]; vv=v_ref[pl.ds(k0,bk),:]
            if causal:
                kpad=ks_ref[pl.ds(k0,bk),1:2]
                ri=lax.broadcasted_iota(jnp.int32,(bk,bq),1)+q0
                ci=lax.broadcasted_iota(jnp.int32,(bk,bq),0)+k0
                ok=((rseg==kpad)&(ci<=ri))|(ci==ri)
            else:
                ok=rseg==ks_ref[pl.ds(k0,bk),0:1]
            ps=[];dss=[]
            dq=None
            for h in range(heads):
                st=dot(kv,qm[pl.ds(h*bq,bq),:],1,1)
                p=jnp.where(ok,jnp.exp(st-lse[h:h+1,:]),0.0)
                dp=dot(vv,dom[pl.ds(h*bq,bq),:],1,1)
                ds=(p*(dp-delta[h:h+1,:])).astype(BF)
                ps.append(p.astype(BF)); dss.append(ds)
                km=jnp.where(head_mask(bk,width,h),kv,BF(0))
                t=dot(ds,km,0,0)
                dq=t if dq is None else dq+t
            dqa[...]+=dq
            pcat=jnp.concatenate(ps,axis=1); dcat=jnp.concatenate(dss,axis=1)
            dva[pl.ds(k0,bk),:]+=dot(pcat,dom[...],1,0)
            dka[pl.ds(k0,bk),:]+=dot(dcat,qm[...],1,0)
            return 0
        lax.fori_loop(lo_ref[qb],hi_ref[qb],inner,0)
        dq_ref[pl.ds(q0,bq),:width]=(dqa[...]*(HEAD_DIM**-0.5)).astype(BF)
        return 0
    lax.fori_loop(0,count//bq,one,0)
    out_ref = dq_ref if dkv_ref is None else dkv_ref
    first = out_ref.shape[1] - 2*width
    out_ref[:,first:first+width]=dka[...].astype(BF)
    out_ref[:,first+width:]=dva[...].astype(BF)

def attend_bwd(q,k,v,o,do,lse,rseg,kseg,lo,hi,causal,bq=256,bk=256):
    count,width=q.shape; keys=k.shape[0]
    heads=width//HEAD_DIM
    vm=pl.BlockSpec(memory_space=pltpu.VMEM); sm=pl.BlockSpec(memory_space=pltpu.SMEM)
    def kernel(*refs):
        rest=refs if not causal else refs[:11]+(None,)+refs[11:]
        bwd_kernel(causal,heads,bq,bk,*rest)
    shape=jax.ShapeDtypeStruct
    out_shape=(shape((count,3*width),BF),) if causal else (shape((count,width),BF),shape((keys,2*width),BF))
    return pl.pallas_call(kernel,
        out_shape=out_shape,
        in_specs=[sm,sm]+[vm]*8,out_specs=(vm,)*len(out_shape),
        scratch_shapes=[pltpu.VMEM((keys,width),F32),pltpu.VMEM((keys,width),F32),pltpu.VMEM((heads*bq,width),BF),pltpu.VMEM((heads*bq,width),BF),pltpu.VMEM((bq,width),F32)],
        compiler_params=pltpu.CompilerParams(vmem_limit_bytes=40<<20),
        cost_estimate=pl.CostEstimate(flops=30_000_000_000, bytes_accessed=8_000_000, transcendentals=0),
        name="attend_bwd",
    )(lo,hi,q,k,v,o,do,lse,rseg,kseg)

def ranges(tok_lengths, enc_lengths, pad, count, frames, bq, bk):
    tend=jnp.cumsum(tok_lengths,dtype=jnp.int32); eend=jnp.cumsum(enc_lengths,dtype=jnp.int32)
    places=jnp.arange(count,dtype=jnp.int32)
    tseg=jnp.sum((places[:,None]>=tend[None,:]).astype(jnp.int32),axis=1)
    eseg=jnp.sum((jnp.arange(frames,dtype=jnp.int32)[:,None]>=eend[None,:]).astype(jnp.int32),axis=1)
    starts=jnp.arange(count//bq,dtype=jnp.int32)*bq
    first=tseg[::bq]; last=tseg[bq-1::bq]
    onehot=lambda s:(s[:,None]==jnp.arange(tend.shape[0])[None,:]).astype(jnp.int32)
    pick=lambda arr,s: jnp.sum(onehot(s)*arr[None,:],axis=1)
    tstart=tend-tok_lengths; estart=eend-enc_lengths
    slo=pick(tstart,first)//bk; shi=(starts+bq+bk-1)//bk
    clo=pick(estart,first)//bk; chi=(pick(eend,last)+bk-1)//bk
    kpad=jnp.where(pad==1,tseg,-1)
    return tseg,eseg,kpad,slo,shi,clo,chi


def along_rows(left, right):
    return lax.dot_general(
        left, right, (((0,), (0,)), ((), ())), preferred_element_type=jnp.float32
    )


def against(left, weight):
    return lax.dot_general(
        left, weight, (((1,), (1,)), ((), ())), preferred_element_type=jnp.float32
    )


def times(left, weight):
    return jnp.dot(left, weight, preferred_element_type=jnp.float32)


def moments(rows):
    centred = rows - jnp.mean(rows, axis=1, keepdims=True)
    inverse = lax.rsqrt(jnp.mean(centred * centred, axis=1, keepdims=True) + eps)
    return centred * inverse, inverse


def normalize_back(grad_out, unit, inverse, gain):
    scaled = grad_out * gain
    inner = (
        scaled
        - jnp.mean(scaled, axis=1, keepdims=True)
        - unit * jnp.mean(scaled * unit, axis=1, keepdims=True)
    )
    return (inner * inverse, jnp.sum(grad_out * unit, axis=0), jnp.sum(grad_out, axis=0))


class Place:
    def __init__(self):
        self.dp = lax.axis_size("dp")
        self.tensor = lax.axis_size("tensor")
        self.d = lax.axis_index("dp")
        self.t = lax.axis_index("tensor")
        self.core = self.d % 2
        self.half = self.t // 2
        self.side = self.t % 2
        self.keeper = self.core == self.half
        self.shard = jnp.where(self.keeper, self.t, self.t ^ 2)

    def swap(self, value, d_flip, t_flip, only=None):
        pairs = []
        for d in range(self.dp):
            for t in range(self.tensor):
                keeper = d % 2 == t // 2
                if only is None or only == keeper:
                    pairs.append((d * self.tensor + t, (d ^ d_flip) * self.tensor + (t ^ t_flip)))
        return lax.ppermute(value, ("dp", "tensor"), pairs)

    def home(self, value):
        return jnp.where(self.keeper, value, self.swap(value, 1, 2, False))

    def ordered(self, mine, other, which):
        return jnp.where(
            which == 0, jnp.concatenate([mine, other]), jnp.concatenate([other, mine])
        )

    def part(self, value, which, parts):
        size = value.shape[0] // parts
        return lax.dynamic_slice_in_dim(value, which * size, size, 0)

    def both_cores(self, half_rows):
        return self.ordered(half_rows, self.swap(half_rows, 1, 0), self.core)

    def spread_columns(self, value):
        near, far = self.part(value, self.core, 2), self.part(value, 1 - self.core, 2)
        return jnp.concatenate(
            [near, self.swap(far, 1, 0), self.swap(near, 0, 1), self.swap(far, 1, 1)], axis=1
        )

    def order(self):
        return [self.shard, self.shard ^ 2, self.shard ^ 1, self.shard ^ 3]

    def sum_half(self, value):
        near, far = self.part(value, self.core, 2), self.part(value, 1 - self.core, 2)
        return near.astype(jnp.float32) + self.swap(far.astype(jnp.bfloat16), 1, 0).astype(jnp.float32)

    def sum_group_half(self, value):
        mine = self.sum_half(value).astype(jnp.bfloat16)
        return mine.astype(jnp.float32) + self.swap(mine, 0, 1).astype(jnp.float32)

    def sum_group_quarter(self, value):
        mine = self.sum_half(value)
        near, far = self.part(mine, self.side, 2), self.part(mine, 1 - self.side, 2)
        return near + self.swap(far.astype(jnp.bfloat16), 0, 1).astype(jnp.float32)

    def sum_columns(self, grad, order):
        columns = self.dp // 2
        bits = columns.bit_length() - 1
        turned = [sum(((c >> b) & 1) << (bits - 1 - b) for b in range(bits)) for c in range(columns)]
        groups = [[2 * (turned[c] if order == 0 else c) + core for c in range(columns)] for core in range(2)]
        return lax.psum_scatter(
            grad.astype(jnp.bfloat16), "dp", scatter_dimension=0, axis_index_groups=groups, tiled=True
        )

    def cross_planes(self, grads):
        return [
            (grad.astype(jnp.float32) + self.swap(grad, 0, 2, False).astype(jnp.float32)).astype(jnp.bfloat16)
            for grad in grads
        ]

    def moved_weight(self, weight):
        piece = self.swap(self.part(weight, self.d, self.dp), 0, 2)
        return jnp.where(self.keeper, weight, lax.all_gather(piece, "dp", axis=0, tiled=True))

    def whole_weight(self, weight):
        piece = self.part(weight, self.d, self.dp)
        every = lax.all_gather(piece, ("dp", "tensor"), axis=0, tiled=False)
        every = every.reshape((self.dp, self.tensor) + piece.shape)
        return jnp.swapaxes(every, 0, 1).reshape((self.tensor,) + weight.shape)


class Copies:
    def __init__(self, send_sem, recv_sem):
        self.send_sem, self.recv_sem, self.known = send_sem, recv_sem, {}

    def __call__(self, name, src, dst, device):
        at = self.known.setdefault(name, len(self.known))
        return pltpu.make_async_remote_copy(
            src_ref=src,
            dst_ref=dst,
            send_sem=self.send_sem.at[at],
            recv_sem=self.recv_sem.at[at],
            device_id=device,
            device_id_type=pl.DeviceIdType.MESH,
        )


def greet(devices):
    barrier = pltpu.get_barrier_semaphore()
    for device in devices:
        pl.semaphore_signal(
            barrier, inc=1, device_id=device, device_id_type=pl.DeviceIdType.MESH
        )
    pl.semaphore_wait(barrier, len(devices))


def rows_of(ref, start, size, step=16):
    return ref.at[pl.ds(pl.multiple_of(start, step), size)]


def norm_rows(src, src_first, dst, dst_first, rows, gain, shift):
    chunk = 64

    def body(i, _):
        at = i * chunk
        x = src[pl.ds(pl.multiple_of(src_first + at, 16), chunk), :].astype(jnp.float32)
        unit, inverse = moments(x)
        dst[pl.ds(pl.multiple_of(dst_first + at, 16), chunk), :] = (
            unit * gain[...] + shift[...]
        ).astype(jnp.bfloat16)
        return 0

    lax.fori_loop(0, rows // chunk, body, 0)


def sum_kernel(dp, arrays, units, spans, *refs):
    it = iter(refs)
    take = lambda count: [next(it) for _ in range(count)]
    ins = take(arrays)
    row_arrays = len(spans)
    parts = take(row_arrays)
    small_in, tokens, grad_in, gain = take(4)
    outs = take(arrays)
    row_outs = take(row_arrays)
    (small_out,) = take(1)
    bits = [b for b in (2, 4, 8, 16, 32, 64) if b < dp]
    steps = len(bits)
    land, hold = [], []
    for unit in units:
        hold.append(take(0 if unit[4] else steps))
        land.append(take((steps + 1, 1, 0)[unit[4]]))
    encoder_rows, token_rows = range(row_arrays)
    row_land = [take(2) for _ in range(row_arrays)]
    row_hold = [take(2) for _ in range(row_arrays)]
    small_hold, small_land, small_send, small_recv, row_send, row_recv, send_sem, recv_sem = take(8)
    d, t = lax.axis_index("dp"), lax.axis_index("tensor")
    core, side = d % 2, t % 2
    keeper = core == t // 2
    other = jnp.logical_not(keeper)
    MESH = pl.DeviceIdType.MESH

    around = [(d ^ b, t) for b in bits] + [(d ^ 1, t), (d, t ^ 2), (d, t ^ 1)]
    greet(around + [(d ^ 1, t ^ 2)])

    def my(bit):
        return (d // bit) % 2

    def order(u):
        return bits if units[u][3] == 0 else bits[::-1]

    def source(u, step):
        array, first, rows, _, summed = units[u]
        if summed:
            return ins[array], first >> steps
        return (ins[array], first) if step == 0 else (hold[u][step - 1], 0)

    def copy(u, stage, src, dst, device):
        return pltpu.make_async_remote_copy(
            src_ref=src, dst_ref=dst, send_sem=send_sem.at[u, stage], recv_sem=recv_sem.at[u, stage],
            device_id=device, device_id_type=MESH,
        )

    def quarter(u):
        place = units[u][1]
        for step, bit in enumerate(order(u)):
            place = place + my(bit) * (units[u][2] >> (step + 1))
        return place

    def scatter_copy(u, step):
        ref, first = source(u, step)
        size = units[u][2] >> (step + 1)
        bit = order(u)[step]
        return copy(u, step, rows_of(ref, first + (1 - my(bit)) * size, size), land[u][step], (d ^ bit, t))

    def plane_copy(u):
        ref, first = source(u, steps)
        return copy(u, steps, rows_of(ref, first, units[u][2] >> steps), land[u][-1], (d, t ^ 2))

    def gather_copy(u, step):
        array, first, rows = units[u][:3]
        bit = order(u)[steps - 1 - step]
        size = rows >> (steps - step)
        start = quarter(u)
        for back in range(step):
            start = start - my(order(u)[steps - 1 - back]) * (rows >> (steps - back))
        block = rows_of(outs[array], start, size)
        return copy(u, steps + 1 + step, block, block, (d ^ bit, t))

    def core_copy(u):
        array, first, rows = units[u][:3]
        block = outs[array].at[pl.ds(first, rows)]
        return copy(u, 2 * steps + 1, block, block, (d ^ 1, t))

    def add(dst, dst_first, left, left_first, right, rows):
        chunk = min(rows, 32)

        def body(i, _):
            at = i * chunk
            a = left[pl.ds(pl.multiple_of(left_first + at, 16), chunk), :].astype(jnp.float32)
            b = right[pl.ds(pl.multiple_of(at, 16), chunk), :].astype(jnp.float32)
            dst[pl.ds(pl.multiple_of(dst_first + at, 16), chunk), :] = (a + b).astype(jnp.bfloat16)
            return 0

        lax.fori_loop(0, rows // chunk, body, 0)

    def begin(u, stage):
        if stage < steps:
            scatter_copy(u, stage).start()
        elif stage == steps:

            @pl.when(other)
            def _():
                plane_copy(u).start()
        else:

            @pl.when(keeper)
            def _():
                (gather_copy(u, stage - steps - 1) if stage <= 2 * steps else core_copy(u)).start()

    def end(u, stage):
        array, first, rows = units[u][:3]
        if stage < steps:
            one = scatter_copy(u, stage)
            one.wait_recv()
            ref, row = source(u, stage)
            size = rows >> (stage + 1)
            add(hold[u][stage], 0, ref, row + my(order(u)[stage]) * size, land[u][stage], size)
            one.wait_send()
        elif stage == steps and units[u][4] == 2:

            @pl.when(keeper)
            def _():
                size = rows >> steps
                ref, row = source(u, steps)
                outs[array][pl.ds(pl.multiple_of(quarter(u), 16), size), :] = ref[pl.ds(row, size), :]
        elif stage == steps:

            @pl.when(other)
            def _():
                plane_copy(u).wait_send()

            @pl.when(keeper)
            def _():
                plane_copy(u).wait_recv()
                ref, row = source(u, steps)
                add(outs[array], quarter(u), ref, row, land[u][-1], rows >> steps)
        elif stage <= 2 * steps:

            @pl.when(keeper)
            def _():
                gather_copy(u, stage - steps - 1).wait()
        else:

            @pl.when(keeper)
            def _():
                core_copy(u).wait_send()

            @pl.when(other)
            def _():
                core_copy(u).wait_recv()

    def row_copy(a, stage):
        size = spans[a]
        if stage == 0:
            src, dst, device = rows_of(parts[a], (1 - core) * 2 * size, 2 * size), row_land[a][0], (d ^ 1, t)
        elif stage == 1:
            src, dst, device = rows_of(row_hold[a][0], (1 - side) * size, size), row_land[a][1], (d, t ^ 1)
        else:
            src, dst, device = row_hold[a][1], row_outs[a], (d ^ 1, t ^ 2)
        return pltpu.make_async_remote_copy(
            src_ref=src, dst_ref=dst, send_sem=row_send.at[a, stage], recv_sem=row_recv.at[a, stage],
            device_id=device, device_id_type=MESH,
        )

    def row_half(a):
        row_copy(a, 0).wait()
        add(row_hold[a][0], 0, parts[a], core * 2 * spans[a], row_land[a][0], 2 * spans[a])

    def row_home(a):
        row_copy(a, 1).wait()
        size = spans[a]

        def body(i, _):
            at = pl.ds(pl.multiple_of(i * 32, 32), 32)
            total = row_hold[a][0][pl.ds(pl.multiple_of(side * size + i * 32, 32), 32), :].astype(jnp.float32)
            total = total + row_land[a][1][at, :].astype(jnp.float32)
            if a == token_rows:
                here = pl.ds(pl.multiple_of(side * size + i * 32, 32), 32)
                unit, inverse = moments(tokens[here, :].astype(jnp.float32))
                total = grad_in[here, :] + normalize_back(total, unit, inverse, gain[...])[0]
            row_hold[a][1][at, :] = total.astype(jnp.bfloat16)
            return 0

        lax.fori_loop(0, size // 32, body, 0)

        @pl.when(keeper)
        def _():
            row_outs[a][...] = row_hold[a][1][...]

        @pl.when(other)
        def _():
            row_copy(a, 2).start()

    def small_copy(step):
        return pltpu.make_async_remote_copy(
            src_ref=small_hold.at[step], dst_ref=small_land.at[step], send_sem=small_send.at[step],
            recv_sem=small_recv.at[step], device_id=around[step], device_id_type=MESH,
        )

    def small_step(step):
        small_copy(step).wait()
        total = small_hold[step] + small_land[step]
        if step + 1 < len(around):
            small_hold[step + 1] = total
            small_copy(step + 1).start()
        else:
            small_out[...] = total

    last = 2 * steps + 2
    first_stage = (0, steps, steps + 1)
    turns = [
        list(range(last + 1)),
        list(range(steps + 3)),
        list(range(steps + 2)),
    ]

    def tick(now):
        for state in (0, 1, 2):
            if now not in turns[state]:
                continue
            turn = turns[state].index(now)
            stage = first_stage[state] + turn
            for u in range(len(units)):
                if units[u][4] != state:
                    continue
                if state == 2 and turn == 0:
                    end(u, steps)
                if turn > 0:
                    end(u, stage - 1)
                if stage < last:
                    begin(u, stage)

    small_hold[0] = small_in[...]
    small_copy(0).start()
    for a in (token_rows, encoder_rows):
        row_copy(a, 0).start()
    tick(0)
    row_half(token_rows)
    row_copy(token_rows, 1).start()
    row_half(encoder_rows)
    small_step(0)
    row_home(token_rows)
    row_copy(encoder_rows, 1).start()
    for now in range(1, last + 1):
        tick(now)
        if now < len(around):
            small_step(now)
        if now == min(2, steps):
            row_home(encoder_rows)

    @pl.when(other)
    def _():
        for a in range(row_arrays):
            row_copy(a, 2).wait()


def sum_all(grads, units, parts, norm_grads, tokens, grad_in, gain, collective_id):
    dp = lax.axis_size("dp")
    steps = 0
    while 2 << steps < dp:
        steps += 1
    bf16, f32 = jnp.bfloat16, jnp.float32
    shapes = [(grad.shape[0], grad.shape[1]) for grad in grads]
    scratch = []
    for array, first, rows, side, done in units:
        width = grads[array].shape[1]
        if done:
            shapes[array] = (rows, width)
        else:
            scratch += [pltpu.VMEM((rows >> (k + 1), width), bf16) for k in range(steps)] * 2
        if done < 2:
            scratch.append(pltpu.VMEM((rows >> steps, width), bf16))
    stages = 2 * steps + 2
    vmem = pl.BlockSpec(memory_space=pltpu.VMEM)
    spans = [part.shape[0] // 4 for part in parts]
    wide = tokens.shape[1]
    semaphores = pltpu.SemaphoreType.DMA
    return pl.pallas_call(
        functools.partial(sum_kernel, dp, len(grads), units, spans),
        out_shape=[jax.ShapeDtypeStruct(shape, bf16) for shape in shapes]
        + [jax.ShapeDtypeStruct((span, wide), bf16) for span in spans]
        + [jax.ShapeDtypeStruct(norm_grads.shape, f32)],
        in_specs=[vmem] * (len(grads) + len(parts) + 4),
        out_specs=[vmem] * (len(grads) + len(parts) + 1),
        scratch_shapes=scratch
        + [pltpu.VMEM((many * span, wide), bf16) for span in spans for many in (2, 1)] * 2
        + [pltpu.VMEM((steps + 3,) + norm_grads.shape, f32)] * 2
        + [semaphores((steps + 3,))] * 2
        + [semaphores((len(parts), 3))] * 2
        + [semaphores((len(units), stages))] * 2,
        compiler_params=pltpu.CompilerParams(
            collective_id=collective_id, has_side_effects=True, vmem_limit_bytes=60 << 20
        ),
        cost_estimate=pl.CostEstimate(flops=80_000_000_000, bytes_accessed=16_000_000, transcendentals=0),
        name="sum_all",
    )(*grads, *parts, norm_grads, tokens, grad_in, gain[None])


class Move:
    def __init__(self, name, copy, sources, moved, d, t):
        self.name, self.copy, self.sources, self.moved = name, copy, sources, moved
        self.d, self.t, self.column = d, t, (d // 2) % 4
        self.keeper = d % 2 == t // 2
        self.other = jnp.logical_not(self.keeper)

    def block(self, ref):
        part = ref.shape[0] // 4
        return rows_of(ref, self.column * part, part)

    def fetch(self, a):
        return self.copy(
            (self.name, a), self.block(self.sources[a]), self.block(self.moved[a]), (self.d, self.t ^ 2)
        )

    def share(self, a, m):
        block = self.block(self.moved[a])
        return self.copy((self.name, a, m), block, block, (self.d ^ (2 * m), self.t))

    def start(self):
        @pl.when(self.keeper)
        def _():
            for a in range(len(self.moved)):
                self.fetch(a).start()

    def relay(self, which):
        @pl.when(self.other)
        def _():
            for a in which:
                self.fetch(a).wait_recv()
                for m in (1, 2, 3):
                    self.share(a, m).start()

    def ready(self, which):
        @pl.when(self.keeper)
        def _():
            for a in which:
                self.moved[a][...] = self.sources[a][...]

        @pl.when(self.other)
        def _():
            for a in which:
                for m in (1, 2, 3):
                    self.share(a, m).wait_recv()

    def finish(self):
        @pl.when(self.keeper)
        def _():
            for a in range(len(self.moved)):
                self.fetch(a).wait_send()

        @pl.when(self.other)
        def _():
            for a in range(len(self.moved)):
                for m in (1, 2, 3):
                    self.share(a, m).wait_send()


class HalfRows:
    def __init__(self, name, copy, rows, half, first, far_first, d, t):
        self.name, self.copy, self.rows, self.half, self.first = name, copy, rows, half, first
        self.far_first = far_first
        self.d, self.t, self.side = d, t, t % 2
        self.keeper = d % 2 == t // 2
        self.other = jnp.logical_not(self.keeper)
        self.count = rows.shape[0]
        self.piece = self.count // 4

    def place(self, s, p):
        return rows_of(self.half, self.first + s * self.count + p * self.piece, self.piece)

    def own(self, p):
        return self.rows.at[pl.ds(p * self.piece, self.piece)]

    def swap(self, p):
        at = rows_of(self.half, self.far_first + self.side * self.count + p * self.piece, self.piece)
        return self.copy((self.name, "swap", p), self.own(p), at, (self.d ^ 1, self.t ^ 2))

    def through(self, p, source):
        return self.copy((self.name, "pass", p), source, self.place(self.side, p), (self.d, self.t ^ 1))

    def start(self):
        @pl.when(self.other)
        def _():
            for p in range(4):
                self.swap(p).start()

        @pl.when(self.keeper)
        def _():
            for p in range(4):
                self.through(p, self.own(p)).start()
            at = pl.multiple_of(self.first + self.side * self.count, 16)
            self.half[pl.ds(at, self.count), :] = self.rows[...]

    def relay(self):
        @pl.when(self.other)
        def _():
            for p in range(4):
                self.swap(p).wait_recv()
                self.through(p, self.place(self.side, p)).start()

    def arrive(self):
        for p in range(4):
            block = self.place(1 - self.side, p)
            self.copy((self.name, "pass", p), block, block, (self.d, self.t ^ 1)).wait_recv()

    def finish(self):
        @pl.when(self.keeper)
        def _():
            for p in range(4):
                self.through(p, self.own(p)).wait_send()

        @pl.when(self.other)
        def _():
            for p in range(4):
                self.swap(p).wait_send()
                self.through(p, self.place(self.side, p)).wait_send()


class Whole:
    def __init__(self, name, copy, source, whole, d, t):
        self.name, self.copy, self.source, self.whole = name, copy, source, whole
        self.d, self.t = d, t
        self.away = jnp.where(d % 2 == t // 2, 0, 1)
        self.rows = source.shape[0]
        self.slim = self.rows // 8
        self.half_at = (d % 2) * (4 * self.slim)
        self.at = self.half_at + ((d // 2) % 4) * self.slim

    def block(self, j):
        return rows_of(self.whole, j * self.rows + self.at, self.slim)

    def far(self):
        return self.copy(
            (self.name, "far"), rows_of(self.source, self.at, self.slim), self.block(self.away), (self.d, self.t ^ 2)
        )

    def near(self, late):
        j = 1 - self.away if late else self.away
        return self.copy((self.name, "near", late), self.block(j), self.block(j + 2), (self.d, self.t ^ 1))

    def level(self, j, m):
        block = rows_of(self.whole, j * self.rows + self.at, self.slim)
        return self.copy((self.name, "level", j, m), block, block, (self.d ^ (2 * m), self.t))

    def hand(self, j):
        return self.copy(
            (self.name, "hand", j),
            rows_of(self.whole, j * self.rows + self.half_at, 4 * self.slim),
            rows_of(self.whole, (j ^ 1) * self.rows + self.half_at, 4 * self.slim),
            (self.d ^ 1, self.t),
        )

    def start(self):
        self.far().start()
        self.whole[pl.ds(pl.multiple_of(self.away * self.rows + self.at, 16), self.slim), :] = self.source[
            pl.ds(pl.multiple_of(self.at, 16), self.slim), :
        ]
        self.near(False).start()

    def pass_on(self):
        self.far().wait_recv()
        self.near(True).start()
        for m in (1, 2, 3):
            for j in (0, 1):
                self.level(j, m).start()

    def across(self):
        self.near(False).wait_recv()
        self.near(True).wait_recv()
        for m in (1, 2, 3):
            for j in (2, 3):
                self.level(j, m).start()

    def hand_over(self):
        for m in (1, 2, 3):
            for j in range(4):
                self.level(j, m).wait_recv()
        for j in range(4):
            self.hand(j).start()

    def finish(self):
        self.far().wait_send()
        self.near(False).wait_send()
        self.near(True).wait_send()
        for m in (1, 2, 3):
            for j in range(4):
                self.level(j, m).wait_send()
        for j in range(4):
            self.hand(j).wait()


def start_kernel(*refs):
    (tokens, gain, shift, *weights, out_weight, next_out, encoder, expand) = refs[:10]
    (rows_half, normed, query, keyed, valued, moved, whole, next_whole, encoder_out, expand_slice) = refs[10:20]
    send_sem, recv_sem = refs[20:]
    d, t = lax.axis_index("dp"), lax.axis_index("tensor")
    core, side = d % 2, t % 2
    keeper = core == t // 2
    other = jnp.logical_not(keeper)
    count = tokens.shape[0]
    copy = Copies(send_sem, recv_sem)
    move = Move("move", copy, weights, [moved.at[a] for a in range(3)], d, t)
    every = Whole("whole", copy, out_weight, whole, d, t)
    after = Whole("next", copy, next_out, next_whole, d, t)
    rows = HalfRows("tokens", copy, tokens, rows_half, 0, 0, d, t)

    greet(
        [(d ^ 2, t), (d ^ 4, t), (d ^ 6, t), (d ^ 1, t), (d, t ^ 1), (d, t ^ 2), (d ^ 1, t ^ 2)]
    )

    def give(name, s):
        block = rows_of(normed, core * (2 * count) + s * count, count)
        return copy(("give", name), block, block, (d ^ 1, t))

    encoder_copy = copy("encoder", encoder, encoder_out, (d ^ 1, t))
    slim = expand_slice.shape[0]
    hop = copy("hop", rows_of(expand, d * slim, slim), expand_slice, (d, t ^ 2))

    every.start()
    after.start()
    rows.start()
    move.start()
    every.pass_on()
    after.pass_on()

    @pl.when(keeper)
    def _():
        encoder_copy.start()

    every.across()
    after.across()
    rows.relay()
    mine = core * (2 * count)
    norm_rows(rows_half, side * count, normed, mine + side * count, count, gain, shift)
    give(0, side).start()
    move.relay(range(3))
    hop.start()
    rows.arrive()
    norm_rows(rows_half, (1 - side) * count, normed, mine + (1 - side) * count, count, gain, shift)
    give(1, 1 - side).start()
    every.hand_over()
    after.hand_over()

    @pl.when(keeper)
    def _():
        encoder_out[...] = encoder[...]

    def project(first):
        def body(i, _):
            at = pl.ds(pl.multiple_of(first + i * 256, 256), 256)
            for a, out in enumerate((query, keyed, valued)):
                out[at, :] = jnp.dot(
                    normed[at, :], moved[a], preferred_element_type=jnp.float32
                ).astype(jnp.bfloat16)
            return 0

        lax.fori_loop(0, (2 * count) // 256, body, 0)

    move.ready(range(3))
    project(mine)
    give(0, side).wait()
    give(1, 1 - side).wait()
    project((1 - core) * (2 * count))
    every.finish()
    after.finish()
    move.finish()
    rows.finish()
    hop.wait()

    @pl.when(keeper)
    def _():
        encoder_copy.wait_send()

    @pl.when(other)
    def _():
        encoder_copy.wait_recv()


def start_layer(tokens, gain, shift, weights, out_weight, next_out, encoder, expand, collective_id):
    rows, wide = tokens.shape
    dp = lax.axis_size("dp")
    width = weights[0].shape[1]
    bf16 = jnp.bfloat16
    shape = jax.ShapeDtypeStruct
    vmem = pl.BlockSpec(memory_space=pltpu.VMEM)
    return pl.pallas_call(
        start_kernel,
        out_shape=(
            shape((2 * rows, wide), bf16),
            shape((4 * rows, wide), bf16),
            shape((4 * rows, width), bf16),
            shape((4 * rows, width), bf16),
            shape((4 * rows, width), bf16),
            shape((3,) + weights[0].shape, bf16),
            shape((4 * out_weight.shape[0], out_weight.shape[1]), bf16),
            shape((4 * next_out.shape[0], next_out.shape[1]), bf16),
            shape(encoder.shape, bf16),
            shape((expand.shape[0] // dp, expand.shape[1]), bf16),
        ),
        in_specs=[vmem] * 9 + [pl.BlockSpec(memory_space=pl.ANY)],
        out_specs=(vmem,) * 9 + (pl.BlockSpec(memory_space=pl.ANY),),
        scratch_shapes=[
            pltpu.SemaphoreType.DMA((72,)),
            pltpu.SemaphoreType.DMA((72,)),
        ],
        compiler_params=pltpu.CompilerParams(
            collective_id=collective_id, has_side_effects=True, vmem_limit_bytes=56 << 20
        ),
        cost_estimate=pl.CostEstimate(flops=35_000_000_000, bytes_accessed=16_000_000, transcendentals=0),
        name="start_layer",
    )(tokens, gain[None], shift[None], *weights, out_weight, next_out, encoder, expand)


def add_dot(left, right, over_rows=False):
    return lax.dot_general(
        left, right, (((1,), (1 if over_rows else 0,)), ((), ())), preferred_element_type=jnp.float32
    )


class Exchange:
    def __init__(self, copy, mine, land, core, d, t, chunk):
        self.copy, self.mine, self.land, self.core, self.chunk = copy, mine, land, core, chunk
        self.half = mine.shape[0] // 2
        self.to = [(d ^ 1, t), (d, t ^ 1), (d ^ 1, t ^ 1)]

    def one(self, j, ch):
        core = self.core if j == 1 else 1 - self.core
        return self.copy(
            ("exchange", j, ch),
            rows_of(self.mine, core * self.half + ch * self.chunk, self.chunk),
            self.land.at[j, pl.ds(ch * self.chunk, self.chunk)],
            self.to[j],
        )

    def start(self, ch):
        for j in (1, 2, 0):
            self.one(j, ch).start()

    def arrive(self, ch):
        for j in range(3):
            self.one(j, ch).wait_recv()

    def pieces(self, ch):
        first = self.core * self.half + ch * self.chunk
        own = self.mine[pl.ds(pl.multiple_of(first, 16), self.chunk), :]
        return [own] + [self.land[j, pl.ds(ch * self.chunk, self.chunk), :] for j in range(3)]

    def sent(self, ch):
        for j in range(3):
            self.one(j, ch).wait_send()


def by_rows(rows, step, body):
    def turn(i, _):
        body(pl.multiple_of(i * step, step))
        return 0

    lax.fori_loop(0, rows // step, turn, 0)


def forward_kernel(*refs):
    (mixed, out_all, start, gain, shift, *weights) = refs[:8]
    (after, normed, result, moved) = refs[8:12]
    (land, product, send_sem, recv_sem) = refs[12:]
    d, t = lax.axis_index("dp"), lax.axis_index("tensor")
    core = d % 2
    chunk = product.shape[0]
    half = after.shape[0]
    width = mixed.shape[1]
    copy = Copies(send_sem, recv_sem)
    greet(
        [(d ^ 1, t), (d, t ^ 1), (d ^ 1, t ^ 1), (d ^ 2, t), (d ^ 4, t), (d ^ 6, t), (d, t ^ 2)]
    )
    exchange = Exchange(copy, mixed, land, core, d, t, chunk)
    move = Move("move", copy, weights, [moved.at[a] for a in range(3)], d, t)

    def give(ch):
        block = rows_of(normed, core * half + ch * chunk, chunk)
        return copy(("give", ch), block, block, (d ^ 1, t))

    chunks = half // chunk
    for ch in range(chunks):
        exchange.start(ch)
    move.start()
    for ch in range(chunks):
        exchange.arrive(ch)
        product[...] = sum(
            add_dot(piece, out_all[j * width : (j + 1) * width, :])
            for j, piece in enumerate(exchange.pieces(ch))
        )

        def rows(at, ch=ch):
            x = start[pl.ds(pl.multiple_of(ch * chunk + at, 16), 32), :].astype(jnp.float32)
            x = x + product[pl.ds(at, 32), :]
            after[pl.ds(pl.multiple_of(ch * chunk + at, 16), 32), :] = x
            unit, inverse = moments(x)
            normed[pl.ds(pl.multiple_of(core * half + ch * chunk + at, 16), 32), :] = (
                unit * gain[...] + shift[...]
            ).astype(jnp.bfloat16)

        by_rows(chunk, 32, rows)
        give(ch).start()
        if ch < 3:
            move.relay([ch])

    def project(first, rows):
        at = pl.ds(pl.multiple_of(first, 16), rows)
        result[at, :] = add_dot(normed[at, :], moved[0]).astype(jnp.bfloat16)

    move.ready([0])
    project(core * half, half)
    for ch in range(chunks):
        give(ch).wait()
    project((1 - core) * half, half)
    move.ready([1, 2])
    for ch in range(chunks):
        exchange.sent(ch)
    move.finish()


def forward_step(mixed, out_all, start, gain, shift, weights, collective_id):
    rows, width = mixed.shape
    half, wide = start.shape
    chunk = half // 4
    shape = jax.ShapeDtypeStruct
    vmem = pl.BlockSpec(memory_space=pltpu.VMEM)
    return pl.pallas_call(
        forward_kernel,
        out_shape=(
            shape((half, wide), jnp.float32),
            shape((rows, wide), jnp.bfloat16),
            shape((rows, width), jnp.bfloat16),
            shape((3,) + weights[0].shape, jnp.bfloat16),
        ),
        in_specs=[vmem] * 8,
        out_specs=(vmem,) * 4,
        scratch_shapes=[
            pltpu.VMEM((3, half, width), jnp.bfloat16),
            pltpu.VMEM((chunk, wide), jnp.float32),
            pltpu.SemaphoreType.DMA((56,)),
            pltpu.SemaphoreType.DMA((56,)),
        ],
        compiler_params=pltpu.CompilerParams(
            collective_id=collective_id, has_side_effects=True, vmem_limit_bytes=56 << 20
        ),
        cost_estimate=pl.CostEstimate(flops=20_000_000_000, bytes_accessed=8_000_000, transcendentals=0),
        name="forward_step",
    )(mixed, out_all, start, gain[None], shift[None], *weights)


def backward_kernel(*refs):
    wide = refs[2].shape[1]
    (grad_query, query_all, after, gain, grad_in, weight, out_near, out_far) = refs[:8]
    (grad_res, grad_top, result, norm_grads, output) = refs[8:13]
    (land, product, out_rows, send_sem, recv_sem) = refs[13:]
    d, t = lax.axis_index("dp"), lax.axis_index("tensor")
    core = d % 2
    chunk = product.shape[0]
    half = after.shape[0]
    copy = Copies(send_sem, recv_sem)
    greet([(d ^ 1, t), (d, t ^ 1), (d ^ 1, t ^ 1), (d ^ 1, t ^ 2)])
    exchange = Exchange(copy, grad_query, land, core, d, t, chunk)

    def give(ch):
        block = rows_of(grad_top, core * half + ch * chunk, chunk)
        return copy(("give", ch), block, block, (d ^ 1, t))

    chunks = half // chunk
    for ch in range(chunks):
        exchange.start(ch)
    keeper = core == t // 2
    home = copy("home", out_rows, output, (d ^ 1, t ^ 2))
    out_rows[...] = (out_near[...] + out_far[...].astype(jnp.float32)).astype(jnp.bfloat16)

    @pl.when(keeper)
    def _():
        output[...] = out_rows[...]

    norm_grads[...] = jnp.zeros_like(norm_grads)
    for ch in range(chunks):
        exchange.arrive(ch)
        product[...] = sum(add_dot(piece, query_all[j * wide : (j + 1) * wide, :], True) for j, piece in enumerate(exchange.pieces(ch)))

        def rows(at, ch=ch):
            here = pl.ds(pl.multiple_of(ch * chunk + at, 16), 32)
            unit, inverse = moments(after[here, :])
            back, gain_grad, shift_grad = normalize_back(product[pl.ds(at, 32), :], unit, inverse, gain[...])
            total = grad_in[here, :] + back
            grad_res[here, :] = total
            grad_top[pl.ds(pl.multiple_of(core * half + ch * chunk + at, 16), 32), :] = total.astype(jnp.bfloat16)
            norm_grads[0:1, :] += gain_grad[None]
            norm_grads[1:2, :] += shift_grad[None]

        by_rows(chunk, 32, rows)
        give(ch).start()
        if ch == chunks - 2:

            @pl.when(jnp.logical_not(keeper))
            def _():
                home.start()


    def project(first, rows):
        at = pl.ds(pl.multiple_of(first, 16), rows)
        result[at, :] = add_dot(grad_top[at, :], weight[...], True).astype(jnp.bfloat16)

    project(core * half, half)
    for ch in range(chunks):
        give(ch).wait()
    project((1 - core) * half, half)
    for ch in range(chunks):
        exchange.sent(ch)

    @pl.when(jnp.logical_not(keeper))
    def _():
        home.wait()


def backward_step(grad_query, query_all, after, gain, grad_in, weight, out_near, out_far, collective_id):
    rows, width = grad_query.shape
    half, wide = after.shape
    chunk = half // 4
    shape = jax.ShapeDtypeStruct
    vmem = pl.BlockSpec(memory_space=pltpu.VMEM)
    return pl.pallas_call(
        backward_kernel,
        out_shape=(
            shape((half, wide), jnp.float32),
            shape((rows, wide), jnp.bfloat16),
            shape((rows, weight.shape[0]), jnp.bfloat16),
            shape((8, wide), jnp.float32),
            shape(out_far.shape, jnp.bfloat16),
        ),
        in_specs=[vmem] * 8,
        out_specs=(vmem,) * 5,
        scratch_shapes=[
            pltpu.VMEM((3, half, width), jnp.bfloat16),
            pltpu.VMEM((chunk, wide), jnp.float32),
            pltpu.VMEM(out_far.shape, jnp.bfloat16),
            pltpu.SemaphoreType.DMA((20,)),
            pltpu.SemaphoreType.DMA((20,)),
        ],
        compiler_params=pltpu.CompilerParams(
            collective_id=collective_id, has_side_effects=True, vmem_limit_bytes=56 << 20
        ),
        cost_estimate=pl.CostEstimate(flops=20_000_000_000, bytes_accessed=8_000_000, transcendentals=0),
        name="backward_step",
    )(grad_query, query_all, after, gain[None], grad_in, weight, out_near, out_far)


def hidden_kernel(*refs):
    (mixed, out_all, start, gain, shift, cot, cot_pair, next_query, *ff_weights) = refs[:12]
    (after, normed, hidden, grad_pre, grad_res, grad_top, result, norm_grads, query_all, grad_out, out_near, out_give) = refs[12:24]
    (land, product, own, far_send, far_land, sum_send, sum_land, expand, reduce) = refs[24:33]
    (out_own, out_send, out_land, send_sem, recv_sem, local_sem) = refs[33:]
    d, t = lax.axis_index("dp"), lax.axis_index("tensor")
    core = d % 2
    chunk = product.shape[0]
    half = after.shape[0]
    width = mixed.shape[1]
    chunks = half // chunk
    copy = Copies(send_sem, recv_sem)
    greet(
        [(d ^ 1, t), (d, t ^ 1), (d ^ 1, t ^ 1), (d ^ 2, t), (d ^ 4, t), (d ^ 6, t), (d, t ^ 2)]
    )
    exchange = Exchange(copy, mixed, land, core, d, t, chunk)
    every = Whole("query", copy, next_query, query_all, d, t)

    def give(name, ref, ch):
        block = rows_of(ref, core * half + ch * chunk, chunk)
        return copy((name, ch), block, block, (d ^ 1, t))

    def slab(ref, ch):
        return ref.at[pl.ds(ch * chunk, chunk)]

    def far(ch):
        return copy(("far", ch), slab(far_send, ch), slab(far_land, ch), (d ^ 1, t))

    def whole(ch):
        return copy(("whole", ch), slab(sum_send, ch), slab(sum_land, ch), (d, t ^ 1))

    def out_copy(ch):
        return copy(("out", ch), slab(out_send, ch), slab(out_land, ch), (d ^ 1, t))

    def residual(ch):
        exchange.arrive(ch)
        product[...] = sum(
            add_dot(piece, out_all[j * width : (j + 1) * width, :])
            for j, piece in enumerate(exchange.pieces(ch))
        )

        def rows(at):
            here = pl.ds(pl.multiple_of(ch * chunk + at, 16), 32)
            x = start[here, :] + product[pl.ds(at, 32), :]
            after[here, :] = x
            unit, inverse = moments(x)
            normed[pl.ds(pl.multiple_of(core * half + ch * chunk + at, 16), 32), :] = (
                unit * gain[...] + shift[...]
            ).astype(jnp.bfloat16)

        by_rows(chunk, 32, rows)
        give("normed", normed, ch).start()

    def feed(first):
        every = pl.ds(pl.multiple_of(first, 16), chunk)
        product[...] = add_dot(normed[every, :], expand[...])
        own[...] = add_dot(grad_out[every, :], reduce[...], True)

        def rows(at):
            here = pl.ds(pl.multiple_of(first + at, 16), 32)
            z = product[pl.ds(at, 32), :]
            inner = jnp.tanh(tanh_coeff * (z + cubic_coeff * z * z * z))
            hidden[here, :] = (0.5 * z * (1.0 + inner)).astype(jnp.bfloat16)
            slope = 0.5 * (1.0 + inner) + 0.5 * z * (1.0 - inner * inner) * tanh_coeff * (
                1.0 + 3.0 * cubic_coeff * z * z
            )
            upper = own[pl.ds(at, 32), :].astype(jnp.bfloat16).astype(jnp.float32)
            grad_pre[here, :] = (upper * slope).astype(jnp.bfloat16)

        by_rows(chunk, 32, rows)
        return add_dot(grad_pre[pl.ds(pl.multiple_of(first, 16), chunk), :], expand[...], True)

    def both(ch):
        copy(
            ("normed", ch), *([rows_of(normed, (1 - core) * half + ch * chunk, chunk)] * 2), (d ^ 1, t)
        ).wait_recv()
        far_send[pl.ds(ch * chunk, chunk), :] = feed((1 - core) * half + ch * chunk).astype(jnp.bfloat16)
        far(ch).start()
        own[...] = feed(core * half + ch * chunk)
        far(ch).wait_recv()

        def rows(at):
            here = pl.ds(pl.multiple_of(ch * chunk + at, 16), 32)
            sum_send[here, :] = (own[pl.ds(at, 32), :] + far_land[here, :].astype(jnp.float32)).astype(jnp.bfloat16)

        by_rows(chunk, 32, rows)
        whole(ch).start()
        at = pl.ds(ch * chunk, chunk)
        for core_at, out in ((1 - core, out_send), (core, out_own)):
            every_row = pl.ds(pl.multiple_of(core_at * half + ch * chunk, 16), chunk)
            out[at, :] = add_dot(hidden[every_row, :], reduce[...]).astype(jnp.bfloat16)
            if out is out_send:
                out_copy(ch).start()

    def back(ch):
        whole(ch).wait_recv()

        def rows(at):
            here = pl.ds(pl.multiple_of(ch * chunk + at, 16), 32)
            grad = sum_send[here, :].astype(jnp.float32) + sum_land[here, :].astype(jnp.float32)
            unit, inverse = moments(after[here, :])
            down, gain_grad, shift_grad = normalize_back(grad, unit, inverse, gain[...])
            top = grad_out[pl.ds(pl.multiple_of(core * half + ch * chunk + at, 16), 32), :]
            total = top.astype(jnp.float32) + down
            grad_res[here, :] = total
            grad_top[pl.ds(pl.multiple_of(core * half + ch * chunk + at, 16), 32), :] = total.astype(jnp.bfloat16)
            norm_grads[0:1, :] += gain_grad[None]
            norm_grads[1:2, :] += shift_grad[None]

        by_rows(chunk, 32, rows)
        give("top", grad_top, ch).start()

    def project(first, rows):
        at = pl.ds(pl.multiple_of(first, 16), rows)
        result[at, :] = add_dot(grad_top[at, :], out_all[:width, :], True).astype(jnp.bfloat16)

    for ch in range(chunks):
        exchange.start(ch)
    keeper = core == t // 2

    def fetch(which, act):
        for a, weight in enumerate((expand, reduce)):
            act(pltpu.make_async_copy(ff_weights[2 * which + a], weight, local_sem.at[a]))

    def both_ways(act):
        @pl.when(keeper)
        def _():
            fetch(0, act)

        @pl.when(jnp.logical_not(keeper))
        def _():
            fetch(1, act)

    both_ways(lambda one: one.start())
    count = cot.shape[0]
    side = t % 2
    grad_out[pl.ds(pl.multiple_of(core * half + side * count, 16), count), :] = cot[...]
    grad_out[pl.ds(pl.multiple_of(core * half + (1 - side) * count, 16), count), :] = cot_pair[...]
    block = rows_of(grad_out, core * half, half)
    spread = copy("cot", block, block, (d ^ 1, t))
    spread.start()
    every.start()
    norm_grads[...] = jnp.zeros_like(norm_grads)
    residual(0)
    residual(1)
    both_ways(lambda one: one.wait())
    every.pass_on()
    spread.wait()
    both(0)
    residual(2)
    both(1)
    residual(3)
    both(2)
    every.across()
    back(0)
    both(3)
    back(1)
    back(2)
    every.hand_over()
    back(3)
    project(core * half, half)
    for ch in range(chunks):
        copy(
            ("top", ch), *([rows_of(grad_top, (1 - core) * half + ch * chunk, chunk)] * 2), (d ^ 1, t)
        ).wait_recv()
    project((1 - core) * half, half)
    for ch in range(chunks):
        exchange.sent(ch)
        give("normed", normed, ch).wait_send()
        give("top", grad_top, ch).wait_send()
        far(ch).wait_send()
        whole(ch).wait_send()
    every.finish()
    for ch in range(chunks):
        out_copy(ch).wait()

    def out_rows(at):
        near = pl.ds(pl.multiple_of(side * count + at, 32), 32)
        give_at = pl.ds(pl.multiple_of((1 - side) * count + at, 32), 32)
        here = pl.ds(at, 32)
        out_near[here, :] = (
            after[near, :] + out_own[near, :].astype(jnp.float32) + out_land[near, :].astype(jnp.float32)
        )
        out_give[here, :] = (
            out_own[give_at, :].astype(jnp.float32) + out_land[give_at, :].astype(jnp.float32)
        ).astype(jnp.bfloat16)

    by_rows(count, 32, out_rows)


def hidden_step(mixed, out_all, start, gain, shift, cot, cot_pair, next_query, ff_weights, collective_id):
    rows, width = mixed.shape
    half, wide = start.shape
    inner = ff_weights[0].shape[1]
    chunk = half // 4
    bf16, f32 = jnp.bfloat16, jnp.float32
    shape = jax.ShapeDtypeStruct
    vmem = pl.BlockSpec(memory_space=pltpu.VMEM)
    return pl.pallas_call(
        hidden_kernel,
        out_shape=(
            shape((half, wide), f32),
            shape((rows, wide), bf16),
            shape((rows, inner), bf16),
            shape((rows, inner), bf16),
            shape((half, wide), f32),
            shape((rows, wide), bf16),
            shape((rows, width), bf16),
            shape((8, wide), f32),
            shape((4 * next_query.shape[0], next_query.shape[1]), bf16),
            shape((rows, wide), bf16),
            shape(cot.shape, f32),
            shape(cot.shape, bf16),
        ),
        in_specs=[vmem] * 8 + [pl.BlockSpec(memory_space=pl.ANY)] * 4,
        out_specs=(vmem,) * 12,
        scratch_shapes=[
            pltpu.VMEM((3, half, width), bf16),
            pltpu.VMEM((chunk, max(wide, inner)), f32),
            pltpu.VMEM((chunk, max(wide, inner)), f32),
            pltpu.VMEM((half, wide), bf16),
            pltpu.VMEM((half, wide), bf16),
            pltpu.VMEM((half, wide), bf16),
            pltpu.VMEM((half, wide), bf16),
            pltpu.VMEM(ff_weights[0].shape, bf16),
            pltpu.VMEM(ff_weights[1].shape, bf16),
            pltpu.VMEM((half, wide), bf16),
            pltpu.VMEM((half, wide), bf16),
            pltpu.VMEM((half, wide), bf16),
            pltpu.SemaphoreType.DMA((56,)),
            pltpu.SemaphoreType.DMA((56,)),
            pltpu.SemaphoreType.DMA((2,)),
        ],
        compiler_params=pltpu.CompilerParams(
            collective_id=collective_id, has_side_effects=True, vmem_limit_bytes=60 << 20
        ),
        cost_estimate=pl.CostEstimate(flops=50_000_000_000, bytes_accessed=16_000_000, transcendentals=0),
        name="hidden_step",
    )(mixed, out_all, start, gain[None], shift[None], cot, cot_pair, next_query, *ff_weights)


def on_device(
    tokens,
    encoder_states,
    tok_lengths,
    enc_lengths,
    pad_mask,
    first_gain,
    first_shift,
    causal_query,
    causal_key,
    causal_value,
    causal_out,
    second_gain,
    second_shift,
    cross_query,
    cross_key,
    cross_value,
    cross_out,
    third_gain,
    third_shift,
    expand_weight,
    reduce_weight,
    cotangent,
):
    place = Place()
    width = causal_query.shape[1]
    length = pad_mask.shape[0]
    frames = encoder_states.shape[0]

    def of_group(value):
        return jnp.where(place.keeper, value, place.swap(value, 1, 0))

    def half_rows(quarter):
        return place.ordered(quarter, place.swap(quarter, 0, 1), place.side)

    def quarter_of(half):
        return place.part(half, place.side, 2)

    tok_lengths, enc_lengths, pad_mask = of_group(tok_lengths), of_group(enc_lengths), of_group(pad_mask)
    block_q, block_k = 256, 512
    token_seg, frame_seg, key_seg, self_lo, self_hi, cross_lo, cross_hi = ranges(
        tok_lengths[0], enc_lengths[0], pad_mask, length, frames, block_q, block_k
    )
    self_keys = jnp.stack([token_seg, key_seg] + [token_seg] * 6)
    cross_keys = jnp.stack([frame_seg] * 8)
    seg_col, seg_row = token_seg[:, None], token_seg[None, :]

    tokens_half, first_all, query, keyed, valued, moved, causal_out_perm, cross_out_perm, encoder, expand_piece = start_layer(
        tokens,
        first_gain,
        first_shift,
        (causal_query, causal_key, causal_value),
        causal_out,
        cross_out,
        encoder_states,
        expand_weight,
        1,
    )
    causal_out_here = causal_out_perm[:width]
    hidden_width = expand_weight.shape[1]
    expand_moved = lax.all_gather(expand_piece, "dp", axis=0, tiled=True)
    reduce_piece = place.part(reduce_weight, place.d, place.dp)
    reduce_piece, query = lax.optimization_barrier((reduce_piece, query))
    reduce_piece = place.swap(reduce_piece, 0, 2)

    mixed, self_logsum = attend_fwd(
        query, keyed, valued, seg_col, self_keys, self_lo, self_hi, True, block_q, block_k
    )
    mixed, reduce_piece, cot_here = lax.optimization_barrier((mixed, reduce_piece, cotangent))
    reduce_moved = lax.all_gather(reduce_piece, "dp", axis=0, tiled=True)
    cot_here = place.home(cot_here)
    after_self, second_all, cquery, cross_moved = forward_step(
        mixed,
        causal_out_perm,
        tokens_half,
        second_gain,
        second_shift,
        (cross_query, cross_key, cross_value),
        2,
    )
    cquery, cot_here = lax.optimization_barrier((cquery, cot_here))
    cot_pair = place.swap(cot_here, 0, 1)
    ckeyed = times(encoder, cross_moved[1]).astype(jnp.bfloat16)
    cvalued = times(encoder, cross_moved[2]).astype(jnp.bfloat16)
    cross_weight = jnp.concatenate([cross_moved[1], cross_moved[2]], axis=1)
    first_weight = jnp.concatenate([moved[0], moved[1], moved[2]], axis=1)
    cmixed, cross_logsum = attend_fwd(
        cquery, ckeyed, cvalued, seg_col, cross_keys, cross_lo, cross_hi, False, block_q, block_k
    )
    after_cross, third_all, hidden, grad_expand_in, grad_res, grad_top2, grad_cmixed, third_grads, cross_query_every, grad_top, out_near, out_give = hidden_step(
        cmixed, cross_out_perm, after_self, third_gain, third_shift, cot_here, cot_pair, cross_query,
        (expand_weight, reduce_weight, expand_moved, reduce_moved), 3
    )
    third_gain_grad, third_shift_grad = third_grads[0], third_grads[1]
    out_far = place.swap(out_give, 0, 1)
    reduce_grad = along_rows(hidden, grad_top)
    expand_grad = along_rows(third_all, grad_expand_in)

    cross_out_grad = along_rows(cmixed, grad_top2)
    expand_grad, reduce_grad = place.sum_columns(expand_grad, 0), place.sum_columns(reduce_grad, 1)
    grad_cquery, grad_cross_in = attend_bwd(
        cquery, ckeyed, cvalued, cmixed, grad_cmixed, cross_logsum, seg_row, cross_keys.T,
        cross_lo, cross_hi, False, block_q, block_k,
    )
    bf16 = jnp.bfloat16
    cross_grad = along_rows(encoder, grad_cross_in).astype(bf16)
    cross_grads = jnp.concatenate(
        [cross_grad[:, :width], cross_grad[:, width:], along_rows(second_all, grad_cquery).astype(bf16)]
    )
    cross_grads = place.sum_columns(cross_grads, 1)
    encoder_term = against(grad_cross_in, cross_weight).astype(bf16)
    grad_res, grad_top, grad_mixed, second_grads, output = backward_step(
        grad_cquery, cross_query_every, after_self, second_gain, grad_res, causal_out_here, out_near, out_far, 4
    )
    second_gain_grad, second_shift_grad = second_grads[0], second_grads[1]
    causal_out_grad = along_rows(mixed, grad_top)
    grad_mixed, expand_grad, reduce_grad = lax.optimization_barrier((grad_mixed, expand_grad, reduce_grad))
    expand_grad, reduce_grad = place.cross_planes([expand_grad, reduce_grad])
    (grad_in,) = attend_bwd(
        query, keyed, valued, mixed, grad_mixed, self_logsum, seg_row, self_keys.T,
        self_lo, self_hi, True, block_q, block_k,
    )
    causal_grad = along_rows(first_all, grad_in).astype(bf16)
    first_term = against(grad_in, first_weight)
    first_rows = (first_all.astype(jnp.float32) - first_shift) / first_gain
    first_gain_grad = jnp.sum(first_term * first_rows, axis=0)
    first_shift_grad = jnp.sum(first_term, axis=0)
    deep = causal_query.shape[0]
    once = (place.side == 0).astype(jnp.float32)
    none = jnp.zeros_like(first_gain_grad)
    norm_grads = jnp.stack(
        [
            first_gain_grad,
            first_shift_grad,
            second_gain_grad * once,
            second_shift_grad * once,
            third_gain_grad * once,
            third_shift_grad * once,
            none,
            none,
        ]
    )
    *sums, encoder_grad, tokens_grad, norm_grads = sum_all(
        [
            expand_grad,
            reduce_grad,
            cross_grads,
            jnp.concatenate([cross_out_grad.astype(bf16), causal_out_grad.astype(bf16)]),
            causal_grad,
        ],
        [
            (4, 0, deep // 2, 0, 0),
            (4, deep // 2, deep // 2, 1, 0),
            *(
                [(3, 0, width, 0, 0), (3, width, width, 1, 0)]
                if width % (8 * place.dp) == 0
                else [(3, 0, 2 * width, 0, 0)]
            ),
            (2, 0, 3 * deep, 1, 1),
            (0, 0, expand_weight.shape[0], 0, 2),
            (1, 0, reduce_weight.shape[0], 1, 2),
        ],
        [encoder_term, first_term.astype(bf16)],
        norm_grads,
        tokens_half,
        grad_res,
        first_gain,
        0,
    )
    (
        first_gain_grad,
        first_shift_grad,
        second_gain_grad,
        second_shift_grad,
        third_gain_grad,
        third_shift_grad,
    ) = (norm_grads[i] for i in range(6))
    sums = [total.astype(jnp.float32) if at != 2 and at != 3 else total for at, total in enumerate(sums)]
    expand_grad, reduce_grad = sums[:2]
    cross_key_grad, cross_value_grad, cross_query_grad = (
        sums[2][i * deep : (i + 1) * deep].astype(jnp.float32) for i in range(3)
    )
    cross_out_grad, causal_out_grad = sums[3][:width].astype(jnp.float32), sums[3][width:].astype(jnp.float32)
    causal_query_grad, causal_key_grad, causal_value_grad = (
        sums[4][:, i * width : (i + 1) * width] for i in range(3)
    )
    return (
        output,
        tokens_grad,
        encoder_grad,
        first_gain_grad,
        first_shift_grad,
        causal_query_grad,
        causal_key_grad,
        causal_value_grad,
        causal_out_grad,
        second_gain_grad,
        second_shift_grad,
        cross_query_grad,
        cross_key_grad,
        cross_value_grad,
        cross_out_grad,
        third_gain_grad,
        third_shift_grad,
        expand_grad,
        reduce_grad,
    )


def solution(mesh):
    in_specs = (
        P(("dp", "tensor"), None),
        P("dp", None),
        P("dp", None),
        P("dp", None),
        P("dp"),
        P(),
        P(),
        P(None, "tensor"),
        P(None, "tensor"),
        P(None, "tensor"),
        P("tensor", None),
        P(),
        P(),
        P(None, "tensor"),
        P(None, "tensor"),
        P(None, "tensor"),
        P("tensor", None),
        P(),
        P(),
        P(None, "tensor"),
        P("tensor", None),
        P(("dp", "tensor"), None),
    )
    out_specs = (
        P(("dp", "tensor"), None),
        P(("dp", "tensor"), None),
        P(("dp", "tensor"), None),
        P(),
        P(),
        P(None, "tensor"),
        P(None, "tensor"),
        P(None, "tensor"),
        P("tensor", None),
        P(),
        P(),
        P(None, "tensor"),
        P(None, "tensor"),
        P(None, "tensor"),
        P("tensor", None),
        P(),
        P(),
        P(None, "tensor"),
        P("tensor", None),
    )
    return jax.shard_map(
        on_device, mesh=mesh, in_specs=in_specs, out_specs=out_specs, check_vma=False
    )
```

```python
import functools

import jax
import jax.numpy as jnp
from jax import lax
from jax.experimental import pallas as pl
from jax.experimental.pallas import tpu as pltpu
from jax.sharding import PartitionSpec as P

HEAD_DIM = 64


eps = 1e-05
tanh_coeff = 0.7978845608
cubic_coeff = 0.044715


def smooth_gate(values):
    inner = jnp.tanh(tanh_coeff * (values + cubic_coeff * values * values * values))
    return 0.5 * values * (1.0 + inner)


def smooth_slope(values):
    inner = jnp.tanh(tanh_coeff * (values + cubic_coeff * values * values * values))
    return 0.5 * (1.0 + inner) + 0.5 * values * (1.0 - inner * inner) * tanh_coeff * (
        1.0 + 3.0 * cubic_coeff * values * values
    )


BF=jnp.bfloat16
F32=jnp.float32

def head_mask(rows, width, h):
    lane = lax.broadcasted_iota(jnp.int32, (rows, width), 1)
    return (lane // HEAD_DIM) == h

def dot(a,b,ca,cb):
    return lax.dot_general(a,b,(((ca,),(cb,)),((),())),preferred_element_type=F32)

def fwd_kernel(causal, heads, bq, bk, lo_ref, hi_ref, q_ref, k_ref, v_ref, rs_ref, ks_ref, o_ref, lse_ref, acc):
    count, width = q_ref.shape
    def one(qb, _):
        q0 = pl.multiple_of(qb*bq, bq)
        qv = q_ref[pl.ds(q0,bq),:] * BF(HEAD_DIM**-0.5)
        rseg = rs_ref[pl.ds(q0,bq),0:1]
        qm = [jnp.where(head_mask(bq,width,h), qv, BF(0)) for h in range(heads)]
        acc[...] = jnp.zeros_like(acc)
        lane = lax.broadcasted_iota(jnp.int32,(bq,128),1)
        def inner(kb, carry):
            k0 = pl.multiple_of(kb*bk, bk)
            kv = k_ref[pl.ds(k0,bk),:]
            vv = v_ref[pl.ds(k0,bk),:]
            kseg = ks_ref[0:1,pl.ds(k0,bk)]
            if causal:
                kpad = ks_ref[1:2,pl.ds(k0,bk)]
                ri = lax.broadcasted_iota(jnp.int32,(bq,bk),0)+q0
                ci = lax.broadcasted_iota(jnp.int32,(bq,bk),1)+k0
                ok = ((rseg==kpad)&(ci<=ri))|(ci==ri)
            else:
                ok = rseg==kseg
            ms, ls = carry
            new_m, new_l = [], []
            parts=None
            alphas=[]
            for h in range(heads):
                s = dot(qm[h],kv,1,1)
                s = jnp.where(ok,s,-1e30)
                m = jnp.maximum(ms[h], jnp.max(s,axis=1,keepdims=True))
                p = jnp.exp(s-m)
                al = jnp.exp(ms[h]-m)
                new_m.append(m); new_l.append(ls[h]*al+jnp.sum(p,axis=1,keepdims=True))
                vm = jnp.where(head_mask(bk,width,h),vv,BF(0))
                t = dot(p.astype(BF),vm,1,0)
                parts = t if parts is None else parts+t
                alphas.append(al)
            lane2 = lax.broadcasted_iota(jnp.int32,(bq,width),1)//HEAD_DIM
            sc = alphas[heads-1]
            for h in range(heads-1):
                sc = jnp.where(lane2==h, alphas[h], sc)
            acc[...] = acc[...]*sc + parts
            return (tuple(new_m),tuple(new_l))
        init = (tuple(jnp.full((bq,1),-1e30,F32) for _ in range(heads)), tuple(jnp.zeros((bq,1),F32) for _ in range(heads)))
        ms, ls = lax.fori_loop(lo_ref[qb], hi_ref[qb], inner, init)
        lane2 = lax.broadcasted_iota(jnp.int32,(bq,width),1)//HEAD_DIM
        inv = [1.0/l for l in ls]
        sc = inv[heads-1]
        for h in range(heads-1):
            sc = jnp.where(lane2==h, inv[h], sc)
        o_ref[pl.ds(q0,bq),:] = (acc[...]*sc).astype(BF)
        st = jnp.zeros((bq,128),F32)
        for h in range(heads):
            st = jnp.where(lane==h, ms[h]+jnp.log(ls[h]), st)
        stt = jnp.transpose(st)
        lse_ref[:,pl.ds(q0,bq)] = stt[0:8,:]
        return 0
    lax.fori_loop(0,count//bq,one,0)

def attend_fwd(q,k,v,rseg,kseg,lo,hi,causal,bq=256,bk=256):
    count,width=q.shape
    heads=width//HEAD_DIM
    vm=pl.BlockSpec(memory_space=pltpu.VMEM); sm=pl.BlockSpec(memory_space=pltpu.SMEM)
    return pl.pallas_call(functools.partial(fwd_kernel,causal,heads,bq,bk),
        out_shape=(jax.ShapeDtypeStruct((count,width),BF),jax.ShapeDtypeStruct((8,count),F32)),
        in_specs=[sm,sm,vm,vm,vm,vm,vm],out_specs=(vm,vm),
        scratch_shapes=[pltpu.VMEM((bq,width),F32)],
        compiler_params=pltpu.CompilerParams(vmem_limit_bytes=40<<20),
        cost_estimate=pl.CostEstimate(flops=22_000_000_000, bytes_accessed=8_000_000, transcendentals=0),
        name="attend_fwd",
    )(lo,hi,q,k,v,rseg,kseg)

def bwd_kernel(causal, heads, bq, bk, lo_ref, hi_ref, q_ref, k_ref, v_ref, o_ref, do_ref, lse_ref, rs_ref, ks_ref,
               dq_ref, dkv_ref, dka, dva, qm, dom, dqa):
    count,width=q_ref.shape
    dka[...]=jnp.zeros_like(dka); dva[...]=jnp.zeros_like(dva)
    def one(qb,_):
        q0=pl.multiple_of(qb*bq,bq)
        qv=q_ref[pl.ds(q0,bq),:]*BF(HEAD_DIM**-0.5)
        dov=do_ref[pl.ds(q0,bq),:]
        prod=dov.astype(F32)*o_ref[pl.ds(q0,bq),:].astype(F32)
        row=lax.broadcasted_iota(jnp.int32,(8,width),0); col=lax.broadcasted_iota(jnp.int32,(8,width),1)//HEAD_DIM
        sel=(row==col).astype(F32)
        delta=lax.dot_general(sel,prod,(((1,),(1,)),((),())),precision=lax.Precision.HIGHEST,preferred_element_type=F32)
        for h in range(heads):
            hm=head_mask(bq,width,h)
            qm[pl.ds(h*bq,bq),:]=jnp.where(hm,qv,BF(0))
            dom[pl.ds(h*bq,bq),:]=jnp.where(hm,dov,BF(0))
        dqa[...]=jnp.zeros_like(dqa)
        rseg=rs_ref[0:1,pl.ds(q0,bq)]
        lse=lse_ref[:,pl.ds(q0,bq)]
        def inner(kb,_):
            k0=pl.multiple_of(kb*bk,bk)
            kv=k_ref[pl.ds(k0,bk),:]; vv=v_ref[pl.ds(k0,bk),:]
            if causal:
                kpad=ks_ref[pl.ds(k0,bk),1:2]
                ri=lax.broadcasted_iota(jnp.int32,(bk,bq),1)+q0
                ci=lax.broadcasted_iota(jnp.int32,(bk,bq),0)+k0
                ok=((rseg==kpad)&(ci<=ri))|(ci==ri)
            else:
                ok=rseg==ks_ref[pl.ds(k0,bk),0:1]
            ps=[];dss=[]
            dq=None
            for h in range(heads):
                st=dot(kv,qm[pl.ds(h*bq,bq),:],1,1)
                p=jnp.where(ok,jnp.exp(st-lse[h:h+1,:]),0.0)
                dp=dot(vv,dom[pl.ds(h*bq,bq),:],1,1)
                ds=(p*(dp-delta[h:h+1,:])).astype(BF)
                ps.append(p.astype(BF)); dss.append(ds)
                km=jnp.where(head_mask(bk,width,h),kv,BF(0))
                t=dot(ds,km,0,0)
                dq=t if dq is None else dq+t
            dqa[...]+=dq
            pcat=jnp.concatenate(ps,axis=1); dcat=jnp.concatenate(dss,axis=1)
            dva[pl.ds(k0,bk),:]+=dot(pcat,dom[...],1,0)
            dka[pl.ds(k0,bk),:]+=dot(dcat,qm[...],1,0)
            return 0
        lax.fori_loop(lo_ref[qb],hi_ref[qb],inner,0)
        dq_ref[pl.ds(q0,bq),:width]=(dqa[...]*(HEAD_DIM**-0.5)).astype(BF)
        return 0
    lax.fori_loop(0,count//bq,one,0)
    out_ref = dq_ref if dkv_ref is None else dkv_ref
    first = out_ref.shape[1] - 2*width
    out_ref[:,first:first+width]=dka[...].astype(BF)
    out_ref[:,first+width:]=dva[...].astype(BF)

def attend_bwd(q,k,v,o,do,lse,rseg,kseg,lo,hi,causal,bq=256,bk=256):
    count,width=q.shape; keys=k.shape[0]
    heads=width//HEAD_DIM
    vm=pl.BlockSpec(memory_space=pltpu.VMEM); sm=pl.BlockSpec(memory_space=pltpu.SMEM)
    def kernel(*refs):
        rest=refs if not causal else refs[:11]+(None,)+refs[11:]
        bwd_kernel(causal,heads,bq,bk,*rest)
    shape=jax.ShapeDtypeStruct
    out_shape=(shape((count,3*width),BF),) if causal else (shape((count,width),BF),shape((keys,2*width),BF))
    return pl.pallas_call(kernel,
        out_shape=out_shape,
        in_specs=[sm,sm]+[vm]*8,out_specs=(vm,)*len(out_shape),
        scratch_shapes=[pltpu.VMEM((keys,width),F32),pltpu.VMEM((keys,width),F32),pltpu.VMEM((heads*bq,width),BF),pltpu.VMEM((heads*bq,width),BF),pltpu.VMEM((bq,width),F32)],
        compiler_params=pltpu.CompilerParams(vmem_limit_bytes=40<<20),
        cost_estimate=pl.CostEstimate(flops=30_000_000_000, bytes_accessed=8_000_000, transcendentals=0),
        name="attend_bwd",
    )(lo,hi,q,k,v,o,do,lse,rseg,kseg)

def ranges(tok_lengths, enc_lengths, pad, count, frames, bq, bk):
    tend=jnp.cumsum(tok_lengths,dtype=jnp.int32); eend=jnp.cumsum(enc_lengths,dtype=jnp.int32)
    places=jnp.arange(count,dtype=jnp.int32)
    tseg=jnp.sum((places[:,None]>=tend[None,:]).astype(jnp.int32),axis=1)
    eseg=jnp.sum((jnp.arange(frames,dtype=jnp.int32)[:,None]>=eend[None,:]).astype(jnp.int32),axis=1)
    starts=jnp.arange(count//bq,dtype=jnp.int32)*bq
    first=tseg[::bq]; last=tseg[bq-1::bq]
    onehot=lambda s:(s[:,None]==jnp.arange(tend.shape[0])[None,:]).astype(jnp.int32)
    pick=lambda arr,s: jnp.sum(onehot(s)*arr[None,:],axis=1)
    tstart=tend-tok_lengths; estart=eend-enc_lengths
    slo=pick(tstart,first)//bk; shi=(starts+bq+bk-1)//bk
    clo=pick(estart,first)//bk; chi=(pick(eend,last)+bk-1)//bk
    kpad=jnp.where(pad==1,tseg,-1)
    return tseg,eseg,kpad,slo,shi,clo,chi


def along_rows(left, right):
    return lax.dot_general(
        left, right, (((0,), (0,)), ((), ())), preferred_element_type=jnp.float32
    )


def against(left, weight):
    return lax.dot_general(
        left, weight, (((1,), (1,)), ((), ())), preferred_element_type=jnp.float32
    )


def times(left, weight):
    return jnp.dot(left, weight, preferred_element_type=jnp.float32)


def moments(rows):
    centred = rows - jnp.mean(rows, axis=1, keepdims=True)
    inverse = lax.rsqrt(jnp.mean(centred * centred, axis=1, keepdims=True) + eps)
    return centred * inverse, inverse


def normalize_back(grad_out, unit, inverse, gain):
    scaled = grad_out * gain
    inner = (
        scaled
        - jnp.mean(scaled, axis=1, keepdims=True)
        - unit * jnp.mean(scaled * unit, axis=1, keepdims=True)
    )
    return (inner * inverse, jnp.sum(grad_out * unit, axis=0), jnp.sum(grad_out, axis=0))


class Place:
    def __init__(self):
        self.dp = lax.axis_size("dp")
        self.tensor = lax.axis_size("tensor")
        self.d = lax.axis_index("dp")
        self.t = lax.axis_index("tensor")
        self.core = self.d % 2
        self.half = self.t // 2
        self.side = self.t % 2
        self.keeper = self.core == self.half
        self.shard = jnp.where(self.keeper, self.t, self.t ^ 2)

    def swap(self, value, d_flip, t_flip, only=None):
        pairs = []
        for d in range(self.dp):
            for t in range(self.tensor):
                keeper = d % 2 == t // 2
                if only is None or only == keeper:
                    pairs.append((d * self.tensor + t, (d ^ d_flip) * self.tensor + (t ^ t_flip)))
        return lax.ppermute(value, ("dp", "tensor"), pairs)

    def home(self, value):
        return jnp.where(self.keeper, value, self.swap(value, 1, 2, False))

    def ordered(self, mine, other, which):
        return jnp.where(
            which == 0, jnp.concatenate([mine, other]), jnp.concatenate([other, mine])
        )

    def part(self, value, which, parts):
        size = value.shape[0] // parts
        return lax.dynamic_slice_in_dim(value, which * size, size, 0)

    def both_cores(self, half_rows):
        return self.ordered(half_rows, self.swap(half_rows, 1, 0), self.core)

    def spread_columns(self, value):
        near, far = self.part(value, self.core, 2), self.part(value, 1 - self.core, 2)
        return jnp.concatenate(
            [near, self.swap(far, 1, 0), self.swap(near, 0, 1), self.swap(far, 1, 1)], axis=1
        )

    def order(self):
        return [self.shard, self.shard ^ 2, self.shard ^ 1, self.shard ^ 3]

    def sum_half(self, value):
        near, far = self.part(value, self.core, 2), self.part(value, 1 - self.core, 2)
        return near.astype(jnp.float32) + self.swap(far.astype(jnp.bfloat16), 1, 0).astype(jnp.float32)

    def sum_group_half(self, value):
        mine = self.sum_half(value).astype(jnp.bfloat16)
        return mine.astype(jnp.float32) + self.swap(mine, 0, 1).astype(jnp.float32)

    def sum_group_quarter(self, value):
        mine = self.sum_half(value)
        near, far = self.part(mine, self.side, 2), self.part(mine, 1 - self.side, 2)
        return near + self.swap(far.astype(jnp.bfloat16), 0, 1).astype(jnp.float32)

    def sum_columns(self, grad, order):
        columns = self.dp // 2
        bits = columns.bit_length() - 1
        turned = [sum(((c >> b) & 1) << (bits - 1 - b) for b in range(bits)) for c in range(columns)]
        groups = [[2 * (turned[c] if order == 0 else c) + core for c in range(columns)] for core in range(2)]
        return lax.psum_scatter(
            grad.astype(jnp.bfloat16), "dp", scatter_dimension=0, axis_index_groups=groups, tiled=True
        )

    def cross_planes(self, grads):
        return [
            (grad.astype(jnp.float32) + self.swap(grad, 0, 2, False).astype(jnp.float32)).astype(jnp.bfloat16)
            for grad in grads
        ]

    def moved_weight(self, weight):
        piece = self.swap(self.part(weight, self.d, self.dp), 0, 2)
        return jnp.where(self.keeper, weight, lax.all_gather(piece, "dp", axis=0, tiled=True))

    def whole_weight(self, weight):
        piece = self.part(weight, self.d, self.dp)
        every = lax.all_gather(piece, ("dp", "tensor"), axis=0, tiled=False)
        every = every.reshape((self.dp, self.tensor) + piece.shape)
        return jnp.swapaxes(every, 0, 1).reshape((self.tensor,) + weight.shape)


class Copies:
    def __init__(self, send_sem, recv_sem):
        self.send_sem, self.recv_sem, self.known = send_sem, recv_sem, {}

    def __call__(self, name, src, dst, device):
        at = self.known.setdefault(name, len(self.known))
        return pltpu.make_async_remote_copy(
            src_ref=src,
            dst_ref=dst,
            send_sem=self.send_sem.at[at],
            recv_sem=self.recv_sem.at[at],
            device_id=device,
            device_id_type=pl.DeviceIdType.MESH,
        )


def greet(devices):
    barrier = pltpu.get_barrier_semaphore()
    for device in devices:
        pl.semaphore_signal(
            barrier, inc=1, device_id=device, device_id_type=pl.DeviceIdType.MESH
        )
    pl.semaphore_wait(barrier, len(devices))


def rows_of(ref, start, size, step=16):
    return ref.at[pl.ds(pl.multiple_of(start, step), size)]


def norm_rows(src, src_first, dst, dst_first, rows, gain, shift):
    chunk = 64

    def body(i, _):
        at = i * chunk
        x = src[pl.ds(pl.multiple_of(src_first + at, 16), chunk), :].astype(jnp.float32)
        unit, inverse = moments(x)
        dst[pl.ds(pl.multiple_of(dst_first + at, 16), chunk), :] = (
            unit * gain[...] + shift[...]
        ).astype(jnp.bfloat16)
        return 0

    lax.fori_loop(0, rows // chunk, body, 0)


def sum_kernel(dp, arrays, units, span, *refs):
    it = iter(refs)
    take = lambda count: [next(it) for _ in range(count)]
    ins = take(arrays)
    fars = take(2)
    part, home_near, home_far, small_in, tokens, grad_in, gain = take(7)
    outs = take(arrays)
    row_out, home_out, small_out = take(3)
    bits = [b for b in (2, 4, 8, 16, 32, 64) if b < dp]
    steps = len(bits)
    land, hold = [], []
    for unit in units:
        hold.append(take(0 if unit[4] else steps))
        land.append(take((steps + 1, 1, 0)[unit[4]]))
    row_land, row_hold = take(2), take(2)
    (home_hold,) = take(1)
    small_hold, small_land, small_send, small_recv, row_send, row_recv, send_sem, recv_sem = take(8)
    d, t = lax.axis_index("dp"), lax.axis_index("tensor")
    core, side = d % 2, t % 2
    keeper = core == t // 2
    other = jnp.logical_not(keeper)
    MESH = pl.DeviceIdType.MESH

    around = [(d ^ b, t) for b in bits] + [(d ^ 1, t), (d, t ^ 2), (d, t ^ 1)]
    greet(around + [(d ^ 1, t ^ 2)])

    def my(bit):
        return (d // bit) % 2

    def order(u):
        return bits if units[u][3] == 0 else bits[::-1]

    def source(u, step):
        array, first, rows, _, summed = units[u]
        if summed:
            return ins[array], first >> steps
        return (ins[array], first) if step == 0 else (hold[u][step - 1], 0)

    def copy(u, stage, src, dst, device):
        return pltpu.make_async_remote_copy(
            src_ref=src, dst_ref=dst, send_sem=send_sem.at[u, stage], recv_sem=recv_sem.at[u, stage],
            device_id=device, device_id_type=MESH,
        )

    def quarter(u):
        place = units[u][1]
        for step, bit in enumerate(order(u)):
            place = place + my(bit) * (units[u][2] >> (step + 1))
        return place

    def scatter_copy(u, step):
        ref, first = source(u, step)
        size = units[u][2] >> (step + 1)
        bit = order(u)[step]
        return copy(u, step, rows_of(ref, first + (1 - my(bit)) * size, size), land[u][step], (d ^ bit, t))

    def plane_copy(u):
        ref, first = source(u, steps)
        return copy(u, steps, rows_of(ref, first, units[u][2] >> steps), land[u][-1], (d, t ^ 2))

    def gather_copy(u, step):
        array, first, rows = units[u][:3]
        bit = order(u)[steps - 1 - step]
        size = rows >> (steps - step)
        start = quarter(u)
        for back in range(step):
            start = start - my(order(u)[steps - 1 - back]) * (rows >> (steps - back))
        block = rows_of(outs[array], start, size)
        return copy(u, steps + 1 + step, block, block, (d ^ bit, t))

    def core_copy(u):
        array, first, rows = units[u][:3]
        block = outs[array].at[pl.ds(first, rows)]
        return copy(u, 2 * steps + 1, block, block, (d ^ 1, t))

    def add(dst, dst_first, left, left_first, right, rows):
        chunk = min(rows, 32)

        def body(i, _):
            at = i * chunk
            a = left[pl.ds(pl.multiple_of(left_first + at, 16), chunk), :].astype(jnp.float32)
            b = right[pl.ds(pl.multiple_of(at, 16), chunk), :].astype(jnp.float32)
            dst[pl.ds(pl.multiple_of(dst_first + at, 16), chunk), :] = (a + b).astype(jnp.bfloat16)
            return 0

        lax.fori_loop(0, rows // chunk, body, 0)

    def begin(u, stage):
        if stage < steps:
            scatter_copy(u, stage).start()
        elif stage == steps:

            @pl.when(other)
            def _():
                plane_copy(u).start()
        else:

            @pl.when(keeper)
            def _():
                (gather_copy(u, stage - steps - 1) if stage <= 2 * steps else core_copy(u)).start()

    def end(u, stage):
        array, first, rows = units[u][:3]
        if stage < steps:
            one = scatter_copy(u, stage)
            one.wait_recv()
            ref, row = source(u, stage)
            size = rows >> (stage + 1)
            add(hold[u][stage], 0, ref, row + my(order(u)[stage]) * size, land[u][stage], size)
            one.wait_send()
        elif stage == steps and units[u][4] == 2:

            @pl.when(keeper)
            def _():
                size = rows >> steps
                ref, row = source(u, steps)
                add(outs[array], quarter(u), ref, row, fars[array], size)
        elif stage == steps:

            @pl.when(other)
            def _():
                plane_copy(u).wait_send()

            @pl.when(keeper)
            def _():
                plane_copy(u).wait_recv()
                ref, row = source(u, steps)
                add(outs[array], quarter(u), ref, row, land[u][-1], rows >> steps)
        elif stage <= 2 * steps:

            @pl.when(keeper)
            def _():
                gather_copy(u, stage - steps - 1).wait()
        else:

            @pl.when(keeper)
            def _():
                core_copy(u).wait_send()

            @pl.when(other)
            def _():
                core_copy(u).wait_recv()

    def row_copy(stage):
        if stage == 0:
            src, dst, device = rows_of(part, (1 - core) * 2 * span, 2 * span), row_land[0], (d ^ 1, t)
        elif stage == 1:
            src, dst, device = rows_of(row_hold[0], (1 - side) * span, span), row_land[1], (d, t ^ 1)
        elif stage == 2:
            src, dst, device = row_hold[1], row_out, (d ^ 1, t ^ 2)
        else:
            src, dst, device = home_hold, home_out, (d ^ 1, t ^ 2)
        return pltpu.make_async_remote_copy(
            src_ref=src, dst_ref=dst, send_sem=row_send.at[stage], recv_sem=row_recv.at[stage],
            device_id=device, device_id_type=MESH,
        )

    def row_half():
        row_copy(0).wait()
        add(row_hold[0], 0, part, core * 2 * span, row_land[0], 2 * span)
        row_copy(1).start()

    def to_owner(hold_ref, out_ref, stage):
        @pl.when(keeper)
        def _():
            out_ref[...] = hold_ref[...]

        @pl.when(other)
        def _():
            row_copy(stage).start()

    def row_home():
        row_copy(1).wait()

        def body(i, _):
            at = pl.ds(pl.multiple_of(i * 32, 32), 32)
            here = pl.ds(pl.multiple_of(side * span + i * 32, 32), 32)
            total = row_hold[0][here, :].astype(jnp.float32) + row_land[1][at, :].astype(jnp.float32)
            unit, inverse = moments(tokens[here, :].astype(jnp.float32))
            total = grad_in[here, :] + normalize_back(total, unit, inverse, gain[...])[0]
            row_hold[1][at, :] = total.astype(jnp.bfloat16)
            return 0

        lax.fori_loop(0, span // 32, body, 0)
        to_owner(row_hold[1], row_out, 2)

    def small_copy(step):
        return pltpu.make_async_remote_copy(
            src_ref=small_hold.at[step], dst_ref=small_land.at[step], send_sem=small_send.at[step],
            recv_sem=small_recv.at[step], device_id=around[step], device_id_type=MESH,
        )

    def small_step(step):
        small_copy(step).wait()
        total = small_hold[step] + small_land[step]
        if step + 1 < len(around):
            small_hold[step + 1] = total
            small_copy(step + 1).start()
        else:
            small_out[...] = total

    last = 2 * steps + 2
    first_stage = (0, steps, steps + 1)
    turns = [
        list(range(last + 1)),
        list(range(steps + 3)),
        list(range(steps + 2)),
    ]

    def tick(now):
        for state in (0, 1, 2):
            if now not in turns[state]:
                continue
            turn = turns[state].index(now)
            stage = first_stage[state] + turn
            for u in range(len(units)):
                if units[u][4] != state:
                    continue
                if state == 2 and turn == 0:
                    end(u, steps)
                if turn > 0:
                    end(u, stage - 1)
                if stage < last:
                    begin(u, stage)

    small_hold[0] = small_in[...]
    small_copy(0).start()
    row_copy(0).start()
    tick(0)
    add(home_hold, 0, home_near, 0, home_far, home_hold.shape[0])
    row_half()
    small_step(0)
    row_home()
    for now in range(1, last + 1):
        tick(now)
        if now < len(around):
            small_step(now)
        if now == steps + 1:
            to_owner(home_hold, home_out, 3)

    @pl.when(other)
    def _():
        row_copy(2).wait()
        row_copy(3).wait()


def sum_all(grads, fars, units, part, home, norm_grads, tokens, grad_in, gain, collective_id):
    dp = lax.axis_size("dp")
    steps = 0
    while 2 << steps < dp:
        steps += 1
    bf16, f32 = jnp.bfloat16, jnp.float32
    shapes = [(grad.shape[0], grad.shape[1]) for grad in grads]
    scratch = []
    for array, first, rows, side, done in units:
        width = grads[array].shape[1]
        if done:
            shapes[array] = (rows, width)
        else:
            scratch += [pltpu.VMEM((rows >> (k + 1), width), bf16) for k in range(steps)] * 2
        if done < 2:
            scratch.append(pltpu.VMEM((rows >> steps, width), bf16))
    stages = 2 * steps + 2
    vmem = pl.BlockSpec(memory_space=pltpu.VMEM)
    span = part.shape[0] // 4
    wide = tokens.shape[1]
    semaphores = pltpu.SemaphoreType.DMA
    return pl.pallas_call(
        functools.partial(sum_kernel, dp, len(grads), units, span),
        out_shape=[jax.ShapeDtypeStruct(shape, bf16) for shape in shapes]
        + [jax.ShapeDtypeStruct((span, wide), bf16), jax.ShapeDtypeStruct(home[0].shape, bf16)]
        + [jax.ShapeDtypeStruct(norm_grads.shape, f32)],
        in_specs=[vmem] * (len(grads) + 9),
        out_specs=[vmem] * (len(grads) + 3),
        scratch_shapes=scratch
        + [pltpu.VMEM((many * span, wide), bf16) for many in (2, 1)] * 2
        + [pltpu.VMEM(home[0].shape, bf16)]
        + [pltpu.VMEM((steps + 3,) + norm_grads.shape, f32)] * 2
        + [semaphores((steps + 3,))] * 2
        + [semaphores((4,))] * 2
        + [semaphores((len(units), stages))] * 2,
        compiler_params=pltpu.CompilerParams(
            collective_id=collective_id, has_side_effects=True, vmem_limit_bytes=60 << 20
        ),
        cost_estimate=pl.CostEstimate(flops=80_000_000_000, bytes_accessed=16_000_000, transcendentals=0),
        name="sum_all",
    )(*grads, *fars, part, *home, norm_grads, tokens, grad_in, gain[None])


class Move:
    def __init__(self, name, copy, sources, moved, d, t):
        self.name, self.copy, self.sources, self.moved = name, copy, sources, moved
        self.d, self.t, self.column = d, t, (d // 2) % 4
        self.keeper = d % 2 == t // 2
        self.other = jnp.logical_not(self.keeper)

    def block(self, ref):
        part = ref.shape[0] // 4
        return rows_of(ref, self.column * part, part)

    def fetch(self, a):
        return self.copy(
            (self.name, a), self.block(self.sources[a]), self.block(self.moved[a]), (self.d, self.t ^ 2)
        )

    def share(self, a, m):
        block = self.block(self.moved[a])
        return self.copy((self.name, a, m), block, block, (self.d ^ (2 * m), self.t))

    def start(self):
        @pl.when(self.keeper)
        def _():
            for a in range(len(self.moved)):
                self.fetch(a).start()

    def relay(self, which):
        @pl.when(self.other)
        def _():
            for a in which:
                self.fetch(a).wait_recv()
                for m in (1, 2, 3):
                    self.share(a, m).start()

    def ready(self, which):
        @pl.when(self.keeper)
        def _():
            for a in which:
                self.moved[a][...] = self.sources[a][...]

        @pl.when(self.other)
        def _():
            for a in which:
                for m in (1, 2, 3):
                    self.share(a, m).wait_recv()

    def finish(self):
        @pl.when(self.keeper)
        def _():
            for a in range(len(self.moved)):
                self.fetch(a).wait_send()

        @pl.when(self.other)
        def _():
            for a in range(len(self.moved)):
                for m in (1, 2, 3):
                    self.share(a, m).wait_send()


class HalfRows:
    def __init__(self, name, copy, rows, half, first, far_first, d, t):
        self.name, self.copy, self.rows, self.half, self.first = name, copy, rows, half, first
        self.far_first = far_first
        self.d, self.t, self.side = d, t, t % 2
        self.keeper = d % 2 == t // 2
        self.other = jnp.logical_not(self.keeper)
        self.count = rows.shape[0]
        self.piece = self.count // 4

    def place(self, s, p):
        return rows_of(self.half, self.first + s * self.count + p * self.piece, self.piece)

    def own(self, p):
        return self.rows.at[pl.ds(p * self.piece, self.piece)]

    def swap(self, p):
        at = rows_of(self.half, self.far_first + self.side * self.count + p * self.piece, self.piece)
        return self.copy((self.name, "swap", p), self.own(p), at, (self.d ^ 1, self.t ^ 2))

    def through(self, p, source):
        return self.copy((self.name, "pass", p), source, self.place(self.side, p), (self.d, self.t ^ 1))

    def start(self):
        @pl.when(self.other)
        def _():
            for p in range(4):
                self.swap(p).start()

        @pl.when(self.keeper)
        def _():
            for p in range(4):
                self.through(p, self.own(p)).start()
            at = pl.multiple_of(self.first + self.side * self.count, 16)
            self.half[pl.ds(at, self.count), :] = self.rows[...]

    def relay(self):
        @pl.when(self.other)
        def _():
            for p in range(4):
                self.swap(p).wait_recv()
                self.through(p, self.place(self.side, p)).start()

    def arrive(self):
        for p in range(4):
            block = self.place(1 - self.side, p)
            self.copy((self.name, "pass", p), block, block, (self.d, self.t ^ 1)).wait_recv()

    def finish(self):
        @pl.when(self.keeper)
        def _():
            for p in range(4):
                self.through(p, self.own(p)).wait_send()

        @pl.when(self.other)
        def _():
            for p in range(4):
                self.swap(p).wait_send()
                self.through(p, self.place(self.side, p)).wait_send()


class Whole:
    def __init__(self, name, copy, source, whole, d, t):
        self.name, self.copy, self.source, self.whole = name, copy, source, whole
        self.d, self.t = d, t
        self.away = jnp.where(d % 2 == t // 2, 0, 1)
        self.rows = source.shape[0]
        self.slim = self.rows // 8
        self.half_at = (d % 2) * (4 * self.slim)
        self.at = self.half_at + ((d // 2) % 4) * self.slim

    def block(self, j):
        return rows_of(self.whole, j * self.rows + self.at, self.slim)

    def far(self):
        return self.copy(
            (self.name, "far"), rows_of(self.source, self.at, self.slim), self.block(self.away), (self.d, self.t ^ 2)
        )

    def near(self, late):
        j = 1 - self.away if late else self.away
        return self.copy((self.name, "near", late), self.block(j), self.block(j + 2), (self.d, self.t ^ 1))

    def level(self, j, m):
        block = rows_of(self.whole, j * self.rows + self.at, self.slim)
        return self.copy((self.name, "level", j, m), block, block, (self.d ^ (2 * m), self.t))

    def hand(self, j):
        return self.copy(
            (self.name, "hand", j),
            rows_of(self.whole, j * self.rows + self.half_at, 4 * self.slim),
            rows_of(self.whole, (j ^ 1) * self.rows + self.half_at, 4 * self.slim),
            (self.d ^ 1, self.t),
        )

    def start(self):
        self.far().start()
        self.whole[pl.ds(pl.multiple_of(self.away * self.rows + self.at, 16), self.slim), :] = self.source[
            pl.ds(pl.multiple_of(self.at, 16), self.slim), :
        ]
        self.near(False).start()

    def pass_on(self):
        self.far().wait_recv()
        self.near(True).start()
        for m in (1, 2, 3):
            for j in (0, 1):
                self.level(j, m).start()

    def across(self):
        self.near(False).wait_recv()
        self.near(True).wait_recv()
        for m in (1, 2, 3):
            for j in (2, 3):
                self.level(j, m).start()

    def hand_over(self):
        for m in (1, 2, 3):
            for j in range(4):
                self.level(j, m).wait_recv()
        for j in range(4):
            self.hand(j).start()

    def finish(self):
        self.far().wait_send()
        self.near(False).wait_send()
        self.near(True).wait_send()
        for m in (1, 2, 3):
            for j in range(4):
                self.level(j, m).wait_send()
        for j in range(4):
            self.hand(j).wait()


def start_kernel(*refs):
    (tokens, gain, shift, *weights, out_weight, next_out, encoder, expand) = refs[:10]
    (rows_half, normed, query, keyed, valued, moved, whole, next_whole, encoder_out, expand_slice) = refs[10:20]
    send_sem, recv_sem = refs[20:]
    d, t = lax.axis_index("dp"), lax.axis_index("tensor")
    core, side = d % 2, t % 2
    keeper = core == t // 2
    other = jnp.logical_not(keeper)
    count = tokens.shape[0]
    copy = Copies(send_sem, recv_sem)
    move = Move("move", copy, weights, [moved.at[a] for a in range(3)], d, t)
    every = Whole("whole", copy, out_weight, whole, d, t)
    after = Whole("next", copy, next_out, next_whole, d, t)
    rows = HalfRows("tokens", copy, tokens, rows_half, 0, 0, d, t)

    greet(
        [(d ^ 2, t), (d ^ 4, t), (d ^ 6, t), (d ^ 1, t), (d, t ^ 1), (d, t ^ 2), (d ^ 1, t ^ 2)]
    )

    def give(name, s):
        block = rows_of(normed, core * (2 * count) + s * count, count)
        return copy(("give", name), block, block, (d ^ 1, t))

    encoder_copy = copy("encoder", encoder, encoder_out, (d ^ 1, t))
    slim = expand_slice.shape[0]
    hop = copy("hop", rows_of(expand, d * slim, slim), expand_slice, (d, t ^ 2))

    every.start()
    after.start()
    rows.start()
    move.start()
    every.pass_on()
    after.pass_on()

    @pl.when(keeper)
    def _():
        encoder_copy.start()

    every.across()
    after.across()
    rows.relay()
    mine = core * (2 * count)
    norm_rows(rows_half, side * count, normed, mine + side * count, count, gain, shift)
    give(0, side).start()
    move.relay(range(3))
    hop.start()
    rows.arrive()
    norm_rows(rows_half, (1 - side) * count, normed, mine + (1 - side) * count, count, gain, shift)
    give(1, 1 - side).start()
    every.hand_over()
    after.hand_over()

    @pl.when(keeper)
    def _():
        encoder_out[...] = encoder[...]

    def project(first):
        def body(i, _):
            at = pl.ds(pl.multiple_of(first + i * 256, 256), 256)
            for a, out in enumerate((query, keyed, valued)):
                out[at, :] = jnp.dot(
                    normed[at, :], moved[a], preferred_element_type=jnp.float32
                ).astype(jnp.bfloat16)
            return 0

        lax.fori_loop(0, (2 * count) // 256, body, 0)

    move.ready(range(3))
    project(mine)
    give(0, side).wait()
    give(1, 1 - side).wait()
    project((1 - core) * (2 * count))
    every.finish()
    after.finish()
    move.finish()
    rows.finish()
    hop.wait()

    @pl.when(keeper)
    def _():
        encoder_copy.wait_send()

    @pl.when(other)
    def _():
        encoder_copy.wait_recv()


def start_layer(tokens, gain, shift, weights, out_weight, next_out, encoder, expand, collective_id):
    rows, wide = tokens.shape
    dp = lax.axis_size("dp")
    width = weights[0].shape[1]
    bf16 = jnp.bfloat16
    shape = jax.ShapeDtypeStruct
    vmem = pl.BlockSpec(memory_space=pltpu.VMEM)
    return pl.pallas_call(
        start_kernel,
        out_shape=(
            shape((2 * rows, wide), bf16),
            shape((4 * rows, wide), bf16),
            shape((4 * rows, width), bf16),
            shape((4 * rows, width), bf16),
            shape((4 * rows, width), bf16),
            shape((3,) + weights[0].shape, bf16),
            shape((4 * out_weight.shape[0], out_weight.shape[1]), bf16),
            shape((4 * next_out.shape[0], next_out.shape[1]), bf16),
            shape(encoder.shape, bf16),
            shape((expand.shape[0] // dp, expand.shape[1]), bf16),
        ),
        in_specs=[vmem] * 9 + [pl.BlockSpec(memory_space=pl.ANY)],
        out_specs=(vmem,) * 9 + (pl.BlockSpec(memory_space=pl.ANY),),
        scratch_shapes=[
            pltpu.SemaphoreType.DMA((72,)),
            pltpu.SemaphoreType.DMA((72,)),
        ],
        compiler_params=pltpu.CompilerParams(
            collective_id=collective_id, has_side_effects=True, vmem_limit_bytes=56 << 20
        ),
        cost_estimate=pl.CostEstimate(flops=35_000_000_000, bytes_accessed=16_000_000, transcendentals=0),
        name="start_layer",
    )(tokens, gain[None], shift[None], *weights, out_weight, next_out, encoder, expand)


def add_dot(left, right, over_rows=False):
    return lax.dot_general(
        left, right, (((1,), (1 if over_rows else 0,)), ((), ())), preferred_element_type=jnp.float32
    )


class Exchange:
    def __init__(self, copy, mine, land, core, d, t, chunk):
        self.copy, self.mine, self.land, self.core, self.chunk = copy, mine, land, core, chunk
        self.half = mine.shape[0] // 2
        self.to = [(d ^ 1, t), (d, t ^ 1), (d ^ 1, t ^ 1)]

    def one(self, j, ch):
        core = self.core if j == 1 else 1 - self.core
        return self.copy(
            ("exchange", j, ch),
            rows_of(self.mine, core * self.half + ch * self.chunk, self.chunk),
            self.land.at[j, pl.ds(ch * self.chunk, self.chunk)],
            self.to[j],
        )

    def start(self, ch):
        for j in (1, 2, 0):
            self.one(j, ch).start()

    def arrive(self, ch):
        for j in range(3):
            self.one(j, ch).wait_recv()

    def pieces(self, ch):
        first = self.core * self.half + ch * self.chunk
        own = self.mine[pl.ds(pl.multiple_of(first, 16), self.chunk), :]
        return [own] + [self.land[j, pl.ds(ch * self.chunk, self.chunk), :] for j in range(3)]

    def sent(self, ch):
        for j in range(3):
            self.one(j, ch).wait_send()


def by_rows(rows, step, body):
    def turn(i, _):
        body(pl.multiple_of(i * step, step))
        return 0

    lax.fori_loop(0, rows // step, turn, 0)


def forward_kernel(*refs):
    (mixed, out_all, start, gain, shift, *weights) = refs[:8]
    (after, normed, result, moved) = refs[8:12]
    (land, product, send_sem, recv_sem) = refs[12:]
    d, t = lax.axis_index("dp"), lax.axis_index("tensor")
    core = d % 2
    chunk = product.shape[0]
    half = after.shape[0]
    width = mixed.shape[1]
    copy = Copies(send_sem, recv_sem)
    greet(
        [(d ^ 1, t), (d, t ^ 1), (d ^ 1, t ^ 1), (d ^ 2, t), (d ^ 4, t), (d ^ 6, t), (d, t ^ 2)]
    )
    exchange = Exchange(copy, mixed, land, core, d, t, chunk)
    move = Move("move", copy, weights, [moved.at[a] for a in range(3)], d, t)

    def give(ch):
        block = rows_of(normed, core * half + ch * chunk, chunk)
        return copy(("give", ch), block, block, (d ^ 1, t))

    chunks = half // chunk
    for ch in range(chunks):
        exchange.start(ch)
    move.start()
    for ch in range(chunks):
        exchange.arrive(ch)
        product[...] = sum(
            add_dot(piece, out_all[j * width : (j + 1) * width, :])
            for j, piece in enumerate(exchange.pieces(ch))
        )

        def rows(at, ch=ch):
            x = start[pl.ds(pl.multiple_of(ch * chunk + at, 16), 32), :].astype(jnp.float32)
            x = x + product[pl.ds(at, 32), :]
            after[pl.ds(pl.multiple_of(ch * chunk + at, 16), 32), :] = x
            unit, inverse = moments(x)
            normed[pl.ds(pl.multiple_of(core * half + ch * chunk + at, 16), 32), :] = (
                unit * gain[...] + shift[...]
            ).astype(jnp.bfloat16)

        by_rows(chunk, 32, rows)
        give(ch).start()
        if ch < 3:
            move.relay([ch])

    def project(first, rows):
        at = pl.ds(pl.multiple_of(first, 16), rows)
        result[at, :] = add_dot(normed[at, :], moved[0]).astype(jnp.bfloat16)

    move.ready([0])
    project(core * half, half)
    for ch in range(chunks):
        give(ch).wait()
    project((1 - core) * half, half)
    move.ready([1, 2])
    for ch in range(chunks):
        exchange.sent(ch)
    move.finish()


def forward_step(mixed, out_all, start, gain, shift, weights, collective_id):
    rows, width = mixed.shape
    half, wide = start.shape
    chunk = half // 4
    shape = jax.ShapeDtypeStruct
    vmem = pl.BlockSpec(memory_space=pltpu.VMEM)
    return pl.pallas_call(
        forward_kernel,
        out_shape=(
            shape((half, wide), jnp.float32),
            shape((rows, wide), jnp.bfloat16),
            shape((rows, width), jnp.bfloat16),
            shape((3,) + weights[0].shape, jnp.bfloat16),
        ),
        in_specs=[vmem] * 8,
        out_specs=(vmem,) * 4,
        scratch_shapes=[
            pltpu.VMEM((3, half, width), jnp.bfloat16),
            pltpu.VMEM((chunk, wide), jnp.float32),
            pltpu.SemaphoreType.DMA((56,)),
            pltpu.SemaphoreType.DMA((56,)),
        ],
        compiler_params=pltpu.CompilerParams(
            collective_id=collective_id, has_side_effects=True, vmem_limit_bytes=56 << 20
        ),
        cost_estimate=pl.CostEstimate(flops=20_000_000_000, bytes_accessed=8_000_000, transcendentals=0),
        name="forward_step",
    )(mixed, out_all, start, gain[None], shift[None], *weights)


def backward_kernel(*refs):
    wide = refs[2].shape[1]
    (grad_query, query_all, after, gain, grad_in, weight, out_near, out_far, term) = refs[:9]
    (grad_res, grad_top, result, norm_grads, output, term_near, term_give) = refs[9:16]
    (land, product, out_rows, term_land, send_sem, recv_sem) = refs[16:]
    d, t = lax.axis_index("dp"), lax.axis_index("tensor")
    core = d % 2
    chunk = product.shape[0]
    half = after.shape[0]
    copy = Copies(send_sem, recv_sem)
    greet([(d ^ 1, t), (d, t ^ 1), (d ^ 1, t ^ 1), (d ^ 1, t ^ 2)])
    exchange = Exchange(copy, grad_query, land, core, d, t, chunk)

    def give(ch):
        block = rows_of(grad_top, core * half + ch * chunk, chunk)
        return copy(("give", ch), block, block, (d ^ 1, t))

    chunks = half // chunk
    for ch in range(chunks):
        exchange.start(ch)
    span, side = term_land.shape[0], t % 2
    term_far = copy("term", rows_of(term, (1 - core) * span, span), term_land, (d ^ 1, t))
    term_far.start()
    keeper = core == t // 2
    home = copy("home", out_rows, output, (d ^ 1, t ^ 2))
    out_rows[...] = (out_near[...] + out_far[...].astype(jnp.float32)).astype(jnp.bfloat16)

    @pl.when(keeper)
    def _():
        output[...] = out_rows[...]

    norm_grads[...] = jnp.zeros_like(norm_grads)
    for ch in range(chunks):
        exchange.arrive(ch)
        product[...] = sum(add_dot(piece, query_all[j * wide : (j + 1) * wide, :], True) for j, piece in enumerate(exchange.pieces(ch)))

        def rows(at, ch=ch):
            here = pl.ds(pl.multiple_of(ch * chunk + at, 16), 32)
            unit, inverse = moments(after[here, :])
            back, gain_grad, shift_grad = normalize_back(product[pl.ds(at, 32), :], unit, inverse, gain[...])
            total = grad_in[here, :] + back
            grad_res[here, :] = total
            grad_top[pl.ds(pl.multiple_of(core * half + ch * chunk + at, 16), 32), :] = total.astype(jnp.bfloat16)
            norm_grads[0:1, :] += gain_grad[None]
            norm_grads[1:2, :] += shift_grad[None]

        by_rows(chunk, 32, rows)
        give(ch).start()
        if ch == chunks - 2:

            @pl.when(jnp.logical_not(keeper))
            def _():
                home.start()


    def project(first, rows):
        at = pl.ds(pl.multiple_of(first, 16), rows)
        result[at, :] = add_dot(grad_top[at, :], weight[...], True).astype(jnp.bfloat16)

    project(core * half, half)
    for ch in range(chunks):
        give(ch).wait()
    project((1 - core) * half, half)
    term_far.wait()

    def term_rows(at):
        for which, out in ((side, term_near), (1 - side, term_give)):
            first = which * (span // 2) + at
            near = term[pl.ds(pl.multiple_of(core * span + first, 32), 32), :].astype(jnp.float32)
            far = term_land[pl.ds(pl.multiple_of(first, 32), 32), :].astype(jnp.float32)
            out[pl.ds(at, 32), :] = (near + far).astype(jnp.bfloat16)

    by_rows(span // 2, 32, term_rows)
    for ch in range(chunks):
        exchange.sent(ch)

    @pl.when(jnp.logical_not(keeper))
    def _():
        home.wait()


def backward_step(grad_query, query_all, after, gain, grad_in, weight, out_near, out_far, term, collective_id):
    rows, width = grad_query.shape
    half, wide = after.shape
    chunk = half // 4
    shape = jax.ShapeDtypeStruct
    vmem = pl.BlockSpec(memory_space=pltpu.VMEM)
    return pl.pallas_call(
        backward_kernel,
        out_shape=(
            shape((half, wide), jnp.float32),
            shape((rows, wide), jnp.bfloat16),
            shape((rows, weight.shape[0]), jnp.bfloat16),
            shape((8, wide), jnp.float32),
            shape(out_far.shape, jnp.bfloat16),
            shape((term.shape[0] // 4, wide), jnp.bfloat16),
            shape((term.shape[0] // 4, wide), jnp.bfloat16),
        ),
        in_specs=[vmem] * 9,
        out_specs=(vmem,) * 7,
        scratch_shapes=[
            pltpu.VMEM((3, half, width), jnp.bfloat16),
            pltpu.VMEM((chunk, wide), jnp.float32),
            pltpu.VMEM(out_far.shape, jnp.bfloat16),
            pltpu.VMEM((term.shape[0] // 2, wide), jnp.bfloat16),
            pltpu.SemaphoreType.DMA((20,)),
            pltpu.SemaphoreType.DMA((20,)),
        ],
        compiler_params=pltpu.CompilerParams(
            collective_id=collective_id, has_side_effects=True, vmem_limit_bytes=56 << 20
        ),
        cost_estimate=pl.CostEstimate(flops=20_000_000_000, bytes_accessed=8_000_000, transcendentals=0),
        name="backward_step",
    )(grad_query, query_all, after, gain[None], grad_in, weight, out_near, out_far, term)


def hidden_kernel(*refs):
    (mixed, out_all, start, gain, shift, cot, cot_pair, next_query, *ff_weights) = refs[:12]
    (after, expand_grad, reduce_grad, grad_res, grad_top, result, norm_grads, query_all, out_near, out_give) = refs[12:22]
    (land, product, own, far_send, far_land, sum_send, sum_land, expand, reduce) = refs[22:31]
    (out_own, out_send, out_land, normed, hidden, grad_pre, grad_out) = refs[31:38]
    (send_sem, recv_sem, local_sem) = refs[38:]
    d, t = lax.axis_index("dp"), lax.axis_index("tensor")
    core = d % 2
    chunk = product.shape[0]
    half = after.shape[0]
    width = mixed.shape[1]
    chunks = half // chunk
    copy = Copies(send_sem, recv_sem)
    greet(
        [(d ^ 1, t), (d, t ^ 1), (d ^ 1, t ^ 1), (d ^ 2, t), (d ^ 4, t), (d ^ 6, t), (d, t ^ 2)]
    )
    exchange = Exchange(copy, mixed, land, core, d, t, chunk)
    every = Whole("query", copy, next_query, query_all, d, t)

    def give(name, ref, ch):
        block = rows_of(ref, core * half + ch * chunk, chunk)
        return copy((name, ch), block, block, (d ^ 1, t))

    def slab(ref, ch):
        return ref.at[pl.ds(ch * chunk, chunk)]

    def far(ch):
        return copy(("far", ch), slab(far_send, ch), slab(far_land, ch), (d ^ 1, t))

    def whole(ch):
        return copy(("whole", ch), slab(sum_send, ch), slab(sum_land, ch), (d, t ^ 1))

    def out_copy(ch):
        return copy(("out", ch), slab(out_send, ch), slab(out_land, ch), (d ^ 1, t))

    def residual(ch):
        exchange.arrive(ch)
        product[...] = sum(
            add_dot(piece, out_all[j * width : (j + 1) * width, :])
            for j, piece in enumerate(exchange.pieces(ch))
        )

        def rows(at):
            here = pl.ds(pl.multiple_of(ch * chunk + at, 16), 32)
            x = start[here, :] + product[pl.ds(at, 32), :]
            after[here, :] = x
            unit, inverse = moments(x)
            normed[pl.ds(pl.multiple_of(core * half + ch * chunk + at, 16), 32), :] = (
                unit * gain[...] + shift[...]
            ).astype(jnp.bfloat16)

        by_rows(chunk, 32, rows)
        give("normed", normed, ch).start()

    def feed(first):
        every = pl.ds(pl.multiple_of(first, 16), chunk)
        product[...] = add_dot(normed[every, :], expand[...])
        own[...] = add_dot(grad_out[every, :], reduce[...], True)

        def rows(at):
            here = pl.ds(pl.multiple_of(first + at, 16), 32)
            z = product[pl.ds(at, 32), :]
            inner = jnp.tanh(tanh_coeff * (z + cubic_coeff * z * z * z))
            hidden[here, :] = (0.5 * z * (1.0 + inner)).astype(jnp.bfloat16)
            slope = 0.5 * (1.0 + inner) + 0.5 * z * (1.0 - inner * inner) * tanh_coeff * (
                1.0 + 3.0 * cubic_coeff * z * z
            )
            upper = own[pl.ds(at, 32), :].astype(jnp.bfloat16).astype(jnp.float32)
            grad_pre[here, :] = (upper * slope).astype(jnp.bfloat16)

        by_rows(chunk, 32, rows)
        return add_dot(grad_pre[pl.ds(pl.multiple_of(first, 16), chunk), :], expand[...], True)

    def both(ch):
        copy(
            ("normed", ch), *([rows_of(normed, (1 - core) * half + ch * chunk, chunk)] * 2), (d ^ 1, t)
        ).wait_recv()
        far_send[pl.ds(ch * chunk, chunk), :] = feed((1 - core) * half + ch * chunk).astype(jnp.bfloat16)
        far(ch).start()
        own[...] = feed(core * half + ch * chunk)
        far(ch).wait_recv()

        def rows(at):
            here = pl.ds(pl.multiple_of(ch * chunk + at, 16), 32)
            sum_send[here, :] = (own[pl.ds(at, 32), :] + far_land[here, :].astype(jnp.float32)).astype(jnp.bfloat16)

        by_rows(chunk, 32, rows)
        whole(ch).start()
        at = pl.ds(ch * chunk, chunk)
        for core_at, out in ((1 - core, out_send), (core, out_own)):
            every_row = pl.ds(pl.multiple_of(core_at * half + ch * chunk, 16), chunk)
            out[at, :] = add_dot(hidden[every_row, :], reduce[...]).astype(jnp.bfloat16)
            if out is out_send:
                out_copy(ch).start()

    def back(ch):
        whole(ch).wait_recv()

        def rows(at):
            here = pl.ds(pl.multiple_of(ch * chunk + at, 16), 32)
            grad = sum_send[here, :].astype(jnp.float32) + sum_land[here, :].astype(jnp.float32)
            unit, inverse = moments(after[here, :])
            down, gain_grad, shift_grad = normalize_back(grad, unit, inverse, gain[...])
            top = grad_out[pl.ds(pl.multiple_of(core * half + ch * chunk + at, 16), 32), :]
            total = top.astype(jnp.float32) + down
            grad_res[here, :] = total
            grad_top[pl.ds(pl.multiple_of(core * half + ch * chunk + at, 16), 32), :] = total.astype(jnp.bfloat16)
            norm_grads[0:1, :] += gain_grad[None]
            norm_grads[1:2, :] += shift_grad[None]

        by_rows(chunk, 32, rows)
        give("top", grad_top, ch).start()

    def weight_grad(out, left, right, first):
        def body(i, _):
            at = pl.ds(pl.multiple_of((first + i) * 128, 128), 128)
            out[at, :] = lax.dot_general(
                left[:, at], right[...], (((0,), (0,)), ((), ())), preferred_element_type=jnp.float32
            ).astype(jnp.bfloat16)
            return 0

        lax.fori_loop(0, out.shape[0] // 256, body, 0)

    def project(first, rows):
        at = pl.ds(pl.multiple_of(first, 16), rows)
        result[at, :] = add_dot(grad_top[at, :], out_all[:width, :], True).astype(jnp.bfloat16)

    for ch in range(chunks):
        exchange.start(ch)
    keeper = core == t // 2

    def fetch(which, act):
        for a, weight in enumerate((expand, reduce)):
            act(pltpu.make_async_copy(ff_weights[2 * which + a], weight, local_sem.at[a]))

    def both_ways(act):
        @pl.when(keeper)
        def _():
            fetch(0, act)

        @pl.when(jnp.logical_not(keeper))
        def _():
            fetch(1, act)

    both_ways(lambda one: one.start())
    count = cot.shape[0]
    side = t % 2
    grad_out[pl.ds(pl.multiple_of(core * half + side * count, 16), count), :] = cot[...]
    grad_out[pl.ds(pl.multiple_of(core * half + (1 - side) * count, 16), count), :] = cot_pair[...]
    block = rows_of(grad_out, core * half, half)
    spread = copy("cot", block, block, (d ^ 1, t))
    spread.start()
    every.start()
    norm_grads[...] = jnp.zeros_like(norm_grads)
    residual(0)
    residual(1)
    both_ways(lambda one: one.wait())
    every.pass_on()
    spread.wait()
    both(0)
    residual(2)
    both(1)
    residual(3)
    both(2)
    every.across()
    back(0)
    both(3)
    weight_grad(reduce_grad, hidden, grad_out, 0)
    back(1)
    weight_grad(reduce_grad, hidden, grad_out, reduce_grad.shape[0] // 256)
    every.hand_over()
    back(2)
    weight_grad(expand_grad, normed, grad_pre, 0)
    back(3)
    project(core * half, half)
    weight_grad(expand_grad, normed, grad_pre, expand_grad.shape[0] // 256)
    for ch in range(chunks):
        copy(
            ("top", ch), *([rows_of(grad_top, (1 - core) * half + ch * chunk, chunk)] * 2), (d ^ 1, t)
        ).wait_recv()
    project((1 - core) * half, half)
    for ch in range(chunks):
        exchange.sent(ch)
        give("normed", normed, ch).wait_send()
        give("top", grad_top, ch).wait_send()
        far(ch).wait_send()
        whole(ch).wait_send()
    every.finish()
    for ch in range(chunks):
        out_copy(ch).wait()

    def out_rows(at):
        near = pl.ds(pl.multiple_of(side * count + at, 32), 32)
        give_at = pl.ds(pl.multiple_of((1 - side) * count + at, 32), 32)
        here = pl.ds(at, 32)
        out_near[here, :] = (
            after[near, :] + out_own[near, :].astype(jnp.float32) + out_land[near, :].astype(jnp.float32)
        )
        out_give[here, :] = (
            out_own[give_at, :].astype(jnp.float32) + out_land[give_at, :].astype(jnp.float32)
        ).astype(jnp.bfloat16)

    by_rows(count, 32, out_rows)


def hidden_step(mixed, out_all, start, gain, shift, cot, cot_pair, next_query, ff_weights, collective_id):
    rows, width = mixed.shape
    half, wide = start.shape
    inner = ff_weights[0].shape[1]
    chunk = half // 4
    bf16, f32 = jnp.bfloat16, jnp.float32
    shape = jax.ShapeDtypeStruct
    vmem = pl.BlockSpec(memory_space=pltpu.VMEM)
    return pl.pallas_call(
        hidden_kernel,
        out_shape=(
            shape((half, wide), f32),
            shape((wide, inner), bf16),
            shape((inner, wide), bf16),
            shape((half, wide), f32),
            shape((rows, wide), bf16),
            shape((rows, width), bf16),
            shape((8, wide), f32),
            shape((4 * next_query.shape[0], next_query.shape[1]), bf16),
            shape(cot.shape, f32),
            shape(cot.shape, bf16),
        ),
        in_specs=[vmem] * 8 + [pl.BlockSpec(memory_space=pl.ANY)] * 4,
        out_specs=(vmem,) * 10,
        scratch_shapes=[
            pltpu.VMEM((3, half, width), bf16),
            pltpu.VMEM((chunk, max(wide, inner)), f32),
            pltpu.VMEM((chunk, max(wide, inner)), f32),
            pltpu.VMEM((half, wide), bf16),
            pltpu.VMEM((half, wide), bf16),
            pltpu.VMEM((half, wide), bf16),
            pltpu.VMEM((half, wide), bf16),
            pltpu.VMEM(ff_weights[0].shape, bf16),
            pltpu.VMEM(ff_weights[1].shape, bf16),
            pltpu.VMEM((half, wide), bf16),
            pltpu.VMEM((half, wide), bf16),
            pltpu.VMEM((half, wide), bf16),
            pltpu.VMEM((rows, wide), bf16),
            pltpu.VMEM((rows, inner), bf16),
            pltpu.VMEM((rows, inner), bf16),
            pltpu.VMEM((rows, wide), bf16),
            pltpu.SemaphoreType.DMA((56,)),
            pltpu.SemaphoreType.DMA((56,)),
            pltpu.SemaphoreType.DMA((2,)),
        ],
        compiler_params=pltpu.CompilerParams(
            collective_id=collective_id, has_side_effects=True, vmem_limit_bytes=60 << 20
        ),
        cost_estimate=pl.CostEstimate(flops=50_000_000_000, bytes_accessed=16_000_000, transcendentals=0),
        name="hidden_step",
    )(mixed, out_all, start, gain[None], shift[None], cot, cot_pair, next_query, *ff_weights)


def on_device(
    tokens,
    encoder_states,
    tok_lengths,
    enc_lengths,
    pad_mask,
    first_gain,
    first_shift,
    causal_query,
    causal_key,
    causal_value,
    causal_out,
    second_gain,
    second_shift,
    cross_query,
    cross_key,
    cross_value,
    cross_out,
    third_gain,
    third_shift,
    expand_weight,
    reduce_weight,
    cotangent,
):
    place = Place()
    width = causal_query.shape[1]
    length = pad_mask.shape[0]
    frames = encoder_states.shape[0]

    def of_group(value):
        return jnp.where(place.keeper, value, place.swap(value, 1, 0))

    def half_rows(quarter):
        return place.ordered(quarter, place.swap(quarter, 0, 1), place.side)

    def quarter_of(half):
        return place.part(half, place.side, 2)

    tok_lengths, enc_lengths, pad_mask = of_group(tok_lengths), of_group(enc_lengths), of_group(pad_mask)
    block_q, block_k = 256, 512
    token_seg, frame_seg, key_seg, self_lo, self_hi, cross_lo, cross_hi = ranges(
        tok_lengths[0], enc_lengths[0], pad_mask, length, frames, block_q, block_k
    )
    self_keys = jnp.stack([token_seg, key_seg] + [token_seg] * 6)
    cross_keys = jnp.stack([frame_seg] * 8)
    seg_col, seg_row = token_seg[:, None], token_seg[None, :]

    tokens_half, first_all, query, keyed, valued, moved, causal_out_perm, cross_out_perm, encoder, expand_piece = start_layer(
        tokens,
        first_gain,
        first_shift,
        (causal_query, causal_key, causal_value),
        causal_out,
        cross_out,
        encoder_states,
        expand_weight,
        1,
    )
    causal_out_here = causal_out_perm[:width]
    hidden_width = expand_weight.shape[1]
    expand_moved = lax.all_gather(expand_piece, "dp", axis=0, tiled=True)
    reduce_piece = place.part(reduce_weight, place.d, place.dp)
    reduce_piece, query = lax.optimization_barrier((reduce_piece, query))
    reduce_piece = place.swap(reduce_piece, 0, 2)

    mixed, self_logsum = attend_fwd(
        query, keyed, valued, seg_col, self_keys, self_lo, self_hi, True, block_q, block_k
    )
    mixed, reduce_piece, cot_here = lax.optimization_barrier((mixed, reduce_piece, cotangent))
    reduce_moved = lax.all_gather(reduce_piece, "dp", axis=0, tiled=True)
    cot_here = place.home(cot_here)
    after_self, second_all, cquery, cross_moved = forward_step(
        mixed,
        causal_out_perm,
        tokens_half,
        second_gain,
        second_shift,
        (cross_query, cross_key, cross_value),
        2,
    )
    cquery, cot_here = lax.optimization_barrier((cquery, cot_here))
    cot_pair = place.swap(cot_here, 0, 1)
    ckeyed = times(encoder, cross_moved[1]).astype(jnp.bfloat16)
    cvalued = times(encoder, cross_moved[2]).astype(jnp.bfloat16)
    cross_weight = jnp.concatenate([cross_moved[1], cross_moved[2]], axis=1)
    first_weight = jnp.concatenate([moved[0], moved[1], moved[2]], axis=1)
    cmixed, cross_logsum = attend_fwd(
        cquery, ckeyed, cvalued, seg_col, cross_keys, cross_lo, cross_hi, False, block_q, block_k
    )
    after_cross, expand_grad, reduce_grad, grad_res, grad_top2, grad_cmixed, third_grads, cross_query_every, out_near, out_give = hidden_step(
        cmixed, cross_out_perm, after_self, third_gain, third_shift, cot_here, cot_pair, cross_query,
        (expand_weight, reduce_weight, expand_moved, reduce_moved), 3
    )
    third_gain_grad, third_shift_grad = third_grads[0], third_grads[1]
    out_far = place.swap(out_give, 0, 1)

    cross_out_grad = along_rows(cmixed, grad_top2)
    expand_grad, reduce_grad = place.sum_columns(expand_grad, 0), place.sum_columns(reduce_grad, 1)
    grad_cquery, grad_cross_in = attend_bwd(
        cquery, ckeyed, cvalued, cmixed, grad_cmixed, cross_logsum, seg_row, cross_keys.T,
        cross_lo, cross_hi, False, block_q, block_k,
    )
    bf16 = jnp.bfloat16
    cross_grad = along_rows(encoder, grad_cross_in).astype(bf16)
    cross_grads = jnp.concatenate(
        [cross_grad[:, :width], cross_grad[:, width:], along_rows(second_all, grad_cquery).astype(bf16)]
    )
    cross_grads = place.sum_columns(cross_grads, 1)
    encoder_term = against(grad_cross_in, cross_weight).astype(bf16)
    grad_res, grad_top, grad_mixed, second_grads, output, encoder_near, encoder_give = backward_step(
        grad_cquery, cross_query_every, after_self, second_gain, grad_res, causal_out_here, out_near, out_far, encoder_term, 4
    )
    encoder_far = place.swap(encoder_give, 0, 1)
    second_gain_grad, second_shift_grad = second_grads[0], second_grads[1]
    causal_out_grad = along_rows(mixed, grad_top)
    grad_mixed, expand_grad, reduce_grad = lax.optimization_barrier((grad_mixed, expand_grad, reduce_grad))
    expand_far, reduce_far = place.swap(expand_grad, 0, 2, False), place.swap(reduce_grad, 0, 2, False)
    (grad_in,) = attend_bwd(
        query, keyed, valued, mixed, grad_mixed, self_logsum, seg_row, self_keys.T,
        self_lo, self_hi, True, block_q, block_k,
    )
    causal_grad = along_rows(first_all, grad_in).astype(bf16)
    first_term = against(grad_in, first_weight)
    first_rows = (first_all.astype(jnp.float32) - first_shift) / first_gain
    first_gain_grad = jnp.sum(first_term * first_rows, axis=0)
    first_shift_grad = jnp.sum(first_term, axis=0)
    deep = causal_query.shape[0]
    once = (place.side == 0).astype(jnp.float32)
    none = jnp.zeros_like(first_gain_grad)
    norm_grads = jnp.stack(
        [
            first_gain_grad,
            first_shift_grad,
            second_gain_grad * once,
            second_shift_grad * once,
            third_gain_grad * once,
            third_shift_grad * once,
            none,
            none,
        ]
    )
    *sums, tokens_grad, encoder_grad, norm_grads = sum_all(
        [
            expand_grad,
            reduce_grad,
            cross_grads,
            jnp.concatenate([cross_out_grad.astype(bf16), causal_out_grad.astype(bf16)]),
            causal_grad,
        ],
        (expand_far, reduce_far),
        [
            (4, 0, deep // 2, 0, 0),
            (4, deep // 2, deep // 2, 1, 0),
            *(
                [(3, 0, width, 0, 0), (3, width, width, 1, 0)]
                if width % (8 * place.dp) == 0
                else [(3, 0, 2 * width, 0, 0)]
            ),
            (2, 0, 3 * deep, 1, 1),
            (0, 0, expand_weight.shape[0], 0, 2),
            (1, 0, reduce_weight.shape[0], 1, 2),
        ],
        first_term.astype(bf16),
        (encoder_near, encoder_far),
        norm_grads,
        tokens_half,
        grad_res,
        first_gain,
        0,
    )
    (
        first_gain_grad,
        first_shift_grad,
        second_gain_grad,
        second_shift_grad,
        third_gain_grad,
        third_shift_grad,
    ) = (norm_grads[i] for i in range(6))
    sums = [total.astype(jnp.float32) if at != 2 and at != 3 else total for at, total in enumerate(sums)]
    expand_grad, reduce_grad = sums[:2]
    cross_key_grad, cross_value_grad, cross_query_grad = (
        sums[2][i * deep : (i + 1) * deep].astype(jnp.float32) for i in range(3)
    )
    cross_out_grad, causal_out_grad = sums[3][:width].astype(jnp.float32), sums[3][width:].astype(jnp.float32)
    causal_query_grad, causal_key_grad, causal_value_grad = (
        sums[4][:, i * width : (i + 1) * width] for i in range(3)
    )
    return (
        output,
        tokens_grad,
        encoder_grad,
        first_gain_grad,
        first_shift_grad,
        causal_query_grad,
        causal_key_grad,
        causal_value_grad,
        causal_out_grad,
        second_gain_grad,
        second_shift_grad,
        cross_query_grad,
        cross_key_grad,
        cross_value_grad,
        cross_out_grad,
        third_gain_grad,
        third_shift_grad,
        expand_grad,
        reduce_grad,
    )


def solution(mesh):
    in_specs = (
        P(("dp", "tensor"), None),
        P("dp", None),
        P("dp", None),
        P("dp", None),
        P("dp"),
        P(),
        P(),
        P(None, "tensor"),
        P(None, "tensor"),
        P(None, "tensor"),
        P("tensor", None),
        P(),
        P(),
        P(None, "tensor"),
        P(None, "tensor"),
        P(None, "tensor"),
        P("tensor", None),
        P(),
        P(),
        P(None, "tensor"),
        P("tensor", None),
        P(("dp", "tensor"), None),
    )
    out_specs = (
        P(("dp", "tensor"), None),
        P(("dp", "tensor"), None),
        P(("dp", "tensor"), None),
        P(),
        P(),
        P(None, "tensor"),
        P(None, "tensor"),
        P(None, "tensor"),
        P("tensor", None),
        P(),
        P(),
        P(None, "tensor"),
        P(None, "tensor"),
        P(None, "tensor"),
        P("tensor", None),
        P(),
        P(),
        P(None, "tensor"),
        P("tensor", None),
    )
    return jax.shard_map(
        on_device, mesh=mesh, in_specs=in_specs, out_specs=out_specs, check_vma=False
    )
```

```python
import functools

import jax
import jax.numpy as jnp
from jax import lax
from jax.experimental import pallas as pl
from jax.experimental.pallas import tpu as pltpu
from jax.sharding import PartitionSpec as P

HEAD_DIM = 64


eps = 1e-05
tanh_coeff = 0.7978845608
cubic_coeff = 0.044715


def smooth_gate(values):
    inner = jnp.tanh(tanh_coeff * (values + cubic_coeff * values * values * values))
    return 0.5 * values * (1.0 + inner)


def smooth_slope(values):
    inner = jnp.tanh(tanh_coeff * (values + cubic_coeff * values * values * values))
    return 0.5 * (1.0 + inner) + 0.5 * values * (1.0 - inner * inner) * tanh_coeff * (
        1.0 + 3.0 * cubic_coeff * values * values
    )


BF=jnp.bfloat16
F32=jnp.float32

def head_mask(rows, width, h):
    lane = lax.broadcasted_iota(jnp.int32, (rows, width), 1)
    return (lane // HEAD_DIM) == h

def dot(a,b,ca,cb):
    return lax.dot_general(a,b,(((ca,),(cb,)),((),())),preferred_element_type=F32)

def fwd_kernel(causal, heads, bq, bk, lo_ref, hi_ref, q_ref, kv_ref, rs_ref, ks_ref, o_ref, lse_ref, acc):
    count, width = q_ref.shape
    def one(qb, _):
        q0 = pl.multiple_of(qb*bq, bq)
        qv = q_ref[pl.ds(q0,bq),:] * BF(HEAD_DIM**-0.5)
        rseg = rs_ref[pl.ds(q0,bq),0:1]
        qm = [jnp.where(head_mask(bq,width,h), qv, BF(0)) for h in range(heads)]
        acc[...] = jnp.zeros_like(acc)
        lane = lax.broadcasted_iota(jnp.int32,(bq,128),1)
        def inner(kb, carry):
            k0 = pl.multiple_of(kb*bk, bk)
            kv = kv_ref[pl.ds(k0,bk),:width]
            vv = kv_ref[pl.ds(k0,bk),width:]
            kseg = ks_ref[0:1,pl.ds(k0,bk)]
            if causal:
                kpad = ks_ref[1:2,pl.ds(k0,bk)]
                ri = lax.broadcasted_iota(jnp.int32,(bq,bk),0)+q0
                ci = lax.broadcasted_iota(jnp.int32,(bq,bk),1)+k0
                ok = ((rseg==kpad)&(ci<=ri))|(ci==ri)
            else:
                ok = rseg==kseg
            ms, ls = carry
            new_m, new_l = [], []
            parts=None
            alphas=[]
            for h in range(heads):
                s = dot(qm[h],kv,1,1)
                s = jnp.where(ok,s,-1e30)
                m = jnp.maximum(ms[h], jnp.max(s,axis=1,keepdims=True))
                p = jnp.exp(s-m)
                al = jnp.exp(ms[h]-m)
                new_m.append(m); new_l.append(ls[h]*al+jnp.sum(p,axis=1,keepdims=True))
                vm = jnp.where(head_mask(bk,width,h),vv,BF(0))
                t = dot(p.astype(BF),vm,1,0)
                parts = t if parts is None else parts+t
                alphas.append(al)
            lane2 = lax.broadcasted_iota(jnp.int32,(bq,width),1)//HEAD_DIM
            sc = alphas[heads-1]
            for h in range(heads-1):
                sc = jnp.where(lane2==h, alphas[h], sc)
            acc[...] = acc[...]*sc + parts
            return (tuple(new_m),tuple(new_l))
        init = (tuple(jnp.full((bq,1),-1e30,F32) for _ in range(heads)), tuple(jnp.zeros((bq,1),F32) for _ in range(heads)))
        ms, ls = lax.fori_loop(lo_ref[qb], hi_ref[qb], inner, init)
        lane2 = lax.broadcasted_iota(jnp.int32,(bq,width),1)//HEAD_DIM
        inv = [1.0/l for l in ls]
        sc = inv[heads-1]
        for h in range(heads-1):
            sc = jnp.where(lane2==h, inv[h], sc)
        o_ref[pl.ds(q0,bq),:] = (acc[...]*sc).astype(BF)
        st = jnp.zeros((bq,128),F32)
        for h in range(heads):
            st = jnp.where(lane==h, ms[h]+jnp.log(ls[h]), st)
        stt = jnp.transpose(st)
        lse_ref[:,pl.ds(q0,bq)] = stt[0:8,:]
        return 0
    lax.fori_loop(0,count//bq,one,0)

def attend_fwd(q,kv,rseg,kseg,lo,hi,causal,bq=256,bk=256):
    count,width=q.shape
    heads=width//HEAD_DIM
    vm=pl.BlockSpec(memory_space=pltpu.VMEM); sm=pl.BlockSpec(memory_space=pltpu.SMEM)
    return pl.pallas_call(functools.partial(fwd_kernel,causal,heads,bq,bk),
        out_shape=(jax.ShapeDtypeStruct((count,width),BF),jax.ShapeDtypeStruct((8,count),F32)),
        in_specs=[sm,sm,vm,vm,vm,vm],out_specs=(vm,vm),
        scratch_shapes=[pltpu.VMEM((bq,width),F32)],
        compiler_params=pltpu.CompilerParams(vmem_limit_bytes=40<<20),
        cost_estimate=pl.CostEstimate(flops=22_000_000_000, bytes_accessed=8_000_000, transcendentals=0),
        name="attend_fwd",
    )(lo,hi,q,kv,rseg,kseg)

def bwd_kernel(causal, heads, bq, bk, lo_ref, hi_ref, q_ref, kv_ref, o_ref, do_ref, lse_ref, rs_ref, ks_ref,
               dq_ref, dkv_ref, dka, dva, qm, dom, dqa):
    count,width=q_ref.shape
    dka[...]=jnp.zeros_like(dka); dva[...]=jnp.zeros_like(dva)
    def one(qb,_):
        q0=pl.multiple_of(qb*bq,bq)
        qv=q_ref[pl.ds(q0,bq),:]*BF(HEAD_DIM**-0.5)
        dov=do_ref[pl.ds(q0,bq),:]
        prod=dov.astype(F32)*o_ref[pl.ds(q0,bq),:].astype(F32)
        row=lax.broadcasted_iota(jnp.int32,(8,width),0); col=lax.broadcasted_iota(jnp.int32,(8,width),1)//HEAD_DIM
        sel=(row==col).astype(F32)
        delta=lax.dot_general(sel,prod,(((1,),(1,)),((),())),precision=lax.Precision.HIGHEST,preferred_element_type=F32)
        for h in range(heads):
            hm=head_mask(bq,width,h)
            qm[pl.ds(h*bq,bq),:]=jnp.where(hm,qv,BF(0))
            dom[pl.ds(h*bq,bq),:]=jnp.where(hm,dov,BF(0))
        dqa[...]=jnp.zeros_like(dqa)
        rseg=rs_ref[0:1,pl.ds(q0,bq)]
        lse=lse_ref[:,pl.ds(q0,bq)]
        def inner(kb,_):
            k0=pl.multiple_of(kb*bk,bk)
            kv=kv_ref[pl.ds(k0,bk),:width]; vv=kv_ref[pl.ds(k0,bk),width:]
            if causal:
                kpad=ks_ref[pl.ds(k0,bk),1:2]
                ri=lax.broadcasted_iota(jnp.int32,(bk,bq),1)+q0
                ci=lax.broadcasted_iota(jnp.int32,(bk,bq),0)+k0
                ok=((rseg==kpad)&(ci<=ri))|(ci==ri)
            else:
                ok=rseg==ks_ref[pl.ds(k0,bk),0:1]
            ps=[];dss=[]
            dq=None
            for h in range(heads):
                st=dot(kv,qm[pl.ds(h*bq,bq),:],1,1)
                p=jnp.where(ok,jnp.exp(st-lse[h:h+1,:]),0.0)
                dp=dot(vv,dom[pl.ds(h*bq,bq),:],1,1)
                ds=(p*(dp-delta[h:h+1,:])).astype(BF)
                ps.append(p.astype(BF)); dss.append(ds)
                km=jnp.where(head_mask(bk,width,h),kv,BF(0))
                t=dot(ds,km,0,0)
                dq=t if dq is None else dq+t
            dqa[...]+=dq
            pcat=jnp.concatenate(ps,axis=1); dcat=jnp.concatenate(dss,axis=1)
            dva[pl.ds(k0,bk),:]+=dot(pcat,dom[...],1,0)
            dka[pl.ds(k0,bk),:]+=dot(dcat,qm[...],1,0)
            return 0
        lax.fori_loop(lo_ref[qb],hi_ref[qb],inner,0)
        dq_ref[pl.ds(q0,bq),:width]=(dqa[...]*(HEAD_DIM**-0.5)).astype(BF)
        return 0
    lax.fori_loop(0,count//bq,one,0)
    out_ref = dq_ref if dkv_ref is None else dkv_ref
    first = out_ref.shape[1] - 2*width
    out_ref[:,first:first+width]=dka[...].astype(BF)
    out_ref[:,first+width:]=dva[...].astype(BF)

def attend_bwd(q,kv,o,do,lse,rseg,kseg,lo,hi,causal,bq=256,bk=256):
    count,width=q.shape; keys=kv.shape[0]
    heads=width//HEAD_DIM
    vm=pl.BlockSpec(memory_space=pltpu.VMEM); sm=pl.BlockSpec(memory_space=pltpu.SMEM)
    def kernel(*refs):
        rest=refs if not causal else refs[:10]+(None,)+refs[10:]
        bwd_kernel(causal,heads,bq,bk,*rest)
    shape=jax.ShapeDtypeStruct
    out_shape=(shape((count,3*width),BF),) if causal else (shape((count,width),BF),shape((keys,2*width),BF))
    return pl.pallas_call(kernel,
        out_shape=out_shape,
        in_specs=[sm,sm]+[vm]*7,out_specs=(vm,)*len(out_shape),
        scratch_shapes=[pltpu.VMEM((keys,width),F32),pltpu.VMEM((keys,width),F32),pltpu.VMEM((heads*bq,width),BF),pltpu.VMEM((heads*bq,width),BF),pltpu.VMEM((bq,width),F32)],
        compiler_params=pltpu.CompilerParams(vmem_limit_bytes=40<<20),
        cost_estimate=pl.CostEstimate(flops=30_000_000_000, bytes_accessed=8_000_000, transcendentals=0),
        name="attend_bwd",
    )(lo,hi,q,kv,o,do,lse,rseg,kseg)

def ranges(tok_lengths, enc_lengths, pad, count, frames, bq, bk):
    tend=jnp.cumsum(tok_lengths,dtype=jnp.int32); eend=jnp.cumsum(enc_lengths,dtype=jnp.int32)
    places=jnp.arange(count,dtype=jnp.int32)
    tseg=jnp.sum((places[:,None]>=tend[None,:]).astype(jnp.int32),axis=1)
    eseg=jnp.sum((jnp.arange(frames,dtype=jnp.int32)[:,None]>=eend[None,:]).astype(jnp.int32),axis=1)
    starts=jnp.arange(count//bq,dtype=jnp.int32)*bq
    first=tseg[::bq]; last=tseg[bq-1::bq]
    onehot=lambda s:(s[:,None]==jnp.arange(tend.shape[0])[None,:]).astype(jnp.int32)
    pick=lambda arr,s: jnp.sum(onehot(s)*arr[None,:],axis=1)
    tstart=tend-tok_lengths; estart=eend-enc_lengths
    slo=pick(tstart,first)//bk; shi=(starts+bq+bk-1)//bk
    clo=pick(estart,first)//bk; chi=(pick(eend,last)+bk-1)//bk
    kpad=jnp.where(pad==1,tseg,-1)
    return tseg,eseg,kpad,slo,shi,clo,chi


def along_rows(left, right):
    return lax.dot_general(
        left, right, (((0,), (0,)), ((), ())), preferred_element_type=jnp.float32
    )


def against(left, weight):
    return lax.dot_general(
        left, weight, (((1,), (1,)), ((), ())), preferred_element_type=jnp.float32
    )


def times(left, weight):
    return jnp.dot(left, weight, preferred_element_type=jnp.float32)


def moments(rows):
    centred = rows - jnp.mean(rows, axis=1, keepdims=True)
    inverse = lax.rsqrt(jnp.mean(centred * centred, axis=1, keepdims=True) + eps)
    return centred * inverse, inverse


def normalize_back(grad_out, unit, inverse, gain):
    scaled = grad_out * gain
    inner = (
        scaled
        - jnp.mean(scaled, axis=1, keepdims=True)
        - unit * jnp.mean(scaled * unit, axis=1, keepdims=True)
    )
    return (inner * inverse, jnp.sum(grad_out * unit, axis=0), jnp.sum(grad_out, axis=0))


class Place:
    def __init__(self):
        self.dp = lax.axis_size("dp")
        self.tensor = lax.axis_size("tensor")
        self.d = lax.axis_index("dp")
        self.t = lax.axis_index("tensor")
        self.core = self.d % 2
        self.half = self.t // 2
        self.side = self.t % 2
        self.keeper = self.core == self.half
        self.shard = jnp.where(self.keeper, self.t, self.t ^ 2)

    def swap(self, value, d_flip, t_flip, only=None):
        pairs = []
        for d in range(self.dp):
            for t in range(self.tensor):
                keeper = d % 2 == t // 2
                if only is None or only == keeper:
                    pairs.append((d * self.tensor + t, (d ^ d_flip) * self.tensor + (t ^ t_flip)))
        return lax.ppermute(value, ("dp", "tensor"), pairs)

    def home(self, value):
        return jnp.where(self.keeper, value, self.swap(value, 1, 2, False))

    def ordered(self, mine, other, which):
        return jnp.where(
            which == 0, jnp.concatenate([mine, other]), jnp.concatenate([other, mine])
        )

    def part(self, value, which, parts):
        size = value.shape[0] // parts
        return lax.dynamic_slice_in_dim(value, which * size, size, 0)

    def both_cores(self, half_rows):
        return self.ordered(half_rows, self.swap(half_rows, 1, 0), self.core)

    def spread_columns(self, value):
        near, far = self.part(value, self.core, 2), self.part(value, 1 - self.core, 2)
        return jnp.concatenate(
            [near, self.swap(far, 1, 0), self.swap(near, 0, 1), self.swap(far, 1, 1)], axis=1
        )

    def order(self):
        return [self.shard, self.shard ^ 2, self.shard ^ 1, self.shard ^ 3]

    def sum_half(self, value):
        near, far = self.part(value, self.core, 2), self.part(value, 1 - self.core, 2)
        return near.astype(jnp.float32) + self.swap(far.astype(jnp.bfloat16), 1, 0).astype(jnp.float32)

    def sum_group_half(self, value):
        mine = self.sum_half(value).astype(jnp.bfloat16)
        return mine.astype(jnp.float32) + self.swap(mine, 0, 1).astype(jnp.float32)

    def sum_group_quarter(self, value):
        mine = self.sum_half(value)
        near, far = self.part(mine, self.side, 2), self.part(mine, 1 - self.side, 2)
        return near + self.swap(far.astype(jnp.bfloat16), 0, 1).astype(jnp.float32)

    def sum_columns(self, grad, order):
        columns = self.dp // 2
        bits = columns.bit_length() - 1
        turned = [sum(((c >> b) & 1) << (bits - 1 - b) for b in range(bits)) for c in range(columns)]
        groups = [[2 * (turned[c] if order == 0 else c) + core for c in range(columns)] for core in range(2)]
        return lax.psum_scatter(
            grad.astype(jnp.bfloat16), "dp", scatter_dimension=0, axis_index_groups=groups, tiled=True
        )

    def cross_planes(self, grads):
        return [
            (grad.astype(jnp.float32) + self.swap(grad, 0, 2, False).astype(jnp.float32)).astype(jnp.bfloat16)
            for grad in grads
        ]

    def moved_weight(self, weight):
        piece = self.swap(self.part(weight, self.d, self.dp), 0, 2)
        return jnp.where(self.keeper, weight, lax.all_gather(piece, "dp", axis=0, tiled=True))

    def whole_weight(self, weight):
        piece = self.part(weight, self.d, self.dp)
        every = lax.all_gather(piece, ("dp", "tensor"), axis=0, tiled=False)
        every = every.reshape((self.dp, self.tensor) + piece.shape)
        return jnp.swapaxes(every, 0, 1).reshape((self.tensor,) + weight.shape)


class Copies:
    def __init__(self, send_sem, recv_sem):
        self.send_sem, self.recv_sem, self.known = send_sem, recv_sem, {}

    def __call__(self, name, src, dst, device):
        at = self.known.setdefault(name, len(self.known))
        return pltpu.make_async_remote_copy(
            src_ref=src,
            dst_ref=dst,
            send_sem=self.send_sem.at[at],
            recv_sem=self.recv_sem.at[at],
            device_id=device,
            device_id_type=pl.DeviceIdType.MESH,
        )


def greet(devices):
    barrier = pltpu.get_barrier_semaphore()
    for device in devices:
        pl.semaphore_signal(
            barrier, inc=1, device_id=device, device_id_type=pl.DeviceIdType.MESH
        )
    pl.semaphore_wait(barrier, len(devices))


def rows_of(ref, start, size, step=16):
    return ref.at[pl.ds(pl.multiple_of(start, step), size)]


def norm_rows(src, src_first, dst, dst_first, rows, gain, shift):
    chunk = 64

    def body(i, _):
        at = i * chunk
        x = src[pl.ds(pl.multiple_of(src_first + at, 16), chunk), :].astype(jnp.float32)
        unit, inverse = moments(x)
        dst[pl.ds(pl.multiple_of(dst_first + at, 16), chunk), :] = (
            unit * gain[...] + shift[...]
        ).astype(jnp.bfloat16)
        return 0

    lax.fori_loop(0, rows // chunk, body, 0)


def sum_kernel(dp, arrays, units, span, *refs):
    it = iter(refs)
    take = lambda count: [next(it) for _ in range(count)]
    ins = take(arrays)
    fars = take(2)
    part, home_near, home_far, small_in, tokens, grad_in, gain = take(7)
    outs = take(arrays)
    row_out, home_out, small_out = take(3)
    bits = [b for b in (2, 4, 8, 16, 32, 64) if b < dp]
    steps = len(bits)
    land, hold = [], []
    for unit in units:
        hold.append(take(0 if unit[4] else steps))
        land.append(take((steps + 1, 1, 0)[unit[4]]))
    row_land, row_hold = take(2), take(2)
    (home_hold,) = take(1)
    home_half = home_hold.shape[0] // 2
    small_hold, small_land, small_send, small_recv, row_send, row_recv, send_sem, recv_sem = take(8)
    d, t = lax.axis_index("dp"), lax.axis_index("tensor")
    core, side = d % 2, t % 2
    keeper = core == t // 2
    other = jnp.logical_not(keeper)
    MESH = pl.DeviceIdType.MESH

    around = [(d ^ b, t) for b in bits] + [(d ^ 1, t), (d, t ^ 2), (d, t ^ 1)]
    greet(around + [(d ^ 1, t ^ 2)])

    def my(bit):
        return (d // bit) % 2

    def order(u):
        return bits if units[u][3] == 0 else bits[::-1]

    def source(u, step):
        array, first, rows, _, summed = units[u]
        if summed:
            return ins[array], first >> steps
        return (ins[array], first) if step == 0 else (hold[u][step - 1], 0)

    def copy(u, stage, src, dst, device):
        return pltpu.make_async_remote_copy(
            src_ref=src, dst_ref=dst, send_sem=send_sem.at[u, stage], recv_sem=recv_sem.at[u, stage],
            device_id=device, device_id_type=MESH,
        )

    def quarter(u):
        place = units[u][1]
        for step, bit in enumerate(order(u)):
            place = place + my(bit) * (units[u][2] >> (step + 1))
        return place

    def scatter_copy(u, step):
        ref, first = source(u, step)
        size = units[u][2] >> (step + 1)
        bit = order(u)[step]
        return copy(u, step, rows_of(ref, first + (1 - my(bit)) * size, size), land[u][step], (d ^ bit, t))

    def plane_copy(u):
        ref, first = source(u, steps)
        return copy(u, steps, rows_of(ref, first, units[u][2] >> steps), land[u][-1], (d, t ^ 2))

    def gather_copy(u, step):
        array, first, rows = units[u][:3]
        bit = order(u)[steps - 1 - step]
        size = rows >> (steps - step)
        start = quarter(u)
        for back in range(step):
            start = start - my(order(u)[steps - 1 - back]) * (rows >> (steps - back))
        block = rows_of(outs[array], start, size)
        return copy(u, steps + 1 + step, block, block, (d ^ bit, t))

    def core_copy(u):
        array, first, rows = units[u][:3]
        block = outs[array].at[pl.ds(first, rows)]
        return copy(u, 2 * steps + 1, block, block, (d ^ 1, t))

    def add(dst, dst_first, left, left_first, right, rows):
        chunk = min(rows, 32)

        def body(i, _):
            at = i * chunk
            a = left[pl.ds(pl.multiple_of(left_first + at, 16), chunk), :].astype(jnp.float32)
            b = right[pl.ds(pl.multiple_of(at, 16), chunk), :].astype(jnp.float32)
            dst[pl.ds(pl.multiple_of(dst_first + at, 16), chunk), :] = (a + b).astype(jnp.bfloat16)
            return 0

        lax.fori_loop(0, rows // chunk, body, 0)

    def begin(u, stage):
        if stage < steps:
            scatter_copy(u, stage).start()
        elif stage == steps:

            @pl.when(other)
            def _():
                plane_copy(u).start()
        else:

            @pl.when(keeper)
            def _():
                (gather_copy(u, stage - steps - 1) if stage <= 2 * steps else core_copy(u)).start()

    def end(u, stage):
        array, first, rows = units[u][:3]
        if stage < steps:
            one = scatter_copy(u, stage)
            one.wait_recv()
            ref, row = source(u, stage)
            size = rows >> (stage + 1)
            add(hold[u][stage], 0, ref, row + my(order(u)[stage]) * size, land[u][stage], size)
            one.wait_send()
        elif stage == steps and units[u][4] == 2:

            @pl.when(keeper)
            def _():
                size = rows >> steps
                ref, row = source(u, steps)
                add(outs[array], quarter(u), ref, row, fars[array], size)
        elif stage == steps:

            @pl.when(other)
            def _():
                plane_copy(u).wait_send()

            @pl.when(keeper)
            def _():
                plane_copy(u).wait_recv()
                ref, row = source(u, steps)
                add(outs[array], quarter(u), ref, row, land[u][-1], rows >> steps)
        elif stage <= 2 * steps:

            @pl.when(keeper)
            def _():
                gather_copy(u, stage - steps - 1).wait()
        else:

            @pl.when(keeper)
            def _():
                core_copy(u).wait_send()

            @pl.when(other)
            def _():
                core_copy(u).wait_recv()

    def row_copy(stage):
        if stage == 0:
            src, dst, device = rows_of(part, (1 - core) * 2 * span, 2 * span), row_land[0], (d ^ 1, t)
        elif stage == 1:
            src, dst, device = rows_of(row_hold[0], (1 - side) * span, span), row_land[1], (d, t ^ 1)
        elif stage == 2:
            src, dst, device = row_hold[1], row_out, (d ^ 1, t ^ 2)
        else:
            rows = pl.ds((stage % 3) * home_half, home_half)
            src, dst, device = home_hold.at[rows], home_out.at[rows], (d ^ 1, t ^ 2)
        return pltpu.make_async_remote_copy(
            src_ref=src, dst_ref=dst, send_sem=row_send.at[stage], recv_sem=row_recv.at[stage],
            device_id=device, device_id_type=MESH,
        )

    def row_half():
        row_copy(0).wait()
        add(row_hold[0], 0, part, core * 2 * span, row_land[0], 2 * span)
        row_copy(1).start()

    def to_owner(hold_ref, out_ref, stage):
        @pl.when(keeper)
        def _():
            out_ref[...] = hold_ref[...]

        @pl.when(other)
        def _():
            row_copy(stage).start()

    def row_home():
        row_copy(1).wait()

        def body(i, _):
            at = pl.ds(pl.multiple_of(i * 32, 32), 32)
            here = pl.ds(pl.multiple_of(side * span + i * 32, 32), 32)
            total = row_hold[0][here, :].astype(jnp.float32) + row_land[1][at, :].astype(jnp.float32)
            unit, inverse = moments(tokens[here, :].astype(jnp.float32))
            total = grad_in[here, :] + normalize_back(total, unit, inverse, gain[...])[0]
            row_hold[1][at, :] = total.astype(jnp.bfloat16)
            return 0

        lax.fori_loop(0, span // 32, body, 0)
        to_owner(row_hold[1], row_out, 2)

    def small_copy(step):
        return pltpu.make_async_remote_copy(
            src_ref=small_hold.at[step], dst_ref=small_land.at[step], send_sem=small_send.at[step],
            recv_sem=small_recv.at[step], device_id=around[step], device_id_type=MESH,
        )

    def small_step(step):
        small_copy(step).wait()
        total = small_hold[step] + small_land[step]
        if step + 1 < len(around):
            small_hold[step + 1] = total
            small_copy(step + 1).start()
        else:
            small_out[...] = total

    last = 2 * steps + 2
    first_stage = (0, steps, steps + 1)
    turns = [
        list(range(last + 1)),
        list(range(steps + 3)),
        list(range(steps + 2)),
    ]

    def tick(now):
        for state in (0, 1, 2):
            if now not in turns[state]:
                continue
            turn = turns[state].index(now)
            stage = first_stage[state] + turn
            for u in range(len(units)):
                if units[u][4] != state:
                    continue
                if state == 2 and turn == 0:
                    end(u, steps)
                if turn > 0:
                    end(u, stage - 1)
                if stage < last:
                    begin(u, stage)

    small_hold[0] = small_in[...]
    small_copy(0).start()
    row_copy(0).start()
    tick(0)
    add(home_hold, 0, home_near, 0, home_far, home_hold.shape[0])
    to_owner(home_hold, home_out, 3)
    row_half()
    small_step(0)
    row_home()
    for now in range(1, last + 1):
        tick(now)
        if now < len(around):
            small_step(now)
        if now == steps + 1:

            @pl.when(other)
            def _():
                row_copy(4).start()


    @pl.when(other)
    def _():
        row_copy(2).wait()
        row_copy(3).wait()
        row_copy(4).wait()


def sum_all(grads, fars, units, part, home, norm_grads, tokens, grad_in, gain, collective_id):
    dp = lax.axis_size("dp")
    steps = 0
    while 2 << steps < dp:
        steps += 1
    bf16, f32 = jnp.bfloat16, jnp.float32
    shapes = [(grad.shape[0], grad.shape[1]) for grad in grads]
    scratch = []
    for array, first, rows, side, done in units:
        width = grads[array].shape[1]
        if done:
            shapes[array] = (rows, width)
        else:
            scratch += [pltpu.VMEM((rows >> (k + 1), width), bf16) for k in range(steps)] * 2
        if done < 2:
            scratch.append(pltpu.VMEM((rows >> steps, width), bf16))
    stages = 2 * steps + 2
    vmem = pl.BlockSpec(memory_space=pltpu.VMEM)
    span = part.shape[0] // 4
    wide = tokens.shape[1]
    semaphores = pltpu.SemaphoreType.DMA
    return pl.pallas_call(
        functools.partial(sum_kernel, dp, len(grads), units, span),
        out_shape=[jax.ShapeDtypeStruct(shape, bf16) for shape in shapes]
        + [jax.ShapeDtypeStruct((span, wide), bf16), jax.ShapeDtypeStruct(home[0].shape, bf16)]
        + [jax.ShapeDtypeStruct(norm_grads.shape, f32)],
        in_specs=[vmem] * (len(grads) + 9),
        out_specs=[vmem] * (len(grads) + 3),
        scratch_shapes=scratch
        + [pltpu.VMEM((many * span, wide), bf16) for many in (2, 1)] * 2
        + [pltpu.VMEM(home[0].shape, bf16)]
        + [pltpu.VMEM((steps + 3,) + norm_grads.shape, f32)] * 2
        + [semaphores((steps + 3,))] * 2
        + [semaphores((5,))] * 2
        + [semaphores((len(units), stages))] * 2,
        compiler_params=pltpu.CompilerParams(
            collective_id=collective_id, has_side_effects=True, vmem_limit_bytes=60 << 20
        ),
        cost_estimate=pl.CostEstimate(flops=80_000_000_000, bytes_accessed=16_000_000, transcendentals=0),
        name="sum_all",
    )(*grads, *fars, part, *home, norm_grads, tokens, grad_in, gain[None])


class Move:
    def __init__(self, name, copy, sources, moved, d, t):
        self.name, self.copy, self.sources, self.moved = name, copy, sources, moved
        self.d, self.t, self.column = d, t, (d // 2) % 4
        self.keeper = d % 2 == t // 2
        self.other = jnp.logical_not(self.keeper)

    def block(self, ref):
        part = ref.shape[0] // 4
        return rows_of(ref, self.column * part, part)

    def fetch(self, a):
        return self.copy(
            (self.name, a), self.block(self.sources[a]), self.block(self.moved[a]), (self.d, self.t ^ 2)
        )

    def share(self, a, m):
        block = self.block(self.moved[a])
        return self.copy((self.name, a, m), block, block, (self.d ^ (2 * m), self.t))

    def start(self):
        @pl.when(self.keeper)
        def _():
            for a in range(len(self.moved)):
                self.fetch(a).start()

    def relay(self, which):
        @pl.when(self.other)
        def _():
            for a in which:
                self.fetch(a).wait_recv()
                for m in (1, 2, 3):
                    self.share(a, m).start()

    def ready(self, which):
        @pl.when(self.keeper)
        def _():
            for a in which:
                self.moved[a][...] = self.sources[a][...]

        @pl.when(self.other)
        def _():
            for a in which:
                for m in (1, 2, 3):
                    self.share(a, m).wait_recv()

    def finish(self):
        @pl.when(self.keeper)
        def _():
            for a in range(len(self.moved)):
                self.fetch(a).wait_send()

        @pl.when(self.other)
        def _():
            for a in range(len(self.moved)):
                for m in (1, 2, 3):
                    self.share(a, m).wait_send()


class HalfRows:
    def __init__(self, name, copy, rows, half, first, far_first, d, t):
        self.name, self.copy, self.rows, self.half, self.first = name, copy, rows, half, first
        self.far_first = far_first
        self.d, self.t, self.side = d, t, t % 2
        self.keeper = d % 2 == t // 2
        self.other = jnp.logical_not(self.keeper)
        self.count = rows.shape[0]
        self.piece = self.count // 4

    def place(self, s, p):
        return rows_of(self.half, self.first + s * self.count + p * self.piece, self.piece)

    def own(self, p):
        return self.rows.at[pl.ds(p * self.piece, self.piece)]

    def swap(self, p):
        at = rows_of(self.half, self.far_first + self.side * self.count + p * self.piece, self.piece)
        return self.copy((self.name, "swap", p), self.own(p), at, (self.d ^ 1, self.t ^ 2))

    def through(self, p, source):
        return self.copy((self.name, "pass", p), source, self.place(self.side, p), (self.d, self.t ^ 1))

    def start(self):
        @pl.when(self.other)
        def _():
            for p in range(4):
                self.swap(p).start()

        @pl.when(self.keeper)
        def _():
            for p in range(4):
                self.through(p, self.own(p)).start()
            at = pl.multiple_of(self.first + self.side * self.count, 16)
            self.half[pl.ds(at, self.count), :] = self.rows[...]

    def relay(self):
        @pl.when(self.other)
        def _():
            for p in range(4):
                self.swap(p).wait_recv()
                self.through(p, self.place(self.side, p)).start()

    def arrive(self):
        for p in range(4):
            block = self.place(1 - self.side, p)
            self.copy((self.name, "pass", p), block, block, (self.d, self.t ^ 1)).wait_recv()

    def finish(self):
        @pl.when(self.keeper)
        def _():
            for p in range(4):
                self.through(p, self.own(p)).wait_send()

        @pl.when(self.other)
        def _():
            for p in range(4):
                self.swap(p).wait_send()
                self.through(p, self.place(self.side, p)).wait_send()


class Whole:
    def __init__(self, name, copy, source, whole, d, t):
        self.name, self.copy, self.source, self.whole = name, copy, source, whole
        self.d, self.t = d, t
        self.away = jnp.where(d % 2 == t // 2, 0, 1)
        self.rows = source.shape[0]
        self.slim = self.rows // 8
        self.half_at = (d % 2) * (4 * self.slim)
        self.at = self.half_at + ((d // 2) % 4) * self.slim

    def block(self, j):
        return rows_of(self.whole, j * self.rows + self.at, self.slim)

    def far(self):
        return self.copy(
            (self.name, "far"), rows_of(self.source, self.at, self.slim), self.block(self.away), (self.d, self.t ^ 2)
        )

    def near(self, late):
        j = 1 - self.away if late else self.away
        return self.copy((self.name, "near", late), self.block(j), self.block(j + 2), (self.d, self.t ^ 1))

    def level(self, j, m):
        block = rows_of(self.whole, j * self.rows + self.at, self.slim)
        return self.copy((self.name, "level", j, m), block, block, (self.d ^ (2 * m), self.t))

    def hand(self, j):
        return self.copy(
            (self.name, "hand", j),
            rows_of(self.whole, j * self.rows + self.half_at, 4 * self.slim),
            rows_of(self.whole, (j ^ 1) * self.rows + self.half_at, 4 * self.slim),
            (self.d ^ 1, self.t),
        )

    def start(self):
        self.far().start()
        self.whole[pl.ds(pl.multiple_of(self.away * self.rows + self.at, 16), self.slim), :] = self.source[
            pl.ds(pl.multiple_of(self.at, 16), self.slim), :
        ]
        self.near(False).start()

    def pass_on(self):
        self.far().wait_recv()
        self.near(True).start()
        for m in (1, 2, 3):
            for j in (0, 1):
                self.level(j, m).start()

    def across(self):
        self.near(False).wait_recv()
        self.near(True).wait_recv()
        for m in (1, 2, 3):
            for j in (2, 3):
                self.level(j, m).start()

    def hand_over(self):
        for m in (1, 2, 3):
            for j in range(4):
                self.level(j, m).wait_recv()
        for j in range(4):
            self.hand(j).start()

    def finish(self):
        self.far().wait_send()
        self.near(False).wait_send()
        self.near(True).wait_send()
        for m in (1, 2, 3):
            for j in range(4):
                self.level(j, m).wait_send()
        for j in range(4):
            self.hand(j).wait()


def start_kernel(*refs):
    (tokens, gain, shift, *weights, out_weight, next_out, encoder, expand) = refs[:10]
    (rows_half, normed, query, keyed, moved, whole, next_whole, encoder_out, expand_slice) = refs[10:19]
    send_sem, recv_sem = refs[19:]
    d, t = lax.axis_index("dp"), lax.axis_index("tensor")
    core, side = d % 2, t % 2
    keeper = core == t // 2
    other = jnp.logical_not(keeper)
    count = tokens.shape[0]
    width = query.shape[1]
    copy = Copies(send_sem, recv_sem)
    move = Move("move", copy, weights, [moved.at[:, pl.ds(a * width, width)] for a in range(3)], d, t)
    every = Whole("whole", copy, out_weight, whole, d, t)
    after = Whole("next", copy, next_out, next_whole, d, t)
    rows = HalfRows("tokens", copy, tokens, rows_half, 0, 0, d, t)

    greet(
        [(d ^ 2, t), (d ^ 4, t), (d ^ 6, t), (d ^ 1, t), (d, t ^ 1), (d, t ^ 2), (d ^ 1, t ^ 2)]
    )

    def give(name, s):
        block = rows_of(normed, core * (2 * count) + s * count, count)
        return copy(("give", name), block, block, (d ^ 1, t))

    encoder_copy = copy("encoder", encoder, encoder_out, (d ^ 1, t))
    slim = expand_slice.shape[0]
    hop = copy("hop", rows_of(expand, d * slim, slim), expand_slice, (d, t ^ 2))

    every.start()
    after.start()
    rows.start()
    move.start()
    every.pass_on()
    after.pass_on()

    @pl.when(keeper)
    def _():
        encoder_copy.start()

    every.across()
    after.across()
    rows.relay()
    mine = core * (2 * count)
    norm_rows(rows_half, side * count, normed, mine + side * count, count, gain, shift)
    give(0, side).start()
    move.relay(range(3))
    hop.start()
    rows.arrive()
    norm_rows(rows_half, (1 - side) * count, normed, mine + (1 - side) * count, count, gain, shift)
    give(1, 1 - side).start()
    every.hand_over()
    after.hand_over()

    @pl.when(keeper)
    def _():
        encoder_out[...] = encoder[...]

    def project(first):
        def body(i, _):
            at = pl.ds(pl.multiple_of(first + i * 256, 256), 256)
            total = jnp.dot(normed[at, :], moved[...], preferred_element_type=jnp.float32).astype(jnp.bfloat16)
            query[at, :] = total[:, :width]
            keyed[at, :] = total[:, width:]
            return 0

        lax.fori_loop(0, (2 * count) // 256, body, 0)

    move.ready(range(3))
    project(mine)
    give(0, side).wait()
    give(1, 1 - side).wait()
    project((1 - core) * (2 * count))
    every.finish()
    after.finish()
    move.finish()
    rows.finish()
    hop.wait()

    @pl.when(keeper)
    def _():
        encoder_copy.wait_send()

    @pl.when(other)
    def _():
        encoder_copy.wait_recv()


def start_layer(tokens, gain, shift, weights, out_weight, next_out, encoder, expand, collective_id):
    rows, wide = tokens.shape
    dp = lax.axis_size("dp")
    width = weights[0].shape[1]
    bf16 = jnp.bfloat16
    shape = jax.ShapeDtypeStruct
    vmem = pl.BlockSpec(memory_space=pltpu.VMEM)
    return pl.pallas_call(
        start_kernel,
        out_shape=(
            shape((2 * rows, wide), bf16),
            shape((4 * rows, wide), bf16),
            shape((4 * rows, width), bf16),
            shape((4 * rows, 2 * width), bf16),
            shape((wide, 3 * width), bf16),
            shape((4 * out_weight.shape[0], out_weight.shape[1]), bf16),
            shape((4 * next_out.shape[0], next_out.shape[1]), bf16),
            shape(encoder.shape, bf16),
            shape((expand.shape[0] // dp, expand.shape[1]), bf16),
        ),
        in_specs=[vmem] * 9 + [pl.BlockSpec(memory_space=pl.ANY)],
        out_specs=(vmem,) * 8 + (pl.BlockSpec(memory_space=pl.ANY),),
        scratch_shapes=[
            pltpu.SemaphoreType.DMA((72,)),
            pltpu.SemaphoreType.DMA((72,)),
        ],
        compiler_params=pltpu.CompilerParams(
            collective_id=collective_id, has_side_effects=True, vmem_limit_bytes=56 << 20
        ),
        cost_estimate=pl.CostEstimate(flops=35_000_000_000, bytes_accessed=16_000_000, transcendentals=0),
        name="start_layer",
    )(tokens, gain[None], shift[None], *weights, out_weight, next_out, encoder, expand)


def add_dot(left, right, over_rows=False):
    return lax.dot_general(
        left, right, (((1,), (1 if over_rows else 0,)), ((), ())), preferred_element_type=jnp.float32
    )


class Exchange:
    def __init__(self, copy, mine, land, core, d, t, chunk):
        self.copy, self.mine, self.land, self.core, self.chunk = copy, mine, land, core, chunk
        self.half = mine.shape[0] // 2
        self.to = [(d ^ 1, t), (d, t ^ 1), (d ^ 1, t ^ 1)]

    def one(self, j, ch):
        core = self.core if j == 1 else 1 - self.core
        return self.copy(
            ("exchange", j, ch),
            rows_of(self.mine, core * self.half + ch * self.chunk, self.chunk),
            self.land.at[j, pl.ds(ch * self.chunk, self.chunk)],
            self.to[j],
        )

    def start(self, ch):
        for j in (1, 2, 0):
            self.one(j, ch).start()

    def arrive(self, ch):
        for j in range(3):
            self.one(j, ch).wait_recv()

    def pieces(self, ch):
        first = self.core * self.half + ch * self.chunk
        own = self.mine[pl.ds(pl.multiple_of(first, 16), self.chunk), :]
        return [own] + [self.land[j, pl.ds(ch * self.chunk, self.chunk), :] for j in range(3)]

    def sent(self, ch):
        for j in range(3):
            self.one(j, ch).wait_send()


def by_rows(rows, step, body):
    def turn(i, _):
        body(pl.multiple_of(i * step, step))
        return 0

    lax.fori_loop(0, rows // step, turn, 0)


def forward_kernel(*refs):
    (mixed, out_all, start, gain, shift, *weights) = refs[:8]
    (after, normed, result, moved, pair) = refs[8:13]
    (land, product, send_sem, recv_sem) = refs[13:]
    d, t = lax.axis_index("dp"), lax.axis_index("tensor")
    core = d % 2
    chunk = product.shape[0]
    half = after.shape[0]
    width = mixed.shape[1]
    copy = Copies(send_sem, recv_sem)
    greet(
        [(d ^ 1, t), (d, t ^ 1), (d ^ 1, t ^ 1), (d ^ 2, t), (d ^ 4, t), (d ^ 6, t), (d, t ^ 2)]
    )
    exchange = Exchange(copy, mixed, land, core, d, t, chunk)
    move = Move("move", copy, weights, [moved, pair.at[:, pl.ds(0, width)], pair.at[:, pl.ds(width, width)]], d, t)

    def give(ch):
        block = rows_of(normed, core * half + ch * chunk, chunk)
        return copy(("give", ch), block, block, (d ^ 1, t))

    chunks = half // chunk
    for ch in range(chunks):
        exchange.start(ch)
    move.start()
    for ch in range(chunks):
        exchange.arrive(ch)
        product[...] = sum(
            add_dot(piece, out_all[j * width : (j + 1) * width, :])
            for j, piece in enumerate(exchange.pieces(ch))
        )

        def rows(at, ch=ch):
            x = start[pl.ds(pl.multiple_of(ch * chunk + at, 16), 32), :].astype(jnp.float32)
            x = x + product[pl.ds(at, 32), :]
            after[pl.ds(pl.multiple_of(ch * chunk + at, 16), 32), :] = x
            unit, inverse = moments(x)
            normed[pl.ds(pl.multiple_of(core * half + ch * chunk + at, 16), 32), :] = (
                unit * gain[...] + shift[...]
            ).astype(jnp.bfloat16)

        by_rows(chunk, 32, rows)
        give(ch).start()
        if ch < 3:
            move.relay([ch])

    def project(first, rows):
        at = pl.ds(pl.multiple_of(first, 16), rows)
        result[at, :] = add_dot(normed[at, :], moved[...]).astype(jnp.bfloat16)

    move.ready([0])
    project(core * half, half)
    for ch in range(chunks):
        give(ch).wait()
    project((1 - core) * half, half)
    move.ready([1, 2])
    for ch in range(chunks):
        exchange.sent(ch)
    move.finish()


def forward_step(mixed, out_all, start, gain, shift, weights, collective_id):
    rows, width = mixed.shape
    half, wide = start.shape
    chunk = half // 4
    shape = jax.ShapeDtypeStruct
    vmem = pl.BlockSpec(memory_space=pltpu.VMEM)
    return pl.pallas_call(
        forward_kernel,
        out_shape=(
            shape((half, wide), jnp.float32),
            shape((rows, wide), jnp.bfloat16),
            shape((rows, width), jnp.bfloat16),
            shape(weights[0].shape, jnp.bfloat16),
            shape((weights[0].shape[0], 2 * width), jnp.bfloat16),
        ),
        in_specs=[vmem] * 8,
        out_specs=(vmem,) * 5,
        scratch_shapes=[
            pltpu.VMEM((3, half, width), jnp.bfloat16),
            pltpu.VMEM((chunk, wide), jnp.float32),
            pltpu.SemaphoreType.DMA((56,)),
            pltpu.SemaphoreType.DMA((56,)),
        ],
        compiler_params=pltpu.CompilerParams(
            collective_id=collective_id, has_side_effects=True, vmem_limit_bytes=56 << 20
        ),
        cost_estimate=pl.CostEstimate(flops=20_000_000_000, bytes_accessed=8_000_000, transcendentals=0),
        name="forward_step",
    )(mixed, out_all, start, gain[None], shift[None], *weights)


def backward_kernel(*refs):
    wide = refs[2].shape[1]
    (grad_query, query_all, after, gain, grad_in, weight, out_near, out_far, term) = refs[:9]
    (grad_res, grad_top, result, norm_grads, output, term_near, term_give) = refs[9:16]
    (land, product, out_rows, term_land, send_sem, recv_sem) = refs[16:]
    d, t = lax.axis_index("dp"), lax.axis_index("tensor")
    core = d % 2
    chunk = product.shape[0]
    half = after.shape[0]
    copy = Copies(send_sem, recv_sem)
    greet([(d ^ 1, t), (d, t ^ 1), (d ^ 1, t ^ 1), (d ^ 1, t ^ 2)])
    exchange = Exchange(copy, grad_query, land, core, d, t, chunk)

    def give(ch):
        block = rows_of(grad_top, core * half + ch * chunk, chunk)
        return copy(("give", ch), block, block, (d ^ 1, t))

    chunks = half // chunk
    for ch in range(chunks):
        exchange.start(ch)
    span, side = term_land.shape[0], t % 2
    term_far = copy("term", rows_of(term, (1 - core) * span, span), term_land, (d ^ 1, t))
    term_far.start()
    keeper = core == t // 2
    home = copy("home", out_rows, output, (d ^ 1, t ^ 2))
    out_rows[...] = (out_near[...] + out_far[...].astype(jnp.float32)).astype(jnp.bfloat16)

    @pl.when(keeper)
    def _():
        output[...] = out_rows[...]

    norm_grads[...] = jnp.zeros_like(norm_grads)
    for ch in range(chunks):
        exchange.arrive(ch)
        product[...] = sum(add_dot(piece, query_all[j * wide : (j + 1) * wide, :], True) for j, piece in enumerate(exchange.pieces(ch)))

        def rows(at, ch=ch):
            here = pl.ds(pl.multiple_of(ch * chunk + at, 16), 32)
            unit, inverse = moments(after[here, :])
            back, gain_grad, shift_grad = normalize_back(product[pl.ds(at, 32), :], unit, inverse, gain[...])
            total = grad_in[here, :] + back
            grad_res[here, :] = total
            grad_top[pl.ds(pl.multiple_of(core * half + ch * chunk + at, 16), 32), :] = total.astype(jnp.bfloat16)
            norm_grads[0:1, :] += gain_grad[None]
            norm_grads[1:2, :] += shift_grad[None]

        by_rows(chunk, 32, rows)
        give(ch).start()
        if ch == chunks - 2:

            @pl.when(jnp.logical_not(keeper))
            def _():
                home.start()


    def project(first, rows):
        at = pl.ds(pl.multiple_of(first, 16), rows)
        result[at, :] = add_dot(grad_top[at, :], weight[: result.shape[1], :], True).astype(jnp.bfloat16)

    project(core * half, half)
    for ch in range(chunks):
        give(ch).wait()
    project((1 - core) * half, half)
    term_far.wait()

    def term_rows(at):
        for which, out in ((side, term_near), (1 - side, term_give)):
            first = which * (span // 2) + at
            near = term[pl.ds(pl.multiple_of(core * span + first, 32), 32), :].astype(jnp.float32)
            far = term_land[pl.ds(pl.multiple_of(first, 32), 32), :].astype(jnp.float32)
            out[pl.ds(at, 32), :] = (near + far).astype(jnp.bfloat16)

    by_rows(span // 2, 32, term_rows)
    for ch in range(chunks):
        exchange.sent(ch)

    @pl.when(jnp.logical_not(keeper))
    def _():
        home.wait()


def backward_step(grad_query, query_all, after, gain, grad_in, weight, out_near, out_far, term, collective_id):
    rows, width = grad_query.shape
    half, wide = after.shape
    chunk = half // 4
    shape = jax.ShapeDtypeStruct
    vmem = pl.BlockSpec(memory_space=pltpu.VMEM)
    return pl.pallas_call(
        backward_kernel,
        out_shape=(
            shape((half, wide), jnp.float32),
            shape((rows, wide), jnp.bfloat16),
            shape((rows, width), jnp.bfloat16),
            shape((8, wide), jnp.float32),
            shape(out_far.shape, jnp.bfloat16),
            shape((term.shape[0] // 4, wide), jnp.bfloat16),
            shape((term.shape[0] // 4, wide), jnp.bfloat16),
        ),
        in_specs=[vmem] * 9,
        out_specs=(vmem,) * 7,
        scratch_shapes=[
            pltpu.VMEM((3, half, width), jnp.bfloat16),
            pltpu.VMEM((chunk, wide), jnp.float32),
            pltpu.VMEM(out_far.shape, jnp.bfloat16),
            pltpu.VMEM((term.shape[0] // 2, wide), jnp.bfloat16),
            pltpu.SemaphoreType.DMA((20,)),
            pltpu.SemaphoreType.DMA((20,)),
        ],
        compiler_params=pltpu.CompilerParams(
            collective_id=collective_id, has_side_effects=True, vmem_limit_bytes=56 << 20
        ),
        cost_estimate=pl.CostEstimate(flops=20_000_000_000, bytes_accessed=8_000_000, transcendentals=0),
        name="backward_step",
    )(grad_query, query_all, after, gain[None], grad_in, weight, out_near, out_far, term)


def hidden_kernel(*refs):
    (mixed, out_all, start, gain, shift, cot, cot_pair, next_query, *ff_weights) = refs[:12]
    (after, expand_grad, reduce_grad, grad_res, grad_top, result, norm_grads, query_all, out_near, out_give) = refs[12:22]
    (land, product, own, far_send, far_land, sum_send, sum_land, expand, reduce) = refs[22:31]
    (out_own, out_send, out_land, normed, hidden, grad_pre, grad_out) = refs[31:38]
    (send_sem, recv_sem, local_sem) = refs[38:]
    d, t = lax.axis_index("dp"), lax.axis_index("tensor")
    core = d % 2
    chunk = product.shape[0]
    half = after.shape[0]
    width = mixed.shape[1]
    chunks = half // chunk
    copy = Copies(send_sem, recv_sem)
    greet(
        [(d ^ 1, t), (d, t ^ 1), (d ^ 1, t ^ 1), (d ^ 2, t), (d ^ 4, t), (d ^ 6, t), (d, t ^ 2)]
    )
    exchange = Exchange(copy, mixed, land, core, d, t, chunk)
    every = Whole("query", copy, next_query, query_all, d, t)

    def give(name, ref, ch):
        block = rows_of(ref, core * half + ch * chunk, chunk)
        return copy((name, ch), block, block, (d ^ 1, t))

    def slab(ref, ch):
        return ref.at[pl.ds(ch * chunk, chunk)]

    def far(ch):
        return copy(("far", ch), slab(far_send, ch), slab(far_land, ch), (d ^ 1, t))

    def whole(ch):
        return copy(("whole", ch), slab(sum_send, ch), slab(sum_land, ch), (d, t ^ 1))

    def out_copy(ch):
        return copy(("out", ch), slab(out_send, ch), slab(out_land, ch), (d ^ 1, t))

    def residual(ch):
        exchange.arrive(ch)
        product[...] = sum(
            add_dot(piece, out_all[j * width : (j + 1) * width, :])
            for j, piece in enumerate(exchange.pieces(ch))
        )

        def rows(at):
            here = pl.ds(pl.multiple_of(ch * chunk + at, 16), 32)
            x = start[here, :] + product[pl.ds(at, 32), :]
            after[here, :] = x
            unit, inverse = moments(x)
            normed[pl.ds(pl.multiple_of(core * half + ch * chunk + at, 16), 32), :] = (
                unit * gain[...] + shift[...]
            ).astype(jnp.bfloat16)

        by_rows(chunk, 32, rows)
        give("normed", normed, ch).start()

    def feed(first):
        every = pl.ds(pl.multiple_of(first, 16), chunk)
        product[...] = add_dot(normed[every, :], expand[...])
        own[...] = add_dot(grad_out[every, :], reduce[...], True)

        def rows(at):
            here = pl.ds(pl.multiple_of(first + at, 16), 32)
            z = product[pl.ds(at, 32), :]
            inner = jnp.tanh(tanh_coeff * (z + cubic_coeff * z * z * z))
            hidden[here, :] = (0.5 * z * (1.0 + inner)).astype(jnp.bfloat16)
            slope = 0.5 * (1.0 + inner) + 0.5 * z * (1.0 - inner * inner) * tanh_coeff * (
                1.0 + 3.0 * cubic_coeff * z * z
            )
            upper = own[pl.ds(at, 32), :].astype(jnp.bfloat16).astype(jnp.float32)
            grad_pre[here, :] = (upper * slope).astype(jnp.bfloat16)

        by_rows(chunk, 32, rows)
        return add_dot(grad_pre[pl.ds(pl.multiple_of(first, 16), chunk), :], expand[...], True)

    def both(ch):
        copy(
            ("normed", ch), *([rows_of(normed, (1 - core) * half + ch * chunk, chunk)] * 2), (d ^ 1, t)
        ).wait_recv()
        far_send[pl.ds(ch * chunk, chunk), :] = feed((1 - core) * half + ch * chunk).astype(jnp.bfloat16)
        far(ch).start()
        own[...] = feed(core * half + ch * chunk)
        far(ch).wait_recv()

        def rows(at):
            here = pl.ds(pl.multiple_of(ch * chunk + at, 16), 32)
            sum_send[here, :] = (own[pl.ds(at, 32), :] + far_land[here, :].astype(jnp.float32)).astype(jnp.bfloat16)

        by_rows(chunk, 32, rows)
        whole(ch).start()
        at = pl.ds(ch * chunk, chunk)
        for core_at, out in ((1 - core, out_send), (core, out_own)):
            every_row = pl.ds(pl.multiple_of(core_at * half + ch * chunk, 16), chunk)
            out[at, :] = add_dot(hidden[every_row, :], reduce[...]).astype(jnp.bfloat16)
            if out is out_send:
                out_copy(ch).start()

    def back(ch):
        whole(ch).wait_recv()

        def rows(at):
            here = pl.ds(pl.multiple_of(ch * chunk + at, 16), 32)
            grad = sum_send[here, :].astype(jnp.float32) + sum_land[here, :].astype(jnp.float32)
            unit, inverse = moments(after[here, :])
            down, gain_grad, shift_grad = normalize_back(grad, unit, inverse, gain[...])
            top = grad_out[pl.ds(pl.multiple_of(core * half + ch * chunk + at, 16), 32), :]
            total = top.astype(jnp.float32) + down
            grad_res[here, :] = total
            grad_top[pl.ds(pl.multiple_of(core * half + ch * chunk + at, 16), 32), :] = total.astype(jnp.bfloat16)
            norm_grads[0:1, :] += gain_grad[None]
            norm_grads[1:2, :] += shift_grad[None]

        by_rows(chunk, 32, rows)
        give("top", grad_top, ch).start()

    def weight_grad(out, left, right, first):
        def body(i, _):
            at = pl.ds(pl.multiple_of((first + i) * 128, 128), 128)
            out[at, :] = lax.dot_general(
                left[:, at], right[...], (((0,), (0,)), ((), ())), preferred_element_type=jnp.float32
            ).astype(jnp.bfloat16)
            return 0

        lax.fori_loop(0, out.shape[0] // 256, body, 0)

    def project(first, rows):
        at = pl.ds(pl.multiple_of(first, 16), rows)
        result[at, :] = add_dot(grad_top[at, :], out_all[:width, :], True).astype(jnp.bfloat16)

    for ch in range(chunks):
        exchange.start(ch)
    keeper = core == t // 2

    def fetch(which, act):
        for a, weight in enumerate((expand, reduce)):
            act(pltpu.make_async_copy(ff_weights[2 * which + a], weight, local_sem.at[a]))

    def both_ways(act):
        @pl.when(keeper)
        def _():
            fetch(0, act)

        @pl.when(jnp.logical_not(keeper))
        def _():
            fetch(1, act)

    both_ways(lambda one: one.start())
    count = cot.shape[0]
    side = t % 2
    grad_out[pl.ds(pl.multiple_of(core * half + side * count, 16), count), :] = cot[...]
    grad_out[pl.ds(pl.multiple_of(core * half + (1 - side) * count, 16), count), :] = cot_pair[...]
    block = rows_of(grad_out, core * half, half)
    spread = copy("cot", block, block, (d ^ 1, t))
    spread.start()
    every.start()
    norm_grads[...] = jnp.zeros_like(norm_grads)
    residual(0)
    residual(1)
    both_ways(lambda one: one.wait())
    every.pass_on()
    spread.wait()
    both(0)
    residual(2)
    both(1)
    residual(3)
    both(2)
    every.across()
    back(0)
    both(3)
    weight_grad(reduce_grad, hidden, grad_out, 0)
    back(1)
    weight_grad(reduce_grad, hidden, grad_out, reduce_grad.shape[0] // 256)
    every.hand_over()
    back(2)
    weight_grad(expand_grad, normed, grad_pre, 0)
    back(3)
    project(core * half, half)
    weight_grad(expand_grad, normed, grad_pre, expand_grad.shape[0] // 256)
    for ch in range(chunks):
        copy(
            ("top", ch), *([rows_of(grad_top, (1 - core) * half + ch * chunk, chunk)] * 2), (d ^ 1, t)
        ).wait_recv()
    project((1 - core) * half, half)
    for ch in range(chunks):
        exchange.sent(ch)
        give("normed", normed, ch).wait_send()
        give("top", grad_top, ch).wait_send()
        far(ch).wait_send()
        whole(ch).wait_send()
    every.finish()
    for ch in range(chunks):
        out_copy(ch).wait()

    def out_rows(at):
        near = pl.ds(pl.multiple_of(side * count + at, 32), 32)
        give_at = pl.ds(pl.multiple_of((1 - side) * count + at, 32), 32)
        here = pl.ds(at, 32)
        out_near[here, :] = (
            after[near, :] + out_own[near, :].astype(jnp.float32) + out_land[near, :].astype(jnp.float32)
        )
        out_give[here, :] = (
            out_own[give_at, :].astype(jnp.float32) + out_land[give_at, :].astype(jnp.float32)
        ).astype(jnp.bfloat16)

    by_rows(count, 32, out_rows)


def hidden_step(mixed, out_all, start, gain, shift, cot, cot_pair, next_query, ff_weights, collective_id):
    rows, width = mixed.shape
    half, wide = start.shape
    inner = ff_weights[0].shape[1]
    chunk = half // 4
    bf16, f32 = jnp.bfloat16, jnp.float32
    shape = jax.ShapeDtypeStruct
    vmem = pl.BlockSpec(memory_space=pltpu.VMEM)
    return pl.pallas_call(
        hidden_kernel,
        out_shape=(
            shape((half, wide), f32),
            shape((wide, inner), bf16),
            shape((inner, wide), bf16),
            shape((half, wide), f32),
            shape((rows, wide), bf16),
            shape((rows, width), bf16),
            shape((8, wide), f32),
            shape((4 * next_query.shape[0], next_query.shape[1]), bf16),
            shape(cot.shape, f32),
            shape(cot.shape, bf16),
        ),
        in_specs=[vmem] * 8 + [pl.BlockSpec(memory_space=pl.ANY)] * 4,
        out_specs=(vmem,) * 10,
        scratch_shapes=[
            pltpu.VMEM((3, half, width), bf16),
            pltpu.VMEM((chunk, max(wide, inner)), f32),
            pltpu.VMEM((chunk, max(wide, inner)), f32),
            pltpu.VMEM((half, wide), bf16),
            pltpu.VMEM((half, wide), bf16),
            pltpu.VMEM((half, wide), bf16),
            pltpu.VMEM((half, wide), bf16),
            pltpu.VMEM(ff_weights[0].shape, bf16),
            pltpu.VMEM(ff_weights[1].shape, bf16),
            pltpu.VMEM((half, wide), bf16),
            pltpu.VMEM((half, wide), bf16),
            pltpu.VMEM((half, wide), bf16),
            pltpu.VMEM((rows, wide), bf16),
            pltpu.VMEM((rows, inner), bf16),
            pltpu.VMEM((rows, inner), bf16),
            pltpu.VMEM((rows, wide), bf16),
            pltpu.SemaphoreType.DMA((56,)),
            pltpu.SemaphoreType.DMA((56,)),
            pltpu.SemaphoreType.DMA((2,)),
        ],
        compiler_params=pltpu.CompilerParams(
            collective_id=collective_id, has_side_effects=True, vmem_limit_bytes=60 << 20
        ),
        cost_estimate=pl.CostEstimate(flops=50_000_000_000, bytes_accessed=16_000_000, transcendentals=0),
        name="hidden_step",
    )(mixed, out_all, start, gain[None], shift[None], cot, cot_pair, next_query, *ff_weights)


def on_device(
    tokens,
    encoder_states,
    tok_lengths,
    enc_lengths,
    pad_mask,
    first_gain,
    first_shift,
    causal_query,
    causal_key,
    causal_value,
    causal_out,
    second_gain,
    second_shift,
    cross_query,
    cross_key,
    cross_value,
    cross_out,
    third_gain,
    third_shift,
    expand_weight,
    reduce_weight,
    cotangent,
):
    place = Place()
    width = causal_query.shape[1]
    length = pad_mask.shape[0]
    frames = encoder_states.shape[0]

    def of_group(value):
        return jnp.where(place.keeper, value, place.swap(value, 1, 0))

    def half_rows(quarter):
        return place.ordered(quarter, place.swap(quarter, 0, 1), place.side)

    def quarter_of(half):
        return place.part(half, place.side, 2)

    tok_lengths, enc_lengths, pad_mask = of_group(tok_lengths), of_group(enc_lengths), of_group(pad_mask)
    block_q, block_k = 256, 512
    token_seg, frame_seg, key_seg, self_lo, self_hi, cross_lo, cross_hi = ranges(
        tok_lengths[0], enc_lengths[0], pad_mask, length, frames, block_q, block_k
    )
    self_keys = jnp.stack([token_seg, key_seg] + [token_seg] * 6)
    cross_keys = jnp.stack([frame_seg] * 8)
    seg_col, seg_row = token_seg[:, None], token_seg[None, :]

    tokens_half, first_all, query, keyed, first_weight, causal_out_perm, cross_out_perm, encoder, expand_piece = start_layer(
        tokens,
        first_gain,
        first_shift,
        (causal_query, causal_key, causal_value),
        causal_out,
        cross_out,
        encoder_states,
        expand_weight,
        1,
    )
    hidden_width = expand_weight.shape[1]
    expand_moved = lax.all_gather(expand_piece, "dp", axis=0, tiled=True)
    reduce_piece = place.part(reduce_weight, place.d, place.dp)
    reduce_piece, query = lax.optimization_barrier((reduce_piece, query))
    reduce_piece = place.swap(reduce_piece, 0, 2)

    mixed, self_logsum = attend_fwd(
        query, keyed, seg_col, self_keys, self_lo, self_hi, True, block_q, block_k
    )
    mixed, reduce_piece, cot_here = lax.optimization_barrier((mixed, reduce_piece, cotangent))
    reduce_moved = lax.all_gather(reduce_piece, "dp", axis=0, tiled=True)
    cot_here = place.home(cot_here)
    after_self, second_all, cquery, _, cross_weight = forward_step(
        mixed,
        causal_out_perm,
        tokens_half,
        second_gain,
        second_shift,
        (cross_query, cross_key, cross_value),
        2,
    )
    cquery, cot_here = lax.optimization_barrier((cquery, cot_here))
    cot_pair = place.swap(cot_here, 0, 1)
    ckeyed = times(encoder, cross_weight).astype(jnp.bfloat16)
    cmixed, cross_logsum = attend_fwd(
        cquery, ckeyed, seg_col, cross_keys, cross_lo, cross_hi, False, block_q, block_k
    )
    after_cross, expand_grad, reduce_grad, grad_res, grad_top2, grad_cmixed, third_grads, cross_query_every, out_near, out_give = hidden_step(
        cmixed, cross_out_perm, after_self, third_gain, third_shift, cot_here, cot_pair, cross_query,
        (expand_weight, reduce_weight, expand_moved, reduce_moved), 3
    )
    third_gain_grad, third_shift_grad = third_grads[0], third_grads[1]
    out_far = place.swap(out_give, 0, 1)

    cross_out_grad = along_rows(cmixed, grad_top2)
    expand_grad, reduce_grad = place.sum_columns(expand_grad, 0), place.sum_columns(reduce_grad, 1)
    grad_cquery, grad_cross_in = attend_bwd(
        cquery, ckeyed, cmixed, grad_cmixed, cross_logsum, seg_row, cross_keys.T,
        cross_lo, cross_hi, False, block_q, block_k,
    )
    bf16 = jnp.bfloat16
    cross_grad = along_rows(encoder, grad_cross_in).astype(bf16)
    cross_grads = jnp.concatenate(
        [cross_grad[:, :width], cross_grad[:, width:], along_rows(second_all, grad_cquery).astype(bf16)]
    )
    cross_grads = place.sum_columns(cross_grads, 1)
    encoder_term = against(grad_cross_in, cross_weight).astype(bf16)
    grad_res, grad_top, grad_mixed, second_grads, output, encoder_near, encoder_give = backward_step(
        grad_cquery, cross_query_every, after_self, second_gain, grad_res, causal_out_perm, out_near, out_far, encoder_term, 4
    )
    encoder_far = place.swap(encoder_give, 0, 1)
    second_gain_grad, second_shift_grad = second_grads[0], second_grads[1]
    causal_out_grad = along_rows(mixed, grad_top)
    grad_mixed, expand_grad, reduce_grad = lax.optimization_barrier((grad_mixed, expand_grad, reduce_grad))
    expand_far, reduce_far = place.swap(expand_grad, 0, 2, False), place.swap(reduce_grad, 0, 2, False)
    (grad_in,) = attend_bwd(
        query, keyed, mixed, grad_mixed, self_logsum, seg_row, self_keys.T,
        self_lo, self_hi, True, block_q, block_k,
    )
    causal_grad = along_rows(first_all, grad_in).astype(bf16)
    first_term = against(grad_in, first_weight)
    first_rows = (first_all.astype(jnp.float32) - first_shift) / first_gain
    first_gain_grad = jnp.sum(first_term * first_rows, axis=0)
    first_shift_grad = jnp.sum(first_term, axis=0)
    deep = causal_query.shape[0]
    once = (place.side == 0).astype(jnp.float32)
    none = jnp.zeros_like(first_gain_grad)
    norm_grads = jnp.stack(
        [
            first_gain_grad,
            first_shift_grad,
            second_gain_grad * once,
            second_shift_grad * once,
            third_gain_grad * once,
            third_shift_grad * once,
            none,
            none,
        ]
    )
    *sums, tokens_grad, encoder_grad, norm_grads = sum_all(
        [
            expand_grad,
            reduce_grad,
            cross_grads,
            jnp.concatenate([cross_out_grad.astype(bf16), causal_out_grad.astype(bf16)]),
            causal_grad,
        ],
        (expand_far, reduce_far),
        [
            (4, 0, deep // 2, 0, 0),
            (4, deep // 2, deep // 2, 1, 0),
            *(
                [(3, 0, width, 0, 0), (3, width, width, 1, 0)]
                if width % (8 * place.dp) == 0
                else [(3, 0, 2 * width, 0, 0)]
            ),
            (2, 0, 3 * deep, 1, 1),
            (0, 0, expand_weight.shape[0], 0, 2),
            (1, 0, reduce_weight.shape[0], 1, 2),
        ],
        first_term.astype(bf16),
        (encoder_near, encoder_far),
        norm_grads,
        tokens_half,
        grad_res,
        first_gain,
        0,
    )
    (
        first_gain_grad,
        first_shift_grad,
        second_gain_grad,
        second_shift_grad,
        third_gain_grad,
        third_shift_grad,
    ) = (norm_grads[i] for i in range(6))
    sums = [total.astype(jnp.float32) if at != 2 and at != 3 else total for at, total in enumerate(sums)]
    expand_grad, reduce_grad = sums[:2]
    cross_key_grad, cross_value_grad, cross_query_grad = (
        sums[2][i * deep : (i + 1) * deep].astype(jnp.float32) for i in range(3)
    )
    cross_out_grad, causal_out_grad = sums[3][:width].astype(jnp.float32), sums[3][width:].astype(jnp.float32)
    causal_query_grad, causal_key_grad, causal_value_grad = (
        sums[4][:, i * width : (i + 1) * width] for i in range(3)
    )
    return (
        output,
        tokens_grad,
        encoder_grad,
        first_gain_grad,
        first_shift_grad,
        causal_query_grad,
        causal_key_grad,
        causal_value_grad,
        causal_out_grad,
        second_gain_grad,
        second_shift_grad,
        cross_query_grad,
        cross_key_grad,
        cross_value_grad,
        cross_out_grad,
        third_gain_grad,
        third_shift_grad,
        expand_grad,
        reduce_grad,
    )


def solution(mesh):
    in_specs = (
        P(("dp", "tensor"), None),
        P("dp", None),
        P("dp", None),
        P("dp", None),
        P("dp"),
        P(),
        P(),
        P(None, "tensor"),
        P(None, "tensor"),
        P(None, "tensor"),
        P("tensor", None),
        P(),
        P(),
        P(None, "tensor"),
        P(None, "tensor"),
        P(None, "tensor"),
        P("tensor", None),
        P(),
        P(),
        P(None, "tensor"),
        P("tensor", None),
        P(("dp", "tensor"), None),
    )
    out_specs = (
        P(("dp", "tensor"), None),
        P(("dp", "tensor"), None),
        P(("dp", "tensor"), None),
        P(),
        P(),
        P(None, "tensor"),
        P(None, "tensor"),
        P(None, "tensor"),
        P("tensor", None),
        P(),
        P(),
        P(None, "tensor"),
        P(None, "tensor"),
        P(None, "tensor"),
        P("tensor", None),
        P(),
        P(),
        P(None, "tensor"),
        P("tensor", None),
    )
    return jax.shard_map(
        on_device, mesh=mesh, in_specs=in_specs, out_specs=out_specs, check_vma=False
    )
```

```python
import functools

import jax
import jax.numpy as jnp
from jax import lax
from jax.experimental import pallas as pl
from jax.experimental.pallas import tpu as pltpu
from jax.sharding import PartitionSpec as P

HEAD_DIM = 64


eps = 1e-05
tanh_coeff = 0.7978845608
cubic_coeff = 0.044715


def smooth_gate(values):
    inner = jnp.tanh(tanh_coeff * (values + cubic_coeff * values * values * values))
    return 0.5 * values * (1.0 + inner)


def smooth_slope(values):
    inner = jnp.tanh(tanh_coeff * (values + cubic_coeff * values * values * values))
    return 0.5 * (1.0 + inner) + 0.5 * values * (1.0 - inner * inner) * tanh_coeff * (
        1.0 + 3.0 * cubic_coeff * values * values
    )


BF=jnp.bfloat16
F32=jnp.float32

def head_mask(rows, width, h):
    lane = lax.broadcasted_iota(jnp.int32, (rows, width), 1)
    return (lane // HEAD_DIM) == h

def dot(a,b,ca,cb):
    return lax.dot_general(a,b,(((ca,),(cb,)),((),())),preferred_element_type=F32)

def fwd_kernel(causal, heads, bq, bk, lo_ref, hi_ref, q_ref, kv_ref, rs_ref, ks_ref, o_ref, lse_ref, acc):
    count, width = q_ref.shape
    def one(qb, _):
        q0 = pl.multiple_of(qb*bq, bq)
        qv = q_ref[pl.ds(q0,bq),:] * BF(HEAD_DIM**-0.5)
        rseg = rs_ref[pl.ds(q0,bq),0:1]
        qm = [jnp.where(head_mask(bq,width,h), qv, BF(0)) for h in range(heads)]
        acc[...] = jnp.zeros_like(acc)
        lane = lax.broadcasted_iota(jnp.int32,(bq,128),1)
        def inner(kb, carry):
            k0 = pl.multiple_of(kb*bk, bk)
            kv = kv_ref[pl.ds(k0,bk),:width]
            vv = kv_ref[pl.ds(k0,bk),width:]
            kseg = ks_ref[0:1,pl.ds(k0,bk)]
            if causal:
                kpad = ks_ref[1:2,pl.ds(k0,bk)]
                ri = lax.broadcasted_iota(jnp.int32,(bq,bk),0)+q0
                ci = lax.broadcasted_iota(jnp.int32,(bq,bk),1)+k0
                ok = ((rseg==kpad)&(ci<=ri))|(ci==ri)
            else:
                ok = rseg==kseg
            ms, ls = carry
            new_m, new_l = [], []
            parts=None
            alphas=[]
            for h in range(heads):
                s = dot(qm[h],kv,1,1)
                s = jnp.where(ok,s,-1e30)
                m = jnp.maximum(ms[h], jnp.max(s,axis=1,keepdims=True))
                p = jnp.exp(s-m)
                al = jnp.exp(ms[h]-m)
                new_m.append(m); new_l.append(ls[h]*al+jnp.sum(p,axis=1,keepdims=True))
                vm = jnp.where(head_mask(bk,width,h),vv,BF(0))
                t = dot(p.astype(BF),vm,1,0)
                parts = t if parts is None else parts+t
                alphas.append(al)
            lane2 = lax.broadcasted_iota(jnp.int32,(bq,width),1)//HEAD_DIM
            sc = alphas[heads-1]
            for h in range(heads-1):
                sc = jnp.where(lane2==h, alphas[h], sc)
            acc[...] = acc[...]*sc + parts
            return (tuple(new_m),tuple(new_l))
        init = (tuple(jnp.full((bq,1),-1e30,F32) for _ in range(heads)), tuple(jnp.zeros((bq,1),F32) for _ in range(heads)))
        ms, ls = lax.fori_loop(lo_ref[qb], hi_ref[qb], inner, init)
        lane2 = lax.broadcasted_iota(jnp.int32,(bq,width),1)//HEAD_DIM
        inv = [1.0/l for l in ls]
        sc = inv[heads-1]
        for h in range(heads-1):
            sc = jnp.where(lane2==h, inv[h], sc)
        o_ref[pl.ds(q0,bq),:] = (acc[...]*sc).astype(BF)
        st = jnp.zeros((bq,128),F32)
        for h in range(heads):
            st = jnp.where(lane==h, ms[h]+jnp.log(ls[h]), st)
        stt = jnp.transpose(st)
        lse_ref[:,pl.ds(q0,bq)] = stt[0:8,:]
        return 0
    lax.fori_loop(0,count//bq,one,0)

def attend_fwd(q,kv,rseg,kseg,lo,hi,causal,bq=256,bk=256):
    count,width=q.shape
    heads=width//HEAD_DIM
    vm=pl.BlockSpec(memory_space=pltpu.VMEM); sm=pl.BlockSpec(memory_space=pltpu.SMEM)
    return pl.pallas_call(functools.partial(fwd_kernel,causal,heads,bq,bk),
        out_shape=(jax.ShapeDtypeStruct((count,width),BF),jax.ShapeDtypeStruct((8,count),F32)),
        in_specs=[sm,sm,vm,vm,vm,vm],out_specs=(vm,vm),
        scratch_shapes=[pltpu.VMEM((bq,width),F32)],
        compiler_params=pltpu.CompilerParams(vmem_limit_bytes=40<<20),
        cost_estimate=pl.CostEstimate(flops=22_000_000_000, bytes_accessed=8_000_000, transcendentals=0),
        name="attend_fwd",
    )(lo,hi,q,kv,rseg,kseg)

def bwd_kernel(causal, heads, bq, bk, lo_ref, hi_ref, q_ref, kv_ref, o_ref, do_ref, lse_ref, rs_ref, ks_ref,
               dq_ref, dkv_ref, dka, dva, qm, dom, dqa):
    count,width=q_ref.shape
    dka[...]=jnp.zeros_like(dka); dva[...]=jnp.zeros_like(dva)
    def one(qb,_):
        q0=pl.multiple_of(qb*bq,bq)
        qv=q_ref[pl.ds(q0,bq),:]*BF(HEAD_DIM**-0.5)
        dov=do_ref[pl.ds(q0,bq),:]
        prod=dov.astype(F32)*o_ref[pl.ds(q0,bq),:].astype(F32)
        row=lax.broadcasted_iota(jnp.int32,(8,width),0); col=lax.broadcasted_iota(jnp.int32,(8,width),1)//HEAD_DIM
        sel=(row==col).astype(F32)
        delta=lax.dot_general(sel,prod,(((1,),(1,)),((),())),precision=lax.Precision.HIGHEST,preferred_element_type=F32)
        for h in range(heads):
            hm=head_mask(bq,width,h)
            qm[pl.ds(h*bq,bq),:]=jnp.where(hm,qv,BF(0))
            dom[pl.ds(h*bq,bq),:]=jnp.where(hm,dov,BF(0))
        dqa[...]=jnp.zeros_like(dqa)
        rseg=rs_ref[0:1,pl.ds(q0,bq)]
        lse=lse_ref[:,pl.ds(q0,bq)]
        def inner(kb,_):
            k0=pl.multiple_of(kb*bk,bk)
            kv=kv_ref[pl.ds(k0,bk),:width]; vv=kv_ref[pl.ds(k0,bk),width:]
            if causal:
                kpad=ks_ref[pl.ds(k0,bk),1:2]
                ri=lax.broadcasted_iota(jnp.int32,(bk,bq),1)+q0
                ci=lax.broadcasted_iota(jnp.int32,(bk,bq),0)+k0
                ok=((rseg==kpad)&(ci<=ri))|(ci==ri)
            else:
                ok=rseg==ks_ref[pl.ds(k0,bk),0:1]
            ps=[];dss=[]
            dq=None
            for h in range(heads):
                st=dot(kv,qm[pl.ds(h*bq,bq),:],1,1)
                p=jnp.where(ok,jnp.exp(st-lse[h:h+1,:]),0.0)
                dp=dot(vv,dom[pl.ds(h*bq,bq),:],1,1)
                ds=(p*(dp-delta[h:h+1,:])).astype(BF)
                ps.append(p.astype(BF)); dss.append(ds)
                km=jnp.where(head_mask(bk,width,h),kv,BF(0))
                t=dot(ds,km,0,0)
                dq=t if dq is None else dq+t
            dqa[...]+=dq
            pcat=jnp.concatenate(ps,axis=1); dcat=jnp.concatenate(dss,axis=1)
            dva[pl.ds(k0,bk),:]+=dot(pcat,dom[...],1,0)
            dka[pl.ds(k0,bk),:]+=dot(dcat,qm[...],1,0)
            return 0
        lax.fori_loop(lo_ref[qb],hi_ref[qb],inner,0)
        dq_ref[pl.ds(q0,bq),:width]=(dqa[...]*(HEAD_DIM**-0.5)).astype(BF)
        return 0
    lax.fori_loop(0,count//bq,one,0)
    out_ref = dq_ref if dkv_ref is None else dkv_ref
    first = out_ref.shape[1] - 2*width
    out_ref[:,first:first+width]=dka[...].astype(BF)
    out_ref[:,first+width:]=dva[...].astype(BF)

def attend_bwd(q,kv,o,do,lse,rseg,kseg,lo,hi,causal,bq=256,bk=256):
    count,width=q.shape; keys=kv.shape[0]
    heads=width//HEAD_DIM
    vm=pl.BlockSpec(memory_space=pltpu.VMEM); sm=pl.BlockSpec(memory_space=pltpu.SMEM)
    def kernel(*refs):
        rest=refs if not causal else refs[:10]+(None,)+refs[10:]
        bwd_kernel(causal,heads,bq,bk,*rest)
    shape=jax.ShapeDtypeStruct
    out_shape=(shape((count,3*width),BF),) if causal else (shape((count,width),BF),shape((keys,2*width),BF))
    return pl.pallas_call(kernel,
        out_shape=out_shape,
        in_specs=[sm,sm]+[vm]*7,out_specs=(vm,)*len(out_shape),
        scratch_shapes=[pltpu.VMEM((keys,width),F32),pltpu.VMEM((keys,width),F32),pltpu.VMEM((heads*bq,width),BF),pltpu.VMEM((heads*bq,width),BF),pltpu.VMEM((bq,width),F32)],
        compiler_params=pltpu.CompilerParams(vmem_limit_bytes=40<<20),
        cost_estimate=pl.CostEstimate(flops=30_000_000_000, bytes_accessed=8_000_000, transcendentals=0),
        name="attend_bwd",
    )(lo,hi,q,kv,o,do,lse,rseg,kseg)

def ranges(tok_lengths, enc_lengths, pad, count, frames, bq, bk):
    tend=jnp.cumsum(tok_lengths,dtype=jnp.int32); eend=jnp.cumsum(enc_lengths,dtype=jnp.int32)
    places=jnp.arange(count,dtype=jnp.int32)
    tseg=jnp.sum((places[:,None]>=tend[None,:]).astype(jnp.int32),axis=1)
    eseg=jnp.sum((jnp.arange(frames,dtype=jnp.int32)[:,None]>=eend[None,:]).astype(jnp.int32),axis=1)
    starts=jnp.arange(count//bq,dtype=jnp.int32)*bq
    first=tseg[::bq]; last=tseg[bq-1::bq]
    onehot=lambda s:(s[:,None]==jnp.arange(tend.shape[0])[None,:]).astype(jnp.int32)
    pick=lambda arr,s: jnp.sum(onehot(s)*arr[None,:],axis=1)
    tstart=tend-tok_lengths; estart=eend-enc_lengths
    slo=pick(tstart,first)//bk; shi=(starts+bq+bk-1)//bk
    clo=pick(estart,first)//bk; chi=(pick(eend,last)+bk-1)//bk
    kpad=jnp.where(pad==1,tseg,-1)
    return tseg,eseg,kpad,slo,shi,clo,chi


def along_rows(left, right):
    return lax.dot_general(
        left, right, (((0,), (0,)), ((), ())), preferred_element_type=jnp.float32
    )


def against(left, weight):
    return lax.dot_general(
        left, weight, (((1,), (1,)), ((), ())), preferred_element_type=jnp.float32
    )


def times(left, weight):
    return jnp.dot(left, weight, preferred_element_type=jnp.float32)


def moments(rows):
    centred = rows - jnp.mean(rows, axis=1, keepdims=True)
    inverse = lax.rsqrt(jnp.mean(centred * centred, axis=1, keepdims=True) + eps)
    return centred * inverse, inverse


def normalize_back(grad_out, unit, inverse, gain):
    scaled = grad_out * gain
    inner = (
        scaled
        - jnp.mean(scaled, axis=1, keepdims=True)
        - unit * jnp.mean(scaled * unit, axis=1, keepdims=True)
    )
    return (inner * inverse, jnp.sum(grad_out * unit, axis=0), jnp.sum(grad_out, axis=0))


class Place:
    def __init__(self):
        self.dp = lax.axis_size("dp")
        self.tensor = lax.axis_size("tensor")
        self.d = lax.axis_index("dp")
        self.t = lax.axis_index("tensor")
        self.core = self.d % 2
        self.half = self.t // 2
        self.side = self.t % 2
        self.keeper = self.core == self.half
        self.shard = jnp.where(self.keeper, self.t, self.t ^ 2)

    def swap(self, value, d_flip, t_flip, only=None):
        pairs = []
        for d in range(self.dp):
            for t in range(self.tensor):
                keeper = d % 2 == t // 2
                if only is None or only == keeper:
                    pairs.append((d * self.tensor + t, (d ^ d_flip) * self.tensor + (t ^ t_flip)))
        return lax.ppermute(value, ("dp", "tensor"), pairs)

    def home(self, value):
        return jnp.where(self.keeper, value, self.swap(value, 1, 2, False))

    def ordered(self, mine, other, which):
        return jnp.where(
            which == 0, jnp.concatenate([mine, other]), jnp.concatenate([other, mine])
        )

    def part(self, value, which, parts):
        size = value.shape[0] // parts
        return lax.dynamic_slice_in_dim(value, which * size, size, 0)

    def both_cores(self, half_rows):
        return self.ordered(half_rows, self.swap(half_rows, 1, 0), self.core)

    def spread_columns(self, value):
        near, far = self.part(value, self.core, 2), self.part(value, 1 - self.core, 2)
        return jnp.concatenate(
            [near, self.swap(far, 1, 0), self.swap(near, 0, 1), self.swap(far, 1, 1)], axis=1
        )

    def order(self):
        return [self.shard, self.shard ^ 2, self.shard ^ 1, self.shard ^ 3]

    def sum_half(self, value):
        near, far = self.part(value, self.core, 2), self.part(value, 1 - self.core, 2)
        return near.astype(jnp.float32) + self.swap(far.astype(jnp.bfloat16), 1, 0).astype(jnp.float32)

    def sum_group_half(self, value):
        mine = self.sum_half(value).astype(jnp.bfloat16)
        return mine.astype(jnp.float32) + self.swap(mine, 0, 1).astype(jnp.float32)

    def sum_group_quarter(self, value):
        mine = self.sum_half(value)
        near, far = self.part(mine, self.side, 2), self.part(mine, 1 - self.side, 2)
        return near + self.swap(far.astype(jnp.bfloat16), 0, 1).astype(jnp.float32)

    def sum_columns(self, grad, order):
        columns = self.dp // 2
        bits = columns.bit_length() - 1
        turned = [sum(((c >> b) & 1) << (bits - 1 - b) for b in range(bits)) for c in range(columns)]
        groups = [[2 * (turned[c] if order == 0 else c) + core for c in range(columns)] for core in range(2)]
        return lax.psum_scatter(
            grad.astype(jnp.bfloat16), "dp", scatter_dimension=0, axis_index_groups=groups, tiled=True
        )

    def cross_planes(self, grads):
        return [
            (grad.astype(jnp.float32) + self.swap(grad, 0, 2, False).astype(jnp.float32)).astype(jnp.bfloat16)
            for grad in grads
        ]

    def moved_weight(self, weight):
        piece = self.swap(self.part(weight, self.d, self.dp), 0, 2)
        return jnp.where(self.keeper, weight, lax.all_gather(piece, "dp", axis=0, tiled=True))

    def whole_weight(self, weight):
        piece = self.part(weight, self.d, self.dp)
        every = lax.all_gather(piece, ("dp", "tensor"), axis=0, tiled=False)
        every = every.reshape((self.dp, self.tensor) + piece.shape)
        return jnp.swapaxes(every, 0, 1).reshape((self.tensor,) + weight.shape)


class Copies:
    def __init__(self, send_sem, recv_sem):
        self.send_sem, self.recv_sem, self.known = send_sem, recv_sem, {}

    def __call__(self, name, src, dst, device):
        at = self.known.setdefault(name, len(self.known))
        return pltpu.make_async_remote_copy(
            src_ref=src,
            dst_ref=dst,
            send_sem=self.send_sem.at[at],
            recv_sem=self.recv_sem.at[at],
            device_id=device,
            device_id_type=pl.DeviceIdType.MESH,
        )


def greet(devices):
    barrier = pltpu.get_barrier_semaphore()
    for device in devices:
        pl.semaphore_signal(
            barrier, inc=1, device_id=device, device_id_type=pl.DeviceIdType.MESH
        )
    pl.semaphore_wait(barrier, len(devices))


def rows_of(ref, start, size, step=16):
    return ref.at[pl.ds(pl.multiple_of(start, step), size)]


def norm_rows(src, src_first, dst, dst_first, rows, gain, shift):
    chunk = 64

    def body(i, _):
        at = i * chunk
        x = src[pl.ds(pl.multiple_of(src_first + at, 16), chunk), :].astype(jnp.float32)
        unit, inverse = moments(x)
        dst[pl.ds(pl.multiple_of(dst_first + at, 16), chunk), :] = (
            unit * gain[...] + shift[...]
        ).astype(jnp.bfloat16)
        return 0

    lax.fori_loop(0, rows // chunk, body, 0)


def sum_kernel(dp, arrays, units, span, *refs):
    it = iter(refs)
    take = lambda count: [next(it) for _ in range(count)]
    ins = take(arrays)
    fars = take(2)
    part, home_near, home_far, small_in, tokens, grad_in, gain = take(7)
    outs = take(arrays)
    row_out, home_out, small_out = take(3)
    bits = [b for b in (2, 4, 8, 16, 32, 64) if b < dp]
    steps = len(bits)
    land, hold = [], []
    for unit in units:
        hold.append(take(0 if unit[4] else steps))
        land.append(take((steps + 1, 1, 0)[unit[4]]))
    row_land, row_hold = take(2), take(2)
    (home_hold,) = take(1)
    home_half = home_hold.shape[0] // 2
    small_hold, small_land, small_send, small_recv, row_send, row_recv, send_sem, recv_sem = take(8)
    d, t = lax.axis_index("dp"), lax.axis_index("tensor")
    core, side = d % 2, t % 2
    keeper = core == t // 2
    other = jnp.logical_not(keeper)
    MESH = pl.DeviceIdType.MESH

    around = [(d ^ b, t) for b in bits] + [(d ^ 1, t), (d, t ^ 2), (d, t ^ 1)]
    greet(around + [(d ^ 1, t ^ 2)])

    def my(bit):
        return (d // bit) % 2

    def order(u):
        return bits if units[u][3] == 0 else bits[::-1]

    def source(u, step):
        array, first, rows, _, summed = units[u]
        if summed:
            return ins[array], first >> steps
        return (ins[array], first) if step == 0 else (hold[u][step - 1], 0)

    def copy(u, stage, src, dst, device):
        return pltpu.make_async_remote_copy(
            src_ref=src, dst_ref=dst, send_sem=send_sem.at[u, stage], recv_sem=recv_sem.at[u, stage],
            device_id=device, device_id_type=MESH,
        )

    def quarter(u):
        place = units[u][1]
        for step, bit in enumerate(order(u)):
            place = place + my(bit) * (units[u][2] >> (step + 1))
        return place

    def scatter_copy(u, step):
        ref, first = source(u, step)
        size = units[u][2] >> (step + 1)
        bit = order(u)[step]
        return copy(u, step, rows_of(ref, first + (1 - my(bit)) * size, size), land[u][step], (d ^ bit, t))

    def plane_copy(u):
        ref, first = source(u, steps)
        return copy(u, steps, rows_of(ref, first, units[u][2] >> steps), land[u][-1], (d, t ^ 2))

    def gather_copy(u, step):
        array, first, rows = units[u][:3]
        bit = order(u)[steps - 1 - step]
        size = rows >> (steps - step)
        start = quarter(u)
        for back in range(step):
            start = start - my(order(u)[steps - 1 - back]) * (rows >> (steps - back))
        block = rows_of(outs[array], start, size)
        return copy(u, steps + 1 + step, block, block, (d ^ bit, t))

    def core_copy(u):
        array, first, rows = units[u][:3]
        block = outs[array].at[pl.ds(first, rows)]
        return copy(u, 2 * steps + 1, block, block, (d ^ 1, t))

    def add(dst, dst_first, left, left_first, right, rows):
        chunk = min(rows, 32)

        def body(i, _):
            at = i * chunk
            a = left[pl.ds(pl.multiple_of(left_first + at, 16), chunk), :].astype(jnp.float32)
            b = right[pl.ds(pl.multiple_of(at, 16), chunk), :].astype(jnp.float32)
            dst[pl.ds(pl.multiple_of(dst_first + at, 16), chunk), :] = (a + b).astype(jnp.bfloat16)
            return 0

        lax.fori_loop(0, rows // chunk, body, 0)

    def begin(u, stage):
        if stage < steps:
            scatter_copy(u, stage).start()
        elif stage == steps:

            @pl.when(other)
            def _():
                plane_copy(u).start()
        else:

            @pl.when(keeper)
            def _():
                (gather_copy(u, stage - steps - 1) if stage <= 2 * steps else core_copy(u)).start()

    def end(u, stage):
        array, first, rows = units[u][:3]
        if stage < steps:
            one = scatter_copy(u, stage)
            one.wait_recv()
            ref, row = source(u, stage)
            size = rows >> (stage + 1)
            add(hold[u][stage], 0, ref, row + my(order(u)[stage]) * size, land[u][stage], size)
            one.wait_send()
        elif stage == steps and units[u][4] == 2:

            @pl.when(keeper)
            def _():
                size = rows >> steps
                ref, row = source(u, steps)
                add(outs[array], quarter(u), ref, row, fars[array], size)
        elif stage == steps:

            @pl.when(other)
            def _():
                plane_copy(u).wait_send()

            @pl.when(keeper)
            def _():
                plane_copy(u).wait_recv()
                ref, row = source(u, steps)
                add(outs[array], quarter(u), ref, row, land[u][-1], rows >> steps)
        elif stage <= 2 * steps:

            @pl.when(keeper)
            def _():
                gather_copy(u, stage - steps - 1).wait()
        else:

            @pl.when(keeper)
            def _():
                core_copy(u).wait_send()

            @pl.when(other)
            def _():
                core_copy(u).wait_recv()

    def row_copy(stage):
        if stage == 0:
            src, dst, device = rows_of(part, (1 - core) * 2 * span, 2 * span), row_land[0], (d ^ 1, t)
        elif stage == 1:
            src, dst, device = rows_of(row_hold[0], (1 - side) * span, span), row_land[1], (d, t ^ 1)
        elif stage == 2:
            src, dst, device = row_hold[1], row_out, (d ^ 1, t ^ 2)
        else:
            rows = pl.ds((stage % 3) * home_half, home_half)
            src, dst, device = home_hold.at[rows], home_out.at[rows], (d ^ 1, t ^ 2)
        return pltpu.make_async_remote_copy(
            src_ref=src, dst_ref=dst, send_sem=row_send.at[stage], recv_sem=row_recv.at[stage],
            device_id=device, device_id_type=MESH,
        )

    def row_half():
        row_copy(0).wait()
        add(row_hold[0], 0, part, core * 2 * span, row_land[0], 2 * span)
        row_copy(1).start()

    def to_owner(hold_ref, out_ref, stage):
        @pl.when(keeper)
        def _():
            out_ref[...] = hold_ref[...]

        @pl.when(other)
        def _():
            row_copy(stage).start()

    def row_home():
        row_copy(1).wait()

        def body(i, _):
            at = pl.ds(pl.multiple_of(i * 32, 32), 32)
            here = pl.ds(pl.multiple_of(side * span + i * 32, 32), 32)
            total = row_hold[0][here, :].astype(jnp.float32) + row_land[1][at, :].astype(jnp.float32)
            unit, inverse = moments(tokens[here, :].astype(jnp.float32))
            total = grad_in[here, :] + normalize_back(total, unit, inverse, gain[...])[0]
            row_hold[1][at, :] = total.astype(jnp.bfloat16)
            return 0

        lax.fori_loop(0, span // 32, body, 0)
        to_owner(row_hold[1], row_out, 2)

    def small_copy(step):
        return pltpu.make_async_remote_copy(
            src_ref=small_hold.at[step], dst_ref=small_land.at[step], send_sem=small_send.at[step],
            recv_sem=small_recv.at[step], device_id=around[step], device_id_type=MESH,
        )

    def small_step(step):
        small_copy(step).wait()
        total = small_hold[step] + small_land[step]
        if step + 1 < len(around):
            small_hold[step + 1] = total
            small_copy(step + 1).start()
        else:
            small_out[...] = total

    last = 2 * steps + 2
    first_stage = (0, steps, steps + 1)
    turns = [
        list(range(last + 1)),
        list(range(steps + 3)),
        list(range(steps + 2)),
    ]

    def tick(now):
        for state in (0, 1, 2):
            if now not in turns[state]:
                continue
            turn = turns[state].index(now)
            stage = first_stage[state] + turn
            for u in range(len(units)):
                if units[u][4] != state:
                    continue
                if state == 2 and turn == 0:
                    end(u, steps)
                if turn > 0:
                    end(u, stage - 1)
                if stage < last:
                    begin(u, stage)

    small_hold[0] = small_in[...]
    small_copy(0).start()
    row_copy(0).start()
    tick(0)
    add(home_hold, 0, home_near, 0, home_far, home_hold.shape[0])
    to_owner(home_hold, home_out, 3)
    row_half()
    small_step(0)
    row_home()
    for now in range(1, last + 1):
        tick(now)
        if now < len(around):
            small_step(now)
        if now == steps + 1:

            @pl.when(other)
            def _():
                row_copy(4).start()


    @pl.when(other)
    def _():
        row_copy(2).wait()
        row_copy(3).wait()
        row_copy(4).wait()


def sum_all(grads, fars, units, part, home, norm_grads, tokens, grad_in, gain, collective_id):
    dp = lax.axis_size("dp")
    steps = 0
    while 2 << steps < dp:
        steps += 1
    bf16, f32 = jnp.bfloat16, jnp.float32
    shapes = [(grad.shape[0], grad.shape[1]) for grad in grads]
    scratch = []
    for array, first, rows, side, done in units:
        width = grads[array].shape[1]
        if done:
            shapes[array] = (rows, width)
        else:
            scratch += [pltpu.VMEM((rows >> (k + 1), width), bf16) for k in range(steps)] * 2
        if done < 2:
            scratch.append(pltpu.VMEM((rows >> steps, width), bf16))
    stages = 2 * steps + 2
    vmem = pl.BlockSpec(memory_space=pltpu.VMEM)
    span = part.shape[0] // 4
    wide = tokens.shape[1]
    semaphores = pltpu.SemaphoreType.DMA
    return pl.pallas_call(
        functools.partial(sum_kernel, dp, len(grads), units, span),
        out_shape=[jax.ShapeDtypeStruct(shape, bf16) for shape in shapes]
        + [jax.ShapeDtypeStruct((span, wide), bf16), jax.ShapeDtypeStruct(home[0].shape, bf16)]
        + [jax.ShapeDtypeStruct(norm_grads.shape, f32)],
        in_specs=[vmem] * (len(grads) + 9),
        out_specs=[vmem] * (len(grads) + 3),
        scratch_shapes=scratch
        + [pltpu.VMEM((many * span, wide), bf16) for many in (2, 1)] * 2
        + [pltpu.VMEM(home[0].shape, bf16)]
        + [pltpu.VMEM((steps + 3,) + norm_grads.shape, f32)] * 2
        + [semaphores((steps + 3,))] * 2
        + [semaphores((5,))] * 2
        + [semaphores((len(units), stages))] * 2,
        compiler_params=pltpu.CompilerParams(
            collective_id=collective_id, has_side_effects=True, vmem_limit_bytes=60 << 20
        ),
        cost_estimate=pl.CostEstimate(flops=80_000_000_000, bytes_accessed=16_000_000, transcendentals=0),
        name="sum_all",
    )(*grads, *fars, part, *home, norm_grads, tokens, grad_in, gain[None])


class Move:
    def __init__(self, name, copy, sources, moved, d, t):
        self.name, self.copy, self.sources, self.moved = name, copy, sources, moved
        self.d, self.t, self.column = d, t, (d // 2) % 4
        self.keeper = d % 2 == t // 2
        self.other = jnp.logical_not(self.keeper)

    def block(self, ref):
        part = ref.shape[0] // 4
        return rows_of(ref, self.column * part, part)

    def fetch(self, a):
        return self.copy(
            (self.name, a), self.block(self.sources[a]), self.block(self.moved[a]), (self.d, self.t ^ 2)
        )

    def share(self, a, m):
        block = self.block(self.moved[a])
        return self.copy((self.name, a, m), block, block, (self.d ^ (2 * m), self.t))

    def start(self):
        @pl.when(self.keeper)
        def _():
            for a in range(len(self.moved)):
                self.fetch(a).start()

    def relay(self, which):
        @pl.when(self.other)
        def _():
            for a in which:
                self.fetch(a).wait_recv()
                for m in (1, 2, 3):
                    self.share(a, m).start()

    def ready(self, which):
        @pl.when(self.keeper)
        def _():
            for a in which:
                self.moved[a][...] = self.sources[a][...]

        @pl.when(self.other)
        def _():
            for a in which:
                for m in (1, 2, 3):
                    self.share(a, m).wait_recv()

    def finish(self):
        @pl.when(self.keeper)
        def _():
            for a in range(len(self.moved)):
                self.fetch(a).wait_send()

        @pl.when(self.other)
        def _():
            for a in range(len(self.moved)):
                for m in (1, 2, 3):
                    self.share(a, m).wait_send()


class HalfRows:
    def __init__(self, name, copy, rows, half, first, far_first, d, t):
        self.name, self.copy, self.rows, self.half, self.first = name, copy, rows, half, first
        self.far_first = far_first
        self.d, self.t, self.side = d, t, t % 2
        self.keeper = d % 2 == t // 2
        self.other = jnp.logical_not(self.keeper)
        self.count = rows.shape[0]
        self.piece = self.count // 4

    def place(self, s, p):
        return rows_of(self.half, self.first + s * self.count + p * self.piece, self.piece)

    def own(self, p):
        return self.rows.at[pl.ds(p * self.piece, self.piece)]

    def swap(self, p):
        at = rows_of(self.half, self.far_first + self.side * self.count + p * self.piece, self.piece)
        return self.copy((self.name, "swap", p), self.own(p), at, (self.d ^ 1, self.t ^ 2))

    def through(self, p, source):
        return self.copy((self.name, "pass", p), source, self.place(self.side, p), (self.d, self.t ^ 1))

    def start(self):
        @pl.when(self.other)
        def _():
            for p in range(4):
                self.swap(p).start()

        @pl.when(self.keeper)
        def _():
            for p in range(4):
                self.through(p, self.own(p)).start()
            at = pl.multiple_of(self.first + self.side * self.count, 16)
            self.half[pl.ds(at, self.count), :] = self.rows[...]

    def relay(self):
        @pl.when(self.other)
        def _():
            for p in range(4):
                self.swap(p).wait_recv()
                self.through(p, self.place(self.side, p)).start()

    def arrive(self):
        for p in range(4):
            block = self.place(1 - self.side, p)
            self.copy((self.name, "pass", p), block, block, (self.d, self.t ^ 1)).wait_recv()

    def finish(self):
        @pl.when(self.keeper)
        def _():
            for p in range(4):
                self.through(p, self.own(p)).wait_send()

        @pl.when(self.other)
        def _():
            for p in range(4):
                self.swap(p).wait_send()
                self.through(p, self.place(self.side, p)).wait_send()


class Whole:
    def __init__(self, name, copy, source, whole, d, t):
        self.name, self.copy, self.source, self.whole = name, copy, source, whole
        self.d, self.t = d, t
        self.away = jnp.where(d % 2 == t // 2, 0, 1)
        self.rows = source.shape[0]
        self.slim = self.rows // 8
        self.half_at = (d % 2) * (4 * self.slim)
        self.at = self.half_at + ((d // 2) % 4) * self.slim

    def block(self, j):
        return rows_of(self.whole, j * self.rows + self.at, self.slim)

    def far(self):
        return self.copy(
            (self.name, "far"), rows_of(self.source, self.at, self.slim), self.block(self.away), (self.d, self.t ^ 2)
        )

    def near(self, late):
        j = 1 - self.away if late else self.away
        return self.copy((self.name, "near", late), self.block(j), self.block(j + 2), (self.d, self.t ^ 1))

    def level(self, j, m):
        block = rows_of(self.whole, j * self.rows + self.at, self.slim)
        return self.copy((self.name, "level", j, m), block, block, (self.d ^ (2 * m), self.t))

    def hand(self, j):
        return self.copy(
            (self.name, "hand", j),
            rows_of(self.whole, j * self.rows + self.half_at, 4 * self.slim),
            rows_of(self.whole, (j ^ 1) * self.rows + self.half_at, 4 * self.slim),
            (self.d ^ 1, self.t),
        )

    def start(self):
        self.far().start()
        self.whole[pl.ds(pl.multiple_of(self.away * self.rows + self.at, 16), self.slim), :] = self.source[
            pl.ds(pl.multiple_of(self.at, 16), self.slim), :
        ]
        self.near(False).start()

    def pass_on(self):
        self.far().wait_recv()
        self.near(True).start()
        for m in (1, 2, 3):
            for j in (0, 1):
                self.level(j, m).start()

    def across(self):
        self.near(False).wait_recv()
        self.near(True).wait_recv()
        for m in (1, 2, 3):
            for j in (2, 3):
                self.level(j, m).start()

    def hand_over(self):
        for m in (1, 2, 3):
            for j in range(4):
                self.level(j, m).wait_recv()
        for j in range(4):
            self.hand(j).start()

    def finish(self):
        self.far().wait_send()
        self.near(False).wait_send()
        self.near(True).wait_send()
        for m in (1, 2, 3):
            for j in range(4):
                self.level(j, m).wait_send()
        for j in range(4):
            self.hand(j).wait()


def start_kernel(*refs):
    (tokens, gain, shift, *weights, out_weight, next_out, encoder, expand) = refs[:10]
    (rows_half, normed, query, keyed, moved, whole, next_whole, encoder_out, expand_slice) = refs[10:19]
    send_sem, recv_sem = refs[19:]
    d, t = lax.axis_index("dp"), lax.axis_index("tensor")
    core, side = d % 2, t % 2
    keeper = core == t // 2
    other = jnp.logical_not(keeper)
    count = tokens.shape[0]
    width = query.shape[1]
    copy = Copies(send_sem, recv_sem)
    move = Move("move", copy, weights, [moved.at[:, pl.ds(a * width, width)] for a in range(3)], d, t)
    every = Whole("whole", copy, out_weight, whole, d, t)
    after = Whole("next", copy, next_out, next_whole, d, t)
    rows = HalfRows("tokens", copy, tokens, rows_half, 0, 0, d, t)

    greet(
        [(d ^ 2, t), (d ^ 4, t), (d ^ 6, t), (d ^ 1, t), (d, t ^ 1), (d, t ^ 2), (d ^ 1, t ^ 2)]
    )

    def give(name, s):
        block = rows_of(normed, core * (2 * count) + s * count, count)
        return copy(("give", name), block, block, (d ^ 1, t))

    encoder_copy = copy("encoder", encoder, encoder_out, (d ^ 1, t))
    slim = expand_slice.shape[0]
    hop = copy("hop", rows_of(expand, d * slim, slim), expand_slice, (d, t ^ 2))

    every.start()
    after.start()
    rows.start()
    move.start()
    every.pass_on()
    after.pass_on()

    @pl.when(keeper)
    def _():
        encoder_copy.start()

    every.across()
    after.across()
    rows.relay()
    mine = core * (2 * count)
    norm_rows(rows_half, side * count, normed, mine + side * count, count, gain, shift)
    give(0, side).start()
    move.relay(range(3))
    hop.start()
    rows.arrive()
    norm_rows(rows_half, (1 - side) * count, normed, mine + (1 - side) * count, count, gain, shift)
    give(1, 1 - side).start()
    every.hand_over()
    after.hand_over()

    @pl.when(keeper)
    def _():
        encoder_out[...] = encoder[...]

    def project(first):
        def body(i, _):
            at = pl.ds(pl.multiple_of(first + i * 256, 256), 256)
            total = jnp.dot(normed[at, :], moved[...], preferred_element_type=jnp.float32).astype(jnp.bfloat16)
            query[at, :] = total[:, :width]
            keyed[at, :] = total[:, width:]
            return 0

        lax.fori_loop(0, (2 * count) // 256, body, 0)

    move.ready(range(3))
    project(mine)
    give(0, side).wait()
    give(1, 1 - side).wait()
    project((1 - core) * (2 * count))
    every.finish()
    after.finish()
    move.finish()
    rows.finish()
    hop.wait()

    @pl.when(keeper)
    def _():
        encoder_copy.wait_send()

    @pl.when(other)
    def _():
        encoder_copy.wait_recv()


def start_layer(tokens, gain, shift, weights, out_weight, next_out, encoder, expand, collective_id):
    rows, wide = tokens.shape
    dp = lax.axis_size("dp")
    width = weights[0].shape[1]
    bf16 = jnp.bfloat16
    shape = jax.ShapeDtypeStruct
    vmem = pl.BlockSpec(memory_space=pltpu.VMEM)
    return pl.pallas_call(
        start_kernel,
        out_shape=(
            shape((2 * rows, wide), bf16),
            shape((4 * rows, wide), bf16),
            shape((4 * rows, width), bf16),
            shape((4 * rows, 2 * width), bf16),
            shape((wide, 3 * width), bf16),
            shape((4 * out_weight.shape[0], out_weight.shape[1]), bf16),
            shape((4 * next_out.shape[0], next_out.shape[1]), bf16),
            shape(encoder.shape, bf16),
            shape((expand.shape[0] // dp, expand.shape[1]), bf16),
        ),
        in_specs=[vmem] * 9 + [pl.BlockSpec(memory_space=pl.ANY)],
        out_specs=(vmem,) * 8 + (pl.BlockSpec(memory_space=pl.ANY),),
        scratch_shapes=[
            pltpu.SemaphoreType.DMA((72,)),
            pltpu.SemaphoreType.DMA((72,)),
        ],
        compiler_params=pltpu.CompilerParams(
            collective_id=collective_id, has_side_effects=True, vmem_limit_bytes=56 << 20
        ),
        cost_estimate=pl.CostEstimate(flops=35_000_000_000, bytes_accessed=16_000_000, transcendentals=0),
        name="start_layer",
    )(tokens, gain[None], shift[None], *weights, out_weight, next_out, encoder, expand)


def add_dot(left, right, over_rows=False):
    return lax.dot_general(
        left, right, (((1,), (1 if over_rows else 0,)), ((), ())), preferred_element_type=jnp.float32
    )


class Exchange:
    def __init__(self, copy, mine, land, core, d, t, chunk):
        self.copy, self.mine, self.land, self.core, self.chunk = copy, mine, land, core, chunk
        self.half = mine.shape[0] // 2
        self.to = [(d ^ 1, t), (d, t ^ 1), (d ^ 1, t ^ 1)]

    def one(self, j, ch):
        core = self.core if j == 1 else 1 - self.core
        return self.copy(
            ("exchange", j, ch),
            rows_of(self.mine, core * self.half + ch * self.chunk, self.chunk),
            self.land.at[j, pl.ds(ch * self.chunk, self.chunk)],
            self.to[j],
        )

    def start(self, ch):
        for j in (1, 2, 0):
            self.one(j, ch).start()

    def arrive(self, ch):
        for j in range(3):
            self.one(j, ch).wait_recv()

    def pieces(self, ch):
        first = self.core * self.half + ch * self.chunk
        own = self.mine[pl.ds(pl.multiple_of(first, 16), self.chunk), :]
        return [own] + [self.land[j, pl.ds(ch * self.chunk, self.chunk), :] for j in range(3)]

    def sent(self, ch):
        for j in range(3):
            self.one(j, ch).wait_send()


def by_rows(rows, step, body):
    def turn(i, _):
        body(pl.multiple_of(i * step, step))
        return 0

    lax.fori_loop(0, rows // step, turn, 0)


def forward_kernel(*refs):
    (mixed, out_all, start, gain, shift, *weights) = refs[:8]
    (after, normed, result, moved, pair) = refs[8:13]
    (land, product, send_sem, recv_sem) = refs[13:]
    d, t = lax.axis_index("dp"), lax.axis_index("tensor")
    core = d % 2
    chunk = product.shape[0]
    half = after.shape[0]
    width = mixed.shape[1]
    copy = Copies(send_sem, recv_sem)
    greet(
        [(d ^ 1, t), (d, t ^ 1), (d ^ 1, t ^ 1), (d ^ 2, t), (d ^ 4, t), (d ^ 6, t), (d, t ^ 2)]
    )
    exchange = Exchange(copy, mixed, land, core, d, t, chunk)
    move = Move("move", copy, weights, [moved, pair.at[:, pl.ds(0, width)], pair.at[:, pl.ds(width, width)]], d, t)

    def give(ch):
        block = rows_of(normed, core * half + ch * chunk, chunk)
        return copy(("give", ch), block, block, (d ^ 1, t))

    chunks = half // chunk
    for ch in range(chunks):
        exchange.start(ch)
    move.start()
    for ch in range(chunks):
        exchange.arrive(ch)
        product[...] = sum(
            add_dot(piece, out_all[j * width : (j + 1) * width, :])
            for j, piece in enumerate(exchange.pieces(ch))
        )

        def rows(at, ch=ch):
            x = start[pl.ds(pl.multiple_of(ch * chunk + at, 16), 32), :].astype(jnp.float32)
            x = x + product[pl.ds(at, 32), :]
            after[pl.ds(pl.multiple_of(ch * chunk + at, 16), 32), :] = x
            unit, inverse = moments(x)
            normed[pl.ds(pl.multiple_of(core * half + ch * chunk + at, 16), 32), :] = (
                unit * gain[...] + shift[...]
            ).astype(jnp.bfloat16)

        by_rows(chunk, 32, rows)
        give(ch).start()
        if ch < 3:
            move.relay([ch])

    def project(first, rows):
        at = pl.ds(pl.multiple_of(first, 16), rows)
        result[at, :] = add_dot(normed[at, :], moved[...]).astype(jnp.bfloat16)

    move.ready([0])
    project(core * half, half)
    for ch in range(chunks):
        give(ch).wait()
    project((1 - core) * half, half)
    move.ready([1, 2])
    for ch in range(chunks):
        exchange.sent(ch)
    move.finish()


def forward_step(mixed, out_all, start, gain, shift, weights, collective_id):
    rows, width = mixed.shape
    half, wide = start.shape
    chunk = half // 4
    shape = jax.ShapeDtypeStruct
    vmem = pl.BlockSpec(memory_space=pltpu.VMEM)
    return pl.pallas_call(
        forward_kernel,
        out_shape=(
            shape((half, wide), jnp.float32),
            shape((rows, wide), jnp.bfloat16),
            shape((rows, width), jnp.bfloat16),
            shape(weights[0].shape, jnp.bfloat16),
            shape((weights[0].shape[0], 2 * width), jnp.bfloat16),
        ),
        in_specs=[vmem] * 8,
        out_specs=(vmem,) * 5,
        scratch_shapes=[
            pltpu.VMEM((3, half, width), jnp.bfloat16),
            pltpu.VMEM((chunk, wide), jnp.float32),
            pltpu.SemaphoreType.DMA((56,)),
            pltpu.SemaphoreType.DMA((56,)),
        ],
        compiler_params=pltpu.CompilerParams(
            collective_id=collective_id, has_side_effects=True, vmem_limit_bytes=56 << 20
        ),
        cost_estimate=pl.CostEstimate(flops=20_000_000_000, bytes_accessed=8_000_000, transcendentals=0),
        name="forward_step",
    )(mixed, out_all, start, gain[None], shift[None], *weights)


def backward_kernel(*refs):
    wide = refs[2].shape[1]
    (grad_query, query_all, after, gain, grad_in, weight, out_near, out_far, term) = refs[:9]
    (grad_res, grad_top, result, norm_grads, output, term_near, term_give) = refs[9:16]
    (land, product, out_rows, term_land, send_sem, recv_sem) = refs[16:]
    d, t = lax.axis_index("dp"), lax.axis_index("tensor")
    core = d % 2
    chunk = product.shape[0]
    half = after.shape[0]
    copy = Copies(send_sem, recv_sem)
    greet([(d ^ 1, t), (d, t ^ 1), (d ^ 1, t ^ 1), (d ^ 1, t ^ 2)])
    exchange = Exchange(copy, grad_query, land, core, d, t, chunk)

    def give(ch):
        block = rows_of(grad_top, core * half + ch * chunk, chunk)
        return copy(("give", ch), block, block, (d ^ 1, t))

    chunks = half // chunk
    for ch in range(chunks):
        exchange.start(ch)
    span, side = term_land.shape[0], t % 2
    term_far = copy("term", rows_of(term, (1 - core) * span, span), term_land, (d ^ 1, t))
    term_far.start()
    keeper = core == t // 2
    home = copy("home", out_rows, output, (d ^ 1, t ^ 2))
    out_rows[...] = (out_near[...] + out_far[...].astype(jnp.float32)).astype(jnp.bfloat16)

    @pl.when(keeper)
    def _():
        output[...] = out_rows[...]

    norm_grads[...] = jnp.zeros_like(norm_grads)
    def term_rows(at):
        for which, out in ((side, term_near), (1 - side, term_give)):
            first = which * (span // 2) + at
            near = term[pl.ds(pl.multiple_of(core * span + first, 32), 32), :].astype(jnp.float32)
            far = term_land[pl.ds(pl.multiple_of(first, 32), 32), :].astype(jnp.float32)
            out[pl.ds(at, 32), :] = (near + far).astype(jnp.bfloat16)

    for ch in range(chunks):
        if ch == chunks - 2:
            term_far.wait()
        if ch >= chunks - 2:
            by_rows(span // 4, 32, lambda at, ch=ch: term_rows((ch - chunks + 2) * (span // 4) + at))
        exchange.arrive(ch)
        product[...] = sum(add_dot(piece, query_all[j * wide : (j + 1) * wide, :], True) for j, piece in enumerate(exchange.pieces(ch)))

        def rows(at, ch=ch):
            here = pl.ds(pl.multiple_of(ch * chunk + at, 16), 32)
            unit, inverse = moments(after[here, :])
            back, gain_grad, shift_grad = normalize_back(product[pl.ds(at, 32), :], unit, inverse, gain[...])
            total = grad_in[here, :] + back
            grad_res[here, :] = total
            grad_top[pl.ds(pl.multiple_of(core * half + ch * chunk + at, 16), 32), :] = total.astype(jnp.bfloat16)
            norm_grads[0:1, :] += gain_grad[None]
            norm_grads[1:2, :] += shift_grad[None]

        by_rows(chunk, 32, rows)
        give(ch).start()
        if ch == chunks - 2:

            @pl.when(jnp.logical_not(keeper))
            def _():
                home.start()


    def project(first, rows):
        at = pl.ds(pl.multiple_of(first, 16), rows)
        result[at, :] = add_dot(grad_top[at, :], weight[: result.shape[1], :], True).astype(jnp.bfloat16)

    project(core * half, half)
    for ch in range(chunks):
        give(ch).wait()
    project((1 - core) * half, half)
    for ch in range(chunks):
        exchange.sent(ch)

    @pl.when(jnp.logical_not(keeper))
    def _():
        home.wait()


def backward_step(grad_query, query_all, after, gain, grad_in, weight, out_near, out_far, term, collective_id):
    rows, width = grad_query.shape
    half, wide = after.shape
    chunk = half // 4
    shape = jax.ShapeDtypeStruct
    vmem = pl.BlockSpec(memory_space=pltpu.VMEM)
    return pl.pallas_call(
        backward_kernel,
        out_shape=(
            shape((half, wide), jnp.float32),
            shape((rows, wide), jnp.bfloat16),
            shape((rows, width), jnp.bfloat16),
            shape((8, wide), jnp.float32),
            shape(out_far.shape, jnp.bfloat16),
            shape((term.shape[0] // 4, wide), jnp.bfloat16),
            shape((term.shape[0] // 4, wide), jnp.bfloat16),
        ),
        in_specs=[vmem] * 9,
        out_specs=(vmem,) * 7,
        scratch_shapes=[
            pltpu.VMEM((3, half, width), jnp.bfloat16),
            pltpu.VMEM((chunk, wide), jnp.float32),
            pltpu.VMEM(out_far.shape, jnp.bfloat16),
            pltpu.VMEM((term.shape[0] // 2, wide), jnp.bfloat16),
            pltpu.SemaphoreType.DMA((20,)),
            pltpu.SemaphoreType.DMA((20,)),
        ],
        compiler_params=pltpu.CompilerParams(
            collective_id=collective_id, has_side_effects=True, vmem_limit_bytes=56 << 20
        ),
        cost_estimate=pl.CostEstimate(flops=20_000_000_000, bytes_accessed=8_000_000, transcendentals=0),
        name="backward_step",
    )(grad_query, query_all, after, gain[None], grad_in, weight, out_near, out_far, term)


def hidden_kernel(*refs):
    (mixed, out_all, start, gain, shift, cot, cot_pair, next_query, *ff_weights) = refs[:12]
    (after, expand_grad, reduce_grad, grad_res, grad_top, result, norm_grads, query_all, out_near, out_give) = refs[12:22]
    (land, product, own, far_send, far_land, sum_send, sum_land, expand, reduce) = refs[22:31]
    (out_own, out_send, out_land, normed, hidden, grad_pre, grad_out) = refs[31:38]
    (send_sem, recv_sem, local_sem) = refs[38:]
    d, t = lax.axis_index("dp"), lax.axis_index("tensor")
    core = d % 2
    chunk = product.shape[0]
    half = after.shape[0]
    width = mixed.shape[1]
    chunks = half // chunk
    copy = Copies(send_sem, recv_sem)
    greet(
        [(d ^ 1, t), (d, t ^ 1), (d ^ 1, t ^ 1), (d ^ 2, t), (d ^ 4, t), (d ^ 6, t), (d, t ^ 2)]
    )
    exchange = Exchange(copy, mixed, land, core, d, t, chunk)
    every = Whole("query", copy, next_query, query_all, d, t)

    def give(name, ref, ch):
        block = rows_of(ref, core * half + ch * chunk, chunk)
        return copy((name, ch), block, block, (d ^ 1, t))

    def slab(ref, ch):
        return ref.at[pl.ds(ch * chunk, chunk)]

    def far(ch):
        return copy(("far", ch), slab(far_send, ch), slab(far_land, ch), (d ^ 1, t))

    def whole(ch):
        return copy(("whole", ch), slab(sum_send, ch), slab(sum_land, ch), (d, t ^ 1))

    def out_copy(ch):
        return copy(("out", ch), slab(out_send, ch), slab(out_land, ch), (d ^ 1, t))

    def residual(ch):
        exchange.arrive(ch)
        product[...] = sum(
            add_dot(piece, out_all[j * width : (j + 1) * width, :])
            for j, piece in enumerate(exchange.pieces(ch))
        )

        def rows(at):
            here = pl.ds(pl.multiple_of(ch * chunk + at, 16), 32)
            x = start[here, :] + product[pl.ds(at, 32), :]
            after[here, :] = x
            unit, inverse = moments(x)
            normed[pl.ds(pl.multiple_of(core * half + ch * chunk + at, 16), 32), :] = (
                unit * gain[...] + shift[...]
            ).astype(jnp.bfloat16)

        by_rows(chunk, 32, rows)
        give("normed", normed, ch).start()

    def feed(first):
        every = pl.ds(pl.multiple_of(first, 16), chunk)
        product[...] = add_dot(normed[every, :], expand[...])
        own[...] = add_dot(grad_out[every, :], reduce[...], True)

        def rows(at):
            here = pl.ds(pl.multiple_of(first + at, 16), 32)
            z = product[pl.ds(at, 32), :]
            inner = jnp.tanh(tanh_coeff * (z + cubic_coeff * z * z * z))
            hidden[here, :] = (0.5 * z * (1.0 + inner)).astype(jnp.bfloat16)
            slope = 0.5 * (1.0 + inner) + 0.5 * z * (1.0 - inner * inner) * tanh_coeff * (
                1.0 + 3.0 * cubic_coeff * z * z
            )
            upper = own[pl.ds(at, 32), :].astype(jnp.bfloat16).astype(jnp.float32)
            grad_pre[here, :] = (upper * slope).astype(jnp.bfloat16)

        by_rows(chunk, 32, rows)
        return add_dot(grad_pre[pl.ds(pl.multiple_of(first, 16), chunk), :], expand[...], True)

    def both(ch):
        copy(
            ("normed", ch), *([rows_of(normed, (1 - core) * half + ch * chunk, chunk)] * 2), (d ^ 1, t)
        ).wait_recv()
        far_send[pl.ds(ch * chunk, chunk), :] = feed((1 - core) * half + ch * chunk).astype(jnp.bfloat16)
        far(ch).start()
        own[...] = feed(core * half + ch * chunk)
        far(ch).wait_recv()

        def rows(at):
            here = pl.ds(pl.multiple_of(ch * chunk + at, 16), 32)
            sum_send[here, :] = (own[pl.ds(at, 32), :] + far_land[here, :].astype(jnp.float32)).astype(jnp.bfloat16)

        by_rows(chunk, 32, rows)
        whole(ch).start()
        at = pl.ds(ch * chunk, chunk)
        for core_at, out in ((1 - core, out_send), (core, out_own)):
            every_row = pl.ds(pl.multiple_of(core_at * half + ch * chunk, 16), chunk)
            out[at, :] = add_dot(hidden[every_row, :], reduce[...]).astype(jnp.bfloat16)
            if out is out_send:
                out_copy(ch).start()

    def back(ch):
        whole(ch).wait_recv()

        def rows(at):
            here = pl.ds(pl.multiple_of(ch * chunk + at, 16), 32)
            grad = sum_send[here, :].astype(jnp.float32) + sum_land[here, :].astype(jnp.float32)
            unit, inverse = moments(after[here, :])
            down, gain_grad, shift_grad = normalize_back(grad, unit, inverse, gain[...])
            top = grad_out[pl.ds(pl.multiple_of(core * half + ch * chunk + at, 16), 32), :]
            total = top.astype(jnp.float32) + down
            grad_res[here, :] = total
            grad_top[pl.ds(pl.multiple_of(core * half + ch * chunk + at, 16), 32), :] = total.astype(jnp.bfloat16)
            norm_grads[0:1, :] += gain_grad[None]
            norm_grads[1:2, :] += shift_grad[None]

        by_rows(chunk, 32, rows)
        give("top", grad_top, ch).start()

    def weight_grad(out, left, right, first):
        def body(i, _):
            at = pl.ds(pl.multiple_of((first + i) * 128, 128), 128)
            out[at, :] = lax.dot_general(
                left[:, at], right[...], (((0,), (0,)), ((), ())), preferred_element_type=jnp.float32
            ).astype(jnp.bfloat16)
            return 0

        lax.fori_loop(0, out.shape[0] // 256, body, 0)

    def project(first, rows):
        at = pl.ds(pl.multiple_of(first, 16), rows)
        result[at, :] = add_dot(grad_top[at, :], out_all[:width, :], True).astype(jnp.bfloat16)

    for ch in range(chunks):
        exchange.start(ch)
    keeper = core == t // 2

    def fetch(which, act):
        for a, weight in enumerate((expand, reduce)):
            act(pltpu.make_async_copy(ff_weights[2 * which + a], weight, local_sem.at[a]))

    def both_ways(act):
        @pl.when(keeper)
        def _():
            fetch(0, act)

        @pl.when(jnp.logical_not(keeper))
        def _():
            fetch(1, act)

    both_ways(lambda one: one.start())
    count = cot.shape[0]
    side = t % 2
    grad_out[pl.ds(pl.multiple_of(core * half + side * count, 16), count), :] = cot[...]
    grad_out[pl.ds(pl.multiple_of(core * half + (1 - side) * count, 16), count), :] = cot_pair[...]
    block = rows_of(grad_out, core * half, half)
    spread = copy("cot", block, block, (d ^ 1, t))
    spread.start()
    every.start()
    norm_grads[...] = jnp.zeros_like(norm_grads)
    residual(0)
    residual(1)
    both_ways(lambda one: one.wait())
    every.pass_on()
    spread.wait()
    both(0)
    residual(2)
    both(1)
    residual(3)
    both(2)
    every.across()
    back(0)
    both(3)
    weight_grad(reduce_grad, hidden, grad_out, 0)
    back(1)
    weight_grad(reduce_grad, hidden, grad_out, reduce_grad.shape[0] // 256)
    every.hand_over()
    back(2)
    weight_grad(expand_grad, normed, grad_pre, 0)
    back(3)
    project(core * half, half)
    weight_grad(expand_grad, normed, grad_pre, expand_grad.shape[0] // 256)
    for ch in range(chunks):
        copy(
            ("top", ch), *([rows_of(grad_top, (1 - core) * half + ch * chunk, chunk)] * 2), (d ^ 1, t)
        ).wait_recv()
    project((1 - core) * half, half)
    for ch in range(chunks):
        exchange.sent(ch)
        give("normed", normed, ch).wait_send()
        give("top", grad_top, ch).wait_send()
        far(ch).wait_send()
        whole(ch).wait_send()
    every.finish()
    for ch in range(chunks):
        out_copy(ch).wait()

    def out_rows(at):
        near = pl.ds(pl.multiple_of(side * count + at, 32), 32)
        give_at = pl.ds(pl.multiple_of((1 - side) * count + at, 32), 32)
        here = pl.ds(at, 32)
        out_near[here, :] = (
            after[near, :] + out_own[near, :].astype(jnp.float32) + out_land[near, :].astype(jnp.float32)
        )
        out_give[here, :] = (
            out_own[give_at, :].astype(jnp.float32) + out_land[give_at, :].astype(jnp.float32)
        ).astype(jnp.bfloat16)

    by_rows(count, 32, out_rows)


def hidden_step(mixed, out_all, start, gain, shift, cot, cot_pair, next_query, ff_weights, collective_id):
    rows, width = mixed.shape
    half, wide = start.shape
    inner = ff_weights[0].shape[1]
    chunk = half // 4
    bf16, f32 = jnp.bfloat16, jnp.float32
    shape = jax.ShapeDtypeStruct
    vmem = pl.BlockSpec(memory_space=pltpu.VMEM)
    return pl.pallas_call(
        hidden_kernel,
        out_shape=(
            shape((half, wide), f32),
            shape((wide, inner), bf16),
            shape((inner, wide), bf16),
            shape((half, wide), f32),
            shape((rows, wide), bf16),
            shape((rows, width), bf16),
            shape((8, wide), f32),
            shape((4 * next_query.shape[0], next_query.shape[1]), bf16),
            shape(cot.shape, f32),
            shape(cot.shape, bf16),
        ),
        in_specs=[vmem] * 8 + [pl.BlockSpec(memory_space=pl.ANY)] * 4,
        out_specs=(vmem,) * 10,
        scratch_shapes=[
            pltpu.VMEM((3, half, width), bf16),
            pltpu.VMEM((chunk, max(wide, inner)), f32),
            pltpu.VMEM((chunk, max(wide, inner)), f32),
            pltpu.VMEM((half, wide), bf16),
            pltpu.VMEM((half, wide), bf16),
            pltpu.VMEM((half, wide), bf16),
            pltpu.VMEM((half, wide), bf16),
            pltpu.VMEM(ff_weights[0].shape, bf16),
            pltpu.VMEM(ff_weights[1].shape, bf16),
            pltpu.VMEM((half, wide), bf16),
            pltpu.VMEM((half, wide), bf16),
            pltpu.VMEM((half, wide), bf16),
            pltpu.VMEM((rows, wide), bf16),
            pltpu.VMEM((rows, inner), bf16),
            pltpu.VMEM((rows, inner), bf16),
            pltpu.VMEM((rows, wide), bf16),
            pltpu.SemaphoreType.DMA((56,)),
            pltpu.SemaphoreType.DMA((56,)),
            pltpu.SemaphoreType.DMA((2,)),
        ],
        compiler_params=pltpu.CompilerParams(
            collective_id=collective_id, has_side_effects=True, vmem_limit_bytes=60 << 20
        ),
        cost_estimate=pl.CostEstimate(flops=50_000_000_000, bytes_accessed=16_000_000, transcendentals=0),
        name="hidden_step",
    )(mixed, out_all, start, gain[None], shift[None], cot, cot_pair, next_query, *ff_weights)


def on_device(
    tokens,
    encoder_states,
    tok_lengths,
    enc_lengths,
    pad_mask,
    first_gain,
    first_shift,
    causal_query,
    causal_key,
    causal_value,
    causal_out,
    second_gain,
    second_shift,
    cross_query,
    cross_key,
    cross_value,
    cross_out,
    third_gain,
    third_shift,
    expand_weight,
    reduce_weight,
    cotangent,
):
    place = Place()
    width = causal_query.shape[1]
    length = pad_mask.shape[0]
    frames = encoder_states.shape[0]

    def of_group(value):
        return jnp.where(place.keeper, value, place.swap(value, 1, 0))

    def half_rows(quarter):
        return place.ordered(quarter, place.swap(quarter, 0, 1), place.side)

    def quarter_of(half):
        return place.part(half, place.side, 2)

    tok_lengths, enc_lengths, pad_mask = of_group(tok_lengths), of_group(enc_lengths), of_group(pad_mask)
    block_q, block_k = 256, 512
    token_seg, frame_seg, key_seg, self_lo, self_hi, cross_lo, cross_hi = ranges(
        tok_lengths[0], enc_lengths[0], pad_mask, length, frames, block_q, block_k
    )
    self_keys = jnp.stack([token_seg, key_seg] + [token_seg] * 6)
    cross_keys = jnp.stack([frame_seg] * 8)
    seg_col, seg_row = token_seg[:, None], token_seg[None, :]

    tokens_half, first_all, query, keyed, first_weight, causal_out_perm, cross_out_perm, encoder, expand_piece = start_layer(
        tokens,
        first_gain,
        first_shift,
        (causal_query, causal_key, causal_value),
        causal_out,
        cross_out,
        encoder_states,
        expand_weight,
        1,
    )
    hidden_width = expand_weight.shape[1]
    expand_moved = lax.all_gather(expand_piece, "dp", axis=0, tiled=True)
    reduce_piece = place.part(reduce_weight, place.d, place.dp)
    reduce_piece, query = lax.optimization_barrier((reduce_piece, query))
    reduce_piece = place.swap(reduce_piece, 0, 2)

    mixed, self_logsum = attend_fwd(
        query, keyed, seg_col, self_keys, self_lo, self_hi, True, block_q, block_k
    )
    mixed, reduce_piece, cot_here = lax.optimization_barrier((mixed, reduce_piece, cotangent))
    reduce_moved = lax.all_gather(reduce_piece, "dp", axis=0, tiled=True)
    cot_here = place.home(cot_here)
    after_self, second_all, cquery, _, cross_weight = forward_step(
        mixed,
        causal_out_perm,
        tokens_half,
        second_gain,
        second_shift,
        (cross_query, cross_key, cross_value),
        2,
    )
    cquery, cot_here = lax.optimization_barrier((cquery, cot_here))
    cot_pair = place.swap(cot_here, 0, 1)
    ckeyed = times(encoder, cross_weight).astype(jnp.bfloat16)
    cmixed, cross_logsum = attend_fwd(
        cquery, ckeyed, seg_col, cross_keys, cross_lo, cross_hi, False, block_q, block_k
    )
    after_cross, expand_grad, reduce_grad, grad_res, grad_top2, grad_cmixed, third_grads, cross_query_every, out_near, out_give = hidden_step(
        cmixed, cross_out_perm, after_self, third_gain, third_shift, cot_here, cot_pair, cross_query,
        (expand_weight, reduce_weight, expand_moved, reduce_moved), 3
    )
    third_gain_grad, third_shift_grad = third_grads[0], third_grads[1]
    out_far = place.swap(out_give, 0, 1)

    cross_out_grad = along_rows(cmixed, grad_top2)
    expand_grad, reduce_grad = place.sum_columns(expand_grad, 0), place.sum_columns(reduce_grad, 1)
    grad_cquery, grad_cross_in = attend_bwd(
        cquery, ckeyed, cmixed, grad_cmixed, cross_logsum, seg_row, cross_keys.T,
        cross_lo, cross_hi, False, block_q, block_k,
    )
    bf16 = jnp.bfloat16
    cross_grad = along_rows(encoder, grad_cross_in).astype(bf16)
    cross_grads = jnp.concatenate(
        [cross_grad[:, :width], cross_grad[:, width:], along_rows(second_all, grad_cquery).astype(bf16)]
    )
    cross_grads = place.sum_columns(cross_grads, 1)
    encoder_term = against(grad_cross_in, cross_weight).astype(bf16)
    grad_res, grad_top, grad_mixed, second_grads, output, encoder_near, encoder_give = backward_step(
        grad_cquery, cross_query_every, after_self, second_gain, grad_res, causal_out_perm, out_near, out_far, encoder_term, 4
    )
    encoder_far = place.swap(encoder_give, 0, 1)
    second_gain_grad, second_shift_grad = second_grads[0], second_grads[1]
    causal_out_grad = along_rows(mixed, grad_top)
    grad_mixed, expand_grad, reduce_grad = lax.optimization_barrier((grad_mixed, expand_grad, reduce_grad))
    expand_far, reduce_far = place.swap(expand_grad, 0, 2, False), place.swap(reduce_grad, 0, 2, False)
    (grad_in,) = attend_bwd(
        query, keyed, mixed, grad_mixed, self_logsum, seg_row, self_keys.T,
        self_lo, self_hi, True, block_q, block_k,
    )
    causal_grad = along_rows(first_all, grad_in).astype(bf16)
    first_term = against(grad_in, first_weight)
    first_rows = (first_all.astype(jnp.float32) - first_shift) / first_gain
    first_gain_grad = jnp.sum(first_term * first_rows, axis=0)
    first_shift_grad = jnp.sum(first_term, axis=0)
    deep = causal_query.shape[0]
    once = (place.side == 0).astype(jnp.float32)
    none = jnp.zeros_like(first_gain_grad)
    norm_grads = jnp.stack(
        [
            first_gain_grad,
            first_shift_grad,
            second_gain_grad * once,
            second_shift_grad * once,
            third_gain_grad * once,
            third_shift_grad * once,
            none,
            none,
        ]
    )
    *sums, tokens_grad, encoder_grad, norm_grads = sum_all(
        [
            expand_grad,
            reduce_grad,
            cross_grads,
            jnp.concatenate([cross_out_grad.astype(bf16), causal_out_grad.astype(bf16)]),
            causal_grad,
        ],
        (expand_far, reduce_far),
        [
            (4, 0, deep // 2, 0, 0),
            (4, deep // 2, deep // 2, 1, 0),
            *(
                [(3, 0, width, 0, 0), (3, width, width, 1, 0)]
                if width % (8 * place.dp) == 0
                else [(3, 0, 2 * width, 0, 0)]
            ),
            (2, 0, 3 * deep, 1, 1),
            (0, 0, expand_weight.shape[0], 0, 2),
            (1, 0, reduce_weight.shape[0], 1, 2),
        ],
        first_term.astype(bf16),
        (encoder_near, encoder_far),
        norm_grads,
        tokens_half,
        grad_res,
        first_gain,
        0,
    )
    (
        first_gain_grad,
        first_shift_grad,
        second_gain_grad,
        second_shift_grad,
        third_gain_grad,
        third_shift_grad,
    ) = (norm_grads[i] for i in range(6))
    sums = [total.astype(jnp.float32) if at != 2 and at != 3 else total for at, total in enumerate(sums)]
    expand_grad, reduce_grad = sums[:2]
    cross_key_grad, cross_value_grad, cross_query_grad = (
        sums[2][i * deep : (i + 1) * deep].astype(jnp.float32) for i in range(3)
    )
    cross_out_grad, causal_out_grad = sums[3][:width].astype(jnp.float32), sums[3][width:].astype(jnp.float32)
    causal_query_grad, causal_key_grad, causal_value_grad = (
        sums[4][:, i * width : (i + 1) * width] for i in range(3)
    )
    return (
        output,
        tokens_grad,
        encoder_grad,
        first_gain_grad,
        first_shift_grad,
        causal_query_grad,
        causal_key_grad,
        causal_value_grad,
        causal_out_grad,
        second_gain_grad,
        second_shift_grad,
        cross_query_grad,
        cross_key_grad,
        cross_value_grad,
        cross_out_grad,
        third_gain_grad,
        third_shift_grad,
        expand_grad,
        reduce_grad,
    )


def solution(mesh):
    in_specs = (
        P(("dp", "tensor"), None),
        P("dp", None),
        P("dp", None),
        P("dp", None),
        P("dp"),
        P(),
        P(),
        P(None, "tensor"),
        P(None, "tensor"),
        P(None, "tensor"),
        P("tensor", None),
        P(),
        P(),
        P(None, "tensor"),
        P(None, "tensor"),
        P(None, "tensor"),
        P("tensor", None),
        P(),
        P(),
        P(None, "tensor"),
        P("tensor", None),
        P(("dp", "tensor"), None),
    )
    out_specs = (
        P(("dp", "tensor"), None),
        P(("dp", "tensor"), None),
        P(("dp", "tensor"), None),
        P(),
        P(),
        P(None, "tensor"),
        P(None, "tensor"),
        P(None, "tensor"),
        P("tensor", None),
        P(),
        P(),
        P(None, "tensor"),
        P(None, "tensor"),
        P(None, "tensor"),
        P("tensor", None),
        P(),
        P(),
        P(None, "tensor"),
        P("tensor", None),
    )
    return jax.shard_map(
        on_device, mesh=mesh, in_specs=in_specs, out_specs=out_specs, check_vma=False
    )
```
